32 devices in a mesh: bpar: 2 (over y), tgt: 4 (over z), prj: 2 (over x), rep: 2 (over core).
Axes of the slice: x: 2, y: 2, z: 4, core: 2. Of those that a mesh axis runs over, the one named last changes fastest.
Arguments:
- tgt_basis: bfloat16 [2, 4096, 512], P(None, 'tgt', 'rep'), may hold values from -6 to 6
- proj_basis: bfloat16 [2, 8, 512, 512], P(None, None, 'prj', 'rep'), may hold values from -0.00390625 to 0.00390625
- quad_weight: float32 [1024], P(('bpar', 'rep')), parts along dimension 0, may hold values from 0.3 to 3
- tgt_energy: float32 [4096], P(('tgt', 'prj', 'rep')), may hold values from -1 to 1
- proj_energy: float32 [8, 512], P(('tgt', 'rep'), 'prj'), may hold values from -1 to 1
- pair_flags: int32 [8, 2], P('bpar'), parts along dimension 0, may hold values 0 or 1
- tile_counts: int32 [8, 2], P('bpar'), parts along dimension 0, may hold values from 1 to 4
- tgt_amp: float32 [8192, 128], P(('bpar', 'tgt', 'prj', 'rep')), parts along dimension 0, may hold values from -6 to 6
- proj_amp: float32 [16, 512, 128], P(('bpar', 'tgt', 'rep'), 'prj'), parts along dimension 0, may hold values from -6 to 6
Outputs:
- new_tgt_amp: float32 [8192, 128], P(('bpar', 'tgt', 'prj', 'rep')), parts along dimension 0
- new_proj_amp: float32 [16, 512, 128], P(('bpar', 'tgt', 'rep'), 'prj'), parts along dimension 0
The draws below stay inside these ranges and needn't reach their ends.
There are 2 independent parts, one for each index of `bpar`. The reference program is written for one: setup_inputs(seed, part) draws one part's arguments, and reference() takes and returns one part's arrays. A program takes and returns all parts, laid end to end along the dimension named above; an argument that names none is the same for every part. Nothing has to cross between parts.
All inputs are finite; a program needn't handle non-finite values.
Results may differ from the reference program's by a relative error of at most 0.02.
Values may be sent and summed in bfloat16 or wider, within the bound.
No kernel may reach another device: no remote copies, remote signals or barrier semaphores. Data moves between devices by JAX's collectives and lax.ppermute only.
A program may use at most 64 MiB of HBM per device.

```python
import math
import jax
import jax.numpy as jnp
from jax import lax

TSD = 1024
PSD = 2048
QUAD = 512
COLS = 64
QTILE = 128
TS = 4096
SUBS = 8
PROWS = 256
N_TGT = 4
N_PRJ = 2


def plant(values, rng, smallest, high):
    dims = values.shape
    spot = [jax.random.randint(jax.random.fold_in(rng, axis), (), 0, dims[axis]) for axis in range(len(dims))]
    values = values.at[tuple(spot)].set(smallest)
    longest = dims.index(max(dims))
    spot[longest] = (spot[longest] + 1) % dims[longest]
    return values.at[tuple(spot)].set(high)


def steps_of(rng, dims, pieces, smallest, largest):
    gain = 1.0
    for dim, shards_of in pieces:
        heights = jax.random.uniform(jax.random.fold_in(jax.random.fold_in(rng, 6), dim), (shards_of,), jnp.float32, smallest / len(pieces), largest / len(pieces))
        gain = gain * jnp.repeat(jnp.exp(heights), dims[dim] // shards_of).reshape((-1,) + (1,) * (len(dims) - 1 - dim))
    return gain


def gaussian(key, dims, spread, limit, split=(), held_as=jnp.bfloat16):
    loudness = steps_of(key, dims, split, -0.22, 0.18) if split else 1.0
    entries = jax.random.normal(key, dims, jnp.float32) * spread * loudness
    return jnp.minimum(jnp.maximum(entries, -limit), limit).astype(held_as)


def setup_inputs(seed: int = 0, part: int = 0) -> dict:
    keys = jax.random.split(jax.random.key(seed), 10)
    part_keys = jax.random.split(jax.random.fold_in(keys[9], part), 10)
    tgt_basis = gaussian(keys[0], (2, TS, QUAD), 1.0, 6.0, ((1, 4), (2, 2)))
    proj_basis = gaussian(keys[1], (2, SUBS, PROWS * N_PRJ, QUAD), (QUAD * PSD * N_PRJ) ** -0.5, 0.00390625, ((2, 2), (3, 2)))
    quad_weight = jnp.clip(jnp.exp(math.log(3.0) - 2.3025851 * jax.random.uniform(part_keys[2], (QUAD,), jnp.float32) ** steps_of(part_keys[2], (QUAD,), ((0, 2),), -0.2, 0.2)), 0.3, 3.0)
    tgt_energy = jnp.clip(jax.random.uniform(keys[3], (TS,), jnp.float32, -1.0, 1.0) * steps_of(keys[3], (TS,), ((0, 16),), -0.4, 0.0), -1.0, 1.0)
    proj_energy = jnp.clip(jax.random.uniform(keys[4], (SUBS, PROWS * N_PRJ), jnp.float32, -1.0, 1.0) * steps_of(keys[4], (SUBS, PROWS * N_PRJ), ((0, 8), (1, 2)), -0.4, 0.0), -1.0, 1.0)
    pair_flags = plant((jax.random.randint(part_keys[5], (N_TGT, N_PRJ), 0, 3) < 2).astype(jnp.int32), jax.random.fold_in(part_keys[5], 1), 0, 1)
    tile_counts = plant(jax.random.randint(part_keys[6], (N_TGT, N_PRJ), 1, 5), jax.random.fold_in(part_keys[6], 1), 1, 4).astype(jnp.int32)
    tgt_amp = gaussian(part_keys[7], (TS, 2 * COLS), 1.0, 6.0, ((0, 16),), jnp.float32)
    proj_amp = gaussian(part_keys[8], (SUBS, PROWS * N_PRJ, 2 * COLS), 1.0, 6.0, ((0, 8), (1, 2)), jnp.float32)
    return dict(tgt_basis=tgt_basis, proj_basis=proj_basis, quad_weight=quad_weight, tgt_energy=tgt_energy, proj_energy=proj_energy, pair_flags=pair_flags, tile_counts=tile_counts, tgt_amp=tgt_amp, proj_amp=proj_amp)


time_step = 0.4


def rotate(energy, state_now, coupled):
    half_cols = state_now.shape[-1] // 2
    summed = energy[..., None] * state_now + coupled
    return jnp.concatenate([summed[..., half_cols:], -summed[..., :half_cols]], axis=-1)


def round_trip(values):
    return lax.optimization_barrier(values.astype(jnp.bfloat16)).astype(jnp.float32)


def pairwise_product(form, left_side, right_side):
    return jnp.einsum(form, left_side, right_side, precision=lax.Precision.HIGHEST)


def coupled_rates(tgt_state, proj_state, tgt_energy, proj_energy, target_real, target_imag, projectile_part_real, projectile_part_imag, weights, live_state_mask):
    tgt_send = round_trip(tgt_state).reshape(N_TGT, TSD, 2 * COLS)
    proj_send = round_trip(proj_state).reshape(SUBS, N_PRJ, PROWS, 2 * COLS)
    amp_real = tgt_send[..., :COLS]
    amp_imag = tgt_send[..., COLS:]
    coef_real = pairwise_product('aiq,aik->aqk', target_real, amp_real) + pairwise_product('aiq,aik->aqk', target_imag, amp_imag)
    coef_imag = pairwise_product('aiq,aik->aqk', target_real, amp_imag) - pairwise_product('aiq,aik->aqk', target_imag, amp_real)
    target_coefficient = round_trip(weights[None, :, None] * jnp.concatenate([coef_real, coef_imag], axis=-1))
    projectile_amplitude_real = proj_send[..., :COLS]
    projectile_amplitude_imag = proj_send[..., COLS:]
    projectile_coefficient_real = pairwise_product('xyvi,xyvt->yit', projectile_part_real, projectile_amplitude_real) + pairwise_product('xyvi,xyvt->yit', projectile_part_imag, projectile_amplitude_imag)
    projectile_coefficient_imag = pairwise_product('xyvi,xyvt->yit', projectile_part_real, projectile_amplitude_imag) - pairwise_product('xyvi,xyvt->yit', projectile_part_imag, projectile_amplitude_real)
    projectile_coefficient = round_trip(weights[None, :, None] * jnp.concatenate([projectile_coefficient_real, projectile_coefficient_imag], axis=-1))
    target_field = pairwise_product('mhg,hge->mge', live_state_mask, projectile_coefficient)
    projectile_field = pairwise_product('nod,ndm->odm', live_state_mask, target_coefficient)
    field_real = target_field[..., :COLS]
    field_imag = target_field[..., COLS:]
    yt_real = pairwise_product('aiq,aqk->aik', target_real, field_real) - pairwise_product('aiq,aqk->aik', target_imag, field_imag)
    yt_imag = pairwise_product('aiq,aqk->aik', target_real, field_imag) + pairwise_product('aiq,aqk->aik', target_imag, field_real)
    tgt_coupled = jnp.concatenate([yt_real, yt_imag], axis=-1).reshape(TS, 2 * COLS)
    projectile_field_real = projectile_field[..., :COLS]
    projectile_field_imag = projectile_field[..., COLS:]
    midpoint_projectile_real = pairwise_product('lvpf,vfw->lvpw', projectile_part_real, projectile_field_real) - pairwise_product('lvpf,vfw->lvpw', projectile_part_imag, projectile_field_imag)
    midpoint_projectile_imag = pairwise_product('lvpf,vfw->lvpw', projectile_part_real, projectile_field_imag) + pairwise_product('lvpf,vfw->lvpw', projectile_part_imag, projectile_field_real)
    proj_coupled = jnp.concatenate([midpoint_projectile_real, midpoint_projectile_imag], axis=-1).reshape(SUBS, N_PRJ * PROWS, 2 * COLS)
    return rotate(tgt_energy, tgt_state, tgt_coupled), rotate(proj_energy, proj_state, proj_coupled)


def reference(tgt_basis, proj_basis, quad_weight, tgt_energy, proj_energy, pair_flags, tile_counts, tgt_amp, proj_amp):
    target_all = tgt_basis.astype(jnp.float32).reshape(2, N_TGT, TSD, QUAD)
    projectile_all = proj_basis.astype(jnp.float32).reshape(2, SUBS, N_PRJ, PROWS, QUAD)
    tile_of = jnp.arange(QUAD, dtype=jnp.int32) // QTILE
    live_state_mask = jnp.logical_and(tile_of[None, None, :] < tile_counts[:, :, None], pair_flags[:, :, None] > 0).astype(jnp.float32)

    def rates_at(tgt_state, proj_state):
        return coupled_rates(tgt_state, proj_state, tgt_energy, proj_energy, target_all[0], target_all[1], projectile_all[0], projectile_all[1], quad_weight, live_state_mask)

    tgt_rate, proj_rate = rates_at(tgt_amp, proj_amp)
    tgt_half = tgt_amp + 0.5 * time_step * tgt_rate
    proj_half = proj_amp + 0.5 * time_step * proj_rate
    tgt_rate, proj_rate = rates_at(tgt_half, proj_half)
    return tgt_amp + time_step * tgt_rate, proj_amp + time_step * proj_rate
```

```python
import functools

import jax
import jax.numpy as jnp
from jax import lax
from jax.experimental import pallas as pl
from jax.experimental.pallas import tpu as pltpu
from jax.sharding import PartitionSpec as P

time_step = 0.4
half_step = 0.5 * time_step
PEERS = ("tgt", "prj")
HBM = pl.BlockSpec(memory_space=pl.ANY)
VMEM = pl.BlockSpec(memory_space=pltpu.VMEM)
SMEM = pl.BlockSpec(memory_space=pltpu.SMEM)


def turned(block):
    half = block.shape[0] // 2
    return jnp.concatenate([block[half:], -block[:half]], axis=0)


def load_basis(tgt_hbm, proj_hbm, tgt_buf, proj_buf, sems):
    rows = tgt_buf.shape[1]
    groups = proj_buf.shape[1]
    row_start = pl.multiple_of(lax.axis_index("prj") * rows, rows)
    group_start = lax.axis_index("tgt") * groups
    copies = []
    for part in range(2):
        copies.append(
            pltpu.make_async_copy(
                tgt_hbm.at[part, pl.ds(row_start, rows)], tgt_buf.at[part], sems.at[part]
            )
        )
        copies.append(
            pltpu.make_async_copy(
                proj_hbm.at[part, pl.ds(group_start, groups)], proj_buf.at[part], sems.at[2 + part]
            )
        )
    for copy in copies:
        copy.start()
    return copies


def views(tgt_buf, proj_buf):
    rows = tgt_buf.shape[1] // 2

    def tgt_view(part, core):
        return tgt_buf[part, pl.ds(pl.multiple_of(core * rows, rows), rows), :]

    def proj_view(part, core):
        return proj_buf[part, core]

    return tgt_view, proj_view


def project(view, states):
    total = None
    for core, amp in states:
        term = jnp.dot(
            amp.astype(jnp.bfloat16), view(0, core), preferred_element_type=jnp.float32
        ) + jnp.dot(
            turned(amp).astype(jnp.bfloat16), view(1, core), preferred_element_type=jnp.float32
        )
        total = term if total is None else total + term
    return total


def expand(view, core, field, turned_field):
    contract = (((1,), (1,)), ((), ()))
    return lax.dot_general(
        turned_field, view(0, core), contract, preferred_element_type=jnp.float32
    ) + lax.dot_general(field, view(1, core), contract, preferred_element_type=jnp.float32)


def spread(out_ref, kind, block):
    peers, _, cols, _ = out_ref.shape
    for peer in range(peers):
        out_ref[peer, kind] = block[peer * cols : (peer + 1) * cols].astype(jnp.bfloat16)


def collect(in_ref, kind):
    peers, _, cols, _ = in_ref.shape
    block = jnp.concatenate([in_ref[peer, kind].astype(jnp.float32) for peer in range(peers)], axis=0)
    return block.astype(jnp.bfloat16), turned(block).astype(jnp.bfloat16)


def first_kernel(
    tgt_hbm, proj_hbm, weight, tgt_own, tgt_other, proj_own, proj_other, out_ref, tgt_buf, proj_buf, sems
):
    copies = load_basis(tgt_hbm, proj_hbm, tgt_buf, proj_buf, sems)
    core = lax.axis_index("rep")
    tgt_view, proj_view = views(tgt_buf, proj_buf)
    weights = weight[...][None, :]
    tgt_states = [(core, tgt_own[...].T), (1 - core, tgt_other[...].T)]
    proj_states = [(core, proj_own[0].T), (1 - core, proj_other[0].T)]
    for copy in copies:
        copy.wait()
    spread(out_ref, 0, weights * project(tgt_view, tgt_states))
    spread(out_ref, 1, weights * project(proj_view, proj_states))


def mask_kernel(flags, counts, in_ref, out_ref):
    n_tgt, n_prj = flags.shape
    core = lax.axis_index("rep")
    width = in_ref.shape[-1] // 2
    for tile in range(2):
        lanes = pl.ds(tile * width, width)
        tile_id = 2 * core + tile

        def active(a, b):
            live = jnp.logical_and(flags[a, b] > 0, tile_id < counts[a, b])
            return jnp.where(live, 1.0, 0.0).astype(jnp.float32)

        def read(a, b, kind):
            return in_ref[a * n_prj + b, kind, :, lanes].astype(jnp.float32)

        zt = [sum(read(a, b, 0) for b in range(n_prj)) for a in range(n_tgt)]
        zp = [sum(read(a, b, 1) for a in range(n_tgt)) for b in range(n_prj)]
        gates = [[active(a, b) for b in range(n_prj)] for a in range(n_tgt)]
        for a in range(n_tgt):
            field = sum(gates[a][b] * zp[b] for b in range(n_prj)).astype(jnp.bfloat16)
            for b in range(n_prj):
                out_ref[a * n_prj + b, 0, :, lanes] = field
        for b in range(n_prj):
            field = sum(gates[a][b] * zt[a] for a in range(n_tgt)).astype(jnp.bfloat16)
            for a in range(n_tgt):
                out_ref[a * n_prj + b, 1, :, lanes] = field


def half_kernel(
    tgt_hbm, proj_hbm, in_ref, tgt_energy, proj_energy, tgt_own, proj_own, send, keep, tgt_buf, proj_buf, sems
):
    copies = load_basis(tgt_hbm, proj_hbm, tgt_buf, proj_buf, sems)
    core = lax.axis_index("rep")
    amps = (tgt_own[...].T, proj_own[0].T)
    energies = (tgt_energy[...][None, :], proj_energy[...])
    fields = (collect(in_ref, 0), collect(in_ref, 1))
    for copy in copies:
        copy.wait()
    for kind, view in enumerate(views(tgt_buf, proj_buf)):
        field, turned_field = fields[kind]
        amp = amps[kind]
        own = amp + half_step * (
            energies[kind] * turned(amp) + expand(view, core, field, turned_field)
        )
        other = half_step * expand(view, 1 - core, field, turned_field)
        keep[kind, 0] = own
        keep[kind, 1] = other
        send[kind, 0] = own.astype(jnp.bfloat16)
        send[kind, 1] = other.astype(jnp.bfloat16)


def second_kernel(
    tgt_hbm, proj_hbm, weight, keep, received, out_ref, half_ref, tgt_buf, proj_buf, sems
):
    copies = load_basis(tgt_hbm, proj_hbm, tgt_buf, proj_buf, sems)
    core = lax.axis_index("rep")
    weights = weight[...][None, :]
    for copy in copies:
        copy.wait()
    for kind, view in enumerate(views(tgt_buf, proj_buf)):
        own = keep[kind, 0] + received[kind, 1].astype(jnp.float32)
        other = keep[kind, 1] + received[kind, 0].astype(jnp.float32)
        half_ref[kind] = own
        spread(out_ref, kind, weights * project(view, [(core, own), (1 - core, other)]))


def last_kernel(
    tgt_hbm,
    proj_hbm,
    in_ref,
    tgt_energy,
    proj_energy,
    tgt_own,
    proj_own,
    half_ref,
    send,
    tgt_keep,
    proj_keep,
    tgt_buf,
    proj_buf,
    sems,
):
    copies = load_basis(tgt_hbm, proj_hbm, tgt_buf, proj_buf, sems)
    core = lax.axis_index("rep")
    energies = (tgt_energy[...][None, :], proj_energy[...])
    fields = (collect(in_ref, 0), collect(in_ref, 1))
    for copy in copies:
        copy.wait()
    for kind, view in enumerate(views(tgt_buf, proj_buf)):
        field, turned_field = fields[kind]
        change = time_step * (
            energies[kind] * turned(half_ref[kind]) + expand(view, core, field, turned_field)
        )
        if kind == 0:
            tgt_keep[...] = tgt_own[...] + change.T
        else:
            proj_keep[0] = proj_own[0] + change.T
        other = time_step * expand(view, 1 - core, field, turned_field)
        send[kind] = other.T.astype(jnp.bfloat16)


def shards(
    tgt_basis,
    proj_basis,
    quad_weight,
    tgt_energy,
    proj_energy,
    pair_flags,
    tile_counts,
    tgt_amp,
    proj_amp,
):
    peers = lax.axis_size(PEERS)
    points = quad_weight.shape[0]
    rows, two_cols = tgt_amp.shape
    group_rows = proj_amp.shape[1]
    basis_scratch = [
        pltpu.VMEM((2, 2 * rows, points), jnp.bfloat16),
        pltpu.VMEM((2, 2, group_rows, points), jnp.bfloat16),
        pltpu.SemaphoreType.DMA((4,)),
    ]
    pieces = jax.ShapeDtypeStruct((peers, 2, two_cols // peers, points), jnp.bfloat16)

    def other_core(block):
        return lax.ppermute(block, "rep", [(0, 1), (1, 0)])

    def exchange(block):
        return lax.all_to_all(block, PEERS, split_axis=0, concat_axis=0, tiled=True)

    def masked(block):
        return pl.pallas_call(
            mask_kernel, out_shape=pieces, in_specs=[SMEM, SMEM, VMEM], out_specs=VMEM
        )(pair_flags, tile_counts, block)

    first = pl.pallas_call(
        first_kernel,
        out_shape=pieces,
        in_specs=[HBM, HBM] + [VMEM] * 5,
        out_specs=VMEM,
        scratch_shapes=basis_scratch,
    )(tgt_basis, proj_basis, quad_weight, tgt_amp, other_core(tgt_amp), proj_amp, other_core(proj_amp))
    fields = exchange(masked(exchange(first)))

    state = (2, 2, two_cols, rows)
    send, keep = pl.pallas_call(
        half_kernel,
        out_shape=(
            jax.ShapeDtypeStruct(state, jnp.bfloat16),
            jax.ShapeDtypeStruct(state, jnp.float32),
        ),
        in_specs=[HBM, HBM] + [VMEM] * 5,
        out_specs=(VMEM, VMEM),
        scratch_shapes=basis_scratch,
    )(tgt_basis, proj_basis, fields, tgt_energy, proj_energy, tgt_amp, proj_amp)
    second, half = pl.pallas_call(
        second_kernel,
        out_shape=(pieces, jax.ShapeDtypeStruct((2, two_cols, rows), jnp.float32)),
        in_specs=[HBM, HBM] + [VMEM] * 3,
        out_specs=(VMEM, VMEM),
        scratch_shapes=basis_scratch,
    )(tgt_basis, proj_basis, quad_weight, keep, other_core(send))
    fields = exchange(masked(exchange(second)))
    send, tgt_keep, proj_keep = pl.pallas_call(
        last_kernel,
        out_shape=(
            jax.ShapeDtypeStruct((2, rows, two_cols), jnp.bfloat16),
            jax.ShapeDtypeStruct(tgt_amp.shape, jnp.float32),
            jax.ShapeDtypeStruct(proj_amp.shape, jnp.float32),
        ),
        in_specs=[HBM, HBM] + [VMEM] * 6,
        out_specs=(VMEM,) * 3,
        scratch_shapes=basis_scratch,
    )(tgt_basis, proj_basis, fields, tgt_energy, proj_energy, tgt_amp, proj_amp, half)
    received = other_core(send).astype(jnp.float32)
    return tgt_keep + received[0], proj_keep + received[1:]


def solution(mesh):
    in_specs = (
        P(None, "tgt", "rep"),
        P(None, None, "prj", "rep"),
        P(("bpar", "rep")),
        P(("tgt", "prj", "rep")),
        P(("tgt", "rep"), "prj"),
        P("bpar", None),
        P("bpar", None),
        P(("bpar", "tgt", "prj", "rep"), None),
        P(("bpar", "tgt", "rep"), "prj", None),
    )
    out_specs = (P(("bpar", "tgt", "prj", "rep"), None), P(("bpar", "tgt", "rep"), "prj", None))
    return jax.shard_map(shards, mesh=mesh, in_specs=in_specs, out_specs=out_specs, check_vma=False)
```

```python
import functools

import jax
import jax.numpy as jnp
from jax import lax
from jax.experimental import pallas as pl
from jax.experimental.pallas import tpu as pltpu
from jax.sharding import PartitionSpec as P

time_step = 0.4
half_step = 0.5 * time_step
PEERS = ("tgt", "prj")
VMEM_LIMIT = 8 * 1024 * 1024
HBM = pl.BlockSpec(memory_space=pl.ANY)
VMEM = pl.BlockSpec(memory_space=pltpu.VMEM)
SMEM = pl.BlockSpec(memory_space=pltpu.SMEM)


def turned(block):
    half = block.shape[0] // 2
    return jnp.concatenate([block[half:], -block[:half]], axis=0)


def load_basis(tgt_hbm, proj_hbm, tgt_buf, proj_buf, sems):
    rows = tgt_buf.shape[1]
    groups = proj_buf.shape[1]
    row_start = pl.multiple_of(lax.axis_index("prj") * rows, rows)
    group_start = lax.axis_index("tgt") * groups
    copies = []
    for part in range(2):
        copies.append(
            pltpu.make_async_copy(
                tgt_hbm.at[part, pl.ds(row_start, rows)], tgt_buf.at[part], sems.at[part]
            )
        )
        copies.append(
            pltpu.make_async_copy(
                proj_hbm.at[part, pl.ds(group_start, groups)], proj_buf.at[part], sems.at[2 + part]
            )
        )
    for copy in copies:
        copy.start()
    return copies


def views(tgt_buf, proj_buf):
    rows = tgt_buf.shape[1] // 2

    def tgt_view(part, core):
        return tgt_buf[part, pl.ds(pl.multiple_of(core * rows, rows), rows), :]

    def proj_view(part, core):
        return proj_buf[part, core]

    return tgt_view, proj_view


def project(view, states):
    total = None
    for core, amp in states:
        term = jnp.dot(
            amp.astype(jnp.bfloat16), view(0, core), preferred_element_type=jnp.float32
        ) + jnp.dot(
            turned(amp).astype(jnp.bfloat16), view(1, core), preferred_element_type=jnp.float32
        )
        total = term if total is None else total + term
    return total


def expand(view, core, field, turned_field):
    contract = (((1,), (1,)), ((), ()))
    return lax.dot_general(
        turned_field, view(0, core), contract, preferred_element_type=jnp.float32
    ) + lax.dot_general(field, view(1, core), contract, preferred_element_type=jnp.float32)


def peer_rows(piece, cols):
    me = lax.axis_index("tgt") * lax.axis_size("prj") + lax.axis_index("prj")
    return pl.ds(pl.multiple_of(jnp.bitwise_xor(me, piece) * cols, cols), cols)


def spread(out_refs, kind, block, rows_buf):
    rows_buf[kind] = block
    for piece, out_ref in enumerate(out_refs):
        rows = peer_rows(piece, out_ref.shape[1])
        out_ref[kind] = rows_buf[kind, rows, :].astype(jnp.bfloat16)


def collect(in_refs, kind, rows_buf):
    for piece, in_ref in enumerate(in_refs):
        rows = peer_rows(piece, in_ref.shape[1])
        rows_buf[kind, rows, :] = in_ref[kind].astype(jnp.float32)
    block = rows_buf[kind]
    return block.astype(jnp.bfloat16), turned(block).astype(jnp.bfloat16)


def first_kernel(
    tgt_hbm, proj_hbm, weight, tgt_own, tgt_other, proj_own, proj_other, out_refs, tgt_buf, proj_buf, sems, rows_buf
):
    copies = load_basis(tgt_hbm, proj_hbm, tgt_buf, proj_buf, sems)
    core = lax.axis_index("rep")
    tgt_view, proj_view = views(tgt_buf, proj_buf)
    weights = weight[...][None, :]
    tgt_states = [(core, tgt_own[...].T), (1 - core, tgt_other[...].T)]
    proj_states = [(core, proj_own[0].T), (1 - core, proj_other[0].T)]
    for copy in copies:
        copy.wait()
    spread(out_refs, 0, weights * project(tgt_view, tgt_states), rows_buf)
    spread(out_refs, 1, weights * project(proj_view, proj_states), rows_buf)


def mask_kernel(flags, counts, in_refs, out_refs):
    n_tgt, n_prj = flags.shape
    core = lax.axis_index("rep")
    tgt_index = lax.axis_index("tgt")
    prj_index = lax.axis_index("prj")
    width = in_refs[0].shape[-1] // 2
    for tile in range(2):
        lanes = pl.ds(tile * width, width)
        tile_id = 2 * core + tile

        def active(a, b):
            a = jnp.bitwise_xor(tgt_index, a)
            b = jnp.bitwise_xor(prj_index, b)
            live = jnp.logical_and(flags[a, b] > 0, tile_id < counts[a, b])
            return jnp.where(live, 1.0, 0.0).astype(jnp.float32)

        def read(a, b, kind):
            return in_refs[a * n_prj + b][kind, :, lanes].astype(jnp.float32)

        zt = [sum(read(a, b, 0) for b in range(n_prj)) for a in range(n_tgt)]
        zp = [sum(read(a, b, 1) for a in range(n_tgt)) for b in range(n_prj)]
        gates = [[active(a, b) for b in range(n_prj)] for a in range(n_tgt)]
        for a in range(n_tgt):
            field = sum(gates[a][b] * zp[b] for b in range(n_prj)).astype(jnp.bfloat16)
            for b in range(n_prj):
                out_refs[a * n_prj + b][0, :, lanes] = field
        for b in range(n_prj):
            field = sum(gates[a][b] * zt[a] for a in range(n_tgt)).astype(jnp.bfloat16)
            for a in range(n_tgt):
                out_refs[a * n_prj + b][1, :, lanes] = field


def half_kernel(
    tgt_hbm, proj_hbm, in_refs, tgt_energy, proj_energy, tgt_own, proj_own, send, keep, tgt_buf, proj_buf, sems, rows_buf
):
    copies = load_basis(tgt_hbm, proj_hbm, tgt_buf, proj_buf, sems)
    core = lax.axis_index("rep")
    amps = (tgt_own[...].T, proj_own[0].T)
    energies = (tgt_energy[...][None, :], proj_energy[...])
    fields = (collect(in_refs, 0, rows_buf), collect(in_refs, 1, rows_buf))
    for copy in copies:
        copy.wait()
    for kind, view in enumerate(views(tgt_buf, proj_buf)):
        field, turned_field = fields[kind]
        amp = amps[kind]
        own = amp + half_step * (
            energies[kind] * turned(amp) + expand(view, core, field, turned_field)
        )
        other = half_step * expand(view, 1 - core, field, turned_field)
        keep[kind, 0] = own
        keep[kind, 1] = other
        send[kind, 0] = own.astype(jnp.bfloat16)
        send[kind, 1] = other.astype(jnp.bfloat16)


def second_kernel(
    tgt_hbm, proj_hbm, weight, keep, received, out_refs, half_ref, tgt_buf, proj_buf, sems, rows_buf
):
    copies = load_basis(tgt_hbm, proj_hbm, tgt_buf, proj_buf, sems)
    core = lax.axis_index("rep")
    weights = weight[...][None, :]
    for copy in copies:
        copy.wait()
    for kind, view in enumerate(views(tgt_buf, proj_buf)):
        own = keep[kind, 0] + received[kind, 1].astype(jnp.float32)
        other = keep[kind, 1] + received[kind, 0].astype(jnp.float32)
        half_ref[kind] = own
        spread(out_refs, kind, weights * project(view, [(core, own), (1 - core, other)]), rows_buf)


def last_kernel(
    tgt_hbm,
    proj_hbm,
    in_refs,
    tgt_energy,
    proj_energy,
    tgt_own,
    proj_own,
    half_ref,
    send,
    tgt_keep,
    proj_keep,
    tgt_buf,
    proj_buf,
    sems,
    rows_buf,
):
    copies = load_basis(tgt_hbm, proj_hbm, tgt_buf, proj_buf, sems)
    core = lax.axis_index("rep")
    energies = (tgt_energy[...][None, :], proj_energy[...])
    fields = (collect(in_refs, 0, rows_buf), collect(in_refs, 1, rows_buf))
    for copy in copies:
        copy.wait()
    for kind, view in enumerate(views(tgt_buf, proj_buf)):
        field, turned_field = fields[kind]
        change = time_step * (
            energies[kind] * turned(half_ref[kind]) + expand(view, core, field, turned_field)
        )
        if kind == 0:
            tgt_keep[...] = tgt_own[...] + change.T
        else:
            proj_keep[0] = proj_own[0] + change.T
        other = time_step * expand(view, 1 - core, field, turned_field)
        send[kind] = other.T.astype(jnp.bfloat16)


def shards(
    tgt_basis,
    proj_basis,
    quad_weight,
    tgt_energy,
    proj_energy,
    pair_flags,
    tile_counts,
    tgt_amp,
    proj_amp,
):
    peers = lax.axis_size(PEERS)
    points = quad_weight.shape[0]
    rows, two_cols = tgt_amp.shape
    group_rows = proj_amp.shape[1]
    cols = two_cols // peers
    scratch = [
        pltpu.VMEM((2, 2 * rows, points), jnp.bfloat16),
        pltpu.VMEM((2, 2, group_rows, points), jnp.bfloat16),
        pltpu.SemaphoreType.DMA((4,)),
        pltpu.VMEM((2, two_cols, points), jnp.float32),
    ]
    pieces = [jax.ShapeDtypeStruct((2, cols, points), jnp.bfloat16)] * peers
    pieces_spec = [VMEM] * peers

    def call(kernel, out_shape, in_specs, out_specs, scratch_shapes=()):
        specs = in_specs + list(out_specs) + [None] * len(scratch_shapes)

        def with_lists(*refs):
            refs = jax.tree.leaves(refs)
            args = [
                [refs.pop(0) for _ in spec] if isinstance(spec, list) else refs.pop(0) for spec in specs
            ]
            kernel(*args)

        return pl.pallas_call(
            with_lists,
            out_shape=out_shape,
            in_specs=in_specs,
            out_specs=out_specs,
            scratch_shapes=scratch_shapes,
            compiler_params=pltpu.CompilerParams(vmem_limit_bytes=VMEM_LIMIT),
        )

    def other_core(block):
        return lax.ppermute(block, "rep", [(0, 1), (1, 0)])

    def exchange(blocks):
        return [
            block if piece == 0 else lax.ppermute(block, PEERS, [(me, me ^ piece) for me in range(peers)])
            for piece, block in enumerate(blocks)
        ]

    def masked(blocks):
        return call(mask_kernel, [pieces], [SMEM, SMEM, pieces_spec], [pieces_spec])(
            pair_flags, tile_counts, blocks
        )[0]

    (first,) = call(first_kernel, [pieces], [HBM, HBM] + [VMEM] * 5, [pieces_spec], scratch)(
        tgt_basis, proj_basis, quad_weight, tgt_amp, other_core(tgt_amp), proj_amp, other_core(proj_amp)
    )
    fields = exchange(masked(exchange(first)))

    state = (2, 2, two_cols, rows)
    send, keep = call(
        half_kernel,
        (jax.ShapeDtypeStruct(state, jnp.bfloat16), jax.ShapeDtypeStruct(state, jnp.float32)),
        [HBM, HBM, pieces_spec] + [VMEM] * 4,
        (VMEM, VMEM),
        scratch,
    )(tgt_basis, proj_basis, fields, tgt_energy, proj_energy, tgt_amp, proj_amp)
    second, half = call(
        second_kernel,
        (pieces, jax.ShapeDtypeStruct((2, two_cols, rows), jnp.float32)),
        [HBM, HBM] + [VMEM] * 3,
        (pieces_spec, VMEM),
        scratch,
    )(tgt_basis, proj_basis, quad_weight, keep, other_core(send))
    fields = exchange(masked(exchange(second)))
    send, tgt_keep, proj_keep = call(
        last_kernel,
        (
            jax.ShapeDtypeStruct((2, rows, two_cols), jnp.bfloat16),
            jax.ShapeDtypeStruct(tgt_amp.shape, jnp.float32),
            jax.ShapeDtypeStruct(proj_amp.shape, jnp.float32),
        ),
        [HBM, HBM, pieces_spec] + [VMEM] * 5,
        (VMEM,) * 3,
        scratch,
    )(tgt_basis, proj_basis, fields, tgt_energy, proj_energy, tgt_amp, proj_amp, half)
    received = other_core(send).astype(jnp.float32)
    return tgt_keep + received[0], proj_keep + received[1:]


def solution(mesh):
    in_specs = (
        P(None, "tgt", "rep"),
        P(None, None, "prj", "rep"),
        P(("bpar", "rep")),
        P(("tgt", "prj", "rep")),
        P(("tgt", "rep"), "prj"),
        P("bpar", None),
        P("bpar", None),
        P(("bpar", "tgt", "prj", "rep"), None),
        P(("bpar", "tgt", "rep"), "prj", None),
    )
    out_specs = (P(("bpar", "tgt", "prj", "rep"), None), P(("bpar", "tgt", "rep"), "prj", None))
    return jax.shard_map(shards, mesh=mesh, in_specs=in_specs, out_specs=out_specs, check_vma=False)
```

```python
import jax
import jax.numpy as jnp
from jax import lax
from jax.experimental import pallas as pl
from jax.experimental.pallas import tpu as pltpu
from jax.sharding import PartitionSpec as P

time_step = 0.4
half_step = 0.5 * time_step
VMEM_LIMIT = 8 * 1024 * 1024
HBM = pl.BlockSpec(memory_space=pl.ANY)
VMEM = pl.BlockSpec(memory_space=pltpu.VMEM)
SMEM = pl.BlockSpec(memory_space=pltpu.SMEM)


def turned(block):
    half = block.shape[0] // 2
    return jnp.concatenate([block[half:], -block[:half]], axis=0)


def bf16(block):
    return block.astype(jnp.bfloat16)


def f32(block):
    return block.astype(jnp.float32)


def views(tgt_buf, proj_buf):
    rows = tgt_buf.shape[1] // 2

    def tgt_view(part, core):
        return tgt_buf[part, pl.ds(pl.multiple_of(core * rows, rows), rows), :]

    def proj_view(part, core):
        return proj_buf[part, core]

    return tgt_view, proj_view


def project(view, core, amp):
    return jnp.dot(
        bf16(amp), view(0, core), preferred_element_type=jnp.float32
    ) + jnp.dot(bf16(turned(amp)), view(1, core), preferred_element_type=jnp.float32)


def expand(view, core, field, turned_field):
    contract = (((1,), (1,)), ((), ()))
    return lax.dot_general(
        turned_field, view(0, core), contract, preferred_element_type=jnp.float32
    ) + lax.dot_general(field, view(1, core), contract, preferred_element_type=jnp.float32)


def load_kernel(
    flags,
    counts,
    tgt_hbm,
    proj_hbm,
    tgt_energy,
    proj_energy,
    tgt_own,
    proj_own,
    tgt_buf,
    proj_buf,
    gates,
    start_ref,
    part_ref,
    sems,
):
    n_prj, n_tgt = flags.shape
    core = lax.axis_index("rep")
    tgt_index = lax.axis_index("tgt")
    prj_index = lax.axis_index("prj")
    rows = tgt_buf.shape[1]
    groups = proj_buf.shape[1]
    row_start = pl.multiple_of(prj_index * rows, rows)
    group_start = tgt_index * groups
    copies = []
    for part in range(2):
        copies.append(
            pltpu.make_async_copy(
                tgt_hbm.at[part, pl.ds(row_start, rows)], tgt_buf.at[part], sems.at[part]
            )
        )
        copies.append(
            pltpu.make_async_copy(
                proj_hbm.at[part, pl.ds(group_start, groups)], proj_buf.at[part], sems.at[2 + part]
            )
        )
    for copy in copies:
        copy.start()

    width = gates.shape[1] // 2

    def write_gate(slot, a, b):
        for tile in range(2):
            live = jnp.logical_and(flags[b, a] > 0, 2 * core + tile < counts[b, a])
            value = jnp.where(live, 1.0, 0.0).astype(jnp.float32)
            gates[slot : slot + 1, tile * width : (tile + 1) * width] = jnp.full(
                (1, width), value, jnp.float32
            )

    for a in range(n_tgt):
        write_gate(a, a, prj_index)
    for b in range(n_prj):
        write_gate(n_tgt + b, tgt_index, jnp.bitwise_xor(prj_index, b))

    amps = (tgt_own[...].T, proj_own[0].T)
    energies = (tgt_energy[...][None, :], proj_energy[...])
    for kind in range(2):
        start_ref[kind] = amps[kind] + half_step * (energies[kind] * turned(amps[kind]))
    for copy in copies:
        copy.wait()
    for kind, view in enumerate(views(tgt_buf, proj_buf)):
        part_ref[kind] = project(view, core, amps[kind])


def first_kernel(tgt_buf, proj_buf, weight, part_ref, tgt_other, proj_other, zt_ref, zp_ref):
    other = 1 - lax.axis_index("rep")
    weights = weight[...][None, :]
    tgt_view, proj_view = views(tgt_buf, proj_buf)
    zt_ref[...] = bf16(weights * (part_ref[0] + project(tgt_view, other, tgt_other[...].T)))
    zp_ref[...] = bf16(weights * (part_ref[1] + project(proj_view, other, proj_other[0].T)))


def sum_kernel(zt_parts, zp_parts, zt_ref, zp_ref):
    zt_ref[...] = bf16(sum(f32(part[...]) for part in zt_parts))
    zp_ref[...] = bf16(sum(f32(zp_parts[a]) for a in range(zp_parts.shape[0])))


def fields_of(gates, zt_all, zp_parts):
    n_tgt = zt_all.shape[0]
    tgt_field = sum(gates[n_tgt + b : n_tgt + b + 1, :] * f32(part[...]) for b, part in enumerate(zp_parts))
    proj_field = sum(gates[a : a + 1, :] * f32(zt_all[a]) for a in range(n_tgt))
    return [(bf16(field), bf16(turned(field))) for field in (tgt_field, proj_field)]


def half_kernel(tgt_buf, proj_buf, gates, zt_all, zp_parts, start_ref, send, keep):
    core = lax.axis_index("rep")
    fields = fields_of(gates, zt_all, zp_parts)
    for kind, view in enumerate(views(tgt_buf, proj_buf)):
        own = start_ref[kind] + half_step * expand(view, core, *fields[kind])
        other = half_step * expand(view, 1 - core, *fields[kind])
        keep[kind, 0] = own
        keep[kind, 1] = other
        send[kind, 0] = bf16(own)
        send[kind, 1] = bf16(other)


def second_kernel(tgt_buf, proj_buf, weight, keep, received, zt_ref, zp_ref, half_ref):
    core = lax.axis_index("rep")
    weights = weight[...][None, :]
    for kind, view in enumerate(views(tgt_buf, proj_buf)):
        own = keep[kind, 0] + f32(received[kind, 1])
        other = keep[kind, 1] + f32(received[kind, 0])
        half_ref[kind] = own
        total = project(view, core, own) + project(view, 1 - core, other)
        (zt_ref, zp_ref)[kind][...] = bf16(weights * total)


def last_kernel(
    tgt_buf,
    proj_buf,
    gates,
    zt_all,
    zp_parts,
    tgt_energy,
    proj_energy,
    tgt_own,
    proj_own,
    half_ref,
    send,
    tgt_keep,
    proj_keep,
):
    core = lax.axis_index("rep")
    energies = (tgt_energy[...][None, :], proj_energy[...])
    fields = fields_of(gates, zt_all, zp_parts)
    for kind, view in enumerate(views(tgt_buf, proj_buf)):
        send[kind] = bf16((time_step * expand(view, 1 - core, *fields[kind])).T)
        change = time_step * (
            energies[kind] * turned(half_ref[kind]) + expand(view, core, *fields[kind])
        )
        if kind == 0:
            tgt_keep[...] = tgt_own[...] + change.T
        else:
            proj_keep[...] = proj_own[0] + change.T


def add_kernel(tgt_keep, proj_keep, received, new_tgt, new_proj):
    new_tgt[...] = tgt_keep[...] + f32(received[0])
    new_proj[0] = proj_keep[...] + f32(received[1])


def shards(
    tgt_basis,
    proj_basis,
    quad_weight,
    tgt_energy,
    proj_energy,
    pair_flags,
    tile_counts,
    tgt_amp,
    proj_amp,
):
    n_tgt = lax.axis_size("tgt")
    n_prj = lax.axis_size("prj")
    points = quad_weight.shape[0]
    rows, two_cols = tgt_amp.shape
    group_rows = proj_amp.shape[1]

    def call(kernel, out_shape, in_specs, scratch_shapes=(), cost=None):
        specs = list(in_specs) + [None] * (len(out_shape) + len(scratch_shapes))

        def with_lists(*refs):
            refs = jax.tree.leaves(refs)
            args = [
                [refs.pop(0) for _ in spec] if isinstance(spec, list) else refs.pop(0) for spec in specs
            ]
            kernel(*args)

        return pl.pallas_call(
            with_lists,
            out_shape=out_shape,
            in_specs=in_specs,
            out_specs=[VMEM] * len(out_shape),
            scratch_shapes=scratch_shapes,
            cost_estimate=cost,
            compiler_params=pltpu.CompilerParams(vmem_limit_bytes=VMEM_LIMIT),
        )

    def in_vmem(shape, dtype):
        return pltpu.VMEM(shape, dtype)

    def other_core(block):
        return lax.ppermute(block, "rep", [(0, 1), (1, 0)])

    def over_prj(block):
        return [block] + [
            lax.ppermute(block, "prj", [(me, me ^ flip) for me in range(n_prj)])
            for flip in range(1, n_prj)
        ]

    def over_tgt(block):
        return lax.all_gather(block, "tgt", axis=0, tiled=False)

    coefs = in_vmem((two_cols, points), jnp.bfloat16)
    states = in_vmem((2, two_cols, rows), jnp.float32)

    def reduced(zt, zp):
        zt_parts, zp_parts = over_prj(zt), over_tgt(zp)
        zt, zp = call(sum_kernel, [coefs, coefs], [[VMEM] * n_prj, VMEM])(zt_parts, zp_parts)
        zp_parts, zt_all = over_prj(zp), over_tgt(zt)
        return zt_all, zp_parts

    tgt_other, proj_other = other_core(tgt_amp), other_core(proj_amp)
    tgt_buf, proj_buf, gates, start, part = call(
        load_kernel,
        [
            in_vmem((2, 2 * rows, points), jnp.bfloat16),
            in_vmem((2, 2, group_rows, points), jnp.bfloat16),
            in_vmem((n_tgt + n_prj, points), jnp.float32),
            states,
            in_vmem((2, two_cols, points), jnp.float32),
        ],
        [SMEM, SMEM, HBM, HBM] + [VMEM] * 4,
        [pltpu.SemaphoreType.DMA((4,))],
        pl.CostEstimate(flops=2 * 4 * rows * two_cols * points, bytes_accessed=3 * 1024 * 1024, transcendentals=0),
    )(
        pair_flags.T,
        tile_counts.T,
        pltpu.with_memory_space_constraint(tgt_basis, pltpu.HBM),
        pltpu.with_memory_space_constraint(proj_basis, pltpu.HBM),
        tgt_energy,
        proj_energy,
        tgt_amp,
        proj_amp,
    )
    zt, zp = call(first_kernel, [coefs, coefs], [VMEM] * 6)(
        tgt_buf, proj_buf, quad_weight, part, tgt_other, proj_other
    )
    zt_all, zp_parts = reduced(zt, zp)
    pair = (2, 2, two_cols, rows)
    lists = [VMEM] * 4 + [[VMEM] * n_prj]
    send, keep = call(
        half_kernel, [in_vmem(pair, jnp.bfloat16), in_vmem(pair, jnp.float32)], lists + [VMEM]
    )(tgt_buf, proj_buf, gates, zt_all, zp_parts, start)
    zt, zp, half = call(second_kernel, [coefs, coefs, states], [VMEM] * 5)(
        tgt_buf, proj_buf, quad_weight, keep, other_core(send)
    )
    zt_all, zp_parts = reduced(zt, zp)
    send, tgt_keep, proj_keep = call(
        last_kernel,
        [
            in_vmem((2, rows, two_cols), jnp.bfloat16),
            in_vmem((rows, two_cols), jnp.float32),
            in_vmem((rows, two_cols), jnp.float32),
        ],
        lists + [VMEM] * 5,
    )(tgt_buf, proj_buf, gates, zt_all, zp_parts, tgt_energy, proj_energy, tgt_amp, proj_amp, half)
    return call(
        add_kernel,
        [
            jax.ShapeDtypeStruct(tgt_amp.shape, jnp.float32),
            jax.ShapeDtypeStruct(proj_amp.shape, jnp.float32),
        ],
        [VMEM] * 3,
    )(tgt_keep, proj_keep, other_core(send))


def solution(mesh):
    in_specs = (
        P(None, "tgt", "rep"),
        P(None, None, "prj", "rep"),
        P(("bpar", "rep")),
        P(("tgt", "prj", "rep")),
        P(("tgt", "rep"), "prj"),
        P("bpar", None),
        P("bpar", None),
        P(("bpar", "tgt", "prj", "rep"), None),
        P(("bpar", "tgt", "rep"), "prj", None),
    )
    out_specs = (P(("bpar", "tgt", "prj", "rep"), None), P(("bpar", "tgt", "rep"), "prj", None))

    def step(*args):
        return tuple(shards(*args))

    return jax.shard_map(step, mesh=mesh, in_specs=in_specs, out_specs=out_specs, check_vma=False)
```

```python
import functools

import jax
import jax.numpy as jnp
from jax import lax
from jax.experimental import pallas as pl
from jax.experimental.pallas import tpu as pltpu
from jax.sharding import PartitionSpec as P

time_step = 0.4
half_step = 0.5 * time_step
VMEM_LIMIT = 8 * 1024 * 1024
HBM = pl.BlockSpec(memory_space=pl.ANY)
VMEM = pl.BlockSpec(memory_space=pltpu.VMEM)


def turned(block):
    half = block.shape[0] // 2
    return jnp.concatenate([block[half:], -block[:half]], axis=0)


def bf16(block):
    return block.astype(jnp.bfloat16)


def f32(block):
    return block.astype(jnp.float32)


def views(tgt_buf, proj_buf):
    rows = tgt_buf.shape[1] // 2

    def tgt_view(part, core):
        return tgt_buf[part, pl.ds(pl.multiple_of(core * rows, rows), rows), :]

    def proj_view(part, core):
        return proj_buf[part, core]

    return tgt_view, proj_view


def project(view, core, amp):
    return jnp.dot(
        bf16(amp), view(0, core), preferred_element_type=jnp.float32
    ) + jnp.dot(bf16(turned(amp)), view(1, core), preferred_element_type=jnp.float32)


def expand(view, core, field, turned_field):
    contract = (((1,), (1,)), ((), ()))
    return lax.dot_general(
        turned_field, view(0, core), contract, preferred_element_type=jnp.float32
    ) + lax.dot_general(field, view(1, core), contract, preferred_element_type=jnp.float32)


def load_kernel(
    flags_hbm,
    counts_hbm,
    weight_hbm,
    tgt_hbm,
    proj_hbm,
    tgt_energy_hbm,
    proj_energy_hbm,
    tgt_own_hbm,
    proj_own_hbm,
    tgt_buf,
    proj_buf,
    gate,
    weight,
    energy,
    amp_ref,
    part_ref,
    flags,
    counts,
    flat_weight,
    flat_energy,
    tgt_own,
    proj_own,
    sems,
):
    core = lax.axis_index("rep")
    tgt_index = lax.axis_index("tgt")
    prj_index = lax.axis_index("prj")
    rows = tgt_buf.shape[1]
    groups = proj_buf.shape[1]
    row_start = pl.multiple_of(prj_index * rows, rows)
    group_start = tgt_index * groups
    pairs = [
        (tgt_own_hbm, tgt_own),
        (proj_own_hbm, proj_own),
        (tgt_hbm.at[0, pl.ds(row_start, rows)], tgt_buf.at[0]),
        (tgt_hbm.at[1, pl.ds(row_start, rows)], tgt_buf.at[1]),
        (proj_hbm.at[0, pl.ds(group_start, groups)], proj_buf.at[0]),
        (proj_hbm.at[1, pl.ds(group_start, groups)], proj_buf.at[1]),
        (flags_hbm, flags),
        (counts_hbm, counts),
        (weight_hbm, flat_weight),
        (tgt_energy_hbm, flat_energy),
        (proj_energy_hbm, energy.at[1]),
    ]
    copies = [pltpu.make_async_copy(src, dst, sems.at[k]) for k, (src, dst) in enumerate(pairs)]
    for copy in copies:
        copy.start()
    for copy in copies:
        copy.wait()
    weight[...] = flat_weight[...][None, :]
    energy[0] = flat_energy[...][None, :]
    width = gate.shape[1] // 2
    for tile in range(2):
        live = jnp.logical_and(
            flags[prj_index, tgt_index] > 0, 2 * core + tile < counts[prj_index, tgt_index]
        )
        value = jnp.where(live, 1.0, 0.0).astype(jnp.float32)
        gate[:, tile * width : (tile + 1) * width] = jnp.full((1, width), value, jnp.float32)
    amps = (tgt_own[...].T, proj_own[0].T)
    for kind, view in enumerate(views(tgt_buf, proj_buf)):
        amp_ref[kind] = amps[kind]
        part_ref[kind] = project(view, core, amps[kind])


def first_kernel(tgt_buf, proj_buf, weight, part_ref, tgt_other, proj_other, zt_ref, zp_ref):
    other = 1 - lax.axis_index("rep")
    tgt_view, proj_view = views(tgt_buf, proj_buf)
    zt_ref[...] = bf16(weight[...] * (part_ref[0] + project(tgt_view, other, tgt_other[...].T)))
    zp_ref[...] = bf16(weight[...] * (part_ref[1] + project(proj_view, other, proj_other[0].T)))


def add_step(gated, gate, parts, *out_refs):
    for kind in range(2):
        own, other = parts[2 * kind : 2 * kind + 2]
        total = f32(own[...]) + f32(other[...])
        out_refs[kind][...] = bf16(gate[...] * total if gated[kind] else total)


def fields_of(parts):
    proj_field = f32(parts[0][...]) + f32(parts[1][...])
    tgt_field = f32(parts[2][...]) + f32(parts[3][...])
    return [(bf16(field), bf16(turned(field))) for field in (tgt_field, proj_field)]


def half_kernel(tgt_buf, proj_buf, parts, energy, amp_ref, send, keep):
    core = lax.axis_index("rep")
    fields = fields_of(parts)
    for kind, view in enumerate(views(tgt_buf, proj_buf)):
        amp = amp_ref[kind]
        own = amp + half_step * (energy[kind] * turned(amp) + expand(view, core, *fields[kind]))
        other = half_step * expand(view, 1 - core, *fields[kind])
        keep[kind, 0] = own
        keep[kind, 1] = other
        send[kind, 0] = bf16(own)
        send[kind, 1] = bf16(other)


def second_kernel(tgt_buf, proj_buf, weight, keep, received, zt_ref, zp_ref, half_ref):
    core = lax.axis_index("rep")
    for kind, view in enumerate(views(tgt_buf, proj_buf)):
        own = keep[kind, 0] + f32(received[kind, 1])
        other = keep[kind, 1] + f32(received[kind, 0])
        half_ref[kind] = own
        total = project(view, core, own) + project(view, 1 - core, other)
        (zt_ref, zp_ref)[kind][...] = bf16(weight[...] * total)


def last_kernel(tgt_buf, proj_buf, parts, energy, amp_ref, half_ref, send, keep):
    core = lax.axis_index("rep")
    fields = fields_of(parts)
    for kind, view in enumerate(views(tgt_buf, proj_buf)):
        send[kind] = bf16((time_step * expand(view, 1 - core, *fields[kind])).T)
        change = energy[kind] * turned(half_ref[kind]) + expand(view, core, *fields[kind])
        keep[kind] = (amp_ref[kind] + time_step * change).T


def add_kernel(keep, received, new_tgt, new_proj):
    new_tgt[...] = keep[0] + f32(received[0])
    new_proj[0] = keep[1] + f32(received[1])


def shards(
    tgt_basis,
    proj_basis,
    quad_weight,
    tgt_energy,
    proj_energy,
    pair_flags,
    tile_counts,
    tgt_amp,
    proj_amp,
):
    points = quad_weight.shape[0]
    rows, two_cols = tgt_amp.shape
    group_rows = proj_amp.shape[1]

    def call(kernel, out_shape, in_specs, scratch_shapes=(), cost=None):
        specs = list(in_specs) + [None] * (len(out_shape) + len(scratch_shapes))

        def with_lists(*refs):
            refs = jax.tree.leaves(refs)
            args = [
                [refs.pop(0) for _ in spec] if isinstance(spec, list) else refs.pop(0) for spec in specs
            ]
            kernel(*args)

        return pl.pallas_call(
            with_lists,
            out_shape=out_shape,
            in_specs=in_specs,
            out_specs=[VMEM] * len(out_shape),
            scratch_shapes=scratch_shapes,
            cost_estimate=cost,
            compiler_params=pltpu.CompilerParams(vmem_limit_bytes=VMEM_LIMIT),
        )

    in_vmem = pltpu.VMEM

    def other_core(block):
        return lax.ppermute(block, "rep", [(0, 1), (1, 0)])

    def steps_along(axis):
        size = lax.axis_size(axis)
        flips = [1 << bit for bit in range(size.bit_length() - 1)]
        return [(axis, [(me, me ^ flip) for me in range(size)]) for flip in flips]

    along_prj, along_tgt = steps_along("prj"), steps_along("tgt")
    zt_steps, zp_steps = along_prj + along_tgt, along_tgt + along_prj
    coefs = in_vmem((two_cols, points), jnp.bfloat16)
    states = in_vmem((2, two_cols, rows), jnp.float32)

    def reduced(zt, zp):
        for step, (zt_step, zp_step) in enumerate(zip(zt_steps, zp_steps)):
            parts = [zt, lax.ppermute(zt, *zt_step), zp, lax.ppermute(zp, *zp_step)]
            if step == len(zt_steps) - 1:
                return parts
            gated = (step + 1 == len(along_prj), step + 1 == len(along_tgt))
            kernel = functools.partial(add_step, gated)
            zt, zp = call(kernel, [coefs, coefs], [VMEM, [VMEM] * 4])(gate, parts)

    tgt_other, proj_other = other_core(tgt_amp), other_core(proj_amp)
    inputs = (
        pair_flags.T,
        tile_counts.T,
        quad_weight,
        tgt_basis,
        proj_basis,
        tgt_energy,
        proj_energy,
        tgt_amp,
        proj_amp,
    )
    tgt_buf, proj_buf, gate, weight, energy, amp, part = call(
        load_kernel,
        [
            in_vmem((2, 2 * rows, points), jnp.bfloat16),
            in_vmem((2, 2, group_rows, points), jnp.bfloat16),
            in_vmem((1, points), jnp.float32),
            in_vmem((1, points), jnp.float32),
            in_vmem((2, 1, rows), jnp.float32),
            states,
            in_vmem((2, two_cols, points), jnp.float32),
        ],
        [HBM] * len(inputs),
        [
            pltpu.SMEM(pair_flags.T.shape, jnp.int32),
            pltpu.SMEM(tile_counts.T.shape, jnp.int32),
            pltpu.VMEM((points,), jnp.float32),
            pltpu.VMEM((rows,), jnp.float32),
            pltpu.VMEM(tgt_amp.shape, jnp.float32),
            pltpu.VMEM(proj_amp.shape, jnp.float32),
            pltpu.SemaphoreType.DMA((11,)),
        ],
        pl.CostEstimate(
            flops=2 * 4 * rows * two_cols * points, bytes_accessed=3 * 1024 * 1024, transcendentals=0
        ),
    )(*[pltpu.with_memory_space_constraint(block, pltpu.HBM) for block in inputs])
    zt, zp = call(first_kernel, [coefs, coefs], [VMEM] * 6)(
        tgt_buf, proj_buf, weight, part, tgt_other, proj_other
    )
    parts = reduced(zt, zp)
    pair = (2, 2, two_cols, rows)
    send, keep = call(
        half_kernel,
        [in_vmem(pair, jnp.bfloat16), in_vmem(pair, jnp.float32)],
        [VMEM, VMEM, [VMEM] * 4, VMEM, VMEM],
    )(tgt_buf, proj_buf, parts, energy, amp)
    zt, zp, half = call(second_kernel, [coefs, coefs, states], [VMEM] * 5)(
        tgt_buf, proj_buf, weight, keep, other_core(send)
    )
    parts = reduced(zt, zp)
    final = (2, rows, two_cols)
    send, keep = call(
        last_kernel,
        [in_vmem(final, jnp.bfloat16), in_vmem(final, jnp.float32)],
        [VMEM, VMEM, [VMEM] * 4, VMEM, VMEM, VMEM],
    )(tgt_buf, proj_buf, parts, energy, amp, half)
    return call(
        add_kernel,
        [
            jax.ShapeDtypeStruct(tgt_amp.shape, jnp.float32),
            jax.ShapeDtypeStruct(proj_amp.shape, jnp.float32),
        ],
        [VMEM] * 2,
    )(keep, other_core(send))


def solution(mesh):
    in_specs = (
        P(None, "tgt", "rep"),
        P(None, None, "prj", "rep"),
        P(("bpar", "rep")),
        P(("tgt", "prj", "rep")),
        P(("tgt", "rep"), "prj"),
        P("bpar", None),
        P("bpar", None),
        P(("bpar", "tgt", "prj", "rep"), None),
        P(("bpar", "tgt", "rep"), "prj", None),
    )
    out_specs = (P(("bpar", "tgt", "prj", "rep"), None), P(("bpar", "tgt", "rep"), "prj", None))

    def step(*args):
        return tuple(shards(*args))

    return jax.shard_map(step, mesh=mesh, in_specs=in_specs, out_specs=out_specs, check_vma=False)
```

```python
import functools

import jax
import jax.numpy as jnp
from jax import lax
from jax.experimental import pallas as pl
from jax.experimental.pallas import tpu as pltpu
from jax.sharding import PartitionSpec as P

time_step = 0.4
half_step = 0.5 * time_step
VMEM_LIMIT = 8 * 1024 * 1024
HBM = pl.BlockSpec(memory_space=pl.ANY)
VMEM = pl.BlockSpec(memory_space=pltpu.VMEM)


def turned(block):
    half = block.shape[0] // 2
    return jnp.concatenate([block[half:], -block[:half]], axis=0)


def bf16(block):
    return block.astype(jnp.bfloat16)


def f32(block):
    return block.astype(jnp.float32)


def views(tgt_buf, proj_buf):
    rows = tgt_buf.shape[1] // 2

    def tgt_view(part, core):
        return tgt_buf[part, pl.ds(pl.multiple_of(core * rows, rows), rows), :]

    def proj_view(part, core):
        return proj_buf[part, core]

    return tgt_view, proj_view


def project(view, core, amp):
    return jnp.dot(
        bf16(amp), view(0, core), preferred_element_type=jnp.float32
    ) + jnp.dot(bf16(turned(amp)), view(1, core), preferred_element_type=jnp.float32)


def expand(view, core, field, turned_field):
    contract = (((1,), (1,)), ((), ()))
    return lax.dot_general(
        turned_field, view(0, core), contract, preferred_element_type=jnp.float32
    ) + lax.dot_general(field, view(1, core), contract, preferred_element_type=jnp.float32)


def load_kernel(
    flags_hbm,
    counts_hbm,
    weight_hbm,
    tgt_hbm,
    proj_hbm,
    tgt_energy_hbm,
    proj_energy_hbm,
    tgt_own_hbm,
    proj_own_hbm,
    tgt_buf,
    proj_buf,
    gate,
    weight,
    energy,
    amp_ref,
    part_ref,
    flags,
    counts,
    flat_weight,
    flat_energy,
    tgt_own,
    proj_own,
    sems,
):
    core = lax.axis_index("rep")
    tgt_index = lax.axis_index("tgt")
    prj_index = lax.axis_index("prj")
    rows = tgt_buf.shape[1]
    groups = proj_buf.shape[1]
    row_start = pl.multiple_of(prj_index * rows, rows)
    group_start = tgt_index * groups
    pairs = [
        (tgt_own_hbm, tgt_own),
        (proj_own_hbm, proj_own),
        (tgt_hbm.at[0, pl.ds(row_start, rows)], tgt_buf.at[0]),
        (tgt_hbm.at[1, pl.ds(row_start, rows)], tgt_buf.at[1]),
        (proj_hbm.at[0, pl.ds(group_start, groups)], proj_buf.at[0]),
        (proj_hbm.at[1, pl.ds(group_start, groups)], proj_buf.at[1]),
        (flags_hbm, flags),
        (counts_hbm, counts),
        (weight_hbm, flat_weight),
        (tgt_energy_hbm, flat_energy),
        (proj_energy_hbm, energy.at[1]),
    ]
    copies = [pltpu.make_async_copy(src, dst, sems.at[k]) for k, (src, dst) in enumerate(pairs)]
    for copy in copies:
        copy.start()
    for copy in copies:
        copy.wait()
    weight[...] = flat_weight[...][None, :]
    energy[0] = flat_energy[...][None, :]
    width = gate.shape[1] // 2
    for tile in range(2):
        live = jnp.logical_and(
            flags[prj_index, tgt_index] > 0, 2 * core + tile < counts[prj_index, tgt_index]
        )
        value = jnp.where(live, 1.0, 0.0).astype(jnp.float32)
        gate[:, tile * width : (tile + 1) * width] = jnp.full((1, width), value, jnp.float32)
    amps = (tgt_own[...].T, proj_own[0].T)
    for kind, view in enumerate(views(tgt_buf, proj_buf)):
        amp_ref[kind] = amps[kind]
        part_ref[kind] = project(view, core, amps[kind])


def first_kernel(tgt_buf, proj_buf, weight, part_ref, tgt_other, proj_other, zt_ref, zp_ref):
    other = 1 - lax.axis_index("rep")
    tgt_view, proj_view = views(tgt_buf, proj_buf)
    zt_ref[...] = bf16(weight[...] * (part_ref[0] + project(tgt_view, other, tgt_other[...].T)))
    zp_ref[...] = bf16(weight[...] * (part_ref[1] + project(proj_view, other, proj_other[0].T)))


def add_step(gated, gate, own, other, out_ref):
    total = f32(own[...]) + f32(other[...])
    out_ref[...] = bf16(gate[...] * total if gated else total)


def fields_of(parts):
    proj_field = f32(parts[0][...]) + f32(parts[1][...])
    tgt_field = f32(parts[2][...]) + f32(parts[3][...])
    return [(bf16(field), bf16(turned(field))) for field in (tgt_field, proj_field)]


def half_kernel(tgt_buf, proj_buf, parts, energy, amp_ref, send, keep):
    core = lax.axis_index("rep")
    fields = fields_of(parts)
    for kind, view in enumerate(views(tgt_buf, proj_buf)):
        amp = amp_ref[kind]
        own = amp + half_step * (energy[kind] * turned(amp) + expand(view, core, *fields[kind]))
        other = half_step * expand(view, 1 - core, *fields[kind])
        keep[kind, 0] = own
        keep[kind, 1] = other
        send[kind, 0] = bf16(own)
        send[kind, 1] = bf16(other)


def second_kernel(tgt_buf, proj_buf, weight, keep, received, zt_ref, zp_ref, half_ref):
    core = lax.axis_index("rep")
    for kind, view in enumerate(views(tgt_buf, proj_buf)):
        own = keep[kind, 0] + f32(received[kind, 1])
        other = keep[kind, 1] + f32(received[kind, 0])
        half_ref[kind] = own
        total = project(view, core, own) + project(view, 1 - core, other)
        (zt_ref, zp_ref)[kind][...] = bf16(weight[...] * total)


def last_kernel(tgt_buf, proj_buf, parts, energy, amp_ref, half_ref, send, keep):
    core = lax.axis_index("rep")
    fields = fields_of(parts)
    for kind, view in enumerate(views(tgt_buf, proj_buf)):
        send[kind] = bf16((time_step * expand(view, 1 - core, *fields[kind])).T)
        change = energy[kind] * turned(half_ref[kind]) + expand(view, core, *fields[kind])
        keep[kind] = (amp_ref[kind] + time_step * change).T


def add_kernel(keep, received, new_tgt, new_proj):
    new_tgt[...] = keep[0] + f32(received[0])
    new_proj[0] = keep[1] + f32(received[1])


def shards(
    tgt_basis,
    proj_basis,
    quad_weight,
    tgt_energy,
    proj_energy,
    pair_flags,
    tile_counts,
    tgt_amp,
    proj_amp,
):
    points = quad_weight.shape[0]
    rows, two_cols = tgt_amp.shape
    group_rows = proj_amp.shape[1]

    def call(kernel, out_shape, in_specs, scratch_shapes=(), cost=None):
        specs = list(in_specs) + [None] * (len(out_shape) + len(scratch_shapes))

        def with_lists(*refs):
            refs = jax.tree.leaves(refs)
            args = [
                [refs.pop(0) for _ in spec] if isinstance(spec, list) else refs.pop(0) for spec in specs
            ]
            kernel(*args)

        return pl.pallas_call(
            with_lists,
            out_shape=out_shape,
            in_specs=in_specs,
            out_specs=[VMEM] * len(out_shape),
            scratch_shapes=scratch_shapes,
            cost_estimate=cost,
            compiler_params=pltpu.CompilerParams(vmem_limit_bytes=VMEM_LIMIT),
        )

    in_vmem = pltpu.VMEM

    def other_core(block):
        return lax.ppermute(block, "rep", [(0, 1), (1, 0)])

    def steps_along(axis):
        size = lax.axis_size(axis)
        flips = [1 << bit for bit in range(size.bit_length() - 1)]
        return [(axis, [(me, me ^ flip) for me in range(size)]) for flip in flips]

    along_prj, along_tgt = steps_along("prj"), steps_along("tgt")
    zt_steps, zp_steps = along_prj + along_tgt, along_tgt + along_prj
    coefs = in_vmem((two_cols, points), jnp.bfloat16)
    states = in_vmem((2, two_cols, rows), jnp.float32)

    def reduced(zt, zp):
        parts = []
        for block, steps, first_steps in ((zt, zt_steps, along_prj), (zp, zp_steps, along_tgt)):
            for step, (axis, pairs) in enumerate(steps, 1):
                other = lax.ppermute(block, axis, pairs)
                if step < len(steps):
                    kernel = functools.partial(add_step, step == len(first_steps))
                    (block,) = call(kernel, [coefs], [VMEM] * 3)(gate, block, other)
            parts += [block, other]
        return parts

    tgt_other, proj_other = other_core(tgt_amp), other_core(proj_amp)
    inputs = (
        pair_flags.T,
        tile_counts.T,
        quad_weight,
        tgt_basis,
        proj_basis,
        tgt_energy,
        proj_energy,
        tgt_amp,
        proj_amp,
    )
    tgt_buf, proj_buf, gate, weight, energy, amp, part = call(
        load_kernel,
        [
            in_vmem((2, 2 * rows, points), jnp.bfloat16),
            in_vmem((2, 2, group_rows, points), jnp.bfloat16),
            in_vmem((1, points), jnp.float32),
            in_vmem((1, points), jnp.float32),
            in_vmem((2, 1, rows), jnp.float32),
            states,
            in_vmem((2, two_cols, points), jnp.float32),
        ],
        [HBM] * len(inputs),
        [
            pltpu.SMEM(pair_flags.T.shape, jnp.int32),
            pltpu.SMEM(tile_counts.T.shape, jnp.int32),
            pltpu.VMEM((points,), jnp.float32),
            pltpu.VMEM((rows,), jnp.float32),
            pltpu.VMEM(tgt_amp.shape, jnp.float32),
            pltpu.VMEM(proj_amp.shape, jnp.float32),
            pltpu.SemaphoreType.DMA((11,)),
        ],
        pl.CostEstimate(
            flops=2 * 4 * rows * two_cols * points, bytes_accessed=3 * 1024 * 1024, transcendentals=0
        ),
    )(*[pltpu.with_memory_space_constraint(block, pltpu.HBM) for block in inputs])
    zt, zp = call(first_kernel, [coefs, coefs], [VMEM] * 6)(
        tgt_buf, proj_buf, weight, part, tgt_other, proj_other
    )
    parts = reduced(zt, zp)
    pair = (2, 2, two_cols, rows)
    send, keep = call(
        half_kernel,
        [in_vmem(pair, jnp.bfloat16), in_vmem(pair, jnp.float32)],
        [VMEM, VMEM, [VMEM] * 4, VMEM, VMEM],
    )(tgt_buf, proj_buf, parts, energy, amp)
    zt, zp, half = call(second_kernel, [coefs, coefs, states], [VMEM] * 5)(
        tgt_buf, proj_buf, weight, keep, other_core(send)
    )
    parts = reduced(zt, zp)
    final = (2, rows, two_cols)
    send, keep = call(
        last_kernel,
        [in_vmem(final, jnp.bfloat16), in_vmem(final, jnp.float32)],
        [VMEM, VMEM, [VMEM] * 4, VMEM, VMEM, VMEM],
    )(tgt_buf, proj_buf, parts, energy, amp, half)
    return call(
        add_kernel,
        [
            jax.ShapeDtypeStruct(tgt_amp.shape, jnp.float32),
            jax.ShapeDtypeStruct(proj_amp.shape, jnp.float32),
        ],
        [VMEM] * 2,
    )(keep, other_core(send))


def solution(mesh):
    in_specs = (
        P(None, "tgt", "rep"),
        P(None, None, "prj", "rep"),
        P(("bpar", "rep")),
        P(("tgt", "prj", "rep")),
        P(("tgt", "rep"), "prj"),
        P("bpar", None),
        P("bpar", None),
        P(("bpar", "tgt", "prj", "rep"), None),
        P(("bpar", "tgt", "rep"), "prj", None),
    )
    out_specs = (P(("bpar", "tgt", "prj", "rep"), None), P(("bpar", "tgt", "rep"), "prj", None))

    def step(*args):
        return tuple(shards(*args))

    return jax.shard_map(step, mesh=mesh, in_specs=in_specs, out_specs=out_specs, check_vma=False)
```

```python
import functools

import jax
import jax.numpy as jnp
from jax import lax
from jax.experimental import pallas as pl
from jax.experimental.pallas import tpu as pltpu
from jax.sharding import PartitionSpec as P

time_step = 0.4
half_step = 0.5 * time_step
VMEM_LIMIT = 8 * 1024 * 1024
DEVICES = ("tgt", "prj", "rep")
HBM = pl.BlockSpec(memory_space=pl.ANY)
VMEM = pl.BlockSpec(memory_space=pltpu.VMEM)


def turned(block):
    half = block.shape[0] // 2
    return jnp.concatenate([block[half:], -block[:half]], axis=0)


def bf16(block):
    return block.astype(jnp.bfloat16)


def f32(block):
    return block.astype(jnp.float32)


def project(basis_real, basis_imag, amp):
    return jnp.dot(bf16(amp), basis_real, preferred_element_type=jnp.float32) + jnp.dot(
        bf16(turned(amp)), basis_imag, preferred_element_type=jnp.float32
    )


def expand(basis_real, basis_imag, field):
    contract = (((1,), (1,)), ((), ()))
    return lax.dot_general(
        turned(field), basis_real, contract, preferred_element_type=jnp.float32
    ) + lax.dot_general(field, basis_imag, contract, preferred_element_type=jnp.float32)


def load_kernel(
    gate_steps,
    flags_hbm,
    counts_hbm,
    weight_hbm,
    tgt_hbm,
    proj_hbm,
    tgt_energy_hbm,
    proj_energy_hbm,
    tgt_own_hbm,
    proj_own_hbm,
    mine,
    send,
    send_own,
    small_send,
    gate,
    weight,
    energy,
    amp_ref,
    flags,
    counts,
    flat_weight,
    flat_energy,
    tgt_own,
    proj_own,
    sems,
):
    core = lax.axis_index("rep")
    tgt_index = lax.axis_index("tgt")
    prj_index = lax.axis_index("prj")
    sources = (tgt_hbm, proj_hbm)
    firsts = (2 * prj_index, 2 * tgt_index)

    def basis_copies(kind):
        same, other = sources[kind], sources[1 - kind]
        return [
            copy
            for part in range(2)
            for copy in (
                pltpu.make_async_copy(
                    other.at[part, pl.ds(firsts[1 - kind], 2)], send.at[part], sems.at[3 * part]
                ),
                pltpu.make_async_copy(
                    same.at[part, pl.ds(firsts[kind], 2)], mine.at[part], sems.at[3 * part + 1]
                ),
                pltpu.make_async_copy(
                    same.at[part, firsts[kind] + 1 - kind], send_own.at[part], sems.at[3 * part + 2]
                ),
            )
        ]

    for kind in range(2):

        @pl.when(core == kind)
        def _():
            for copy in basis_copies(kind):
                copy.start()

    pairs = [
        (flags_hbm, flags),
        (counts_hbm, counts),
        (weight_hbm, flat_weight),
        (tgt_energy_hbm, flat_energy),
        (proj_energy_hbm, energy.at[1]),
        (tgt_own_hbm, tgt_own),
        (proj_own_hbm, proj_own),
    ]
    copies = [pltpu.make_async_copy(src, dst, sems.at[6 + k]) for k, (src, dst) in enumerate(pairs)]
    for copy in copies:
        copy.start()
    for copy in copies:
        copy.wait()
    weight[...] = flat_weight[...][None, :]
    energy[0] = flat_energy[...][None, :]
    small_send[0] = weight[...]
    small_send[1, :, : energy.shape[2]] = energy[1 - core]
    tiles = 2
    width = gate.shape[-1] // tiles
    gate_step = jnp.where(core == 0, *gate_steps)
    for half in range(2):
        for tile in range(tiles):
            live = jnp.logical_and(
                flags[prj_index, tgt_index] > 0, tiles * half + tile < counts[prj_index, tgt_index]
            )
            value = jnp.where(live, 1.0, 0.0).astype(jnp.float32)
            for step in range(gate.shape[0]):
                here = jnp.where(step == gate_step, value, jnp.float32(1.0))
                gate[step, half, :, tile * width : (tile + 1) * width] = jnp.full(
                    (1, width), here, jnp.float32
                )
    amp_ref[0] = tgt_own[...].T
    amp_ref[1] = proj_own[0].T
    for copy in basis_copies(0):
        copy.wait()


def near_kernel(mine, weight, amp_ref, tgt_other, proj_other, near_ref, other_ref):
    core = lax.axis_index("rep")
    other = jnp.where(core == 0, tgt_other[...], proj_other[0]).T
    other_ref[...] = other
    total = project(mine[0, core], mine[1, core], amp_ref[core]) + project(
        mine[0, 1 - core], mine[1, 1 - core], other
    )
    near_ref[...] = bf16(weight[...] * total)


def far_kernel(theirs, small, amp_ref, other_ref, near_ref, z_ref):
    core = lax.axis_index("rep")
    total = project(theirs[0, core], theirs[1, core], amp_ref[core]) + project(
        theirs[0, 1 - core], theirs[1, 1 - core], other_ref[...]
    )
    z_ref[core] = near_ref[...]
    z_ref[1 - core] = bf16(small[0] * total)


def add_kernel(step, gate, own, other, out_ref):
    for half in range(2):
        out_ref[half] = bf16(gate[step, half] * (f32(own[half]) + f32(other[half])))


def second_kernel(
    mine, theirs, field, weight, small, energy, amp_ref, other_ref, z_ref, half_ref
):
    core = lax.axis_index("rep")
    near, far = field[core], field[1 - core]

    def change(segment):
        return expand(mine[0, segment], mine[1, segment], near) + expand(
            theirs[0, segment], theirs[1, segment], far
        )

    amp, other = amp_ref[core], other_ref[...]
    other_energy = small[1, :, : energy.shape[2]]
    amp = amp + half_step * (energy[core] * turned(amp) + change(core))
    other = other + half_step * (other_energy * turned(other) + change(1 - core))
    half_ref[...] = amp
    for basis, half, weights in ((mine, core, weight[...]), (theirs, 1 - core, small[0])):
        total = project(basis[0, core], basis[1, core], amp) + project(
            basis[0, 1 - core], basis[1, 1 - core], other
        )
        z_ref[half] = bf16(weights * total)


def other_half_kernel(sent, own_far, field, energy, amp_ref, half_ref):
    core = lax.axis_index("rep")
    amp = amp_ref[1 - core]
    change = expand(sent[0, core], sent[1, core], field[core]) + expand(
        own_far[0], own_far[1], field[1 - core]
    )
    half_ref[...] = amp + half_step * (energy[1 - core] * turned(amp) + change)


def last_kernel(
    mine,
    theirs,
    sent,
    own_far,
    my_field,
    other_field,
    energy,
    amp_ref,
    my_half,
    other_half,
    new_tgt,
    new_proj,
):
    core = lax.axis_index("rep")
    my_change = expand(mine[0, core], mine[1, core], my_field[core]) + expand(
        theirs[0, core], theirs[1, core], my_field[1 - core]
    )
    other_change = expand(sent[0, core], sent[1, core], other_field[core]) + expand(
        own_far[0], own_far[1], other_field[1 - core]
    )
    my_rate = energy[core] * turned(my_half[...]) + my_change
    other_rate = energy[1 - core] * turned(other_half[...]) + other_change
    my_new = (amp_ref[core] + time_step * my_rate).T
    other_new = (amp_ref[1 - core] + time_step * other_rate).T
    new_tgt[...] = jnp.where(core == 0, my_new, other_new)
    new_proj[0] = jnp.where(core == 0, other_new, my_new)


def shards(
    tgt_basis,
    proj_basis,
    quad_weight,
    tgt_energy,
    proj_energy,
    pair_flags,
    tile_counts,
    tgt_amp,
    proj_amp,
):
    points = quad_weight.shape[0]
    rows, two_cols = tgt_amp.shape
    sizes = [lax.axis_size(axis) for axis in DEVICES]

    def call(kernel, out_shape, in_specs, scratch_shapes=(), cost=None):
        return pl.pallas_call(
            kernel,
            out_shape=out_shape,
            in_specs=in_specs,
            out_specs=[VMEM] * len(out_shape),
            scratch_shapes=scratch_shapes,
            cost_estimate=cost,
            compiler_params=pltpu.CompilerParams(vmem_limit_bytes=VMEM_LIMIT),
        )

    def run(kernel, out_shape, *blocks):
        return call(kernel, out_shape, [VMEM] * len(blocks))(*blocks)

    def other_core(block):
        return lax.ppermute(block, "rep", [(0, 1), (1, 0)])

    n_tgt, n_prj, n_core = sizes
    tgt_flips = [n_prj * n_core << bit for bit in range(n_tgt.bit_length() - 1)]
    prj_flips = [n_core << bit for bit in range(n_prj.bit_length() - 1)]
    steps = list(zip(prj_flips + tgt_flips, tgt_flips + prj_flips))
    gate_steps = (len(prj_flips) - 1, len(tgt_flips) - 1)

    in_vmem = pltpu.VMEM
    basis = in_vmem((2, 2, rows, points), jnp.bfloat16)
    sums = in_vmem((2, two_cols, points), jnp.bfloat16)
    segment = in_vmem((two_cols, rows), jnp.float32)

    def summed(block):
        for step, flips in enumerate(steps):
            pairs = [(me, me ^ flips[me % n_core]) for me in range(n_tgt * n_prj * n_core)]
            other = lax.ppermute(block, DEVICES, pairs)
            (block,) = run(functools.partial(add_kernel, step), [sums], gate, block, other)
        return block

    tgt_other, proj_other = other_core(tgt_amp), other_core(proj_amp)
    inputs = (
        pair_flags.T,
        tile_counts.T,
        quad_weight,
        tgt_basis.reshape(2, -1, rows, points),
        proj_basis,
        tgt_energy,
        proj_energy,
        tgt_amp,
        proj_amp,
    )
    mine, sent, send_own, small_send, gate, weight, energy, amp = call(
        functools.partial(load_kernel, gate_steps),
        [
            basis,
            basis,
            in_vmem((2, rows, points), jnp.bfloat16),
            in_vmem((2, 1, points), jnp.float32),
            in_vmem((len(steps), 2, 1, points), jnp.float32),
            in_vmem((1, points), jnp.float32),
            in_vmem((2, 1, rows), jnp.float32),
            in_vmem((2, two_cols, rows), jnp.float32),
        ],
        [HBM] * len(inputs),
        [
            pltpu.SMEM(pair_flags.T.shape, jnp.int32),
            pltpu.SMEM(tile_counts.T.shape, jnp.int32),
            pltpu.VMEM((points,), jnp.float32),
            pltpu.VMEM((rows,), jnp.float32),
            pltpu.VMEM(tgt_amp.shape, jnp.float32),
            pltpu.VMEM(proj_amp.shape, jnp.float32),
            pltpu.SemaphoreType.DMA((13,)),
        ],
        pl.CostEstimate(flops=0, bytes_accessed=4 * 1024 * 1024, transcendentals=0),
    )(*[pltpu.with_memory_space_constraint(block, pltpu.HBM) for block in inputs])
    theirs, small = other_core(sent), other_core(small_send)
    near, other = run(
        near_kernel,
        [in_vmem((two_cols, points), jnp.bfloat16), segment],
        mine,
        weight,
        amp,
        tgt_other,
        proj_other,
    )
    (z,) = run(far_kernel, [sums], theirs, small, amp, other, near)
    send_own, z = lax.optimization_barrier((send_own, z))
    own_far = other_core(send_own)
    other_field = summed(z)
    z, my_half = run(
        second_kernel,
        [sums, segment],
        mine,
        theirs,
        other_core(other_field),
        weight,
        small,
        energy,
        amp,
        other,
    )
    (other_half,) = run(
        other_half_kernel, [segment], sent, own_far, other_field, energy, amp
    )
    other_field = summed(z)
    return run(
        last_kernel,
        [
            jax.ShapeDtypeStruct(tgt_amp.shape, jnp.float32),
            jax.ShapeDtypeStruct(proj_amp.shape, jnp.float32),
        ],
        mine,
        theirs,
        sent,
        own_far,
        other_core(other_field),
        other_field,
        energy,
        amp,
        my_half,
        other_half,
    )


def solution(mesh):
    in_specs = (
        P(None, "tgt", "rep"),
        P(None, None, "prj", "rep"),
        P(("bpar", "rep")),
        P(("tgt", "prj", "rep")),
        P(("tgt", "rep"), "prj"),
        P("bpar", None),
        P("bpar", None),
        P(("bpar", "tgt", "prj", "rep"), None),
        P(("bpar", "tgt", "rep"), "prj", None),
    )
    out_specs = (P(("bpar", "tgt", "prj", "rep"), None), P(("bpar", "tgt", "rep"), "prj", None))

    def step(*args):
        return tuple(shards(*args))

    return jax.shard_map(step, mesh=mesh, in_specs=in_specs, out_specs=out_specs, check_vma=False)
```

```python
import functools

import jax
import jax.numpy as jnp
from jax import lax
from jax.experimental import pallas as pl
from jax.experimental.pallas import tpu as pltpu
from jax.sharding import PartitionSpec as P

time_step = 0.4
half_step = 0.5 * time_step
VMEM_LIMIT = 8 * 1024 * 1024
DEVICES = ("tgt", "prj", "rep")
HBM = pl.BlockSpec(memory_space=pl.ANY)
VMEM = pl.BlockSpec(memory_space=pltpu.VMEM)


def turned(block):
    half = block.shape[0] // 2
    return jnp.concatenate([block[half:], -block[:half]], axis=0)


def bf16(block):
    return block.astype(jnp.bfloat16)


def f32(block):
    return block.astype(jnp.float32)


def project(basis_real, basis_imag, amp):
    return jnp.dot(bf16(amp), basis_real, preferred_element_type=jnp.float32) + jnp.dot(
        bf16(turned(amp)), basis_imag, preferred_element_type=jnp.float32
    )


def expand(basis_real, basis_imag, field):
    contract = (((1,), (1,)), ((), ()))
    return lax.dot_general(
        turned(field), basis_real, contract, preferred_element_type=jnp.float32
    ) + lax.dot_general(field, basis_imag, contract, preferred_element_type=jnp.float32)


def load_kernel(
    gate_steps,
    flags_hbm,
    counts_hbm,
    weight_hbm,
    tgt_hbm,
    proj_hbm,
    tgt_energy_hbm,
    proj_energy_hbm,
    tgt_own_hbm,
    proj_own_hbm,
    mine,
    send,
    send_own,
    amp_send,
    small_send,
    gate,
    weight,
    energy,
    amp_ref,
    flags,
    counts,
    flat_weight,
    flat_energy,
    tgt_own,
    proj_own,
    sems,
):
    core = lax.axis_index("rep")
    tgt_index = lax.axis_index("tgt")
    prj_index = lax.axis_index("prj")
    sources = (tgt_hbm, proj_hbm)
    firsts = (2 * prj_index, 2 * tgt_index)

    def basis_copies(kind):
        same, other = sources[kind], sources[1 - kind]
        return [
            copy
            for part in range(2)
            for copy in (
                pltpu.make_async_copy(
                    other.at[part, pl.ds(firsts[1 - kind], 2)], send.at[part], sems.at[3 * part]
                ),
                pltpu.make_async_copy(
                    same.at[part, pl.ds(firsts[kind], 2)], mine.at[part], sems.at[3 * part + 1]
                ),
                pltpu.make_async_copy(
                    same.at[part, firsts[kind] + 1 - kind], send_own.at[part], sems.at[3 * part + 2]
                ),
            )
        ]

    for kind in range(2):

        @pl.when(core == kind)
        def _():
            for copy in basis_copies(kind):
                copy.start()

    pairs = [
        (flags_hbm, flags),
        (counts_hbm, counts),
        (weight_hbm, flat_weight),
        (tgt_energy_hbm, flat_energy),
        (proj_energy_hbm, energy.at[1]),
        (tgt_own_hbm, tgt_own),
        (proj_own_hbm, proj_own),
    ]
    copies = [pltpu.make_async_copy(src, dst, sems.at[6 + k]) for k, (src, dst) in enumerate(pairs)]
    for copy in copies:
        copy.start()
    for copy in copies:
        copy.wait()
    weight[0] = flat_weight[...][None, :]
    energy[0] = flat_energy[...][None, :]
    small_send[0] = weight[0]
    small_send[1, :, : energy.shape[2]] = energy[1 - core]
    tiles = 2
    width = gate.shape[-1] // tiles
    gate_step = jnp.where(core == 0, *gate_steps)
    for half, home in enumerate((core, 1 - core)):
        for tile in range(tiles):
            live = jnp.logical_and(
                flags[prj_index, tgt_index] > 0, tiles * home + tile < counts[prj_index, tgt_index]
            )
            value = jnp.where(live, 1.0, 0.0).astype(jnp.float32)
            for step in range(gate.shape[0]):
                here = jnp.where(step == gate_step, value, jnp.float32(1.0))
                gate[step, half, :, tile * width : (tile + 1) * width] = jnp.full(
                    (1, width), here, jnp.float32
                )
    amp_ref[0] = tgt_own[...].T
    amp_ref[1] = proj_own[0].T
    amp_send[...] = amp_ref[1 - core]
    for copy in basis_copies(0):
        copy.wait()


def first_kernel(basis, weight, amp_ref, other_ref, out_ref):
    core = lax.axis_index("rep")
    total = project(basis[0, core], basis[1, core], amp_ref[core]) + project(
        basis[0, 1 - core], basis[1, 1 - core], other_ref[...]
    )
    out_ref[...] = bf16(weight[0] * total)


def add_kernel(step, half, gate, own, other, out_ref):
    out_ref[...] = bf16(gate[step, half] * (f32(own[...]) + f32(other[...])))


def second_kernel(
    mine, theirs, near, far, weight, small, energy, amp_ref, other_ref, near_ref, far_ref, half_ref
):
    core = lax.axis_index("rep")

    def change(segment):
        return expand(mine[0, segment], mine[1, segment], near[...]) + expand(
            theirs[0, segment], theirs[1, segment], far[...]
        )

    amp, other = amp_ref[core], other_ref[...]
    other_energy = small[1, :, : energy.shape[2]]
    amp = amp + half_step * (energy[core] * turned(amp) + change(core))
    other = other + half_step * (other_energy * turned(other) + change(1 - core))
    half_ref[...] = amp
    for basis, out_ref, weights in ((mine, near_ref, weight[0]), (theirs, far_ref, small[0])):
        total = project(basis[0, core], basis[1, core], amp) + project(
            basis[0, 1 - core], basis[1, 1 - core], other
        )
        out_ref[...] = bf16(weights * total)


def other_half_kernel(sent, own_far, near, far, energy, amp_ref, half_ref):
    core = lax.axis_index("rep")
    amp = amp_ref[1 - core]
    change = expand(sent[0, core], sent[1, core], near[...]) + expand(own_far[0], own_far[1], far[...])
    half_ref[...] = amp + half_step * (energy[1 - core] * turned(amp) + change)


def last_kernel(
    mine,
    theirs,
    sent,
    own_far,
    my_near,
    my_far,
    other_near,
    other_far,
    energy,
    amp_ref,
    my_half,
    other_half,
    new_tgt,
    new_proj,
):
    core = lax.axis_index("rep")
    my_change = expand(mine[0, core], mine[1, core], my_near[...]) + expand(
        theirs[0, core], theirs[1, core], my_far[...]
    )
    other_change = expand(sent[0, core], sent[1, core], other_near[...]) + expand(
        own_far[0], own_far[1], other_far[...]
    )
    my_rate = energy[core] * turned(my_half[...]) + my_change
    other_rate = energy[1 - core] * turned(other_half[...]) + other_change
    my_new = (amp_ref[core] + time_step * my_rate).T
    other_new = (amp_ref[1 - core] + time_step * other_rate).T
    new_tgt[...] = jnp.where(core == 0, my_new, other_new)
    new_proj[0] = jnp.where(core == 0, other_new, my_new)


def shards(
    tgt_basis,
    proj_basis,
    quad_weight,
    tgt_energy,
    proj_energy,
    pair_flags,
    tile_counts,
    tgt_amp,
    proj_amp,
):
    points = quad_weight.shape[0]
    rows, two_cols = tgt_amp.shape
    sizes = [lax.axis_size(axis) for axis in DEVICES]

    def call(kernel, out_shape, in_specs, scratch_shapes=(), cost=None):
        return pl.pallas_call(
            kernel,
            out_shape=out_shape,
            in_specs=in_specs,
            out_specs=[VMEM] * len(out_shape),
            scratch_shapes=scratch_shapes,
            cost_estimate=cost,
            compiler_params=pltpu.CompilerParams(vmem_limit_bytes=VMEM_LIMIT),
        )

    def run(kernel, out_shape, *blocks):
        return call(kernel, out_shape, [VMEM] * len(blocks))(*blocks)

    def other_core(block):
        return lax.ppermute(block, "rep", [(0, 1), (1, 0)])

    n_tgt, n_prj, n_core = sizes
    tgt_flips = [n_prj * n_core << bit for bit in range(n_tgt.bit_length() - 1)]
    prj_flips = [n_core << bit for bit in range(n_prj.bit_length() - 1)]
    steps = list(zip(prj_flips + tgt_flips, tgt_flips + prj_flips))
    gate_steps = (len(prj_flips) - 1, len(tgt_flips) - 1)

    in_vmem = pltpu.VMEM
    basis = in_vmem((2, 2, rows, points), jnp.bfloat16)
    sums = in_vmem((two_cols, points), jnp.bfloat16)
    segment = in_vmem((two_cols, rows), jnp.float32)

    def summed(*halves):
        totals = []
        for half, block in enumerate(halves):
            for step, flips in enumerate(steps):
                pairs = [(me, me ^ flips[me % n_core]) for me in range(n_tgt * n_prj * n_core)]
                other = lax.ppermute(block, DEVICES, pairs)
                (block,) = run(functools.partial(add_kernel, step, half), [sums], gate, block, other)
            totals.append(block)
        return totals

    def swapped(near, far):
        return other_core(far), other_core(near)

    inputs = (
        pair_flags.T,
        tile_counts.T,
        quad_weight,
        tgt_basis.reshape(2, -1, rows, points),
        proj_basis,
        tgt_energy,
        proj_energy,
        tgt_amp,
        proj_amp,
    )
    mine, sent, send_own, amp_send, small_send, gate, weight, energy, amp = call(
        functools.partial(load_kernel, gate_steps),
        [
            basis,
            basis,
            in_vmem((2, rows, points), jnp.bfloat16),
            segment,
            in_vmem((2, 1, points), jnp.float32),
            in_vmem((len(steps), 2, 1, points), jnp.float32),
            in_vmem((1, 1, points), jnp.float32),
            in_vmem((2, 1, rows), jnp.float32),
            in_vmem((2, two_cols, rows), jnp.float32),
        ],
        [HBM] * len(inputs),
        [
            pltpu.SMEM(pair_flags.T.shape, jnp.int32),
            pltpu.SMEM(tile_counts.T.shape, jnp.int32),
            pltpu.VMEM((points,), jnp.float32),
            pltpu.VMEM((rows,), jnp.float32),
            pltpu.VMEM(tgt_amp.shape, jnp.float32),
            pltpu.VMEM(proj_amp.shape, jnp.float32),
            pltpu.SemaphoreType.DMA((13,)),
        ],
        pl.CostEstimate(flops=0, bytes_accessed=4 * 1024 * 1024, transcendentals=0),
    )(*[pltpu.with_memory_space_constraint(block, pltpu.HBM) for block in inputs])
    other, small, theirs = other_core(amp_send), other_core(small_send), other_core(sent)
    (near,) = run(first_kernel, [sums], mine, weight, amp, other)
    (far,) = run(first_kernel, [sums], theirs, small, amp, other)
    send_own, far = lax.optimization_barrier((send_own, far))
    own_far = other_core(send_own)
    fields = summed(near, far)
    near, far, my_half = run(
        second_kernel,
        [sums, sums, segment],
        mine,
        theirs,
        *swapped(*fields),
        weight,
        small,
        energy,
        amp,
        other,
    )
    (other_half,) = run(other_half_kernel, [segment], sent, own_far, *fields, energy, amp)
    fields = summed(near, far)
    return run(
        last_kernel,
        [
            jax.ShapeDtypeStruct(tgt_amp.shape, jnp.float32),
            jax.ShapeDtypeStruct(proj_amp.shape, jnp.float32),
        ],
        mine,
        theirs,
        sent,
        own_far,
        *swapped(*fields),
        *fields,
        energy,
        amp,
        my_half,
        other_half,
    )


def solution(mesh):
    in_specs = (
        P(None, "tgt", "rep"),
        P(None, None, "prj", "rep"),
        P(("bpar", "rep")),
        P(("tgt", "prj", "rep")),
        P(("tgt", "rep"), "prj"),
        P("bpar", None),
        P("bpar", None),
        P(("bpar", "tgt", "prj", "rep"), None),
        P(("bpar", "tgt", "rep"), "prj", None),
    )
    out_specs = (P(("bpar", "tgt", "prj", "rep"), None), P(("bpar", "tgt", "rep"), "prj", None))

    def step(*args):
        return tuple(shards(*args))

    return jax.shard_map(step, mesh=mesh, in_specs=in_specs, out_specs=out_specs, check_vma=False)
```

```python
import functools

import jax
import jax.numpy as jnp
from jax import lax
from jax.experimental import pallas as pl
from jax.experimental.pallas import tpu as pltpu
from jax.sharding import PartitionSpec as P

time_step = 0.4
half_step = 0.5 * time_step
VMEM_LIMIT = 8 * 1024 * 1024
DEVICES = ("tgt", "prj", "rep")
HBM = pl.BlockSpec(memory_space=pl.ANY)
VMEM = pl.BlockSpec(memory_space=pltpu.VMEM)


def turned(block):
    half = block.shape[0] // 2
    return jnp.concatenate([block[half:], -block[:half]], axis=0)


def bf16(block):
    return block.astype(jnp.bfloat16)


def f32(block):
    return block.astype(jnp.float32)


def project(basis_real, basis_imag, amp):
    return jnp.dot(bf16(amp), basis_real, preferred_element_type=jnp.float32) + jnp.dot(
        bf16(turned(amp)), basis_imag, preferred_element_type=jnp.float32
    )


def expand(basis_real, basis_imag, field):
    contract = (((1,), (1,)), ((), ()))
    return lax.dot_general(
        turned(field), basis_real, contract, preferred_element_type=jnp.float32
    ) + lax.dot_general(field, basis_imag, contract, preferred_element_type=jnp.float32)


def load_kernel(
    gate_steps,
    flags_hbm,
    counts_hbm,
    weight_hbm,
    tgt_hbm,
    proj_hbm,
    tgt_energy_hbm,
    proj_energy_hbm,
    tgt_own_hbm,
    proj_own_hbm,
    mine,
    send,
    send_own,
    small_send,
    gate,
    weight,
    energy,
    amp_ref,
    part_ref,
    flags,
    counts,
    flat_weight,
    flat_energy,
    tgt_own,
    proj_own,
    sems,
):
    core = lax.axis_index("rep")
    tgt_index = lax.axis_index("tgt")
    prj_index = lax.axis_index("prj")
    sources = (tgt_hbm, proj_hbm)
    firsts = (2 * prj_index, 2 * tgt_index)

    def basis_copies(kind):
        same, other = sources[kind], sources[1 - kind]
        return [
            copy
            for part in range(2)
            for copy in (
                pltpu.make_async_copy(
                    other.at[part, pl.ds(firsts[1 - kind], 2)], send.at[part], sems.at[3 * part]
                ),
                pltpu.make_async_copy(
                    same.at[part, pl.ds(firsts[kind], 2)], mine.at[part], sems.at[3 * part + 1]
                ),
                pltpu.make_async_copy(
                    same.at[part, firsts[kind] + 1 - kind], send_own.at[part], sems.at[3 * part + 2]
                ),
            )
        ]

    for kind in range(2):

        @pl.when(core == kind)
        def _():
            for copy in basis_copies(kind):
                copy.start()

    pairs = [
        (flags_hbm, flags),
        (counts_hbm, counts),
        (weight_hbm, flat_weight),
        (tgt_energy_hbm, flat_energy),
        (proj_energy_hbm, energy.at[1]),
        (tgt_own_hbm, tgt_own),
        (proj_own_hbm, proj_own),
    ]
    copies = [pltpu.make_async_copy(src, dst, sems.at[6 + k]) for k, (src, dst) in enumerate(pairs)]
    for copy in copies:
        copy.start()
    for copy in copies:
        copy.wait()
    weight[0] = flat_weight[...][None, :]
    energy[0] = flat_energy[...][None, :]
    small_send[0] = weight[0]
    small_send[1, :, : energy.shape[2]] = energy[1 - core]
    tiles = 2
    width = gate.shape[-1] // tiles
    gate_step = jnp.where(core == 0, *gate_steps)
    for half, home in enumerate((core, 1 - core)):
        for tile in range(tiles):
            live = jnp.logical_and(
                flags[prj_index, tgt_index] > 0, tiles * home + tile < counts[prj_index, tgt_index]
            )
            value = jnp.where(live, 1.0, 0.0).astype(jnp.float32)
            for step in range(gate.shape[0]):
                here = jnp.where(step == gate_step, value, jnp.float32(1.0))
                gate[step, half, :, tile * width : (tile + 1) * width] = jnp.full(
                    (1, width), here, jnp.float32
                )
    amp_ref[0] = tgt_own[...].T
    amp_ref[1] = proj_own[0].T
    for copy in basis_copies(0):
        copy.wait()
    for slot, (basis, kind) in enumerate(((mine, core), (send, 1 - core))):
        part_ref[slot] = project(basis[0, core], basis[1, core], amp_ref[kind])


def first_kernel(mine, sent, weight, part_ref, tgt_other, proj_other, near_ref, swap_ref, other_ref):
    core = lax.axis_index("rep")
    tgt_amp, proj_amp = tgt_other[...].T, proj_other[0].T
    my_amp = jnp.where(core == 0, tgt_amp, proj_amp)
    other_amp = jnp.where(core == 0, proj_amp, tgt_amp)
    other_ref[...] = my_amp
    for slot, (basis, amp, out_ref) in enumerate(((mine, my_amp, near_ref), (sent, other_amp, swap_ref))):
        total = part_ref[slot] + project(basis[0, 1 - core], basis[1, 1 - core], amp)
        out_ref[...] = bf16(weight[0] * total)


def add_kernel(step, gate, *refs):
    count = len(refs) // 3
    for half in range(count):
        own, other, out_ref = refs[half::count]
        out_ref[...] = bf16(gate[step, half] * (f32(own[...]) + f32(other[...])))


def second_kernel(
    mine, theirs, near, far, weight, small, energy, amp_ref, other_ref, near_ref, far_ref, half_ref
):
    core = lax.axis_index("rep")

    def change(segment):
        return expand(mine[0, segment], mine[1, segment], near[...]) + expand(
            theirs[0, segment], theirs[1, segment], far[...]
        )

    amp, other = amp_ref[core], other_ref[...]
    other_energy = small[1, :, : energy.shape[2]]
    amp = amp + half_step * (energy[core] * turned(amp) + change(core))
    other = other + half_step * (other_energy * turned(other) + change(1 - core))
    half_ref[...] = amp
    for basis, out_ref, weights in ((mine, near_ref, weight[0]), (theirs, far_ref, small[0])):
        total = project(basis[0, core], basis[1, core], amp) + project(
            basis[0, 1 - core], basis[1, 1 - core], other
        )
        out_ref[...] = bf16(weights * total)


def other_half_kernel(sent, own_far, near, far, energy, amp_ref, half_ref):
    core = lax.axis_index("rep")
    amp = amp_ref[1 - core]
    change = expand(sent[0, core], sent[1, core], near[...]) + expand(own_far[0], own_far[1], far[...])
    half_ref[...] = amp + half_step * (energy[1 - core] * turned(amp) + change)


def other_last_kernel(sent, own_far, near, far, energy, amp_ref, half_ref, new_ref):
    core = lax.axis_index("rep")
    change = expand(sent[0, core], sent[1, core], near[...]) + expand(own_far[0], own_far[1], far[...])
    rate = energy[1 - core] * turned(half_ref[...]) + change
    new_ref[...] = (amp_ref[1 - core] + time_step * rate).T


def last_kernel(mine, theirs, near, far, energy, amp_ref, half_ref, other_new, new_tgt, new_proj):
    core = lax.axis_index("rep")
    change = expand(mine[0, core], mine[1, core], near[...]) + expand(
        theirs[0, core], theirs[1, core], far[...]
    )
    rate = energy[core] * turned(half_ref[...]) + change
    my_new = (amp_ref[core] + time_step * rate).T
    new_tgt[...] = jnp.where(core == 0, my_new, other_new[...])
    new_proj[0] = jnp.where(core == 0, other_new[...], my_new)


def shards(
    tgt_basis,
    proj_basis,
    quad_weight,
    tgt_energy,
    proj_energy,
    pair_flags,
    tile_counts,
    tgt_amp,
    proj_amp,
):
    points = quad_weight.shape[0]
    rows, two_cols = tgt_amp.shape
    sizes = [lax.axis_size(axis) for axis in DEVICES]

    def call(kernel, out_shape, in_specs, scratch_shapes=(), cost=None):
        return pl.pallas_call(
            kernel,
            out_shape=out_shape,
            in_specs=in_specs,
            out_specs=[VMEM] * len(out_shape),
            scratch_shapes=scratch_shapes,
            cost_estimate=cost,
            compiler_params=pltpu.CompilerParams(vmem_limit_bytes=VMEM_LIMIT),
        )

    def run(kernel, out_shape, *blocks):
        return call(kernel, out_shape, [VMEM] * len(blocks))(*blocks)

    def other_core(block):
        return lax.ppermute(block, "rep", [(0, 1), (1, 0)])

    n_tgt, n_prj, n_core = sizes
    tgt_flips = [n_prj * n_core << bit for bit in range(n_tgt.bit_length() - 1)]
    prj_flips = [n_core << bit for bit in range(n_prj.bit_length() - 1)]
    steps = list(zip(prj_flips + tgt_flips, tgt_flips + prj_flips))
    gate_steps = (len(prj_flips) - 1, len(tgt_flips) - 1)

    in_vmem = pltpu.VMEM
    basis = in_vmem((2, 2, rows, points), jnp.bfloat16)
    sums = in_vmem((two_cols, points), jnp.bfloat16)
    segment = in_vmem((two_cols, rows), jnp.float32)

    def summed(*halves):
        for step, flips in enumerate(steps):
            pairs = [(me, me ^ flips[me % n_core]) for me in range(n_tgt * n_prj * n_core)]
            others = [lax.ppermute(block, DEVICES, pairs) for block in halves]
            halves = run(functools.partial(add_kernel, step), [sums] * 2, gate, *halves, *others)
        return halves

    def swapped(near, far):
        return other_core(far), other_core(near)

    tgt_other, proj_other = other_core(tgt_amp), other_core(proj_amp)
    inputs = (
        pair_flags.T,
        tile_counts.T,
        quad_weight,
        tgt_basis.reshape(2, -1, rows, points),
        proj_basis,
        tgt_energy,
        proj_energy,
        tgt_amp,
        proj_amp,
    )
    mine, sent, send_own, small_send, gate, weight, energy, amp, part = call(
        functools.partial(load_kernel, gate_steps),
        [
            basis,
            basis,
            in_vmem((2, rows, points), jnp.bfloat16),
            in_vmem((2, 1, points), jnp.float32),
            in_vmem((len(steps), 2, 1, points), jnp.float32),
            in_vmem((1, 1, points), jnp.float32),
            in_vmem((2, 1, rows), jnp.float32),
            in_vmem((2, two_cols, rows), jnp.float32),
            in_vmem((2, two_cols, points), jnp.float32),
        ],
        [HBM] * len(inputs),
        [
            pltpu.SMEM(pair_flags.T.shape, jnp.int32),
            pltpu.SMEM(tile_counts.T.shape, jnp.int32),
            pltpu.VMEM((points,), jnp.float32),
            pltpu.VMEM((rows,), jnp.float32),
            pltpu.VMEM(tgt_amp.shape, jnp.float32),
            pltpu.VMEM(proj_amp.shape, jnp.float32),
            pltpu.SemaphoreType.DMA((13,)),
        ],
        pl.CostEstimate(flops=2 * 4 * rows * two_cols * points, bytes_accessed=4 * 1024 * 1024, transcendentals=0),
    )(*[pltpu.with_memory_space_constraint(block, pltpu.HBM) for block in inputs])
    near, far, other = run(
        first_kernel, [sums, sums, segment], mine, sent, weight, part, tgt_other, proj_other
    )
    far = other_core(far)
    sent, send_own, small_send, far = lax.optimization_barrier((sent, send_own, small_send, far))
    theirs, own_far, small = other_core(sent), other_core(send_own), other_core(small_send)
    fields = summed(near, far)
    near, far, my_half = run(
        second_kernel,
        [sums, sums, segment],
        mine,
        theirs,
        *swapped(*fields),
        weight,
        small,
        energy,
        amp,
        other,
    )
    (other_half,) = run(other_half_kernel, [segment], sent, own_far, *fields, energy, amp)
    fields = summed(near, far)
    (other_new,) = run(
        other_last_kernel,
        [in_vmem((rows, two_cols), jnp.float32)],
        sent,
        own_far,
        *fields,
        energy,
        amp,
        other_half,
    )
    return run(
        last_kernel,
        [
            jax.ShapeDtypeStruct(tgt_amp.shape, jnp.float32),
            jax.ShapeDtypeStruct(proj_amp.shape, jnp.float32),
        ],
        mine,
        theirs,
        *swapped(*fields),
        energy,
        amp,
        my_half,
        other_new,
    )


def solution(mesh):
    in_specs = (
        P(None, "tgt", "rep"),
        P(None, None, "prj", "rep"),
        P(("bpar", "rep")),
        P(("tgt", "prj", "rep")),
        P(("tgt", "rep"), "prj"),
        P("bpar", None),
        P("bpar", None),
        P(("bpar", "tgt", "prj", "rep"), None),
        P(("bpar", "tgt", "rep"), "prj", None),
    )
    out_specs = (P(("bpar", "tgt", "prj", "rep"), None), P(("bpar", "tgt", "rep"), "prj", None))

    def step(*args):
        return tuple(shards(*args))

    return jax.shard_map(step, mesh=mesh, in_specs=in_specs, out_specs=out_specs, check_vma=False)
```

```python
import functools

import jax
import jax.numpy as jnp
from jax import lax
from jax.experimental import pallas as pl
from jax.experimental.pallas import tpu as pltpu
from jax.sharding import PartitionSpec as P

time_step = 0.4
half_step = 0.5 * time_step
VMEM_LIMIT = 8 * 1024 * 1024
DEVICES = ("tgt", "prj", "rep")
HBM = pl.BlockSpec(memory_space=pl.ANY)
VMEM = pl.BlockSpec(memory_space=pltpu.VMEM)


def turned(block):
    half = block.shape[0] // 2
    return jnp.concatenate([block[half:], -block[:half]], axis=0)


def bf16(block):
    return block.astype(jnp.bfloat16)


def f32(block):
    return block.astype(jnp.float32)


def project(basis_real, basis_imag, amp):
    return jnp.dot(bf16(amp), basis_real, preferred_element_type=jnp.float32) + jnp.dot(
        bf16(turned(amp)), basis_imag, preferred_element_type=jnp.float32
    )


def expand(basis_real, basis_imag, field):
    contract = (((1,), (1,)), ((), ()))
    return lax.dot_general(
        turned(field), basis_real, contract, preferred_element_type=jnp.float32
    ) + lax.dot_general(field, basis_imag, contract, preferred_element_type=jnp.float32)


def load_kernel(
    gate_steps,
    flags_hbm,
    counts_hbm,
    weight_hbm,
    tgt_hbm,
    proj_hbm,
    tgt_energy_hbm,
    proj_energy_hbm,
    tgt_own_hbm,
    proj_own_hbm,
    mine,
    send,
    send_own,
    small_send,
    gate,
    weight,
    energy,
    amp_ref,
    part_ref,
    flags,
    counts,
    flat_weight,
    flat_energy,
    tgt_own,
    proj_own,
    sems,
):
    core = lax.axis_index("rep")
    tgt_index = lax.axis_index("tgt")
    prj_index = lax.axis_index("prj")
    sources = (tgt_hbm, proj_hbm)
    firsts = (2 * prj_index, 2 * tgt_index)

    def basis_copies(kind):
        same, other = sources[kind], sources[1 - kind]
        return [
            copy
            for part in range(2)
            for copy in (
                pltpu.make_async_copy(
                    other.at[part, pl.ds(firsts[1 - kind], 2)], send.at[part], sems.at[3 * part]
                ),
                pltpu.make_async_copy(
                    same.at[part, pl.ds(firsts[kind], 2)], mine.at[part], sems.at[3 * part + 1]
                ),
                pltpu.make_async_copy(
                    same.at[part, firsts[kind] + 1 - kind], send_own.at[part], sems.at[3 * part + 2]
                ),
            )
        ]

    for kind in range(2):

        @pl.when(core == kind)
        def _():
            for copy in basis_copies(kind):
                copy.start()

    pairs = [
        (flags_hbm, flags),
        (counts_hbm, counts),
        (weight_hbm, flat_weight),
        (tgt_energy_hbm, flat_energy),
        (proj_energy_hbm, energy.at[1]),
        (tgt_own_hbm, tgt_own),
        (proj_own_hbm, proj_own),
    ]
    copies = [pltpu.make_async_copy(src, dst, sems.at[6 + k]) for k, (src, dst) in enumerate(pairs)]
    for copy in copies:
        copy.start()
    for copy in copies:
        copy.wait()
    weight[0] = flat_weight[...][None, :]
    energy[0] = flat_energy[...][None, :]
    small_send[0] = weight[0]
    small_send[1, :, : energy.shape[2]] = energy[1 - core]
    tiles = 2
    width = gate.shape[-1] // tiles
    gate_step = jnp.where(core == 0, *gate_steps)
    for half, home in enumerate((core, 1 - core)):
        for tile in range(tiles):
            live = jnp.logical_and(
                flags[prj_index, tgt_index] > 0, tiles * home + tile < counts[prj_index, tgt_index]
            )
            value = jnp.where(live, 1.0, 0.0).astype(jnp.float32)
            for step in range(gate.shape[0]):
                here = jnp.where(step == gate_step, value, jnp.float32(1.0))
                gate[step, half, :, tile * width : (tile + 1) * width] = jnp.full(
                    (1, width), here, jnp.float32
                )
    amp_ref[0] = tgt_own[...].T
    amp_ref[1] = proj_own[0].T
    for copy in basis_copies(0):
        copy.wait()
    for slot, (basis, kind) in enumerate(((mine, core), (send, 1 - core))):
        part_ref[slot] = project(basis[0, core], basis[1, core], amp_ref[kind])


def first_kernel(mine, sent, weight, part_ref, tgt_other, proj_other, near_ref, swap_ref, other_ref):
    core = lax.axis_index("rep")
    tgt_amp, proj_amp = tgt_other[...].T, proj_other[0].T
    my_amp = jnp.where(core == 0, tgt_amp, proj_amp)
    other_amp = jnp.where(core == 0, proj_amp, tgt_amp)
    other_ref[...] = my_amp
    for slot, (basis, amp, out_ref) in enumerate(((mine, my_amp, near_ref), (sent, other_amp, swap_ref))):
        total = part_ref[slot] + project(basis[0, 1 - core], basis[1, 1 - core], amp)
        out_ref[...] = bf16(weight[0] * total)


def add_kernel(step, gate, both, out_ref):
    for half in range(2):
        out_ref[half] = bf16(gate[step, half] * (f32(both[0, half]) + f32(both[1, half])))


def pack_kernel(near, far, out_ref):
    out_ref[0] = near[...]
    out_ref[1] = far[...]


def second_kernel(
    mine, theirs, field, weight, small, energy, amp_ref, other_ref, z_ref, half_ref
):
    core = lax.axis_index("rep")
    far, near = field[0], field[1]

    def change(segment):
        return expand(mine[0, segment], mine[1, segment], near) + expand(
            theirs[0, segment], theirs[1, segment], far
        )

    amp, other = amp_ref[core], other_ref[...]
    other_energy = small[1, :, : energy.shape[2]]
    amp = amp + half_step * (energy[core] * turned(amp) + change(core))
    other = other + half_step * (other_energy * turned(other) + change(1 - core))
    half_ref[...] = amp
    for half, (basis, weights) in enumerate(((mine, weight[0]), (theirs, small[0]))):
        total = project(basis[0, core], basis[1, core], amp) + project(
            basis[0, 1 - core], basis[1, 1 - core], other
        )
        z_ref[half] = bf16(weights * total)


def other_half_kernel(sent, own_far, field, energy, amp_ref, half_ref):
    core = lax.axis_index("rep")
    amp = amp_ref[1 - core]
    change = expand(sent[0, core], sent[1, core], field[0]) + expand(own_far[0], own_far[1], field[1])
    half_ref[...] = amp + half_step * (energy[1 - core] * turned(amp) + change)


def other_last_kernel(sent, own_far, field, energy, amp_ref, half_ref, new_ref):
    core = lax.axis_index("rep")
    change = expand(sent[0, core], sent[1, core], field[0]) + expand(own_far[0], own_far[1], field[1])
    rate = energy[1 - core] * turned(half_ref[...]) + change
    new_ref[...] = (amp_ref[1 - core] + time_step * rate).T


def last_kernel(mine, theirs, field, energy, amp_ref, half_ref, other_new, new_tgt, new_proj):
    core = lax.axis_index("rep")
    change = expand(mine[0, core], mine[1, core], field[1]) + expand(
        theirs[0, core], theirs[1, core], field[0]
    )
    rate = energy[core] * turned(half_ref[...]) + change
    my_new = (amp_ref[core] + time_step * rate).T
    new_tgt[...] = jnp.where(core == 0, my_new, other_new[...])
    new_proj[0] = jnp.where(core == 0, other_new[...], my_new)


def shards(
    tgt_basis,
    proj_basis,
    quad_weight,
    tgt_energy,
    proj_energy,
    pair_flags,
    tile_counts,
    tgt_amp,
    proj_amp,
):
    points = quad_weight.shape[0]
    rows, two_cols = tgt_amp.shape
    sizes = [lax.axis_size(axis) for axis in DEVICES]

    def call(kernel, out_shape, in_specs, scratch_shapes=(), cost=None):
        return pl.pallas_call(
            kernel,
            out_shape=out_shape,
            in_specs=in_specs,
            out_specs=[VMEM] * len(out_shape),
            scratch_shapes=scratch_shapes,
            cost_estimate=cost,
            compiler_params=pltpu.CompilerParams(vmem_limit_bytes=VMEM_LIMIT),
        )

    def run(kernel, out_shape, *blocks):
        return call(kernel, out_shape, [VMEM] * len(blocks))(*blocks)

    def other_core(block):
        return lax.ppermute(block, "rep", [(0, 1), (1, 0)])

    n_tgt, n_prj, n_core = sizes
    tgt_flips = [n_prj * n_core << bit for bit in range(n_tgt.bit_length() - 1)]
    prj_flips = [n_core << bit for bit in range(n_prj.bit_length() - 1)]
    steps = list(zip(prj_flips + tgt_flips, tgt_flips + prj_flips))
    gate_steps = (len(prj_flips) - 1, len(tgt_flips) - 1)

    in_vmem = pltpu.VMEM
    basis = in_vmem((2, 2, rows, points), jnp.bfloat16)
    sums = in_vmem((two_cols, points), jnp.bfloat16)
    both_halves = in_vmem((2, two_cols, points), jnp.bfloat16)
    segment = in_vmem((two_cols, rows), jnp.float32)

    def summed(block):
        for step, flips in enumerate(steps):
            pairs = [(me, me ^ flips[me % n_core]) for me in range(n_tgt * n_prj * n_core)]
            groups = [list(pair) for pair in pairs if pair[0] < pair[1]]
            both = lax.all_gather(block, DEVICES, axis_index_groups=groups)
            (block,) = run(functools.partial(add_kernel, step), [both_halves], gate, both)
        return block

    tgt_other, proj_other = other_core(tgt_amp), other_core(proj_amp)
    inputs = (
        pair_flags.T,
        tile_counts.T,
        quad_weight,
        tgt_basis.reshape(2, -1, rows, points),
        proj_basis,
        tgt_energy,
        proj_energy,
        tgt_amp,
        proj_amp,
    )
    mine, sent, send_own, small_send, gate, weight, energy, amp, part = call(
        functools.partial(load_kernel, gate_steps),
        [
            basis,
            basis,
            in_vmem((2, rows, points), jnp.bfloat16),
            in_vmem((2, 1, points), jnp.float32),
            in_vmem((len(steps), 2, 1, points), jnp.float32),
            in_vmem((1, 1, points), jnp.float32),
            in_vmem((2, 1, rows), jnp.float32),
            in_vmem((2, two_cols, rows), jnp.float32),
            in_vmem((2, two_cols, points), jnp.float32),
        ],
        [HBM] * len(inputs),
        [
            pltpu.SMEM(pair_flags.T.shape, jnp.int32),
            pltpu.SMEM(tile_counts.T.shape, jnp.int32),
            pltpu.VMEM((points,), jnp.float32),
            pltpu.VMEM((rows,), jnp.float32),
            pltpu.VMEM(tgt_amp.shape, jnp.float32),
            pltpu.VMEM(proj_amp.shape, jnp.float32),
            pltpu.SemaphoreType.DMA((13,)),
        ],
        pl.CostEstimate(flops=2 * 4 * rows * two_cols * points, bytes_accessed=4 * 1024 * 1024, transcendentals=0),
    )(*[pltpu.with_memory_space_constraint(block, pltpu.HBM) for block in inputs])
    near, far, other = run(
        first_kernel, [sums, sums, segment], mine, sent, weight, part, tgt_other, proj_other
    )
    far = other_core(far)
    sent, send_own, small_send, far = lax.optimization_barrier((sent, send_own, small_send, far))
    theirs, own_far, small = other_core(sent), other_core(send_own), other_core(small_send)
    (z,) = run(pack_kernel, [both_halves], near, far)
    field = summed(z)
    z, my_half = run(
        second_kernel,
        [both_halves, segment],
        mine,
        theirs,
        other_core(field),
        weight,
        small,
        energy,
        amp,
        other,
    )
    (other_half,) = run(other_half_kernel, [segment], sent, own_far, field, energy, amp)
    field = summed(z)
    (other_new,) = run(
        other_last_kernel,
        [in_vmem((rows, two_cols), jnp.float32)],
        sent,
        own_far,
        field,
        energy,
        amp,
        other_half,
    )
    return run(
        last_kernel,
        [
            jax.ShapeDtypeStruct(tgt_amp.shape, jnp.float32),
            jax.ShapeDtypeStruct(proj_amp.shape, jnp.float32),
        ],
        mine,
        theirs,
        other_core(field),
        energy,
        amp,
        my_half,
        other_new,
    )


def solution(mesh):
    in_specs = (
        P(None, "tgt", "rep"),
        P(None, None, "prj", "rep"),
        P(("bpar", "rep")),
        P(("tgt", "prj", "rep")),
        P(("tgt", "rep"), "prj"),
        P("bpar", None),
        P("bpar", None),
        P(("bpar", "tgt", "prj", "rep"), None),
        P(("bpar", "tgt", "rep"), "prj", None),
    )
    out_specs = (P(("bpar", "tgt", "prj", "rep"), None), P(("bpar", "tgt", "rep"), "prj", None))

    def step(*args):
        return tuple(shards(*args))

    return jax.shard_map(step, mesh=mesh, in_specs=in_specs, out_specs=out_specs, check_vma=False)
```

```python
import functools

import jax
import jax.numpy as jnp
from jax import lax
from jax.experimental import pallas as pl
from jax.experimental.pallas import tpu as pltpu
from jax.sharding import PartitionSpec as P

time_step = 0.4
half_step = 0.5 * time_step
VMEM_LIMIT = 8 * 1024 * 1024
DEVICES = ("tgt", "prj", "rep")
HBM = pl.BlockSpec(memory_space=pl.ANY)
VMEM = pl.BlockSpec(memory_space=pltpu.VMEM)


def parity(place):
    odd = 0
    while place:
        odd, place = odd ^ (place & 1), place >> 1
    return odd


def my_kind():
    n_tgt, n_prj = lax.axis_size("tgt"), lax.axis_size("prj")
    place = lax.axis_index("tgt") * n_prj + lax.axis_index("prj")
    kind = lax.axis_index("rep")
    for bit in range((n_tgt * n_prj).bit_length() - 1):
        kind = jnp.bitwise_xor(kind, jnp.bitwise_and(lax.shift_right_logical(place, bit), 1))
    return kind


def ordered(core, first, second):
    return jnp.where(core == 0, first, second), jnp.where(core == 0, second, first)


def turned(block):
    half = block.shape[0] // 2
    return jnp.concatenate([block[half:], -block[:half]], axis=0)


def bf16(block):
    return block.astype(jnp.bfloat16)


def f32(block):
    return block.astype(jnp.float32)


def project(basis_real, basis_imag, amp):
    return jnp.dot(bf16(amp), basis_real, preferred_element_type=jnp.float32) + jnp.dot(
        bf16(turned(amp)), basis_imag, preferred_element_type=jnp.float32
    )


def expand(basis_real, basis_imag, field):
    contract = (((1,), (1,)), ((), ()))
    return lax.dot_general(
        turned(field), basis_real, contract, preferred_element_type=jnp.float32
    ) + lax.dot_general(field, basis_imag, contract, preferred_element_type=jnp.float32)


def load_kernel(
    weight_hbm,
    tgt_hbm,
    proj_hbm,
    tgt_own_hbm,
    proj_own_hbm,
    mine,
    sent,
    weight,
    amp_ref,
    part_ref,
    flat_weight,
    tgt_own,
    proj_own,
    sems,
):
    core = lax.axis_index("rep")
    my = my_kind()
    sources = (
        tgt_hbm.at[:, pl.ds(2 * lax.axis_index("prj"), 2)],
        proj_hbm.at[:, pl.ds(2 * lax.axis_index("tgt"), 2)],
    )

    def basis_copies(kind):
        return [
            pltpu.make_async_copy(sources[source].at[part], basis.at[part], sems.at[2 * slot + part])
            for slot, (source, basis) in enumerate(((kind, mine), (1 - kind, sent)))
            for part in range(2)
        ]

    pairs = [(tgt_own_hbm, tgt_own), (proj_own_hbm, proj_own), (weight_hbm, flat_weight)]
    copies = [pltpu.make_async_copy(src, dst, sems.at[4 + k]) for k, (src, dst) in enumerate(pairs)]
    for copy in copies:
        copy.start()
    for kind in range(2):

        @pl.when(my == kind)
        def _():
            for copy in basis_copies(kind):
                copy.start()

    for copy in copies:
        copy.wait()
    weight[0] = flat_weight[...][None, :]
    amp_ref[0] = tgt_own[...].T
    amp_ref[1] = proj_own[0].T
    for copy in basis_copies(0):
        copy.wait()
    for slot, (basis, kind) in enumerate(((mine, my), (sent, 1 - my))):
        part_ref[slot] = project(basis[0, core], basis[1, core], amp_ref[kind])


def first_kernel(mine, sent, weight, part_ref, tgt_other, proj_other, near_ref, swap_ref, other_ref):
    core = lax.axis_index("rep")
    my = my_kind()
    my_amp, other_amp = ordered(my, tgt_other[...].T, proj_other[0].T)
    other_ref[...] = my_amp
    for slot, (basis, amp, out_ref) in enumerate(((mine, my_amp, near_ref), (sent, other_amp, swap_ref))):
        total = part_ref[slot] + project(basis[0, 1 - core], basis[1, 1 - core], amp)
        out_ref[...] = bf16(weight[0] * total)


def side_kernel(
    gate_steps,
    flags_hbm,
    counts_hbm,
    weight,
    tgt_energy_hbm,
    proj_energy_hbm,
    mine,
    near,
    gate,
    energy,
    small_send,
    send_own,
    flags,
    counts,
    flat_energy,
    sems,
):
    core = lax.axis_index("rep")
    my = my_kind()
    tgt_index = lax.axis_index("tgt")
    prj_index = lax.axis_index("prj")
    pairs = [
        (flags_hbm, flags),
        (counts_hbm, counts),
        (tgt_energy_hbm, flat_energy),
        (proj_energy_hbm, energy.at[1]),
    ]
    copies = [pltpu.make_async_copy(src, dst, sems.at[k]) for k, (src, dst) in enumerate(pairs)]
    for copy in copies:
        copy.start()
    for part in range(2):
        send_own[part] = mine[part, 1 - core]
    for copy in copies:
        copy.wait()
    energy[0] = flat_energy[...][None, :]
    small_send[0] = weight[0]
    small_send[1, :, : energy.shape[2]] = energy[1 - my]
    tiles = 2
    width = gate.shape[-1] // tiles
    gate_step = jnp.where(my == 0, *gate_steps)
    for half in range(2):
        for tile in range(tiles):
            live = jnp.logical_and(
                flags[prj_index, tgt_index] > 0, tiles * half + tile < counts[prj_index, tgt_index]
            )
            value = jnp.where(live, 1.0, 0.0).astype(jnp.float32)
            for step in range(gate.shape[0]):
                here = jnp.where(step == gate_step, value, jnp.float32(1.0))
                gate[step, half, :, tile * width : (tile + 1) * width] = jnp.full(
                    (1, width), here, jnp.float32
                )


def pack_kernel(near, far, low, high):
    low[...], high[...] = ordered(lax.axis_index("rep"), near[...], far[...])


def add_kernel(step, half, gate, own, other, out_ref):
    out_ref[...] = bf16(gate[step, half] * (f32(own[...]) + f32(other[...])))


def second_kernel(
    mine, theirs, low, high, weight, small, energy, amp_ref, other_ref, low_ref, high_ref, half_ref
):
    core = lax.axis_index("rep")
    my = my_kind()
    near, far = ordered(core, low[...], high[...])

    def change(segment):
        return expand(mine[0, segment], mine[1, segment], near) + expand(
            theirs[0, segment], theirs[1, segment], far
        )

    amp, other = amp_ref[my], other_ref[...]
    other_energy = small[1, :, : energy.shape[2]]
    amp = amp + half_step * (energy[my] * turned(amp) + change(core))
    other = other + half_step * (other_energy * turned(other) + change(1 - core))
    half_ref[...] = amp
    near, far = [
        bf16(
            weights
            * (
                project(basis[0, core], basis[1, core], amp)
                + project(basis[0, 1 - core], basis[1, 1 - core], other)
            )
        )
        for basis, weights in ((mine, weight[0]), (theirs, small[0]))
    ]
    low_ref[...], high_ref[...] = ordered(core, near, far)


def other_half_kernel(sent, own_far, low, high, energy, amp_ref, half_ref):
    core = lax.axis_index("rep")
    kind = 1 - my_kind()
    near, far = ordered(core, low[...], high[...])
    amp = amp_ref[kind]
    change = expand(sent[0, core], sent[1, core], near) + expand(own_far[0], own_far[1], far)
    half_ref[...] = amp + half_step * (energy[kind] * turned(amp) + change)


def other_last_kernel(sent, own_far, low, high, energy, amp_ref, half_ref, new_ref):
    core = lax.axis_index("rep")
    kind = 1 - my_kind()
    near, far = ordered(core, low[...], high[...])
    change = expand(sent[0, core], sent[1, core], near) + expand(own_far[0], own_far[1], far)
    rate = energy[kind] * turned(half_ref[...]) + change
    new_ref[...] = (amp_ref[kind] + time_step * rate).T


def last_kernel(mine, theirs, low, high, energy, amp_ref, half_ref, other_new, new_tgt, new_proj):
    core = lax.axis_index("rep")
    my = my_kind()
    near, far = ordered(core, low[...], high[...])
    change = expand(mine[0, core], mine[1, core], near) + expand(theirs[0, core], theirs[1, core], far)
    rate = energy[my] * turned(half_ref[...]) + change
    my_new = (amp_ref[my] + time_step * rate).T
    new_tgt[...], new_proj[0] = ordered(my, my_new, other_new[...])


def shards(
    tgt_basis,
    proj_basis,
    quad_weight,
    tgt_energy,
    proj_energy,
    pair_flags,
    tile_counts,
    tgt_amp,
    proj_amp,
):
    points = quad_weight.shape[0]
    rows, two_cols = tgt_amp.shape
    sizes = [lax.axis_size(axis) for axis in DEVICES]

    def call(kernel, out_shape, in_specs, scratch_shapes=(), cost=None):
        return pl.pallas_call(
            kernel,
            out_shape=out_shape,
            in_specs=in_specs,
            out_specs=[VMEM] * len(out_shape),
            scratch_shapes=scratch_shapes,
            cost_estimate=cost,
            compiler_params=pltpu.CompilerParams(vmem_limit_bytes=VMEM_LIMIT),
        )

    def run(kernel, out_shape, *blocks):
        return call(kernel, out_shape, [VMEM] * len(blocks))(*blocks)

    def other_core(block):
        return lax.ppermute(block, "rep", [(0, 1), (1, 0)])

    n_tgt, n_prj, n_core = sizes
    tgt_flips = [n_prj << bit for bit in range(n_tgt.bit_length() - 1)]
    prj_flips = [1 << bit for bit in range(n_prj.bit_length() - 1)]
    flips = [(prj_flips + along_tgt, along_tgt + prj_flips) for along_tgt in (tgt_flips, tgt_flips[::-1])]
    gate_steps = (len(prj_flips) - 1, len(tgt_flips) - 1)
    n_steps = len(tgt_flips) + len(prj_flips)

    def step_pairs(half, step):
        pairs = []
        for place in range(n_tgt * n_prj):
            for kind in range(2):
                there = place ^ flips[half][kind][step]
                pairs.append((place * n_core + (kind ^ parity(place)), there * n_core + (kind ^ parity(there))))
        return pairs

    in_vmem = pltpu.VMEM
    basis = in_vmem((2, 2, rows, points), jnp.bfloat16)
    sums = in_vmem((two_cols, points), jnp.bfloat16)
    segment = in_vmem((two_cols, rows), jnp.float32)

    def summed(*halves):
        totals = []
        for half, block in enumerate(halves):
            for step in range(n_steps):
                other = lax.ppermute(block, DEVICES, step_pairs(half, step))
                (block,) = run(functools.partial(add_kernel, step, half), [sums], gate, block, other)
            totals.append(block)
        return totals

    def swapped(fields):
        return [other_core(block) for block in fields]

    tgt_other, proj_other = other_core(tgt_amp), other_core(proj_amp)
    def in_hbm(*blocks):
        return [pltpu.with_memory_space_constraint(block, pltpu.HBM) for block in blocks]

    mine, sent, weight, amp, part = call(
        load_kernel,
        [
            basis,
            basis,
            in_vmem((1, 1, points), jnp.float32),
            in_vmem((2, two_cols, rows), jnp.float32),
            in_vmem((2, two_cols, points), jnp.float32),
        ],
        [HBM] * 5,
        [
            pltpu.VMEM((points,), jnp.float32),
            pltpu.VMEM(tgt_amp.shape, jnp.float32),
            pltpu.VMEM(proj_amp.shape, jnp.float32),
            pltpu.SemaphoreType.DMA((7,)),
        ],
        pl.CostEstimate(
            flops=2 * 4 * rows * two_cols * points, bytes_accessed=4 * 1024 * 1024, transcendentals=0
        ),
    )(*in_hbm(quad_weight, tgt_basis.reshape(2, -1, rows, points), proj_basis, tgt_amp, proj_amp))
    near, swap, other = run(
        first_kernel, [sums, sums, segment], mine, sent, weight, part, tgt_other, proj_other
    )
    far = other_core(swap)
    flags, counts = pair_flags.T, tile_counts.T
    gate, energy, small_send, send_own = call(
        functools.partial(side_kernel, gate_steps),
        [
            in_vmem((n_steps, 2, 1, points), jnp.float32),
            in_vmem((2, 1, rows), jnp.float32),
            in_vmem((2, 1, points), jnp.float32),
            in_vmem((2, rows, points), jnp.bfloat16),
        ],
        [HBM, HBM, VMEM, HBM, HBM, VMEM, VMEM],
        [
            pltpu.SMEM(flags.shape, jnp.int32),
            pltpu.SMEM(counts.shape, jnp.int32),
            pltpu.VMEM((rows,), jnp.float32),
            pltpu.SemaphoreType.DMA((4,)),
        ],
    )(*in_hbm(flags, counts), weight, *in_hbm(tgt_energy, proj_energy), mine, near)
    sent, far = lax.optimization_barrier((sent, far))
    theirs, own_far, small = other_core(sent), other_core(send_own), other_core(small_send)
    near, far = run(pack_kernel, [sums, sums], near, far)
    fields = summed(near, far)
    near, far, my_half = run(
        second_kernel,
        [sums, sums, segment],
        mine,
        theirs,
        *swapped(fields),
        weight,
        small,
        energy,
        amp,
        other,
    )
    (other_half,) = run(other_half_kernel, [segment], sent, own_far, *fields, energy, amp)
    fields = summed(near, far)
    (other_new,) = run(
        other_last_kernel,
        [in_vmem((rows, two_cols), jnp.float32)],
        sent,
        own_far,
        *fields,
        energy,
        amp,
        other_half,
    )
    return run(
        last_kernel,
        [
            jax.ShapeDtypeStruct(tgt_amp.shape, jnp.float32),
            jax.ShapeDtypeStruct(proj_amp.shape, jnp.float32),
        ],
        mine,
        theirs,
        *swapped(fields),
        energy,
        amp,
        my_half,
        other_new,
    )


def solution(mesh):
    in_specs = (
        P(None, "tgt", "rep"),
        P(None, None, "prj", "rep"),
        P(("bpar", "rep")),
        P(("tgt", "prj", "rep")),
        P(("tgt", "rep"), "prj"),
        P("bpar", None),
        P("bpar", None),
        P(("bpar", "tgt", "prj", "rep"), None),
        P(("bpar", "tgt", "rep"), "prj", None),
    )
    out_specs = (P(("bpar", "tgt", "prj", "rep"), None), P(("bpar", "tgt", "rep"), "prj", None))

    def step(*args):
        return tuple(shards(*args))

    return jax.shard_map(step, mesh=mesh, in_specs=in_specs, out_specs=out_specs, check_vma=False)
```

```python
import functools

import jax
import jax.numpy as jnp
from jax import lax
from jax.experimental import pallas as pl
from jax.experimental.pallas import tpu as pltpu
from jax.sharding import PartitionSpec as P

time_step = 0.4
half_step = 0.5 * time_step
VMEM_LIMIT = 8 * 1024 * 1024
DEVICES = ("tgt", "prj", "rep")
HBM = pl.BlockSpec(memory_space=pl.ANY)
VMEM = pl.BlockSpec(memory_space=pltpu.VMEM)


def parity(place):
    odd = 0
    while place:
        odd, place = odd ^ (place & 1), place >> 1
    return odd


def my_kind():
    n_tgt, n_prj = lax.axis_size("tgt"), lax.axis_size("prj")
    place = lax.axis_index("tgt") * n_prj + lax.axis_index("prj")
    kind = lax.axis_index("rep")
    for bit in range((n_tgt * n_prj).bit_length() - 1):
        kind = jnp.bitwise_xor(kind, jnp.bitwise_and(lax.shift_right_logical(place, bit), 1))
    return kind


def my_segment(kind):
    place = jnp.where(kind == 0, lax.axis_index("prj"), lax.axis_index("tgt"))
    return 2 * jnp.bitwise_and(place, 1) + lax.axis_index("rep")


def ordered(core, first, second):
    return jnp.where(core == 0, first, second), jnp.where(core == 0, second, first)


def turned(block):
    half = block.shape[0] // 2
    return jnp.concatenate([block[half:], -block[:half]], axis=0)


def bf16(block):
    return block.astype(jnp.bfloat16)


def f32(block):
    return block.astype(jnp.float32)


def project(basis_real, basis_imag, amp):
    return jnp.dot(bf16(amp), basis_real, preferred_element_type=jnp.float32) + jnp.dot(
        bf16(turned(amp)), basis_imag, preferred_element_type=jnp.float32
    )


def expand(basis_real, basis_imag, field):
    contract = (((1,), (1,)), ((), ()))
    return lax.dot_general(
        turned(field), basis_real, contract, preferred_element_type=jnp.float32
    ) + lax.dot_general(field, basis_imag, contract, preferred_element_type=jnp.float32)


def load_kernel(
    weight_hbm,
    tgt_hbm,
    proj_hbm,
    tgt_energy_hbm,
    proj_energy_hbm,
    tgt_own_hbm,
    proj_own_hbm,
    mine,
    sent,
    weight,
    energy,
    amp_ref,
    flat_weight,
    flat_energy,
    tgt_own,
    proj_own,
    sems,
):
    my = my_kind()

    def first_segment(axis):
        place = lax.axis_index(axis)
        return 2 * (place - jnp.bitwise_and(place, 1))

    sources = (
        tgt_hbm.at[:, pl.ds(first_segment("prj"), 4)],
        proj_hbm.at[:, pl.ds(first_segment("tgt"), 4)],
    )

    def basis_copies(kind):
        return [
            pltpu.make_async_copy(sources[source].at[part], basis.at[part], sems.at[2 * slot + part])
            for slot, (source, basis) in enumerate(((1 - kind, sent), (kind, mine)))
            for part in range(2)
        ]

    pairs = [
        (tgt_own_hbm, tgt_own),
        (proj_own_hbm, proj_own),
        (weight_hbm, flat_weight),
        (tgt_energy_hbm, flat_energy),
        (proj_energy_hbm, energy.at[1]),
    ]
    copies = [pltpu.make_async_copy(src, dst, sems.at[4 + k]) for k, (src, dst) in enumerate(pairs)]
    for copy in copies:
        copy.start()
    for kind in range(2):

        @pl.when(my == kind)
        def _():
            for copy in basis_copies(kind):
                copy.start()

    for copy in copies:
        copy.wait()
    weight[0] = flat_weight[...][None, :]
    energy[0] = flat_energy[...][None, :]
    amp_ref[0] = tgt_own[...].T
    amp_ref[1] = proj_own[0].T
    for copy in basis_copies(0):
        copy.wait()


def pack_kernel(
    amp_ref,
    energy,
    tgt_other,
    proj_other,
    tgt_energy_other,
    proj_energy_other,
    near_weight,
    far_weight,
    chip_amp,
    chip_energy,
    weights,
    message,
):
    core = lax.axis_index("rep")
    my = my_kind()
    cols = chip_amp.shape[1]
    other_amp, _ = ordered(my, tgt_other[...].T, proj_other[0].T)
    other_energy, _ = ordered(my, tgt_energy_other[...][None, :], proj_energy_other[...])
    amps = ordered(core, amp_ref[my], other_amp)
    energies = ordered(core, energy[my], other_energy)
    weights[0] = near_weight[0]
    weights[1] = far_weight[...][None, :]
    extra = message.shape[1] - cols
    for segment in range(2):
        chip_amp[segment] = amps[segment]
        chip_energy[segment] = energies[segment]
        message[segment, :cols] = bf16(amps[segment])
        row = lax.broadcasted_iota(jnp.int32, (extra, energies[segment].shape[1]), 0)
        rest = energies[segment]
        block = jnp.zeros(row.shape, jnp.float32)
        for piece in range(3):
            rounded = f32(bf16(rest))
            block = jnp.where(row == piece, rounded, block)
            rest = rest - rounded
        message[segment, cols:] = bf16(block)


def side_kernel(gate_levels, flags_hbm, counts_hbm, amp_ref, mine, gate, send_own, flags, counts, sems):
    my = my_kind()
    tgt_index = lax.axis_index("tgt")
    prj_index = lax.axis_index("prj")
    pairs = [(flags_hbm, flags), (counts_hbm, counts)]
    copies = [pltpu.make_async_copy(src, dst, sems.at[k]) for k, (src, dst) in enumerate(pairs)]
    for copy in copies:
        copy.start()
    other = my_segment(my) + 1 - 2 * lax.axis_index("rep")
    for part in range(2):
        send_own[part] = mine[part, other]
    for copy in copies:
        copy.wait()
    tiles = 2
    width = gate.shape[-1] // tiles
    gate_level = jnp.where(my == 0, *gate_levels)
    for half in range(2):
        for tile in range(tiles):
            live = jnp.logical_and(
                flags[prj_index, tgt_index] > 0, tiles * half + tile < counts[prj_index, tgt_index]
            )
            value = jnp.where(live, 1.0, 0.0).astype(jnp.float32)
            for level in range(gate.shape[0]):
                here = jnp.where(level == gate_level, value, jnp.float32(1.0))
                gate[level, half, :, tile * width : (tile + 1) * width] = jnp.full(
                    (1, width), here, jnp.float32
                )


def chip_kernel(mine, theirs, chip_amp, part_ref):
    first = my_segment(my_kind()) - lax.axis_index("rep")
    for slot, basis in enumerate((mine, theirs)):
        part_ref[slot] = project(basis[0, first], basis[1, first], chip_amp[0]) + project(
            basis[0, first + 1], basis[1, first + 1], chip_amp[1]
        )


def weigh(gate, weights, near, far, low_ref, high_ref):
    low, high = ordered(lax.axis_index("rep"), weights[0] * near, weights[1] * far)
    low_ref[...] = bf16(gate[0, 0] * low)
    high_ref[...] = bf16(gate[0, 1] * high)


def first_kernel(mine, theirs, gate, weights, part_ref, message, low_ref, high_ref):
    first = 2 - my_segment(my_kind()) + lax.axis_index("rep")
    cols = part_ref.shape[1]
    near, far = [
        part_ref[slot]
        + project(basis[0, first], basis[1, first], f32(message[0, :cols]))
        + project(basis[0, first + 1], basis[1, first + 1], f32(message[1, :cols]))
        for slot, basis in enumerate((mine, theirs))
    ]
    weigh(gate, weights, near, far, low_ref, high_ref)


def add_kernel(level, half, gate, own, other, out_ref):
    out_ref[...] = bf16(gate[level, half] * (f32(own[...]) + f32(other[...])))


def second_kernel(
    mine,
    theirs,
    low,
    high,
    gate,
    weights,
    chip_amp,
    chip_energy,
    message,
    low_ref,
    high_ref,
    half_ref,
    send_ref,
):
    core = lax.axis_index("rep")
    first = my_segment(my_kind()) - core
    cols = chip_amp.shape[1]
    fields = ordered(core, low[...], high[...])
    halves = []
    for segment in range(4):
        if segment < 2:
            place, amp, energy = first + segment, chip_amp[segment], chip_energy[segment]
        else:
            place = 2 - first + segment - 2
            amp = f32(message[segment - 2, :cols])
            pieces = f32(message[segment - 2, cols:])
            energy = pieces[0:1] + pieces[1:2] + pieces[2:3]
        change = sum(
            expand(basis[0, place], basis[1, place], field)
            for basis, field in zip((mine, theirs), fields)
        )
        halves.append((place, amp + half_step * (energy * turned(amp) + change)))
    half_ref[...], send_ref[...] = ordered(core, halves[0][1], halves[1][1])
    near, far = [
        sum(project(basis[0, place], basis[1, place], half) for place, half in halves)
        for basis in (mine, theirs)
    ]
    weigh(gate, weights, near, far, low_ref, high_ref)


def other_last_kernel(sent, own_far, low, high, energy, amp_ref, half_ref, new_ref):
    kind = 1 - my_kind()
    place = my_segment(kind)
    near, far = ordered(lax.axis_index("rep"), low[...], high[...])
    change = expand(sent[0, place], sent[1, place], near) + expand(own_far[0], own_far[1], far)
    rate = energy[kind] * turned(half_ref[...]) + change
    new_ref[...] = (amp_ref[kind] + time_step * rate).T


def last_kernel(mine, theirs, low, high, energy, amp_ref, half_ref, other_new, new_tgt, new_proj):
    my = my_kind()
    place = my_segment(my)
    near, far = ordered(lax.axis_index("rep"), low[...], high[...])
    change = expand(mine[0, place], mine[1, place], near) + expand(theirs[0, place], theirs[1, place], far)
    rate = energy[my] * turned(half_ref[...]) + change
    my_new = (amp_ref[my] + time_step * rate).T
    new_tgt[...], new_proj[0] = ordered(my, my_new, other_new[...])


def shards(
    tgt_basis,
    proj_basis,
    quad_weight,
    tgt_energy,
    proj_energy,
    pair_flags,
    tile_counts,
    tgt_amp,
    proj_amp,
):
    points = quad_weight.shape[0]
    rows, two_cols = tgt_amp.shape
    sizes = [lax.axis_size(axis) for axis in DEVICES]

    def call(kernel, out_shape, in_specs, scratch_shapes=(), cost=None):
        return pl.pallas_call(
            kernel,
            out_shape=out_shape,
            in_specs=in_specs,
            out_specs=[VMEM] * len(out_shape),
            scratch_shapes=scratch_shapes,
            cost_estimate=cost,
            compiler_params=pltpu.CompilerParams(vmem_limit_bytes=VMEM_LIMIT),
        )

    def run(kernel, out_shape, *blocks):
        return call(kernel, out_shape, [VMEM] * len(blocks))(*blocks)

    def other_core(block):
        return lax.ppermute(block, "rep", [(0, 1), (1, 0)])

    n_tgt, n_prj, n_core = sizes
    tgt_flips = [n_prj << bit for bit in range(n_tgt.bit_length() - 1)]
    prj_flips = [1 << bit for bit in range(n_prj.bit_length() - 1)]
    flips = (prj_flips + tgt_flips, tgt_flips + prj_flips)
    gate_levels = (len(prj_flips) - 1, len(tgt_flips) - 1)
    n_steps = len(tgt_flips) + len(prj_flips)

    def exchanged(step, block):
        pairs = []
        for place in range(n_tgt * n_prj):
            for kind in range(2):
                there = place ^ flips[kind][step]
                pairs.append((place * n_core + (kind ^ parity(place)), there * n_core + (kind ^ parity(there))))
        return lax.ppermute(block, DEVICES, pairs)

    in_vmem = pltpu.VMEM
    basis = in_vmem((2, 4, rows, points), jnp.bfloat16)
    sums = in_vmem((two_cols, points), jnp.bfloat16)
    segment = in_vmem((two_cols, rows), jnp.float32)

    def summed(*halves):
        totals = []
        for half, block in enumerate(halves):
            for step in range(1, n_steps):
                other = exchanged(step, block)
                (block,) = run(functools.partial(add_kernel, step, half), [sums], gate, block, other)
            totals.append(block)
        return totals

    def swapped(fields):
        return [other_core(block) for block in fields]

    def in_hbm(*blocks):
        return [pltpu.with_memory_space_constraint(block, pltpu.HBM) for block in blocks]

    others = swapped([tgt_amp, proj_amp, tgt_energy, proj_energy])
    far_weight = other_core(quad_weight)
    bases = (tgt_basis.reshape(2, -1, rows, points), proj_basis)
    mine, sent, weight, energy, amp = call(
        load_kernel,
        [
            basis,
            basis,
            in_vmem((1, 1, points), jnp.float32),
            in_vmem((2, 1, rows), jnp.float32),
            in_vmem((2, two_cols, rows), jnp.float32),
        ],
        [HBM] * 7,
        [
            pltpu.VMEM((points,), jnp.float32),
            pltpu.VMEM((rows,), jnp.float32),
            pltpu.VMEM(tgt_amp.shape, jnp.float32),
            pltpu.VMEM(proj_amp.shape, jnp.float32),
            pltpu.SemaphoreType.DMA((9,)),
        ],
        pl.CostEstimate(
            flops=2 * 4 * rows * two_cols * points, bytes_accessed=4 * 1024 * 1024, transcendentals=0
        ),
    )(*in_hbm(quad_weight, *bases, tgt_energy, proj_energy, tgt_amp, proj_amp))
    chip_amp, chip_energy, weights, message = run(
        pack_kernel,
        [
            in_vmem((2, two_cols, rows), jnp.float32),
            in_vmem((2, 1, rows), jnp.float32),
            in_vmem((2, 1, points), jnp.float32),
            in_vmem((2, two_cols + 16, rows), jnp.bfloat16),
        ],
        amp,
        energy,
        *others,
        weight,
        far_weight,
    )
    sent, message = lax.optimization_barrier((sent, message))
    message = exchanged(0, message)
    theirs = other_core(sent)
    flags, counts = pair_flags.T, tile_counts.T
    gate, send_own = call(
        functools.partial(side_kernel, gate_levels),
        [
            in_vmem((n_steps, 2, 1, points), jnp.float32),
            in_vmem((2, rows, points), jnp.bfloat16),
        ],
        [HBM, HBM, VMEM, VMEM],
        [
            pltpu.SMEM(flags.shape, jnp.int32),
            pltpu.SMEM(counts.shape, jnp.int32),
            pltpu.SemaphoreType.DMA((2,)),
        ],
    )(*in_hbm(flags, counts), chip_amp, mine)
    own_far = other_core(send_own)
    (part,) = run(
        chip_kernel, [in_vmem((2, two_cols, points), jnp.float32)], mine, theirs, chip_amp
    )
    halves = run(first_kernel, [sums] * 2, mine, theirs, gate, weights, part, message)
    fields = summed(*halves)
    *halves, my_half, half_send = run(
        second_kernel,
        [sums, sums, segment, segment],
        mine,
        theirs,
        *swapped(fields),
        gate,
        weights,
        chip_amp,
        chip_energy,
        message,
    )
    other_half = other_core(half_send)
    fields = summed(*halves)
    (other_new,) = run(
        other_last_kernel,
        [in_vmem((rows, two_cols), jnp.float32)],
        sent,
        own_far,
        *fields,
        energy,
        amp,
        other_half,
    )
    return run(
        last_kernel,
        [
            jax.ShapeDtypeStruct(tgt_amp.shape, jnp.float32),
            jax.ShapeDtypeStruct(proj_amp.shape, jnp.float32),
        ],
        mine,
        theirs,
        *swapped(fields),
        energy,
        amp,
        my_half,
        other_new,
    )


def solution(mesh):
    in_specs = (
        P(None, "tgt", "rep"),
        P(None, None, "prj", "rep"),
        P(("bpar", "rep")),
        P(("tgt", "prj", "rep")),
        P(("tgt", "rep"), "prj"),
        P("bpar", None),
        P("bpar", None),
        P(("bpar", "tgt", "prj", "rep"), None),
        P(("bpar", "tgt", "rep"), "prj", None),
    )
    out_specs = (P(("bpar", "tgt", "prj", "rep"), None), P(("bpar", "tgt", "rep"), "prj", None))

    def step(*args):
        return tuple(shards(*args))

    return jax.shard_map(step, mesh=mesh, in_specs=in_specs, out_specs=out_specs, check_vma=False)
```

```python
import functools

import jax
import jax.numpy as jnp
from jax import lax
from jax.experimental import pallas as pl
from jax.experimental.pallas import tpu as pltpu
from jax.sharding import PartitionSpec as P

time_step = 0.4
half_step = 0.5 * time_step
VMEM_LIMIT = 8 * 1024 * 1024
DEVICES = ("tgt", "prj", "rep")
HBM = pl.BlockSpec(memory_space=pl.ANY)
VMEM = pl.BlockSpec(memory_space=pltpu.VMEM)


def parity(place):
    odd = 0
    while place:
        odd, place = odd ^ (place & 1), place >> 1
    return odd


def my_kind():
    n_tgt, n_prj = lax.axis_size("tgt"), lax.axis_size("prj")
    place = lax.axis_index("tgt") * n_prj + lax.axis_index("prj")
    kind = lax.axis_index("rep")
    for bit in range((n_tgt * n_prj).bit_length() - 1):
        kind = jnp.bitwise_xor(kind, jnp.bitwise_and(lax.shift_right_logical(place, bit), 1))
    return kind


def by_core(body):
    for core in range(2):

        @pl.when(lax.axis_index("rep") == core)
        def _():
            body(core)


def ordered(core, first, second):
    return jnp.where(core == 0, first, second), jnp.where(core == 0, second, first)


def turned(block):
    half = block.shape[0] // 2
    return jnp.concatenate([block[half:], -block[:half]], axis=0)


def bf16(block):
    return block.astype(jnp.bfloat16)


def f32(block):
    return block.astype(jnp.float32)


def project(basis_real, basis_imag, amp):
    return jnp.dot(bf16(amp), basis_real, preferred_element_type=jnp.float32) + jnp.dot(
        bf16(turned(amp)), basis_imag, preferred_element_type=jnp.float32
    )


def expand(basis_real, basis_imag, field):
    contract = (((1,), (1,)), ((), ()))
    return lax.dot_general(
        turned(field), basis_real, contract, preferred_element_type=jnp.float32
    ) + lax.dot_general(field, basis_imag, contract, preferred_element_type=jnp.float32)


def load_kernel(
    neighbours,
    weight_hbm,
    tgt_hbm,
    proj_hbm,
    tgt_energy_hbm,
    proj_energy_hbm,
    tgt_own_hbm,
    proj_own_hbm,
    mine,
    sent,
    small,
    energy,
    amp_ref,
    flat_weight,
    flat_energy,
    tgt_own,
    proj_own,
    sems,
):
    my = my_kind()
    places = (lax.axis_index("prj"), lax.axis_index("tgt"))
    sources = (tgt_hbm, proj_hbm)

    def basis_copies(my):
        return [
            pltpu.make_async_copy(
                sources[kind].at[part, pl.ds(2 * place, 2)],
                basis.at[part, 2 * chip : 2 * chip + 2],
                sems.at[4 * slot + 2 * chip + part],
            )
            for slot, (kind, basis) in enumerate(((1 - my, sent), (my, mine)))
            for chip, place in enumerate(
                (places[kind], jnp.bitwise_xor(places[kind], neighbours[kind]))
            )
            for part in range(2)
        ]

    pairs = [
        (tgt_own_hbm, tgt_own),
        (proj_own_hbm, proj_own),
        (weight_hbm, flat_weight),
        (tgt_energy_hbm, flat_energy),
        (proj_energy_hbm, energy.at[1]),
    ]
    copies = [pltpu.make_async_copy(src, dst, sems.at[8 + k]) for k, (src, dst) in enumerate(pairs)]
    for copy in copies:
        copy.start()
    for kind in range(2):

        @pl.when(my == kind)
        def _():
            for copy in basis_copies(kind):
                copy.start()

    for copy in copies:
        copy.wait()
    energy[0] = flat_energy[...][None, :]
    small[0] = flat_weight[...][None, :]
    small[1, :, : energy.shape[2]] = energy[1 - my]
    amp_ref[0] = tgt_own[...].T
    amp_ref[1] = proj_own[0].T
    for copy in basis_copies(0):
        copy.wait()


def pack_kernel(amp_ref, mine, tgt_other, proj_other, chip_amp, message, send_own):
    core = lax.axis_index("rep")
    my = my_kind()
    other_amp, _ = ordered(my, tgt_other[...].T, proj_other[0].T)
    amps = ordered(core, amp_ref[my], other_amp)
    for segment in range(2):
        chip_amp[segment] = amps[segment]
        message[segment] = bf16(amps[segment])
    for part in range(2):
        send_own[part] = mine[part, 1 - core]


def small_kernel(small, far_small, energy, weights, energies):
    rows = energy.shape[2]
    core = lax.axis_index("rep")
    weights[0], weights[1] = ordered(core, small[0], far_small[0])
    energies[0], energies[1] = ordered(core, energy[my_kind()], far_small[1, :, :rows])


def side_kernel(gate_levels, flags_hbm, counts_hbm, chip_amp, gate, flags, counts, sems):
    my = my_kind()
    tgt_index = lax.axis_index("tgt")
    prj_index = lax.axis_index("prj")
    pairs = [(flags_hbm, flags), (counts_hbm, counts)]
    copies = [pltpu.make_async_copy(src, dst, sems.at[k]) for k, (src, dst) in enumerate(pairs)]
    for copy in copies:
        copy.start()
    for copy in copies:
        copy.wait()
    tiles = 2
    width = gate.shape[-1] // tiles
    gate_level = jnp.where(my == 0, *gate_levels)
    for half in range(2):
        for tile in range(tiles):
            live = jnp.logical_and(
                flags[prj_index, tgt_index] > 0, tiles * half + tile < counts[prj_index, tgt_index]
            )
            value = jnp.where(live, 1.0, 0.0).astype(jnp.float32)
            for level in range(gate.shape[0]):
                here = jnp.where(level == gate_level, value, jnp.float32(1.0))
                gate[level, half, :, tile * width : (tile + 1) * width] = jnp.full(
                    (1, width), here, jnp.float32
                )


def chip_kernel(mine, theirs, chip_amp, own_far, part_ref):
    def body(core):
        for half, basis in enumerate((mine, theirs) if core == 0 else (theirs, mine)):
            part_ref[half] = sum(
                project(basis[0, segment], basis[1, segment], chip_amp[segment]) for segment in range(2)
            )

    by_core(body)


def first_kernel(mine, theirs, gate, weights, part_ref, message, neighbour_energies, *outs):
    def body(core):
        for half, basis in enumerate((mine, theirs) if core == 0 else (theirs, mine)):
            total = part_ref[half] + sum(
                project(basis[0, 2 + segment], basis[1, 2 + segment], f32(message[segment]))
                for segment in range(2)
            )
            outs[half][...] = bf16(gate[0, half] * (weights[half] * total))

    by_core(body)


def add_kernel(level, half, gate, own, other, out_ref):
    out_ref[...] = bf16(gate[level, half] * (f32(own[...]) + f32(other[...])))


def low_kernel(mine, theirs, low, change_ref):
    def body(core):
        basis = (mine, theirs)[core]
        for segment in range(4):
            change_ref[segment] = expand(basis[0, segment], basis[1, segment], low[...])

    by_core(body)


def second_kernel(
    mine,
    theirs,
    change_ref,
    high,
    gate,
    weights,
    chip_amp,
    energies,
    message,
    neighbour_energies,
    low_ref,
    high_ref,
    half_ref,
    send_ref,
):
    def body(core):
        bases = (mine, theirs) if core == 0 else (theirs, mine)
        halves = []
        for segment in range(4):
            if segment < 2:
                amp, energy = chip_amp[segment], energies[segment]
            else:
                amp, energy = f32(message[segment - 2]), neighbour_energies[segment - 2]
            change = change_ref[segment] + expand(bases[1][0, segment], bases[1][1, segment], high[...])
            halves.append(amp + half_step * (energy * turned(amp) + change))
        half_ref[...] = halves[core]
        send_ref[...] = halves[1 - core]
        for half, out_ref in enumerate((low_ref, high_ref)):
            total = sum(
                project(bases[half][0, segment], bases[half][1, segment], halves[segment])
                for segment in range(4)
            )
            out_ref[...] = bf16(gate[0, half] * (weights[half] * total))

    by_core(body)


def other_last_kernel(sent, own_far, low, high, energy, amp_ref, half_ref, new_ref):
    def body(core):
        near, far = (low, high) if core == 0 else (high, low)
        kind = 1 - my_kind()
        change = expand(sent[0, core], sent[1, core], near[...]) + expand(own_far[0], own_far[1], far[...])
        rate = energy[kind] * turned(half_ref[...]) + change
        new_ref[...] = (amp_ref[kind] + time_step * rate).T

    by_core(body)


def last_kernel(mine, theirs, low, high, energy, amp_ref, half_ref, other_new, new_tgt, new_proj):
    def body(core):
        near, far = (low, high) if core == 0 else (high, low)
        my = my_kind()
        change = expand(mine[0, core], mine[1, core], near[...]) + expand(
            theirs[0, core], theirs[1, core], far[...]
        )
        rate = energy[my] * turned(half_ref[...]) + change
        my_new = (amp_ref[my] + time_step * rate).T
        new_tgt[...], new_proj[0] = ordered(my, my_new, other_new[...])

    by_core(body)


def shards(
    tgt_basis,
    proj_basis,
    quad_weight,
    tgt_energy,
    proj_energy,
    pair_flags,
    tile_counts,
    tgt_amp,
    proj_amp,
):
    points = quad_weight.shape[0]
    rows, two_cols = tgt_amp.shape
    sizes = [lax.axis_size(axis) for axis in DEVICES]

    def call(kernel, out_shape, in_specs, scratch_shapes=(), cost=None):
        return pl.pallas_call(
            kernel,
            out_shape=out_shape,
            in_specs=in_specs,
            out_specs=[VMEM] * len(out_shape),
            scratch_shapes=scratch_shapes,
            cost_estimate=cost,
            compiler_params=pltpu.CompilerParams(vmem_limit_bytes=VMEM_LIMIT),
        )

    def run(kernel, out_shape, *blocks):
        return call(kernel, out_shape, [VMEM] * len(blocks))(*blocks)

    def other_core(block):
        return lax.ppermute(block, "rep", [(0, 1), (1, 0)])

    n_tgt, n_prj, n_core = sizes
    tgt_flips = [n_prj << bit for bit in range(n_tgt.bit_length() - 1)]
    prj_flips = [1 << bit for bit in range(n_prj.bit_length() - 1)]
    flips = (prj_flips + tgt_flips[::-1], tgt_flips[::-1] + prj_flips)
    neighbours = (flips[0][0], flips[1][0] // n_prj)
    gate_levels = (len(prj_flips) - 1, len(tgt_flips) - 1)
    n_steps = len(tgt_flips) + len(prj_flips)

    def exchanged(step, block):
        pairs = []
        for place in range(n_tgt * n_prj):
            for kind in range(2):
                there = place ^ flips[kind][step]
                pairs.append((place * n_core + (kind ^ parity(place)), there * n_core + (kind ^ parity(there))))
        return lax.ppermute(block, DEVICES, pairs)

    in_vmem = pltpu.VMEM
    basis = in_vmem((2, 4, rows, points), jnp.bfloat16)
    sums = in_vmem((two_cols, points), jnp.bfloat16)
    segment = in_vmem((two_cols, rows), jnp.float32)

    def summed(*halves):
        totals = []
        for half, block in enumerate(halves):
            for step in range(1, n_steps):
                other = exchanged(step, block)
                (block,) = run(functools.partial(add_kernel, step, half), [sums], gate, block, other)
            totals.append(block)
        return totals

    def swapped(fields):
        return [other_core(block) for block in fields]

    def in_hbm(*blocks):
        return [pltpu.with_memory_space_constraint(block, pltpu.HBM) for block in blocks]

    tgt_other, proj_other = other_core(tgt_amp), other_core(proj_amp)
    bases = (tgt_basis.reshape(2, -1, rows, points), proj_basis)
    mine, sent, small, energy, amp = call(
        functools.partial(load_kernel, neighbours),
        [
            basis,
            basis,
            in_vmem((2, 1, points), jnp.float32),
            in_vmem((2, 1, rows), jnp.float32),
            in_vmem((2, two_cols, rows), jnp.float32),
        ],
        [HBM] * 7,
        [
            pltpu.VMEM((points,), jnp.float32),
            pltpu.VMEM((rows,), jnp.float32),
            pltpu.VMEM(tgt_amp.shape, jnp.float32),
            pltpu.VMEM(proj_amp.shape, jnp.float32),
            pltpu.SemaphoreType.DMA((13,)),
        ],
        pl.CostEstimate(
            flops=2 * 4 * rows * two_cols * points, bytes_accessed=4 * 1024 * 1024, transcendentals=0
        ),
    )(*in_hbm(quad_weight, *bases, tgt_energy, proj_energy, tgt_amp, proj_amp))
    chip_amp, message, send_own = run(
        pack_kernel,
        [
            in_vmem((2, two_cols, rows), jnp.float32),
            in_vmem((2, two_cols, rows), jnp.bfloat16),
            in_vmem((2, rows, points), jnp.bfloat16),
        ],
        amp,
        mine,
        tgt_other,
        proj_other,
    )
    sent, small, send_own, message = lax.optimization_barrier((sent, small, send_own, message))
    theirs, far_small, own_far = swapped([sent, small, send_own])
    message = exchanged(0, message)
    weights, energies = run(
        small_kernel,
        [in_vmem((2, 1, points), jnp.float32), in_vmem((2, 1, rows), jnp.float32)],
        small,
        far_small,
        energy,
    )
    neighbour_energies = exchanged(0, energies)
    flags, counts = pair_flags.T, tile_counts.T
    (gate,) = call(
        functools.partial(side_kernel, gate_levels),
        [in_vmem((n_steps, 2, 1, points), jnp.float32)],
        [HBM, HBM, VMEM],
        [
            pltpu.SMEM(flags.shape, jnp.int32),
            pltpu.SMEM(counts.shape, jnp.int32),
            pltpu.SemaphoreType.DMA((2,)),
        ],
    )(*in_hbm(flags, counts), chip_amp)
    (part,) = run(
        chip_kernel, [in_vmem((2, two_cols, points), jnp.float32)], mine, theirs, chip_amp, own_far
    )
    halves = run(
        first_kernel, [sums] * 2, mine, theirs, gate, weights, part, message, neighbour_energies
    )
    fields = summed(*halves)
    low, high = swapped(fields)
    (change,) = run(low_kernel, [in_vmem((4, two_cols, rows), jnp.float32)], mine, theirs, low)
    *halves, my_half, half_send = run(
        second_kernel,
        [sums, sums, segment, segment],
        mine,
        theirs,
        change,
        high,
        gate,
        weights,
        chip_amp,
        energies,
        message,
        neighbour_energies,
    )
    other_half = other_core(half_send)
    fields = summed(*halves)
    (other_new,) = run(
        other_last_kernel,
        [in_vmem((rows, two_cols), jnp.float32)],
        sent,
        own_far,
        *fields,
        energy,
        amp,
        other_half,
    )
    return run(
        last_kernel,
        [
            jax.ShapeDtypeStruct(tgt_amp.shape, jnp.float32),
            jax.ShapeDtypeStruct(proj_amp.shape, jnp.float32),
        ],
        mine,
        theirs,
        *swapped(fields),
        energy,
        amp,
        my_half,
        other_new,
    )


def solution(mesh):
    in_specs = (
        P(None, "tgt", "rep"),
        P(None, None, "prj", "rep"),
        P(("bpar", "rep")),
        P(("tgt", "prj", "rep")),
        P(("tgt", "rep"), "prj"),
        P("bpar", None),
        P("bpar", None),
        P(("bpar", "tgt", "prj", "rep"), None),
        P(("bpar", "tgt", "rep"), "prj", None),
    )
    out_specs = (P(("bpar", "tgt", "prj", "rep"), None), P(("bpar", "tgt", "rep"), "prj", None))

    def step(*args):
        return tuple(shards(*args))

    return jax.shard_map(step, mesh=mesh, in_specs=in_specs, out_specs=out_specs, check_vma=False)
```

```python
import functools

import jax
import jax.numpy as jnp
from jax import lax
from jax.experimental import pallas as pl
from jax.experimental.pallas import tpu as pltpu
from jax.sharding import PartitionSpec as P

time_step = 0.4
half_step = 0.5 * time_step
VMEM_LIMIT = 8 * 1024 * 1024
DEVICES = ("tgt", "prj", "rep")
HBM = pl.BlockSpec(memory_space=pl.ANY)
VMEM = pl.BlockSpec(memory_space=pltpu.VMEM)


def parity(place):
    odd = 0
    while place:
        odd, place = odd ^ (place & 1), place >> 1
    return odd


def my_kind():
    n_tgt, n_prj = lax.axis_size("tgt"), lax.axis_size("prj")
    place = lax.axis_index("tgt") * n_prj + lax.axis_index("prj")
    kind = lax.axis_index("rep")
    for bit in range((n_tgt * n_prj).bit_length() - 1):
        kind = jnp.bitwise_xor(kind, jnp.bitwise_and(lax.shift_right_logical(place, bit), 1))
    return kind


def by_core(body):
    for core in range(2):

        @pl.when(lax.axis_index("rep") == core)
        def _():
            body(core)


def ordered(core, first, second):
    return jnp.where(core == 0, first, second), jnp.where(core == 0, second, first)


def turned(block):
    half = block.shape[0] // 2
    return jnp.concatenate([block[half:], -block[:half]], axis=0)


def bf16(block):
    return block.astype(jnp.bfloat16)


def f32(block):
    return block.astype(jnp.float32)


def rows_of(basis, segment, amount):
    return [basis[part, segment * amount : (segment + 1) * amount, :] for part in range(2)]


def project(basis, amp):
    return jnp.dot(bf16(amp), basis[0], preferred_element_type=jnp.float32) + jnp.dot(
        bf16(turned(amp)), basis[1], preferred_element_type=jnp.float32
    )


def expand(basis, field):
    contract = (((1,), (1,)), ((), ()))
    return lax.dot_general(
        turned(field), basis[0], contract, preferred_element_type=jnp.float32
    ) + lax.dot_general(field, basis[1], contract, preferred_element_type=jnp.float32)


PIECES = 16


def split(row):
    index = lax.broadcasted_iota(jnp.int32, (PIECES, row.shape[1]), 0)
    block = jnp.zeros(index.shape, jnp.float32)
    for piece in range(3):
        rounded = f32(bf16(row))
        block = jnp.where(index == piece, rounded, block)
        row = row - rounded
    return bf16(block)


def joined(block):
    pieces = f32(block)
    return pieces[0:1] + pieces[1:2] + pieces[2:3]


def basis_copies(basis, sem, my, neighbours, sources):
    axis = ("prj", "tgt")[my]
    rows = sources[my].shape[2]
    place = lax.axis_index(axis)
    copies = []
    for chip, there in enumerate((place, jnp.bitwise_xor(place, neighbours[my]))):
        for core in range(2):
            segment = 2 * chip + core
            copies.append(
                pltpu.make_async_copy(
                    sources[my].at[:, 2 * there + core],
                    basis.at[:, segment * rows : (segment + 1) * rows],
                    sem.at[segment],
                )
            )
    return copies


def load_kernel(
    neighbours,
    weight_hbm,
    tgt_hbm,
    proj_hbm,
    tgt_energy_hbm,
    proj_energy_hbm,
    tgt_own_hbm,
    proj_own_hbm,
    sent,
    weight,
    energy,
    amp_ref,
    flat_weight,
    flat_energy,
    tgt_own,
    proj_own,
    sems,
):
    my = my_kind()
    sources = (tgt_hbm, proj_hbm)
    rows = energy.shape[2]

    def copies_of(kind):
        last = pltpu.make_async_copy(
            sources[kind].at[:, 2 * lax.axis_index(("prj", "tgt")[kind]) + 1 - lax.axis_index("rep")],
            sent.at[:, 4 * rows : 5 * rows],
            sems.at[4],
        )
        return basis_copies(sent, sems, 1 - kind, neighbours, sources) + [last]

    pairs = [
        (tgt_own_hbm, tgt_own),
        (proj_own_hbm, proj_own),
        (weight_hbm, flat_weight),
        (tgt_energy_hbm, flat_energy),
        (proj_energy_hbm, energy.at[1]),
    ]
    copies = [pltpu.make_async_copy(src, dst, sems.at[5 + k]) for k, (src, dst) in enumerate(pairs)]
    for copy in copies:
        copy.start()
    for kind in range(2):

        @pl.when(my == kind)
        def _():
            for copy in copies_of(kind):
                copy.start()

    for copy in copies:
        copy.wait()
    energy[0] = flat_energy[...][None, :]
    weight[0] = flat_weight[...][None, :]
    for part in range(2):
        sent[part, 5 * rows :] = split(weight[0])
    amp_ref[0] = tgt_own[...].T
    amp_ref[1] = proj_own[0].T
    for copy in copies_of(0):
        copy.wait()


def pack_kernel(
    amp_ref,
    energy,
    tgt_other,
    proj_other,
    tgt_energy_other,
    proj_energy_other,
    chip_amp,
    energies,
    message,
):
    core = lax.axis_index("rep")
    my = my_kind()
    cols = chip_amp.shape[1]
    other_amp, _ = ordered(my, tgt_other[...].T, proj_other[0].T)
    other_energy, _ = ordered(my, tgt_energy_other[...][None, :], proj_energy_other[...])
    amps = ordered(core, amp_ref[my], other_amp)
    rows = ordered(core, energy[my], other_energy)
    for segment in range(2):
        chip_amp[segment] = amps[segment]
        energies[segment] = rows[segment]
        message[segment, :cols] = bf16(amps[segment])
        message[segment, cols:] = split(rows[segment])


def side_kernel(
    gate_levels, neighbours, flags_hbm, counts_hbm, tgt_hbm, proj_hbm, chip_amp, mine, gate, flags, counts, sems
):
    my = my_kind()
    tgt_index = lax.axis_index("tgt")
    prj_index = lax.axis_index("prj")
    sources = (tgt_hbm, proj_hbm)
    pairs = [(flags_hbm, flags), (counts_hbm, counts)]
    copies = [pltpu.make_async_copy(src, dst, sems.at[4 + k]) for k, (src, dst) in enumerate(pairs)]
    for copy in copies:
        copy.start()
    for kind in range(2):

        @pl.when(my == kind)
        def _():
            for copy in basis_copies(mine, sems, kind, neighbours, sources):
                copy.start()

    for copy in copies:
        copy.wait()
    tiles = 2
    width = gate.shape[-1] // tiles
    gate_level = jnp.where(my == 0, *gate_levels)
    for half in range(2):
        for tile in range(tiles):
            live = jnp.logical_and(
                flags[prj_index, tgt_index] > 0, tiles * half + tile < counts[prj_index, tgt_index]
            )
            value = jnp.where(live, 1.0, 0.0).astype(jnp.float32)
            for level in range(gate.shape[0]):
                here = jnp.where(level == gate_level, value, jnp.float32(1.0))
                gate[level, half, :, tile * width : (tile + 1) * width] = jnp.full(
                    (1, width), here, jnp.float32
                )
    for copy in basis_copies(mine, sems, 0, neighbours, sources):
        copy.wait()


def chip_kernel(mine, theirs, chip_amp, weight, part_ref, weights):
    rows = chip_amp.shape[2]

    def body(core):
        for half, basis in enumerate((mine, theirs) if core == 0 else (theirs, mine)):
            part_ref[half] = sum(
                project(rows_of(basis, segment, rows), chip_amp[segment]) for segment in range(2)
            )
        weights[core] = weight[0]
        weights[1 - core] = joined(theirs[0, 5 * rows :, :])

    by_core(body)


def first_kernel(mine, theirs, gate, weights, part_ref, message, *outs):
    rows = message.shape[2]
    cols = part_ref.shape[1]

    def body(core):
        for half, basis in enumerate((mine, theirs) if core == 0 else (theirs, mine)):
            total = part_ref[half] + sum(
                project(rows_of(basis, 2 + segment, rows), f32(message[segment, :cols]))
                for segment in range(2)
            )
            outs[half][...] = bf16(gate[0, half] * (weights[half] * total))

    by_core(body)


def add_kernel(level, half, gate, own, other, out_ref):
    out_ref[...] = bf16(gate[level, half] * (f32(own[...]) + f32(other[...])))


def low_kernel(mine, theirs, low, change_ref):
    def body(core):
        for segment in range(4):
            basis = rows_of((mine, theirs)[core], segment, change_ref.shape[2])
            change_ref[segment] = expand(basis, low[...])

    by_core(body)


def second_kernel(
    mine,
    theirs,
    change_ref,
    high,
    gate,
    weights,
    chip_amp,
    energies,
    message,
    low_ref,
    high_ref,
    half_ref,
    send_ref,
):
    _, cols, rows = chip_amp.shape

    def body(core):
        bases = (mine, theirs) if core == 0 else (theirs, mine)
        halves = []
        for segment in range(4):
            if segment < 2:
                amp, energy = chip_amp[segment], energies[segment]
            else:
                amp, energy = f32(message[segment - 2, :cols]), joined(message[segment - 2, cols:])
            change = change_ref[segment] + expand(rows_of(bases[1], segment, rows), high[...])
            halves.append(amp + half_step * (energy * turned(amp) + change))
        half_ref[...] = halves[core]
        send_ref[...] = halves[1 - core]
        for half, out_ref in enumerate((low_ref, high_ref)):
            total = sum(
                project(rows_of(bases[half], segment, rows), halves[segment]) for segment in range(4)
            )
            out_ref[...] = bf16(gate[0, half] * (weights[half] * total))

    by_core(body)


def other_last_kernel(sent, theirs, low, high, energy, amp_ref, half_ref, new_ref):
    rows = amp_ref.shape[2]

    def body(core):
        near, far = (low, high) if core == 0 else (high, low)
        kind = 1 - my_kind()
        change = expand(rows_of(sent, core, rows), near[...]) + expand(rows_of(theirs, 4, rows), far[...])
        rate = energy[kind] * turned(half_ref[...]) + change
        new_ref[...] = (amp_ref[kind] + time_step * rate).T

    by_core(body)


def last_kernel(mine, theirs, low, high, energy, amp_ref, half_ref, other_new, new_tgt, new_proj):
    rows = amp_ref.shape[2]

    def body(core):
        near, far = (low, high) if core == 0 else (high, low)
        my = my_kind()
        change = expand(rows_of(mine, core, rows), near[...]) + expand(
            rows_of(theirs, core, rows), far[...]
        )
        rate = energy[my] * turned(half_ref[...]) + change
        my_new = (amp_ref[my] + time_step * rate).T
        new_tgt[...], new_proj[0] = ordered(my, my_new, other_new[...])

    by_core(body)


def shards(
    tgt_basis,
    proj_basis,
    quad_weight,
    tgt_energy,
    proj_energy,
    pair_flags,
    tile_counts,
    tgt_amp,
    proj_amp,
):
    points = quad_weight.shape[0]
    rows, two_cols = tgt_amp.shape
    sizes = [lax.axis_size(axis) for axis in DEVICES]

    def call(kernel, out_shape, in_specs, scratch_shapes=(), cost=None):
        return pl.pallas_call(
            kernel,
            out_shape=out_shape,
            in_specs=in_specs,
            out_specs=[VMEM] * len(out_shape),
            scratch_shapes=scratch_shapes,
            cost_estimate=cost,
            compiler_params=pltpu.CompilerParams(vmem_limit_bytes=VMEM_LIMIT),
        )

    def run(kernel, out_shape, *blocks):
        return call(kernel, out_shape, [VMEM] * len(blocks))(*blocks)

    def other_core(block):
        return lax.ppermute(block, "rep", [(0, 1), (1, 0)])

    n_tgt, n_prj, n_core = sizes
    tgt_flips = [n_prj << bit for bit in range(n_tgt.bit_length() - 1)]
    prj_flips = [1 << bit for bit in range(n_prj.bit_length() - 1)]
    flips = (prj_flips + tgt_flips[::-1], tgt_flips[::-1] + prj_flips)
    neighbours = (flips[0][0], flips[1][0] // n_prj)
    gate_levels = (len(prj_flips) - 1, len(tgt_flips) - 1)
    n_steps = len(tgt_flips) + len(prj_flips)

    def exchanged(step, block):
        pairs = []
        for place in range(n_tgt * n_prj):
            for kind in range(2):
                there = place ^ flips[kind][step]
                pairs.append((place * n_core + (kind ^ parity(place)), there * n_core + (kind ^ parity(there))))
        return lax.ppermute(block, DEVICES, pairs)

    in_vmem = pltpu.VMEM
    sums = in_vmem((two_cols, points), jnp.bfloat16)
    segment = in_vmem((two_cols, rows), jnp.float32)

    def summed(*halves):
        totals = []
        for half, block in enumerate(halves):
            for step in range(1, n_steps):
                other = exchanged(step, block)
                (block,) = run(functools.partial(add_kernel, step, half), [sums], gate, block, other)
            totals.append(block)
        return totals

    def swapped(fields):
        return [other_core(block) for block in fields]

    def in_hbm(*blocks):
        return [pltpu.with_memory_space_constraint(block, pltpu.HBM) for block in blocks]

    others = swapped([tgt_amp, proj_amp, tgt_energy, proj_energy])
    bases = in_hbm(tgt_basis.reshape(2, -1, rows, points), proj_basis)
    sent, weight, energy, amp = call(
        functools.partial(load_kernel, neighbours),
        [
            in_vmem((2, 5 * rows + PIECES, points), jnp.bfloat16),
            in_vmem((1, 1, points), jnp.float32),
            in_vmem((2, 1, rows), jnp.float32),
            in_vmem((2, two_cols, rows), jnp.float32),
        ],
        [HBM] * 7,
        [
            pltpu.VMEM((points,), jnp.float32),
            pltpu.VMEM((rows,), jnp.float32),
            pltpu.VMEM(tgt_amp.shape, jnp.float32),
            pltpu.VMEM(proj_amp.shape, jnp.float32),
            pltpu.SemaphoreType.DMA((10,)),
        ],
        pl.CostEstimate(
            flops=2 * 4 * rows * two_cols * points, bytes_accessed=4 * 1024 * 1024, transcendentals=0
        ),
    )(*in_hbm(quad_weight), *bases, *in_hbm(tgt_energy, proj_energy, tgt_amp, proj_amp))
    chip_amp, energies, message = run(
        pack_kernel,
        [
            in_vmem((2, two_cols, rows), jnp.float32),
            in_vmem((2, 1, rows), jnp.float32),
            in_vmem((2, two_cols + PIECES, rows), jnp.bfloat16),
        ],
        amp,
        energy,
        *others,
    )
    sent, message = lax.optimization_barrier((sent, message))
    theirs = other_core(sent)
    message = exchanged(0, message)
    flags, counts = pair_flags.T, tile_counts.T
    mine, gate = call(
        functools.partial(side_kernel, gate_levels, neighbours),
        [
            in_vmem((2, 4 * rows, points), jnp.bfloat16),
            in_vmem((n_steps, 2, 1, points), jnp.float32),
        ],
        [HBM] * 4 + [VMEM],
        [
            pltpu.SMEM(flags.shape, jnp.int32),
            pltpu.SMEM(counts.shape, jnp.int32),
            pltpu.SemaphoreType.DMA((6,)),
        ],
    )(*in_hbm(flags, counts), *bases, chip_amp)
    part, weights = run(
        chip_kernel,
        [in_vmem((2, two_cols, points), jnp.float32), in_vmem((2, 1, points), jnp.float32)],
        mine,
        theirs,
        chip_amp,
        weight,
    )
    halves = run(first_kernel, [sums] * 2, mine, theirs, gate, weights, part, message)
    fields = summed(*halves)
    low, high = swapped(fields)
    (change,) = run(low_kernel, [in_vmem((4, two_cols, rows), jnp.float32)], mine, theirs, low)
    *halves, my_half, half_send = run(
        second_kernel,
        [sums, sums, segment, segment],
        mine,
        theirs,
        change,
        high,
        gate,
        weights,
        chip_amp,
        energies,
        message,
    )
    other_half = other_core(half_send)
    fields = summed(*halves)
    (other_new,) = run(
        other_last_kernel,
        [in_vmem((rows, two_cols), jnp.float32)],
        sent,
        theirs,
        *fields,
        energy,
        amp,
        other_half,
    )
    return run(
        last_kernel,
        [
            jax.ShapeDtypeStruct(tgt_amp.shape, jnp.float32),
            jax.ShapeDtypeStruct(proj_amp.shape, jnp.float32),
        ],
        mine,
        theirs,
        *swapped(fields),
        energy,
        amp,
        my_half,
        other_new,
    )


def solution(mesh):
    in_specs = (
        P(None, "tgt", "rep"),
        P(None, None, "prj", "rep"),
        P(("bpar", "rep")),
        P(("tgt", "prj", "rep")),
        P(("tgt", "rep"), "prj"),
        P("bpar", None),
        P("bpar", None),
        P(("bpar", "tgt", "prj", "rep"), None),
        P(("bpar", "tgt", "rep"), "prj", None),
    )
    out_specs = (P(("bpar", "tgt", "prj", "rep"), None), P(("bpar", "tgt", "rep"), "prj", None))

    def step(*args):
        return tuple(shards(*args))

    return jax.shard_map(step, mesh=mesh, in_specs=in_specs, out_specs=out_specs, check_vma=False)
```

```python
import functools

import jax
import jax.numpy as jnp
from jax import lax
from jax.experimental import pallas as pl
from jax.experimental.pallas import tpu as pltpu
from jax.sharding import PartitionSpec as P

time_step = 0.4
half_step = 0.5 * time_step
VMEM_LIMIT = 8 * 1024 * 1024
DEVICES = ("tgt", "prj", "rep")
HBM = pl.BlockSpec(memory_space=pl.ANY)
VMEM = pl.BlockSpec(memory_space=pltpu.VMEM)


def parity(place):
    odd = 0
    while place:
        odd, place = odd ^ (place & 1), place >> 1
    return odd


def my_kind():
    n_tgt, n_prj = lax.axis_size("tgt"), lax.axis_size("prj")
    place = lax.axis_index("tgt") * n_prj + lax.axis_index("prj")
    kind = lax.axis_index("rep")
    for bit in range((n_tgt * n_prj).bit_length() - 1):
        kind = jnp.bitwise_xor(kind, jnp.bitwise_and(lax.shift_right_logical(place, bit), 1))
    return kind


def by_core(body):
    for core in range(2):

        @pl.when(lax.axis_index("rep") == core)
        def _():
            body(core)


def ordered(core, first, second):
    return jnp.where(core == 0, first, second), jnp.where(core == 0, second, first)


def turned(block):
    half = block.shape[0] // 2
    return jnp.concatenate([block[half:], -block[:half]], axis=0)


def bf16(block):
    return block.astype(jnp.bfloat16)


def f32(block):
    return block.astype(jnp.float32)


def rows_of(basis, segment, amount):
    return [basis[part, segment * amount : (segment + 1) * amount, :] for part in range(2)]


def project(basis, amp):
    return jnp.dot(bf16(amp), basis[0], preferred_element_type=jnp.float32) + jnp.dot(
        bf16(turned(amp)), basis[1], preferred_element_type=jnp.float32
    )


def expand(basis, field):
    contract = (((1,), (1,)), ((), ()))
    return lax.dot_general(
        turned(field), basis[0], contract, preferred_element_type=jnp.float32
    ) + lax.dot_general(field, basis[1], contract, preferred_element_type=jnp.float32)


PIECES = 16


def split(row):
    index = lax.broadcasted_iota(jnp.int32, (PIECES, row.shape[1]), 0)
    block = jnp.zeros(index.shape, jnp.float32)
    for piece in range(3):
        rounded = f32(bf16(row))
        block = jnp.where(index == piece, rounded, block)
        row = row - rounded
    return bf16(block)


def joined(block):
    pieces = f32(block)
    return pieces[0:1] + pieces[1:2] + pieces[2:3]


def basis_copies(basis, sem, my, neighbours, sources):
    axis = ("prj", "tgt")[my]
    rows = sources[my].shape[2]
    place = lax.axis_index(axis)
    copies = []
    for chip, there in enumerate((place, jnp.bitwise_xor(place, neighbours[my]))):
        for core in range(2):
            segment = 2 * chip + core
            copies.append(
                pltpu.make_async_copy(
                    sources[my].at[:, 2 * there + core],
                    basis.at[:, segment * rows : (segment + 1) * rows],
                    sem.at[segment],
                )
            )
    return copies


def load_kernel(
    neighbours,
    weight_hbm,
    tgt_hbm,
    proj_hbm,
    tgt_energy_hbm,
    proj_energy_hbm,
    tgt_own_hbm,
    proj_own_hbm,
    sent,
    weight,
    energy,
    amp_ref,
    flat_weight,
    flat_energy,
    tgt_own,
    proj_own,
    sems,
):
    my = my_kind()
    sources = (tgt_hbm, proj_hbm)
    rows = energy.shape[2]

    def copies_of(kind):
        last = pltpu.make_async_copy(
            sources[kind].at[:, 2 * lax.axis_index(("prj", "tgt")[kind]) + 1 - lax.axis_index("rep")],
            sent.at[:, 4 * rows : 5 * rows],
            sems.at[4],
        )
        return basis_copies(sent, sems, 1 - kind, neighbours, sources) + [last]

    pairs = [
        (tgt_own_hbm, tgt_own),
        (proj_own_hbm, proj_own),
        (weight_hbm, flat_weight),
        (tgt_energy_hbm, flat_energy),
        (proj_energy_hbm, energy.at[1]),
    ]
    copies = [pltpu.make_async_copy(src, dst, sems.at[5 + k]) for k, (src, dst) in enumerate(pairs)]
    for copy in copies:
        copy.start()
    for kind in range(2):

        @pl.when(my == kind)
        def _():
            for copy in copies_of(kind):
                copy.start()

    for copy in copies:
        copy.wait()
    energy[0] = flat_energy[...][None, :]
    weight[0] = flat_weight[...][None, :]
    for part in range(2):
        sent[part, 5 * rows :] = split(weight[0])
    amp_ref[0] = tgt_own[...].T
    amp_ref[1] = proj_own[0].T
    for copy in copies_of(0):
        copy.wait()


def pack_kernel(
    amp_ref,
    energy,
    tgt_other,
    proj_other,
    tgt_energy_other,
    proj_energy_other,
    chip_amp,
    energies,
    message,
):
    core = lax.axis_index("rep")
    my = my_kind()
    cols = chip_amp.shape[1]
    other_amp, _ = ordered(my, tgt_other[...].T, proj_other[0].T)
    other_energy, _ = ordered(my, tgt_energy_other[...][None, :], proj_energy_other[...])
    amps = ordered(core, amp_ref[my], other_amp)
    rows = ordered(core, energy[my], other_energy)
    for segment in range(2):
        chip_amp[segment] = amps[segment]
        energies[segment] = rows[segment]
        message[segment, :cols] = bf16(amps[segment])
        message[segment, cols:] = split(rows[segment])


def side_kernel(
    gate_levels, neighbours, flags_hbm, counts_hbm, tgt_hbm, proj_hbm, chip_amp, mine, gate, flags, counts, sems
):
    my = my_kind()
    tgt_index = lax.axis_index("tgt")
    prj_index = lax.axis_index("prj")
    sources = (tgt_hbm, proj_hbm)
    pairs = [(flags_hbm, flags), (counts_hbm, counts)]
    copies = [pltpu.make_async_copy(src, dst, sems.at[4 + k]) for k, (src, dst) in enumerate(pairs)]
    for copy in copies:
        copy.start()
    for kind in range(2):

        @pl.when(my == kind)
        def _():
            for copy in basis_copies(mine, sems, kind, neighbours, sources):
                copy.start()

    for copy in copies:
        copy.wait()
    tiles = 2
    width = gate.shape[-1] // tiles
    gate_level = jnp.where(my == 0, *gate_levels)
    for half in range(2):
        for tile in range(tiles):
            live = jnp.logical_and(
                flags[prj_index, tgt_index] > 0, tiles * half + tile < counts[prj_index, tgt_index]
            )
            value = jnp.where(live, 1.0, 0.0).astype(jnp.float32)
            for level in range(gate.shape[0]):
                here = jnp.where(level == gate_level, value, jnp.float32(1.0))
                gate[level, half, :, tile * width : (tile + 1) * width] = jnp.full(
                    (1, width), here, jnp.float32
                )
    for copy in basis_copies(mine, sems, 0, neighbours, sources):
        copy.wait()


def chip_kernel(mine, theirs, chip_amp, weight, part_ref, weights):
    rows = chip_amp.shape[2]

    def body(core):
        for half, basis in enumerate((mine, theirs) if core == 0 else (theirs, mine)):
            part_ref[half] = sum(
                project(rows_of(basis, segment, rows), chip_amp[segment]) for segment in range(2)
            )
        weights[core] = weight[0]
        weights[1 - core] = joined(theirs[0, 5 * rows :, :])

    by_core(body)


def first_kernel(mine, theirs, gate, weights, part_ref, message, out_ref):
    rows = message.shape[2]
    cols = part_ref.shape[1]

    def body(core):
        for half, basis in enumerate((mine, theirs) if core == 0 else (theirs, mine)):
            total = part_ref[half] + sum(
                project(rows_of(basis, 2 + segment, rows), f32(message[segment, :cols]))
                for segment in range(2)
            )
            out_ref[half] = bf16(gate[0, half] * (weights[half] * total))

    by_core(body)


def add_kernel(level, gate, own, other, out_ref):
    for half in range(2):
        out_ref[half] = bf16(gate[level, half] * (f32(own[half]) + f32(other[half])))


def second_kernel(
    mine, theirs, field, gate, weights, chip_amp, energies, message, z_ref, half_ref, send_ref
):
    _, cols, rows = chip_amp.shape

    def body(core):
        bases = (mine, theirs) if core == 0 else (theirs, mine)
        halves = []
        for segment in range(4):
            if segment < 2:
                amp, energy = chip_amp[segment], energies[segment]
            else:
                amp, energy = f32(message[segment - 2, :cols]), joined(message[segment - 2, cols:])
            change = sum(
                expand(rows_of(bases[half], segment, rows), field[half]) for half in range(2)
            )
            halves.append(amp + half_step * (energy * turned(amp) + change))
        half_ref[...] = halves[core]
        send_ref[...] = halves[1 - core]
        for half in range(2):
            total = sum(
                project(rows_of(bases[half], segment, rows), halves[segment]) for segment in range(4)
            )
            z_ref[half] = bf16(gate[0, half] * (weights[half] * total))

    by_core(body)


def late_kernel(theirs, sent, field, energy, amp_ref, my_half, other_half, my_part, other_new):
    rows = amp_ref.shape[2]

    def body(core):
        my = my_kind()
        change = expand(rows_of(sent, core, rows), field[core]) + expand(
            rows_of(theirs, 4, rows), field[1 - core]
        )
        rate = energy[1 - my] * turned(other_half[...]) + change
        other_new[...] = (amp_ref[1 - my] + time_step * rate).T
        my_part[...] = amp_ref[my] + time_step * (energy[my] * turned(my_half[...]))

    by_core(body)


def last_kernel(mine, theirs, field, my_part, other_new, new_tgt, new_proj):
    rows = my_part.shape[1]

    def body(core):
        change = expand(rows_of(mine, core, rows), field[core]) + expand(
            rows_of(theirs, core, rows), field[1 - core]
        )
        my_new = (my_part[...] + time_step * change).T
        new_tgt[...], new_proj[0] = ordered(my_kind(), my_new, other_new[...])

    by_core(body)


def shards(
    tgt_basis,
    proj_basis,
    quad_weight,
    tgt_energy,
    proj_energy,
    pair_flags,
    tile_counts,
    tgt_amp,
    proj_amp,
):
    points = quad_weight.shape[0]
    rows, two_cols = tgt_amp.shape
    sizes = [lax.axis_size(axis) for axis in DEVICES]

    def call(kernel, out_shape, in_specs, scratch_shapes=(), cost=None):
        return pl.pallas_call(
            kernel,
            out_shape=out_shape,
            in_specs=in_specs,
            out_specs=[VMEM] * len(out_shape),
            scratch_shapes=scratch_shapes,
            cost_estimate=cost,
            compiler_params=pltpu.CompilerParams(vmem_limit_bytes=VMEM_LIMIT),
        )

    def run(kernel, out_shape, *blocks):
        return call(kernel, out_shape, [VMEM] * len(blocks))(*blocks)

    def other_core(block):
        return lax.ppermute(block, "rep", [(0, 1), (1, 0)])

    n_tgt, n_prj, n_core = sizes
    tgt_flips = [n_prj << bit for bit in range(n_tgt.bit_length() - 1)]
    prj_flips = [1 << bit for bit in range(n_prj.bit_length() - 1)]
    flips = (prj_flips + tgt_flips[::-1], tgt_flips[::-1] + prj_flips)
    neighbours = (flips[0][0], flips[1][0] // n_prj)
    gate_levels = (len(prj_flips) - 1, len(tgt_flips) - 1)
    n_steps = len(tgt_flips) + len(prj_flips)

    def exchanged(step, block):
        pairs = []
        for place in range(n_tgt * n_prj):
            for kind in range(2):
                there = place ^ flips[kind][step]
                pairs.append((place * n_core + (kind ^ parity(place)), there * n_core + (kind ^ parity(there))))
        return lax.ppermute(block, DEVICES, pairs)

    in_vmem = pltpu.VMEM
    sums = in_vmem((2, two_cols, points), jnp.bfloat16)
    segment = in_vmem((two_cols, rows), jnp.float32)

    def summed(block):
        for step in range(1, n_steps):
            other = exchanged(step, block)
            (block,) = run(functools.partial(add_kernel, step), [sums], gate, block, other)
        return block

    def swapped(fields):
        return [other_core(block) for block in fields]

    def in_hbm(*blocks):
        return [pltpu.with_memory_space_constraint(block, pltpu.HBM) for block in blocks]

    others = swapped([tgt_amp, proj_amp, tgt_energy, proj_energy])
    bases = in_hbm(tgt_basis.reshape(2, -1, rows, points), proj_basis)
    sent, weight, energy, amp = call(
        functools.partial(load_kernel, neighbours),
        [
            in_vmem((2, 5 * rows + PIECES, points), jnp.bfloat16),
            in_vmem((1, 1, points), jnp.float32),
            in_vmem((2, 1, rows), jnp.float32),
            in_vmem((2, two_cols, rows), jnp.float32),
        ],
        [HBM] * 7,
        [
            pltpu.VMEM((points,), jnp.float32),
            pltpu.VMEM((rows,), jnp.float32),
            pltpu.VMEM(tgt_amp.shape, jnp.float32),
            pltpu.VMEM(proj_amp.shape, jnp.float32),
            pltpu.SemaphoreType.DMA((10,)),
        ],
        pl.CostEstimate(
            flops=2 * 4 * rows * two_cols * points, bytes_accessed=4 * 1024 * 1024, transcendentals=0
        ),
    )(*in_hbm(quad_weight), *bases, *in_hbm(tgt_energy, proj_energy, tgt_amp, proj_amp))
    chip_amp, energies, message = run(
        pack_kernel,
        [
            in_vmem((2, two_cols, rows), jnp.float32),
            in_vmem((2, 1, rows), jnp.float32),
            in_vmem((2, two_cols + PIECES, rows), jnp.bfloat16),
        ],
        amp,
        energy,
        *others,
    )
    sent, message = lax.optimization_barrier((sent, message))
    theirs = other_core(sent)
    message = exchanged(0, message)
    flags, counts = pair_flags.T, tile_counts.T
    mine, gate = call(
        functools.partial(side_kernel, gate_levels, neighbours),
        [
            in_vmem((2, 4 * rows, points), jnp.bfloat16),
            in_vmem((n_steps, 2, 1, points), jnp.float32),
        ],
        [HBM] * 4 + [VMEM],
        [
            pltpu.SMEM(flags.shape, jnp.int32),
            pltpu.SMEM(counts.shape, jnp.int32),
            pltpu.SemaphoreType.DMA((6,)),
        ],
    )(*in_hbm(flags, counts), *bases, chip_amp)
    part, weights = run(
        chip_kernel,
        [in_vmem((2, two_cols, points), jnp.float32), in_vmem((2, 1, points), jnp.float32)],
        mine,
        theirs,
        chip_amp,
        weight,
    )
    (z,) = run(first_kernel, [sums], mine, theirs, gate, weights, part, message)
    field = summed(z)
    z, my_half, half_send = run(
        second_kernel,
        [sums, segment, segment],
        mine,
        theirs,
        other_core(field),
        gate,
        weights,
        chip_amp,
        energies,
        message,
    )
    other_half = other_core(half_send)
    field = summed(z)
    my_part, other_new = run(
        late_kernel,
        [segment, in_vmem((rows, two_cols), jnp.float32)],
        theirs,
        sent,
        field,
        energy,
        amp,
        my_half,
        other_half,
    )
    return run(
        last_kernel,
        [
            jax.ShapeDtypeStruct(tgt_amp.shape, jnp.float32),
            jax.ShapeDtypeStruct(proj_amp.shape, jnp.float32),
        ],
        mine,
        theirs,
        other_core(field),
        my_part,
        other_new,
    )


def solution(mesh):
    in_specs = (
        P(None, "tgt", "rep"),
        P(None, None, "prj", "rep"),
        P(("bpar", "rep")),
        P(("tgt", "prj", "rep")),
        P(("tgt", "rep"), "prj"),
        P("bpar", None),
        P("bpar", None),
        P(("bpar", "tgt", "prj", "rep"), None),
        P(("bpar", "tgt", "rep"), "prj", None),
    )
    out_specs = (P(("bpar", "tgt", "prj", "rep"), None), P(("bpar", "tgt", "rep"), "prj", None))

    def step(*args):
        return tuple(shards(*args))

    return jax.shard_map(step, mesh=mesh, in_specs=in_specs, out_specs=out_specs, check_vma=False)
```

```python
import functools

import jax
import jax.numpy as jnp
from jax import lax
from jax.experimental import pallas as pl
from jax.experimental.pallas import tpu as pltpu
from jax.sharding import PartitionSpec as P

time_step = 0.4
half_step = 0.5 * time_step
VMEM_LIMIT = 8 * 1024 * 1024
DEVICES = ("tgt", "prj", "rep")
HBM = pl.BlockSpec(memory_space=pl.ANY)
VMEM = pl.BlockSpec(memory_space=pltpu.VMEM)


def parity(place):
    odd = 0
    while place:
        odd, place = odd ^ (place & 1), place >> 1
    return odd


def my_kind():
    n_tgt, n_prj = lax.axis_size("tgt"), lax.axis_size("prj")
    place = lax.axis_index("tgt") * n_prj + lax.axis_index("prj")
    kind = lax.axis_index("rep")
    for bit in range((n_tgt * n_prj).bit_length() - 1):
        kind = jnp.bitwise_xor(kind, jnp.bitwise_and(lax.shift_right_logical(place, bit), 1))
    return kind


def by_core(body):
    for core in range(2):

        @pl.when(lax.axis_index("rep") == core)
        def _():
            body(core)


def ordered(core, first, second):
    return jnp.where(core == 0, first, second), jnp.where(core == 0, second, first)


def turned(block):
    half = block.shape[0] // 2
    return jnp.concatenate([block[half:], -block[:half]], axis=0)


def bf16(block):
    return block.astype(jnp.bfloat16)


def f32(block):
    return block.astype(jnp.float32)


def rows_of(basis, segment, amount):
    return [basis[part, segment * amount : (segment + 1) * amount, :] for part in range(2)]


def project(basis, amp):
    return jnp.dot(bf16(amp), basis[0], preferred_element_type=jnp.float32) + jnp.dot(
        bf16(turned(amp)), basis[1], preferred_element_type=jnp.float32
    )


def expand(basis, field):
    contract = (((1,), (1,)), ((), ()))
    return lax.dot_general(
        turned(field), basis[0], contract, preferred_element_type=jnp.float32
    ) + lax.dot_general(field, basis[1], contract, preferred_element_type=jnp.float32)


PIECES = 16

BEHIND = pl.CostEstimate(flops=1 << 35, bytes_accessed=1 << 16, transcendentals=0)


def split(row):
    index = lax.broadcasted_iota(jnp.int32, (PIECES, row.shape[1]), 0)
    block = jnp.zeros(index.shape, jnp.float32)
    for piece in range(3):
        rounded = f32(bf16(row))
        block = jnp.where(index == piece, rounded, block)
        row = row - rounded
    return bf16(block)


def joined(block):
    pieces = f32(block)
    return pieces[0:1] + pieces[1:2] + pieces[2:3]


def basis_copies(basis, sem, my, neighbours, sources):
    axis = ("prj", "tgt")[my]
    rows = sources[my].shape[2]
    place = lax.axis_index(axis)
    copies = []
    for chip, there in enumerate((place, jnp.bitwise_xor(place, neighbours[my]))):
        for core in range(2):
            segment = 2 * chip + core
            copies.append(
                pltpu.make_async_copy(
                    sources[my].at[:, 2 * there + core],
                    basis.at[:, segment * rows : (segment + 1) * rows],
                    sem.at[segment],
                )
            )
    return copies


def load_kernel(
    tgt_energy_hbm,
    proj_energy_hbm,
    tgt_own_hbm,
    proj_own_hbm,
    energy,
    amp_ref,
    flat_energy,
    tgt_own,
    proj_own,
    sems,
):
    pairs = [
        (tgt_own_hbm, tgt_own),
        (proj_own_hbm, proj_own),
        (tgt_energy_hbm, flat_energy),
        (proj_energy_hbm, energy.at[1]),
    ]
    copies = [pltpu.make_async_copy(src, dst, sems.at[k]) for k, (src, dst) in enumerate(pairs)]
    for copy in copies:
        copy.start()
    for copy in copies:
        copy.wait()
    energy[0] = flat_energy[...][None, :]
    amp_ref[0] = tgt_own[...].T
    amp_ref[1] = proj_own[0].T


def pack_kernel(
    amp_ref,
    energy,
    tgt_other,
    proj_other,
    tgt_energy_other,
    proj_energy_other,
    chip_amp,
    energies,
    message,
):
    core = lax.axis_index("rep")
    my = my_kind()
    cols = chip_amp.shape[1]
    other_amp, _ = ordered(my, tgt_other[...].T, proj_other[0].T)
    other_energy, _ = ordered(my, tgt_energy_other[...][None, :], proj_energy_other[...])
    amps = ordered(core, amp_ref[my], other_amp)
    rows = ordered(core, energy[my], other_energy)
    for segment in range(2):
        chip_amp[segment] = amps[segment]
        energies[segment] = rows[segment]
        message[segment, :cols] = bf16(amps[segment])
        message[segment, cols:] = split(rows[segment])


def gate_kernel(gate_levels, flags_hbm, counts_hbm, chip_amp, gate, flags, counts, sems):
    my = my_kind()
    tgt_index = lax.axis_index("tgt")
    prj_index = lax.axis_index("prj")
    pairs = [(flags_hbm, flags), (counts_hbm, counts)]
    copies = [pltpu.make_async_copy(src, dst, sems.at[k]) for k, (src, dst) in enumerate(pairs)]
    for copy in copies:
        copy.start()
    for copy in copies:
        copy.wait()
    tiles = 2
    width = gate.shape[-1] // tiles
    gate_level = jnp.where(my == 0, *gate_levels)
    for half in range(2):
        for tile in range(tiles):
            live = jnp.logical_and(
                flags[prj_index, tgt_index] > 0, tiles * half + tile < counts[prj_index, tgt_index]
            )
            value = jnp.where(live, 1.0, 0.0).astype(jnp.float32)
            for level in range(gate.shape[0]):
                here = jnp.where(level == gate_level, value, jnp.float32(1.0))
                gate[level, half, :, tile * width : (tile + 1) * width] = jnp.full(
                    (1, width), here, jnp.float32
                )


def basis_kernel(
    neighbours,
    weight_hbm,
    tgt_hbm,
    proj_hbm,
    chip_amp,
    sent,
    mine,
    weight,
    flat_weight,
    sems,
):
    my = my_kind()
    sources = (tgt_hbm, proj_hbm)
    rows = chip_amp.shape[2]

    def copies_of(kind):
        last = pltpu.make_async_copy(
            sources[kind].at[:, 2 * lax.axis_index(("prj", "tgt")[kind]) + 1 - lax.axis_index("rep")],
            sent.at[:, 4 * rows : 5 * rows],
            sems.at[8],
        )
        return (
            basis_copies(sent, sems.at[0:4], 1 - kind, neighbours, sources)
            + [last]
            + basis_copies(mine, sems.at[4:8], kind, neighbours, sources)
        )

    weight_copy = pltpu.make_async_copy(weight_hbm, flat_weight, sems.at[9])
    weight_copy.start()
    for kind in range(2):

        @pl.when(my == kind)
        def _():
            for copy in copies_of(kind):
                copy.start()

    weight_copy.wait()
    weight[0] = flat_weight[...][None, :]
    for part in range(2):
        sent[part, 5 * rows :] = split(weight[0])
    for copy in copies_of(0):
        copy.wait()


def chip_kernel(mine, theirs, chip_amp, weight, part_ref, weights):
    rows = chip_amp.shape[2]

    def body(core):
        for half, basis in enumerate((mine, theirs) if core == 0 else (theirs, mine)):
            part_ref[half] = sum(
                project(rows_of(basis, segment, rows), chip_amp[segment]) for segment in range(2)
            )
        weights[core] = weight[0]
        weights[1 - core] = joined(theirs[0, 5 * rows :, :])

    by_core(body)


def first_kernel(mine, theirs, gate, weights, part_ref, message, *outs):
    rows = message.shape[2]
    cols = part_ref.shape[1]

    def body(core):
        for half, basis in enumerate((mine, theirs) if core == 0 else (theirs, mine)):
            total = part_ref[half] + sum(
                project(rows_of(basis, 2 + segment, rows), f32(message[segment, :cols]))
                for segment in range(2)
            )
            outs[half][...] = bf16(gate[0, half] * (weights[half] * total))

    by_core(body)


def add_kernel(level, half, gate, own, other, out_ref):
    out_ref[...] = bf16(gate[level, half] * (f32(own[...]) + f32(other[...])))


def low_kernel(mine, theirs, low, chip_amp, energies, message, states_ref):
    _, cols, rows = chip_amp.shape

    def body(core):
        for segment in range(4):
            if segment < 2:
                amp, energy = chip_amp[segment], energies[segment]
            else:
                amp, energy = f32(message[segment - 2, :cols]), joined(message[segment - 2, cols:])
            change = expand(rows_of((mine, theirs)[core], segment, rows), low[...])
            states_ref[segment] = amp + half_step * (energy * turned(amp) + change)

    by_core(body)


def second_kernel(mine, theirs, states_ref, high, gate, weights, low_ref, high_ref, half_ref, send_ref):
    rows = states_ref.shape[2]

    def body(core):
        bases = (mine, theirs) if core == 0 else (theirs, mine)
        halves = [
            states_ref[segment] + half_step * expand(rows_of(bases[1], segment, rows), high[...])
            for segment in range(4)
        ]
        half_ref[...] = halves[core]
        send_ref[...] = halves[1 - core]
        for half, out_ref in enumerate((low_ref, high_ref)):
            total = sum(
                project(rows_of(bases[half], segment, rows), halves[segment]) for segment in range(4)
            )
            out_ref[...] = bf16(gate[0, half] * (weights[half] * total))

    by_core(body)


def late_kernel(theirs, sent, low, high, energy, amp_ref, my_half, other_half, my_part, other_new):
    rows = amp_ref.shape[2]

    def body(core):
        my = my_kind()
        near, far = (low, high) if core == 0 else (high, low)
        change = expand(rows_of(sent, core, rows), near[...]) + expand(rows_of(theirs, 4, rows), far[...])
        rate = energy[1 - my] * turned(other_half[...]) + change
        other_new[...] = (amp_ref[1 - my] + time_step * rate).T
        my_part[...] = amp_ref[my] + time_step * (energy[my] * turned(my_half[...]))

    by_core(body)


def last_kernel(mine, theirs, low, high, my_part, other_new, new_tgt, new_proj):
    rows = my_part.shape[1]

    def body(core):
        near, far = (low, high) if core == 0 else (high, low)
        change = expand(rows_of(mine, core, rows), near[...]) + expand(
            rows_of(theirs, core, rows), far[...]
        )
        my_new = (my_part[...] + time_step * change).T
        new_tgt[...], new_proj[0] = ordered(my_kind(), my_new, other_new[...])

    by_core(body)


def shards(
    tgt_basis,
    proj_basis,
    quad_weight,
    tgt_energy,
    proj_energy,
    pair_flags,
    tile_counts,
    tgt_amp,
    proj_amp,
):
    points = quad_weight.shape[0]
    rows, two_cols = tgt_amp.shape
    sizes = [lax.axis_size(axis) for axis in DEVICES]

    def call(kernel, out_shape, in_specs, scratch_shapes=(), cost=None):
        return pl.pallas_call(
            kernel,
            out_shape=out_shape,
            in_specs=in_specs,
            out_specs=[VMEM] * len(out_shape),
            scratch_shapes=scratch_shapes,
            cost_estimate=cost,
            compiler_params=pltpu.CompilerParams(vmem_limit_bytes=VMEM_LIMIT),
        )

    def run(kernel, out_shape, *blocks):
        return call(kernel, out_shape, [VMEM] * len(blocks))(*blocks)

    def other_core(block):
        return lax.ppermute(block, "rep", [(0, 1), (1, 0)])

    n_tgt, n_prj, n_core = sizes
    tgt_flips = [n_prj << bit for bit in range(n_tgt.bit_length() - 1)]
    prj_flips = [1 << bit for bit in range(n_prj.bit_length() - 1)]
    flips = (prj_flips + tgt_flips[::-1], tgt_flips[::-1] + prj_flips)
    neighbours = (flips[0][0], flips[1][0] // n_prj)
    gate_levels = (len(prj_flips) - 1, len(tgt_flips) - 1)
    n_steps = len(tgt_flips) + len(prj_flips)

    def exchanged(step, block):
        pairs = []
        for place in range(n_tgt * n_prj):
            for kind in range(2):
                there = place ^ flips[kind][step]
                pairs.append((place * n_core + (kind ^ parity(place)), there * n_core + (kind ^ parity(there))))
        return lax.ppermute(block, DEVICES, pairs)

    in_vmem = pltpu.VMEM
    sums = in_vmem((two_cols, points), jnp.bfloat16)
    segment = in_vmem((two_cols, rows), jnp.float32)

    def summed(*halves):
        totals = []
        for half, block in enumerate(halves):
            for step in range(1, n_steps):
                other = exchanged(step, block)
                (block,) = run(functools.partial(add_kernel, step, half), [sums], gate, block, other)
            totals.append(block)
        return totals

    def swapped(fields):
        return [other_core(block) for block in fields]

    def in_hbm(*blocks):
        return [pltpu.with_memory_space_constraint(block, pltpu.HBM) for block in blocks]

    others = swapped([tgt_amp, proj_amp, tgt_energy, proj_energy])
    energy, amp = call(
        load_kernel,
        [in_vmem((2, 1, rows), jnp.float32), in_vmem((2, two_cols, rows), jnp.float32)],
        [HBM] * 4,
        [
            pltpu.VMEM((rows,), jnp.float32),
            pltpu.VMEM(tgt_amp.shape, jnp.float32),
            pltpu.VMEM(proj_amp.shape, jnp.float32),
            pltpu.SemaphoreType.DMA((4,)),
        ],
        pl.CostEstimate(
            flops=2 * 4 * rows * two_cols * points, bytes_accessed=4 * 1024 * 1024, transcendentals=0
        ),
    )(*in_hbm(tgt_energy, proj_energy, tgt_amp, proj_amp))
    chip_amp, energies, message = run(
        pack_kernel,
        [
            in_vmem((2, two_cols, rows), jnp.float32),
            in_vmem((2, 1, rows), jnp.float32),
            in_vmem((2, two_cols + PIECES, rows), jnp.bfloat16),
        ],
        amp,
        energy,
        *others,
    )
    message = exchanged(0, message)
    flags, counts = pair_flags.T, tile_counts.T
    (gate,) = call(
        functools.partial(gate_kernel, gate_levels),
        [in_vmem((n_steps, 2, 1, points), jnp.float32)],
        [HBM, HBM, VMEM],
        [
            pltpu.SMEM(flags.shape, jnp.int32),
            pltpu.SMEM(counts.shape, jnp.int32),
            pltpu.SemaphoreType.DMA((2,)),
        ],
        BEHIND,
    )(*in_hbm(flags, counts), chip_amp)
    sent, mine, weight = call(
        functools.partial(basis_kernel, neighbours),
        [
            in_vmem((2, 5 * rows + PIECES, points), jnp.bfloat16),
            in_vmem((2, 4 * rows, points), jnp.bfloat16),
            in_vmem((1, 1, points), jnp.float32),
        ],
        [HBM] * 3 + [VMEM],
        [pltpu.VMEM((points,), jnp.float32), pltpu.SemaphoreType.DMA((10,))],
    )(
        *in_hbm(quad_weight, tgt_basis.reshape(2, -1, rows, points), proj_basis),
        chip_amp,
    )
    theirs = other_core(sent)
    part, weights = run(
        chip_kernel,
        [in_vmem((2, two_cols, points), jnp.float32), in_vmem((2, 1, points), jnp.float32)],
        mine,
        theirs,
        chip_amp,
        weight,
    )
    halves = run(first_kernel, [sums] * 2, mine, theirs, gate, weights, part, message)
    fields = summed(*halves)
    low, high = swapped(fields)
    (states,) = run(
        low_kernel,
        [in_vmem((4, two_cols, rows), jnp.float32)],
        mine,
        theirs,
        low,
        chip_amp,
        energies,
        message,
    )
    *halves, my_half, half_send = run(
        second_kernel,
        [sums, sums, segment, segment],
        mine,
        theirs,
        states,
        high,
        gate,
        weights,
    )
    other_half = other_core(half_send)
    fields = summed(*halves)
    low, high = swapped(fields)
    my_part, other_new = run(
        late_kernel,
        [segment, in_vmem((rows, two_cols), jnp.float32)],
        theirs,
        sent,
        *fields,
        energy,
        amp,
        my_half,
        other_half,
    )
    return run(
        last_kernel,
        [
            jax.ShapeDtypeStruct(tgt_amp.shape, jnp.float32),
            jax.ShapeDtypeStruct(proj_amp.shape, jnp.float32),
        ],
        mine,
        theirs,
        low,
        high,
        my_part,
        other_new,
    )


def solution(mesh):
    in_specs = (
        P(None, "tgt", "rep"),
        P(None, None, "prj", "rep"),
        P(("bpar", "rep")),
        P(("tgt", "prj", "rep")),
        P(("tgt", "rep"), "prj"),
        P("bpar", None),
        P("bpar", None),
        P(("bpar", "tgt", "prj", "rep"), None),
        P(("bpar", "tgt", "rep"), "prj", None),
    )
    out_specs = (P(("bpar", "tgt", "prj", "rep"), None), P(("bpar", "tgt", "rep"), "prj", None))

    def step(*args):
        return tuple(shards(*args))

    return jax.shard_map(step, mesh=mesh, in_specs=in_specs, out_specs=out_specs, check_vma=False)
```

```python
import functools

import jax
import jax.numpy as jnp
from jax import lax
from jax.experimental import pallas as pl
from jax.experimental.pallas import tpu as pltpu
from jax.sharding import PartitionSpec as P

time_step = 0.4
half_step = 0.5 * time_step
VMEM_LIMIT = 8 * 1024 * 1024
DEVICES = ("tgt", "prj", "rep")
HBM = pl.BlockSpec(memory_space=pl.ANY)
VMEM = pl.BlockSpec(memory_space=pltpu.VMEM)


def parity(place):
    odd = 0
    while place:
        odd, place = odd ^ (place & 1), place >> 1
    return odd


def my_kind():
    n_tgt, n_prj = lax.axis_size("tgt"), lax.axis_size("prj")
    place = lax.axis_index("tgt") * n_prj + lax.axis_index("prj")
    kind = lax.axis_index("rep")
    for bit in range((n_tgt * n_prj).bit_length() - 1):
        kind = jnp.bitwise_xor(kind, jnp.bitwise_and(lax.shift_right_logical(place, bit), 1))
    return kind


def by_core(body):
    for core in range(2):

        @pl.when(lax.axis_index("rep") == core)
        def _():
            body(core)


def ordered(core, first, second):
    return jnp.where(core == 0, first, second), jnp.where(core == 0, second, first)


def turned(block):
    half = block.shape[0] // 2
    return jnp.concatenate([block[half:], -block[:half]], axis=0)


def bf16(block):
    return block.astype(jnp.bfloat16)


def f32(block):
    return block.astype(jnp.float32)


def rows_of(basis, segment, amount):
    return [basis[part, segment * amount : (segment + 1) * amount, :] for part in range(2)]


def project(basis, amp):
    return jnp.dot(bf16(amp), basis[0], preferred_element_type=jnp.float32) + jnp.dot(
        bf16(turned(amp)), basis[1], preferred_element_type=jnp.float32
    )


def expand(basis, field):
    contract = (((1,), (1,)), ((), ()))
    return lax.dot_general(
        turned(field), basis[0], contract, preferred_element_type=jnp.float32
    ) + lax.dot_general(field, basis[1], contract, preferred_element_type=jnp.float32)


PIECES = 16

BEHIND = pl.CostEstimate(flops=1 << 35, bytes_accessed=1 << 16, transcendentals=0)


def split(row):
    index = lax.broadcasted_iota(jnp.int32, (PIECES, row.shape[1]), 0)
    block = jnp.zeros(index.shape, jnp.float32)
    for piece in range(3):
        rounded = f32(bf16(row))
        block = jnp.where(index == piece, rounded, block)
        row = row - rounded
    return bf16(block)


def joined(block):
    pieces = f32(block)
    return pieces[0:1] + pieces[1:2] + pieces[2:3]


def basis_copies(basis, sem, my, neighbours, sources):
    axis = ("prj", "tgt")[my]
    rows = sources[my].shape[2]
    place = lax.axis_index(axis)
    copies = []
    for chip, there in enumerate((place, jnp.bitwise_xor(place, neighbours[my]))):
        for core in range(2):
            segment = 2 * chip + core
            copies.append(
                pltpu.make_async_copy(
                    sources[my].at[:, 2 * there + core],
                    basis.at[:, segment * rows : (segment + 1) * rows],
                    sem.at[segment],
                )
            )
    return copies


def load_kernel(
    tgt_energy_hbm,
    proj_energy_hbm,
    tgt_own_hbm,
    proj_own_hbm,
    energy,
    amp_ref,
    flat_energy,
    tgt_own,
    proj_own,
    sems,
):
    pairs = [
        (tgt_own_hbm, tgt_own),
        (proj_own_hbm, proj_own),
        (tgt_energy_hbm, flat_energy),
        (proj_energy_hbm, energy.at[1]),
    ]
    copies = [pltpu.make_async_copy(src, dst, sems.at[k]) for k, (src, dst) in enumerate(pairs)]
    for copy in copies:
        copy.start()
    for copy in copies:
        copy.wait()
    energy[0] = flat_energy[...][None, :]
    amp_ref[0] = tgt_own[...].T
    amp_ref[1] = proj_own[0].T


def pack_kernel(
    amp_ref,
    energy,
    tgt_other,
    proj_other,
    tgt_energy_other,
    proj_energy_other,
    chip_amp,
    energies,
    message,
):
    core = lax.axis_index("rep")
    my = my_kind()
    cols = chip_amp.shape[1]
    other_amp, _ = ordered(my, tgt_other[...].T, proj_other[0].T)
    other_energy, _ = ordered(my, tgt_energy_other[...][None, :], proj_energy_other[...])
    amps = ordered(core, amp_ref[my], other_amp)
    rows = ordered(core, energy[my], other_energy)
    for segment in range(2):
        chip_amp[segment] = amps[segment]
        energies[segment] = rows[segment]
        message[segment, :cols] = bf16(amps[segment])
        message[segment, cols:] = split(rows[segment])


def sent_kernel(neighbours, weight_hbm, tgt_hbm, proj_hbm, chip_amp, sent, weight, flat_weight, sems):
    my = my_kind()
    sources = (tgt_hbm, proj_hbm)
    rows = chip_amp.shape[2]

    def copies_of(kind):
        last = pltpu.make_async_copy(
            sources[kind].at[:, 2 * lax.axis_index(("prj", "tgt")[kind]) + 1 - lax.axis_index("rep")],
            sent.at[:, 4 * rows : 5 * rows],
            sems.at[4],
        )
        return basis_copies(sent, sems, 1 - kind, neighbours, sources) + [last]

    weight_copy = pltpu.make_async_copy(weight_hbm, flat_weight, sems.at[5])
    weight_copy.start()
    for kind in range(2):

        @pl.when(my == kind)
        def _():
            for copy in copies_of(kind):
                copy.start()

    weight_copy.wait()
    weight[0] = flat_weight[...][None, :]
    for part in range(2):
        sent[part, 5 * rows :] = split(weight[0])
    for copy in copies_of(0):
        copy.wait()


def side_kernel(
    gate_levels, neighbours, flags_hbm, counts_hbm, tgt_hbm, proj_hbm, chip_amp, mine, gate, flags, counts, sems
):
    my = my_kind()
    tgt_index = lax.axis_index("tgt")
    prj_index = lax.axis_index("prj")
    sources = (tgt_hbm, proj_hbm)
    pairs = [(flags_hbm, flags), (counts_hbm, counts)]
    copies = [pltpu.make_async_copy(src, dst, sems.at[4 + k]) for k, (src, dst) in enumerate(pairs)]
    for copy in copies:
        copy.start()
    for kind in range(2):

        @pl.when(my == kind)
        def _():
            for copy in basis_copies(mine, sems, kind, neighbours, sources):
                copy.start()

    for copy in copies:
        copy.wait()
    tiles = 2
    width = gate.shape[-1] // tiles
    gate_level = jnp.where(my == 0, *gate_levels)
    for half in range(2):
        for tile in range(tiles):
            live = jnp.logical_and(
                flags[prj_index, tgt_index] > 0, tiles * half + tile < counts[prj_index, tgt_index]
            )
            value = jnp.where(live, 1.0, 0.0).astype(jnp.float32)
            for level in range(gate.shape[0]):
                here = jnp.where(level == gate_level, value, jnp.float32(1.0))
                gate[level, half, :, tile * width : (tile + 1) * width] = jnp.full(
                    (1, width), here, jnp.float32
                )
    for copy in basis_copies(mine, sems, 0, neighbours, sources):
        copy.wait()


def chip_kernel(mine, theirs, chip_amp, weight, part_ref, weights):
    rows = chip_amp.shape[2]

    def body(core):
        for half, basis in enumerate((mine, theirs) if core == 0 else (theirs, mine)):
            part_ref[half] = sum(
                project(rows_of(basis, segment, rows), chip_amp[segment]) for segment in range(2)
            )
        weights[core] = weight[0]
        weights[1 - core] = joined(theirs[0, 5 * rows :, :])

    by_core(body)


def first_kernel(mine, theirs, gate, weights, part_ref, message, *outs):
    rows = message.shape[2]
    cols = part_ref.shape[1]

    def body(core):
        for half, basis in enumerate((mine, theirs) if core == 0 else (theirs, mine)):
            total = part_ref[half] + sum(
                project(rows_of(basis, 2 + segment, rows), f32(message[segment, :cols]))
                for segment in range(2)
            )
            outs[half][...] = bf16(gate[0, half] * (weights[half] * total))

    by_core(body)


def add_kernel(level, half, gate, own, other, out_ref):
    out_ref[...] = bf16(gate[level, half] * (f32(own[...]) + f32(other[...])))


def low_kernel(mine, theirs, low, low_there, chip_amp, energies, message, states_ref):
    _, cols, rows = chip_amp.shape
    field = bf16(f32(low[...]) + f32(low_there[...]))

    def body(core):
        for segment in range(4):
            if segment < 2:
                amp, energy = chip_amp[segment], energies[segment]
            else:
                amp, energy = f32(message[segment - 2, :cols]), joined(message[segment - 2, cols:])
            change = expand(rows_of((mine, theirs)[core], segment, rows), field)
            states_ref[segment] = amp + half_step * (energy * turned(amp) + change)

    by_core(body)


def second_kernel(
    mine, theirs, states_ref, high, high_there, gate, weights, low_ref, high_ref, half_ref, send_ref
):
    rows = states_ref.shape[2]
    field = bf16(f32(high[...]) + f32(high_there[...]))

    def body(core):
        bases = (mine, theirs) if core == 0 else (theirs, mine)
        halves = [
            states_ref[segment] + half_step * expand(rows_of(bases[1], segment, rows), field)
            for segment in range(4)
        ]
        half_ref[...] = halves[core]
        send_ref[...] = halves[1 - core]
        for half, out_ref in enumerate((low_ref, high_ref)):
            total = sum(
                project(rows_of(bases[half], segment, rows), halves[segment]) for segment in range(4)
            )
            out_ref[...] = bf16(gate[0, half] * (weights[half] * total))

    by_core(body)


def late_kernel(theirs, sent, low, high, energy, amp_ref, my_half, other_half, my_part, other_new):
    rows = amp_ref.shape[2]

    def body(core):
        my = my_kind()
        near, far = (low, high) if core == 0 else (high, low)
        change = expand(rows_of(sent, core, rows), near[...]) + expand(rows_of(theirs, 4, rows), far[...])
        rate = energy[1 - my] * turned(other_half[...]) + change
        other_new[...] = (amp_ref[1 - my] + time_step * rate).T
        my_part[...] = amp_ref[my] + time_step * (energy[my] * turned(my_half[...]))

    by_core(body)


def last_kernel(mine, theirs, low, high, my_part, other_new, new_tgt, new_proj):
    rows = my_part.shape[1]

    def body(core):
        near, far = (low, high) if core == 0 else (high, low)
        change = expand(rows_of(mine, core, rows), near[...]) + expand(
            rows_of(theirs, core, rows), far[...]
        )
        my_new = (my_part[...] + time_step * change).T
        new_tgt[...], new_proj[0] = ordered(my_kind(), my_new, other_new[...])

    by_core(body)


def shards(
    tgt_basis,
    proj_basis,
    quad_weight,
    tgt_energy,
    proj_energy,
    pair_flags,
    tile_counts,
    tgt_amp,
    proj_amp,
):
    points = quad_weight.shape[0]
    rows, two_cols = tgt_amp.shape
    sizes = [lax.axis_size(axis) for axis in DEVICES]

    def call(kernel, out_shape, in_specs, scratch_shapes=(), cost=None):
        return pl.pallas_call(
            kernel,
            out_shape=out_shape,
            in_specs=in_specs,
            out_specs=[VMEM] * len(out_shape),
            scratch_shapes=scratch_shapes,
            cost_estimate=cost,
            compiler_params=pltpu.CompilerParams(vmem_limit_bytes=VMEM_LIMIT),
        )

    def run(kernel, out_shape, *blocks):
        return call(kernel, out_shape, [VMEM] * len(blocks))(*blocks)

    def other_core(block):
        return lax.ppermute(block, "rep", [(0, 1), (1, 0)])

    n_tgt, n_prj, n_core = sizes
    tgt_flips = [n_prj << bit for bit in range(n_tgt.bit_length() - 1)]
    prj_flips = [1 << bit for bit in range(n_prj.bit_length() - 1)]
    flips = (prj_flips + tgt_flips[::-1], tgt_flips[::-1] + prj_flips)
    neighbours = (flips[0][0], flips[1][0] // n_prj)
    gate_levels = (len(prj_flips) - 1, len(tgt_flips) - 1)
    n_steps = len(tgt_flips) + len(prj_flips)

    def exchanged(step, block, crossed=0):
        pairs = []
        for place in range(n_tgt * n_prj):
            for kind in range(2):
                there = place ^ flips[kind][step]
                to_core = kind ^ crossed ^ parity(there)
                pairs.append((place * n_core + (kind ^ parity(place)), there * n_core + to_core))
        return lax.ppermute(block, DEVICES, pairs)

    in_vmem = pltpu.VMEM
    sums = in_vmem((two_cols, points), jnp.bfloat16)
    segment = in_vmem((two_cols, rows), jnp.float32)

    def summed(halves, until):
        totals = []
        for half, block in enumerate(halves):
            for step in range(1, until):
                other = exchanged(step, block)
                (block,) = run(functools.partial(add_kernel, step, half), [sums], gate, block, other)
            totals.append(block)
        return totals

    def swapped(fields):
        return [other_core(block) for block in fields]

    def in_hbm(*blocks):
        return [pltpu.with_memory_space_constraint(block, pltpu.HBM) for block in blocks]

    others = swapped([tgt_amp, proj_amp, tgt_energy, proj_energy])
    energy, amp = call(
        load_kernel,
        [in_vmem((2, 1, rows), jnp.float32), in_vmem((2, two_cols, rows), jnp.float32)],
        [HBM] * 4,
        [
            pltpu.VMEM((rows,), jnp.float32),
            pltpu.VMEM(tgt_amp.shape, jnp.float32),
            pltpu.VMEM(proj_amp.shape, jnp.float32),
            pltpu.SemaphoreType.DMA((4,)),
        ],
        pl.CostEstimate(
            flops=2 * 4 * rows * two_cols * points, bytes_accessed=4 * 1024 * 1024, transcendentals=0
        ),
    )(*in_hbm(tgt_energy, proj_energy, tgt_amp, proj_amp))
    chip_amp, energies, message = run(
        pack_kernel,
        [
            in_vmem((2, two_cols, rows), jnp.float32),
            in_vmem((2, 1, rows), jnp.float32),
            in_vmem((2, two_cols + PIECES, rows), jnp.bfloat16),
        ],
        amp,
        energy,
        *others,
    )
    message = exchanged(0, message)
    flags, counts = pair_flags.T, tile_counts.T
    bases = in_hbm(tgt_basis.reshape(2, -1, rows, points), proj_basis)
    sent, weight = call(
        functools.partial(sent_kernel, neighbours),
        [
            in_vmem((2, 5 * rows + PIECES, points), jnp.bfloat16),
            in_vmem((1, 1, points), jnp.float32),
        ],
        [HBM] * 3 + [VMEM],
        [pltpu.VMEM((points,), jnp.float32), pltpu.SemaphoreType.DMA((6,))],
    )(*in_hbm(quad_weight), *bases, chip_amp)
    mine, gate = call(
        functools.partial(side_kernel, gate_levels, neighbours),
        [
            in_vmem((2, 4 * rows, points), jnp.bfloat16),
            in_vmem((n_steps, 2, 1, points), jnp.float32),
        ],
        [HBM] * 4 + [VMEM],
        [
            pltpu.SMEM(flags.shape, jnp.int32),
            pltpu.SMEM(counts.shape, jnp.int32),
            pltpu.SemaphoreType.DMA((6,)),
        ],
        BEHIND,
    )(*in_hbm(flags, counts), *bases, chip_amp)
    theirs = other_core(sent)
    part, weights = run(
        chip_kernel,
        [in_vmem((2, two_cols, points), jnp.float32), in_vmem((2, 1, points), jnp.float32)],
        mine,
        theirs,
        chip_amp,
        weight,
    )
    halves = run(first_kernel, [sums] * 2, mine, theirs, gate, weights, part, message)
    parts = summed(halves, n_steps - 1)
    low, high = [(other_core(block), exchanged(n_steps - 1, block, 1)) for block in parts]
    (states,) = run(
        low_kernel,
        [in_vmem((4, two_cols, rows), jnp.float32)],
        mine,
        theirs,
        *low,
        chip_amp,
        energies,
        message,
    )
    *halves, my_half, half_send = run(
        second_kernel,
        [sums, sums, segment, segment],
        mine,
        theirs,
        states,
        *high,
        gate,
        weights,
    )
    other_half = other_core(half_send)
    fields = summed(halves, n_steps)
    low, high = swapped(fields)
    my_part, other_new = run(
        late_kernel,
        [segment, in_vmem((rows, two_cols), jnp.float32)],
        theirs,
        sent,
        *fields,
        energy,
        amp,
        my_half,
        other_half,
    )
    return run(
        last_kernel,
        [
            jax.ShapeDtypeStruct(tgt_amp.shape, jnp.float32),
            jax.ShapeDtypeStruct(proj_amp.shape, jnp.float32),
        ],
        mine,
        theirs,
        low,
        high,
        my_part,
        other_new,
    )


def solution(mesh):
    in_specs = (
        P(None, "tgt", "rep"),
        P(None, None, "prj", "rep"),
        P(("bpar", "rep")),
        P(("tgt", "prj", "rep")),
        P(("tgt", "rep"), "prj"),
        P("bpar", None),
        P("bpar", None),
        P(("bpar", "tgt", "prj", "rep"), None),
        P(("bpar", "tgt", "rep"), "prj", None),
    )
    out_specs = (P(("bpar", "tgt", "prj", "rep"), None), P(("bpar", "tgt", "rep"), "prj", None))

    def step(*args):
        return tuple(shards(*args))

    return jax.shard_map(step, mesh=mesh, in_specs=in_specs, out_specs=out_specs, check_vma=False)
```

```python
import functools

import jax
import jax.numpy as jnp
from jax import lax
from jax.experimental import pallas as pl
from jax.experimental.pallas import tpu as pltpu
from jax.sharding import PartitionSpec as P

time_step = 0.4
half_step = 0.5 * time_step
VMEM_LIMIT = 8 * 1024 * 1024
DEVICES = ("tgt", "prj", "rep")
HBM = pl.BlockSpec(memory_space=pl.ANY)
VMEM = pl.BlockSpec(memory_space=pltpu.VMEM)


def parity(place):
    odd = 0
    while place:
        odd, place = odd ^ (place & 1), place >> 1
    return odd


def my_kind():
    n_tgt, n_prj = lax.axis_size("tgt"), lax.axis_size("prj")
    place = lax.axis_index("tgt") * n_prj + lax.axis_index("prj")
    kind = lax.axis_index("rep")
    for bit in range((n_tgt * n_prj).bit_length() - 1):
        kind = jnp.bitwise_xor(kind, jnp.bitwise_and(lax.shift_right_logical(place, bit), 1))
    return kind


def by_core(body):
    for core in range(2):

        @pl.when(lax.axis_index("rep") == core)
        def _():
            body(core)


def ordered(core, first, second):
    return jnp.where(core == 0, first, second), jnp.where(core == 0, second, first)


def turned(block):
    half = block.shape[0] // 2
    return jnp.concatenate([block[half:], -block[:half]], axis=0)


def bf16(block):
    return block.astype(jnp.bfloat16)


def f32(block):
    return block.astype(jnp.float32)


def rows_of(bases, segment, amount):
    start = segment % 2 * amount
    return [bases[segment // 2][part, start : start + amount, :] for part in range(2)]


def project(basis, amp):
    return jnp.dot(bf16(amp), basis[0], preferred_element_type=jnp.float32) + jnp.dot(
        bf16(turned(amp)), basis[1], preferred_element_type=jnp.float32
    )


def expand(basis, field):
    contract = (((1,), (1,)), ((), ()))
    return lax.dot_general(
        turned(field), basis[0], contract, preferred_element_type=jnp.float32
    ) + lax.dot_general(field, basis[1], contract, preferred_element_type=jnp.float32)


PIECES = 16

BEHIND = pl.CostEstimate(flops=1 << 35, bytes_accessed=1 << 16, transcendentals=0)


def split(row):
    index = lax.broadcasted_iota(jnp.int32, (PIECES, row.shape[1]), 0)
    block = jnp.zeros(index.shape, jnp.float32)
    for piece in range(3):
        rounded = f32(bf16(row))
        block = jnp.where(index == piece, rounded, block)
        row = row - rounded
    return bf16(block)


def joined(block):
    pieces = f32(block)
    return pieces[0:1] + pieces[1:2] + pieces[2:3]


def basis_copies(bases, sem, my, neighbours, sources):
    rows = sources[my].shape[2]
    place = lax.axis_index(("prj", "tgt")[my])
    copies = []
    for chip, there in enumerate((place, jnp.bitwise_xor(place, neighbours[my]))):
        for core in range(2):
            copies.append(
                pltpu.make_async_copy(
                    sources[my].at[:, 2 * there + core],
                    bases[chip].at[:, core * rows : (core + 1) * rows],
                    sem.at[2 * chip + core],
                )
            )
    return copies


def load_kernel(
    tgt_energy_hbm,
    proj_energy_hbm,
    tgt_own_hbm,
    proj_own_hbm,
    energy,
    amp_ref,
    flat_energy,
    tgt_own,
    proj_own,
    sems,
):
    pairs = [
        (tgt_own_hbm, tgt_own),
        (proj_own_hbm, proj_own),
        (tgt_energy_hbm, flat_energy),
        (proj_energy_hbm, energy.at[1]),
    ]
    copies = [pltpu.make_async_copy(src, dst, sems.at[k]) for k, (src, dst) in enumerate(pairs)]
    for copy in copies:
        copy.start()
    for copy in copies:
        copy.wait()
    energy[0] = flat_energy[...][None, :]
    amp_ref[0] = tgt_own[...].T
    amp_ref[1] = proj_own[0].T


def pack_kernel(
    amp_ref,
    energy,
    tgt_other,
    proj_other,
    tgt_energy_other,
    proj_energy_other,
    chip_amp,
    energies,
    message,
):
    core = lax.axis_index("rep")
    my = my_kind()
    cols = chip_amp.shape[1]
    other_amp, _ = ordered(my, tgt_other[...].T, proj_other[0].T)
    other_energy, _ = ordered(my, tgt_energy_other[...][None, :], proj_energy_other[...])
    amps = ordered(core, amp_ref[my], other_amp)
    rows = ordered(core, energy[my], other_energy)
    for segment in range(2):
        chip_amp[segment] = amps[segment]
        energies[segment] = rows[segment]
        message[segment, :cols] = bf16(amps[segment])
        message[segment, cols:] = split(rows[segment])


def sent_kernel(
    neighbours, weight_hbm, tgt_hbm, proj_hbm, chip_amp, sent_chip, sent_far, sent_own, weight, flat_weight, sems
):
    my = my_kind()
    sources = (tgt_hbm, proj_hbm)
    rows = chip_amp.shape[2]

    def copies_of(kind):
        own = pltpu.make_async_copy(
            sources[kind].at[:, 2 * lax.axis_index(("prj", "tgt")[kind]) + 1 - lax.axis_index("rep")],
            sent_own,
            sems.at[4],
        )
        return basis_copies((sent_chip, sent_far), sems, 1 - kind, neighbours, sources) + [own]

    weight_copy = pltpu.make_async_copy(weight_hbm, flat_weight, sems.at[5])
    weight_copy.start()
    for kind in range(2):

        @pl.when(my == kind)
        def _():
            for copy in copies_of(kind):
                copy.start()

    weight_copy.wait()
    weight[0] = flat_weight[...][None, :]
    for part in range(2):
        sent_chip[part, 2 * rows :] = split(weight[0])
    for copy in copies_of(0):
        copy.wait()


def side_kernel(
    gate_levels,
    neighbours,
    flags_hbm,
    counts_hbm,
    tgt_hbm,
    proj_hbm,
    chip_amp,
    mine_chip,
    mine_far,
    gate,
    flags,
    counts,
    sems,
):
    my = my_kind()
    tgt_index = lax.axis_index("tgt")
    prj_index = lax.axis_index("prj")
    sources = (tgt_hbm, proj_hbm)
    pairs = [(flags_hbm, flags), (counts_hbm, counts)]
    copies = [pltpu.make_async_copy(src, dst, sems.at[4 + k]) for k, (src, dst) in enumerate(pairs)]
    for copy in copies:
        copy.start()
    for kind in range(2):

        @pl.when(my == kind)
        def _():
            for copy in basis_copies((mine_chip, mine_far), sems, kind, neighbours, sources):
                copy.start()

    for copy in copies:
        copy.wait()
    tiles = 2
    width = gate.shape[-1] // tiles
    gate_level = jnp.where(my == 0, *gate_levels)
    for half in range(2):
        for tile in range(tiles):
            live = jnp.logical_and(
                flags[prj_index, tgt_index] > 0, tiles * half + tile < counts[prj_index, tgt_index]
            )
            value = jnp.where(live, 1.0, 0.0).astype(jnp.float32)
            for level in range(gate.shape[0]):
                here = jnp.where(level == gate_level, value, jnp.float32(1.0))
                gate[level, half, :, tile * width : (tile + 1) * width] = jnp.full(
                    (1, width), here, jnp.float32
                )
    for copy in basis_copies((mine_chip, mine_far), sems, 0, neighbours, sources):
        copy.wait()


def chip_kernel(mine_chip, theirs_chip, chip_amp, weight, part_ref, weights):
    mine, theirs = (mine_chip,), (theirs_chip,)
    rows = chip_amp.shape[2]

    def body(core):
        for half, basis in enumerate((mine, theirs) if core == 0 else (theirs, mine)):
            part_ref[half] = sum(
                project(rows_of(basis, segment, rows), chip_amp[segment]) for segment in range(2)
            )
        weights[core] = weight[0]
        weights[1 - core] = joined(theirs_chip[0, 2 * rows :, :])

    by_core(body)


def first_kernel(mine_far, theirs_far, gate, weights, part_ref, message, *outs):
    mine, theirs = (None, mine_far), (None, theirs_far)
    rows = message.shape[2]
    cols = part_ref.shape[1]

    def body(core):
        for half, basis in enumerate((mine, theirs) if core == 0 else (theirs, mine)):
            total = part_ref[half] + sum(
                project(rows_of(basis, 2 + segment, rows), f32(message[segment, :cols]))
                for segment in range(2)
            )
            outs[half][...] = bf16(gate[0, half] * (weights[half] * total))

    by_core(body)


def add_kernel(level, half, gate, own, other, out_ref):
    out_ref[...] = bf16(gate[level, half] * (f32(own[...]) + f32(other[...])))


def low_kernel(
    mine_chip,
    mine_far,
    theirs_chip,
    theirs_far,
    low,
    low_there,
    chip_amp,
    energies,
    message,
    states_ref,
):
    mine, theirs = (mine_chip, mine_far), (theirs_chip, theirs_far)
    _, cols, rows = chip_amp.shape
    field = bf16(f32(low[...]) + f32(low_there[...]))

    def body(core):
        for segment in range(4):
            if segment < 2:
                amp, energy = chip_amp[segment], energies[segment]
            else:
                amp, energy = f32(message[segment - 2, :cols]), joined(message[segment - 2, cols:])
            change = expand(rows_of((mine, theirs)[core], segment, rows), field)
            states_ref[segment] = amp + half_step * (energy * turned(amp) + change)

    by_core(body)


def second_kernel(
    mine_chip,
    mine_far,
    theirs_chip,
    theirs_far,
    states_ref,
    high,
    high_there,
    gate,
    weights,
    low_ref,
    high_ref,
    half_ref,
    send_ref,
):
    mine, theirs = (mine_chip, mine_far), (theirs_chip, theirs_far)
    rows = states_ref.shape[2]
    field = bf16(f32(high[...]) + f32(high_there[...]))

    def body(core):
        bases = (mine, theirs) if core == 0 else (theirs, mine)
        halves = [
            states_ref[segment] + half_step * expand(rows_of(bases[1], segment, rows), field)
            for segment in range(4)
        ]
        half_ref[...] = halves[core]
        send_ref[...] = halves[1 - core]
        for half, out_ref in enumerate((low_ref, high_ref)):
            total = sum(
                project(rows_of(bases[half], segment, rows), halves[segment]) for segment in range(4)
            )
            out_ref[...] = bf16(gate[0, half] * (weights[half] * total))

    by_core(body)


def late_kernel(theirs_own, sent_chip, low, high, energy, amp_ref, my_half, other_half, my_part, other_new):
    rows = amp_ref.shape[2]

    def body(core):
        my = my_kind()
        near, far = (low, high) if core == 0 else (high, low)
        change = expand(rows_of((sent_chip,), core, rows), near[...]) + expand(
            rows_of((theirs_own,), 0, rows), far[...]
        )
        rate = energy[1 - my] * turned(other_half[...]) + change
        other_new[...] = (amp_ref[1 - my] + time_step * rate).T
        my_part[...] = amp_ref[my] + time_step * (energy[my] * turned(my_half[...]))

    by_core(body)


def last_kernel(mine_chip, theirs_chip, low, high, my_part, other_new, new_tgt, new_proj):
    rows = my_part.shape[1]

    def body(core):
        near, far = (low, high) if core == 0 else (high, low)
        change = expand(rows_of((mine_chip,), core, rows), near[...]) + expand(
            rows_of((theirs_chip,), core, rows), far[...]
        )
        my_new = (my_part[...] + time_step * change).T
        new_tgt[...], new_proj[0] = ordered(my_kind(), my_new, other_new[...])

    by_core(body)


def shards(
    tgt_basis,
    proj_basis,
    quad_weight,
    tgt_energy,
    proj_energy,
    pair_flags,
    tile_counts,
    tgt_amp,
    proj_amp,
):
    points = quad_weight.shape[0]
    rows, two_cols = tgt_amp.shape
    sizes = [lax.axis_size(axis) for axis in DEVICES]

    def call(kernel, out_shape, in_specs, scratch_shapes=(), cost=None):
        return pl.pallas_call(
            kernel,
            out_shape=out_shape,
            in_specs=in_specs,
            out_specs=[VMEM] * len(out_shape),
            scratch_shapes=scratch_shapes,
            cost_estimate=cost,
            compiler_params=pltpu.CompilerParams(vmem_limit_bytes=VMEM_LIMIT),
        )

    def run(kernel, out_shape, *blocks):
        return call(kernel, out_shape, [VMEM] * len(blocks))(*blocks)

    def other_core(block):
        return lax.ppermute(block, "rep", [(0, 1), (1, 0)])

    n_tgt, n_prj, n_core = sizes
    tgt_flips = [n_prj << bit for bit in range(n_tgt.bit_length() - 1)]
    prj_flips = [1 << bit for bit in range(n_prj.bit_length() - 1)]
    far_first, near_first = tgt_flips[::-1], tgt_flips
    flips = [(prj_flips + order, far_first + prj_flips) for order in (far_first, near_first)]
    neighbours = (prj_flips[0], far_first[0] // n_prj)
    gate_levels = (len(prj_flips) - 1, len(tgt_flips) - 1)
    n_steps = len(tgt_flips) + len(prj_flips)

    def exchanged(step, block, half=0, crossed=0):
        pairs = []
        for place in range(n_tgt * n_prj):
            for kind in range(2):
                there = place ^ flips[half][kind][step]
                to_core = kind ^ crossed ^ parity(there)
                pairs.append((place * n_core + (kind ^ parity(place)), there * n_core + to_core))
        return lax.ppermute(block, DEVICES, pairs)

    in_vmem = pltpu.VMEM
    sums = in_vmem((two_cols, points), jnp.bfloat16)
    segment = in_vmem((two_cols, rows), jnp.float32)

    def summed(halves, until):
        totals = []
        for half, block in enumerate(halves):
            for step in range(1, until):
                other = exchanged(step, block, half)
                (block,) = run(functools.partial(add_kernel, step, half), [sums], gate, block, other)
            totals.append(block)
        return totals

    def swapped(fields):
        return [other_core(block) for block in fields]

    def in_hbm(*blocks):
        return [pltpu.with_memory_space_constraint(block, pltpu.HBM) for block in blocks]

    others = swapped([tgt_amp, proj_amp, tgt_energy, proj_energy])
    energy, amp = call(
        load_kernel,
        [in_vmem((2, 1, rows), jnp.float32), in_vmem((2, two_cols, rows), jnp.float32)],
        [HBM] * 4,
        [
            pltpu.VMEM((rows,), jnp.float32),
            pltpu.VMEM(tgt_amp.shape, jnp.float32),
            pltpu.VMEM(proj_amp.shape, jnp.float32),
            pltpu.SemaphoreType.DMA((4,)),
        ],
        pl.CostEstimate(
            flops=2 * 4 * rows * two_cols * points, bytes_accessed=4 * 1024 * 1024, transcendentals=0
        ),
    )(*in_hbm(tgt_energy, proj_energy, tgt_amp, proj_amp))
    chip_amp, energies, message = run(
        pack_kernel,
        [
            in_vmem((2, two_cols, rows), jnp.float32),
            in_vmem((2, 1, rows), jnp.float32),
            in_vmem((2, two_cols + PIECES, rows), jnp.bfloat16),
        ],
        amp,
        energy,
        *others,
    )
    message = exchanged(0, message)
    flags, counts = pair_flags.T, tile_counts.T
    bases = in_hbm(tgt_basis.reshape(2, -1, rows, points), proj_basis)
    pair = in_vmem((2, 2 * rows, points), jnp.bfloat16)
    *sent, weight = call(
        functools.partial(sent_kernel, neighbours),
        [
            in_vmem((2, 2 * rows + PIECES, points), jnp.bfloat16),
            pair,
            in_vmem((2, rows, points), jnp.bfloat16),
            in_vmem((1, 1, points), jnp.float32),
        ],
        [HBM] * 3 + [VMEM],
        [pltpu.VMEM((points,), jnp.float32), pltpu.SemaphoreType.DMA((6,))],
    )(*in_hbm(quad_weight), *bases, chip_amp)
    mine_chip, mine_far, gate = call(
        functools.partial(side_kernel, gate_levels, neighbours),
        [
            pair,
            pair,
            in_vmem((n_steps, 2, 1, points), jnp.float32),
        ],
        [HBM] * 4 + [VMEM],
        [
            pltpu.SMEM(flags.shape, jnp.int32),
            pltpu.SMEM(counts.shape, jnp.int32),
            pltpu.SemaphoreType.DMA((6,)),
        ],
        BEHIND,
    )(*in_hbm(flags, counts), *bases, chip_amp)
    theirs_chip, theirs_far, theirs_own = swapped(sent)
    bases = (mine_chip, mine_far, theirs_chip, theirs_far)
    part, weights = run(
        chip_kernel,
        [in_vmem((2, two_cols, points), jnp.float32), in_vmem((2, 1, points), jnp.float32)],
        mine_chip,
        theirs_chip,
        chip_amp,
        weight,
    )
    halves = run(first_kernel, [sums] * 2, mine_far, theirs_far, gate, weights, part, message)
    parts = summed(halves, n_steps - 1)
    low, high = [
        (other_core(block), exchanged(n_steps - 1, block, half, 1)) for half, block in enumerate(parts)
    ]
    (states,) = run(
        low_kernel,
        [in_vmem((4, two_cols, rows), jnp.float32)],
        *bases,
        *low,
        chip_amp,
        energies,
        message,
    )
    *halves, my_half, half_send = run(
        second_kernel,
        [sums, sums, segment, segment],
        *bases,
        states,
        *high,
        gate,
        weights,
    )
    other_half = other_core(half_send)
    fields = summed(halves, n_steps)
    low, high = swapped(fields)
    my_part, other_new = run(
        late_kernel,
        [segment, in_vmem((rows, two_cols), jnp.float32)],
        theirs_own,
        sent[0],
        *fields,
        energy,
        amp,
        my_half,
        other_half,
    )
    return run(
        last_kernel,
        [
            jax.ShapeDtypeStruct(tgt_amp.shape, jnp.float32),
            jax.ShapeDtypeStruct(proj_amp.shape, jnp.float32),
        ],
        mine_chip,
        theirs_chip,
        low,
        high,
        my_part,
        other_new,
    )


def solution(mesh):
    in_specs = (
        P(None, "tgt", "rep"),
        P(None, None, "prj", "rep"),
        P(("bpar", "rep")),
        P(("tgt", "prj", "rep")),
        P(("tgt", "rep"), "prj"),
        P("bpar", None),
        P("bpar", None),
        P(("bpar", "tgt", "prj", "rep"), None),
        P(("bpar", "tgt", "rep"), "prj", None),
    )
    out_specs = (P(("bpar", "tgt", "prj", "rep"), None), P(("bpar", "tgt", "rep"), "prj", None))

    def step(*args):
        return tuple(shards(*args))

    return jax.shard_map(step, mesh=mesh, in_specs=in_specs, out_specs=out_specs, check_vma=False)
```

```python
import functools

import jax
import jax.numpy as jnp
from jax import lax
from jax.experimental import pallas as pl
from jax.experimental.pallas import tpu as pltpu
from jax.sharding import PartitionSpec as P

time_step = 0.4
half_step = 0.5 * time_step
VMEM_LIMIT = 8 * 1024 * 1024
DEVICES = ("tgt", "prj", "rep")
HBM = pl.BlockSpec(memory_space=pl.ANY)
VMEM = pl.BlockSpec(memory_space=pltpu.VMEM)


def parity(place):
    odd = 0
    while place:
        odd, place = odd ^ (place & 1), place >> 1
    return odd


def my_kind():
    n_tgt, n_prj = lax.axis_size("tgt"), lax.axis_size("prj")
    place = lax.axis_index("tgt") * n_prj + lax.axis_index("prj")
    kind = lax.axis_index("rep")
    for bit in range((n_tgt * n_prj).bit_length() - 1):
        kind = jnp.bitwise_xor(kind, jnp.bitwise_and(lax.shift_right_logical(place, bit), 1))
    return kind


def by_core(body):
    for core in range(2):

        @pl.when(lax.axis_index("rep") == core)
        def _():
            body(core)


def ordered(core, first, second):
    return jnp.where(core == 0, first, second), jnp.where(core == 0, second, first)


def turned(block):
    half = block.shape[0] // 2
    return jnp.concatenate([block[half:], -block[:half]], axis=0)


def bf16(block):
    return block.astype(jnp.bfloat16)


def f32(block):
    return block.astype(jnp.float32)


def rows_of(bases, segment, amount):
    start = segment % 2 * amount
    return [bases[segment // 2][part, start : start + amount, :] for part in range(2)]


def project(basis, amp):
    return jnp.dot(bf16(amp), basis[0], preferred_element_type=jnp.float32) + jnp.dot(
        bf16(turned(amp)), basis[1], preferred_element_type=jnp.float32
    )


def expand(basis, field):
    contract = (((1,), (1,)), ((), ()))
    return lax.dot_general(
        turned(field), basis[0], contract, preferred_element_type=jnp.float32
    ) + lax.dot_general(field, basis[1], contract, preferred_element_type=jnp.float32)


PIECES = 16

BEHIND = pl.CostEstimate(flops=1 << 35, bytes_accessed=1 << 16, transcendentals=0)


def split(row):
    index = lax.broadcasted_iota(jnp.int32, (PIECES, row.shape[1]), 0)
    block = jnp.zeros(index.shape, jnp.float32)
    for piece in range(3):
        rounded = f32(bf16(row))
        block = jnp.where(index == piece, rounded, block)
        row = row - rounded
    return bf16(block)


def joined(block):
    pieces = f32(block)
    return pieces[0:1] + pieces[1:2] + pieces[2:3]


def basis_copies(bases, sem, my, neighbours, sources):
    rows = sources[my].shape[2]
    place = lax.axis_index(("prj", "tgt")[my])
    copies = []
    for chip, there in enumerate((place, jnp.bitwise_xor(place, neighbours[my]))):
        for core in range(2):
            copies.append(
                pltpu.make_async_copy(
                    sources[my].at[:, 2 * there + core],
                    bases[chip].at[:, core * rows : (core + 1) * rows],
                    sem.at[2 * chip + core],
                )
            )
    return copies


def load_kernel(
    tgt_energy_hbm,
    proj_energy_hbm,
    tgt_own_hbm,
    proj_own_hbm,
    energy,
    amp_ref,
    flat_energy,
    tgt_own,
    proj_own,
    sems,
):
    pairs = [
        (tgt_own_hbm, tgt_own),
        (proj_own_hbm, proj_own),
        (tgt_energy_hbm, flat_energy),
        (proj_energy_hbm, energy.at[1]),
    ]
    copies = [pltpu.make_async_copy(src, dst, sems.at[k]) for k, (src, dst) in enumerate(pairs)]
    for copy in copies:
        copy.start()
    for copy in copies:
        copy.wait()
    energy[0] = flat_energy[...][None, :]
    amp_ref[0] = tgt_own[...].T
    amp_ref[1] = proj_own[0].T


def pack_kernel(
    amp_ref,
    energy,
    tgt_other,
    proj_other,
    tgt_energy_other,
    proj_energy_other,
    chip_amp,
    energies,
    message,
):
    core = lax.axis_index("rep")
    my = my_kind()
    cols = chip_amp.shape[1]
    other_amp, _ = ordered(my, tgt_other[...].T, proj_other[0].T)
    other_energy, _ = ordered(my, tgt_energy_other[...][None, :], proj_energy_other[...])
    amps = ordered(core, amp_ref[my], other_amp)
    rows = ordered(core, energy[my], other_energy)
    for segment in range(2):
        chip_amp[segment] = amps[segment]
        energies[segment] = rows[segment]
        message[segment, :cols] = bf16(amps[segment])
        message[segment, cols:] = split(rows[segment])


def sent_kernel(
    neighbours, weight_hbm, tgt_hbm, proj_hbm, chip_amp, sent_chip, sent_far, sent_own, weight, flat_weight, sems
):
    my = my_kind()
    sources = (tgt_hbm, proj_hbm)
    rows = chip_amp.shape[2]

    def copies_of(kind):
        own = pltpu.make_async_copy(
            sources[kind].at[:, 2 * lax.axis_index(("prj", "tgt")[kind]) + 1 - lax.axis_index("rep")],
            sent_own,
            sems.at[4],
        )
        return basis_copies((sent_chip, sent_far), sems, 1 - kind, neighbours, sources) + [own]

    weight_copy = pltpu.make_async_copy(weight_hbm, flat_weight, sems.at[5])
    weight_copy.start()
    for kind in range(2):

        @pl.when(my == kind)
        def _():
            for copy in copies_of(kind):
                copy.start()

    weight_copy.wait()
    weight[0] = flat_weight[...][None, :]
    for part in range(2):
        sent_chip[part, 2 * rows :] = split(weight[0])
    for copy in copies_of(0):
        copy.wait()


def side_kernel(
    gate_levels,
    neighbours,
    flags_hbm,
    counts_hbm,
    tgt_hbm,
    proj_hbm,
    chip_amp,
    mine_chip,
    mine_far,
    gate,
    flags,
    counts,
    sems,
):
    my = my_kind()
    tgt_index = lax.axis_index("tgt")
    prj_index = lax.axis_index("prj")
    sources = (tgt_hbm, proj_hbm)
    pairs = [(flags_hbm, flags), (counts_hbm, counts)]
    copies = [pltpu.make_async_copy(src, dst, sems.at[4 + k]) for k, (src, dst) in enumerate(pairs)]
    for copy in copies:
        copy.start()
    for kind in range(2):

        @pl.when(my == kind)
        def _():
            for copy in basis_copies((mine_chip, mine_far), sems, kind, neighbours, sources):
                copy.start()

    for copy in copies:
        copy.wait()
    tiles = 2
    width = gate.shape[-1] // tiles
    gate_level = jnp.where(my == 0, *gate_levels)
    for half in range(2):
        for tile in range(tiles):
            live = jnp.logical_and(
                flags[prj_index, tgt_index] > 0, tiles * half + tile < counts[prj_index, tgt_index]
            )
            value = jnp.where(live, 1.0, 0.0).astype(jnp.float32)
            for level in range(gate.shape[0]):
                here = jnp.where(level == gate_level, value, jnp.float32(1.0))
                gate[level, half, :, tile * width : (tile + 1) * width] = jnp.full(
                    (1, width), here, jnp.float32
                )
    for copy in basis_copies((mine_chip, mine_far), sems, 0, neighbours, sources):
        copy.wait()


def chip_kernel(mine_chip, theirs_chip, chip_amp, weight, part_ref, weights):
    mine, theirs = (mine_chip,), (theirs_chip,)
    rows = chip_amp.shape[2]

    def body(core):
        for half, basis in enumerate((mine, theirs) if core == 0 else (theirs, mine)):
            part_ref[half] = sum(
                project(rows_of(basis, segment, rows), chip_amp[segment]) for segment in range(2)
            )
        weights[core] = weight[0]
        weights[1 - core] = joined(theirs_chip[0, 2 * rows :, :])

    by_core(body)


def first_kernel(mine_far, theirs_far, gate, weights, part_ref, message, *outs):
    mine, theirs = (None, mine_far), (None, theirs_far)
    rows = message.shape[2]
    cols = part_ref.shape[1]

    def body(core):
        for half, basis in enumerate((mine, theirs) if core == 0 else (theirs, mine)):
            total = part_ref[half] + sum(
                project(rows_of(basis, 2 + segment, rows), f32(message[segment, :cols]))
                for segment in range(2)
            )
            outs[half][...] = bf16(gate[0, half] * (weights[half] * total))

    by_core(body)


def add_kernel(level, half, gate, own, other, out_ref):
    out_ref[...] = bf16(gate[level, half] * (f32(own[...]) + f32(other[...])))


def low_kernel(
    mine_chip,
    mine_far,
    theirs_chip,
    theirs_far,
    low,
    low_there,
    chip_amp,
    energies,
    message,
    states_ref,
):
    mine, theirs = (mine_chip, mine_far), (theirs_chip, theirs_far)
    _, cols, rows = chip_amp.shape
    field = bf16(f32(low[...]) + f32(low_there[...]))

    def body(core):
        for segment in range(4):
            if segment < 2:
                amp, energy = chip_amp[segment], energies[segment]
            else:
                amp, energy = f32(message[segment - 2, :cols]), joined(message[segment - 2, cols:])
            change = expand(rows_of((mine, theirs)[core], segment, rows), field)
            states_ref[segment] = amp + half_step * (energy * turned(amp) + change)

    by_core(body)


def second_kernel(
    mine_chip,
    mine_far,
    theirs_chip,
    theirs_far,
    states_ref,
    high,
    high_there,
    gate,
    weights,
    low_ref,
    high_ref,
    half_ref,
    send_ref,
):
    mine, theirs = (mine_chip, mine_far), (theirs_chip, theirs_far)
    rows = states_ref.shape[2]
    field = bf16(f32(high[...]) + f32(high_there[...]))

    def body(core):
        bases = (mine, theirs) if core == 0 else (theirs, mine)
        halves = [
            states_ref[segment] + half_step * expand(rows_of(bases[1], segment, rows), field)
            for segment in range(4)
        ]
        half_ref[...] = halves[core]
        send_ref[...] = halves[1 - core]
        for half, out_ref in enumerate((low_ref, high_ref)):
            total = sum(
                project(rows_of(bases[half], segment, rows), halves[segment]) for segment in range(4)
            )
            out_ref[...] = bf16(gate[0, half] * (weights[half] * total))

    by_core(body)


def late_kernel(theirs_own, sent_chip, low, high, energy, amp_ref, my_half, other_half, my_part, other_new):
    rows = amp_ref.shape[2]

    def body(core):
        my = my_kind()
        near, far = (low, high) if core == 0 else (high, low)
        change = expand(rows_of((sent_chip,), core, rows), near[...]) + expand(
            rows_of((theirs_own,), 0, rows), far[...]
        )
        rate = energy[1 - my] * turned(other_half[...]) + change
        other_new[...] = (amp_ref[1 - my] + time_step * rate).T
        my_part[...] = amp_ref[my] + time_step * (energy[my] * turned(my_half[...]))

    by_core(body)


def last_kernel(mine_chip, theirs_chip, low, high, my_part, other_new, new_tgt, new_proj):
    rows = my_part.shape[1]

    def body(core):
        near, far = (low, high) if core == 0 else (high, low)
        change = expand(rows_of((mine_chip,), core, rows), near[...]) + expand(
            rows_of((theirs_chip,), core, rows), far[...]
        )
        my_new = (my_part[...] + time_step * change).T
        new_tgt[...], new_proj[0] = ordered(my_kind(), my_new, other_new[...])

    by_core(body)


def shards(
    tgt_basis,
    proj_basis,
    quad_weight,
    tgt_energy,
    proj_energy,
    pair_flags,
    tile_counts,
    tgt_amp,
    proj_amp,
):
    points = quad_weight.shape[0]
    rows, two_cols = tgt_amp.shape
    sizes = [lax.axis_size(axis) for axis in DEVICES]

    def call(kernel, out_shape, in_specs, scratch_shapes=(), cost=None):
        return pl.pallas_call(
            kernel,
            out_shape=out_shape,
            in_specs=in_specs,
            out_specs=[VMEM] * len(out_shape),
            scratch_shapes=scratch_shapes,
            cost_estimate=cost,
            compiler_params=pltpu.CompilerParams(vmem_limit_bytes=VMEM_LIMIT),
        )

    def run(kernel, out_shape, *blocks):
        return call(kernel, out_shape, [VMEM] * len(blocks))(*blocks)

    def other_core(block):
        return lax.ppermute(block, "rep", [(0, 1), (1, 0)])

    n_tgt, n_prj, n_core = sizes
    tgt_flips = [n_prj << bit for bit in range(n_tgt.bit_length() - 1)]
    prj_flips = [1 << bit for bit in range(n_prj.bit_length() - 1)]
    far_first, near_first = tgt_flips[::-1], tgt_flips
    flips = [(prj_flips + order, far_first + prj_flips) for order in (far_first, near_first)]
    neighbours = (prj_flips[0], far_first[0] // n_prj)
    gate_levels = (len(prj_flips) - 1, len(tgt_flips) - 1)
    n_steps = len(tgt_flips) + len(prj_flips)

    def exchanged(step, block, order=0, crossed=0):
        pairs = []
        for place in range(n_tgt * n_prj):
            for kind in range(2):
                there = place ^ flips[order][kind][step]
                to_core = kind ^ crossed ^ parity(there)
                pairs.append((place * n_core + (kind ^ parity(place)), there * n_core + to_core))
        return lax.ppermute(block, DEVICES, pairs)

    in_vmem = pltpu.VMEM
    sums = in_vmem((two_cols, points), jnp.bfloat16)
    segment = in_vmem((two_cols, rows), jnp.float32)

    def summed(halves, until, orders):
        totals = []
        for half, block in enumerate(halves):
            for step in range(1, until):
                other = exchanged(step, block, orders[half])
                (block,) = run(functools.partial(add_kernel, step, half), [sums], gate, block, other)
            totals.append(block)
        return totals

    def swapped(fields):
        return [other_core(block) for block in fields]

    def in_hbm(*blocks):
        return [pltpu.with_memory_space_constraint(block, pltpu.HBM) for block in blocks]

    others = swapped([tgt_amp, proj_amp, tgt_energy, proj_energy])
    energy, amp = call(
        load_kernel,
        [in_vmem((2, 1, rows), jnp.float32), in_vmem((2, two_cols, rows), jnp.float32)],
        [HBM] * 4,
        [
            pltpu.VMEM((rows,), jnp.float32),
            pltpu.VMEM(tgt_amp.shape, jnp.float32),
            pltpu.VMEM(proj_amp.shape, jnp.float32),
            pltpu.SemaphoreType.DMA((4,)),
        ],
        pl.CostEstimate(
            flops=2 * 4 * rows * two_cols * points, bytes_accessed=4 * 1024 * 1024, transcendentals=0
        ),
    )(*in_hbm(tgt_energy, proj_energy, tgt_amp, proj_amp))
    chip_amp, energies, message = run(
        pack_kernel,
        [
            in_vmem((2, two_cols, rows), jnp.float32),
            in_vmem((2, 1, rows), jnp.float32),
            in_vmem((2, two_cols + PIECES, rows), jnp.bfloat16),
        ],
        amp,
        energy,
        *others,
    )
    message = exchanged(0, message)
    flags, counts = pair_flags.T, tile_counts.T
    bases = in_hbm(tgt_basis.reshape(2, -1, rows, points), proj_basis)
    pair = in_vmem((2, 2 * rows, points), jnp.bfloat16)
    *sent, weight = call(
        functools.partial(sent_kernel, neighbours),
        [
            in_vmem((2, 2 * rows + PIECES, points), jnp.bfloat16),
            pair,
            in_vmem((2, rows, points), jnp.bfloat16),
            in_vmem((1, 1, points), jnp.float32),
        ],
        [HBM] * 3 + [VMEM],
        [pltpu.VMEM((points,), jnp.float32), pltpu.SemaphoreType.DMA((6,))],
    )(*in_hbm(quad_weight), *bases, chip_amp)
    mine_chip, mine_far, gate = call(
        functools.partial(side_kernel, gate_levels, neighbours),
        [
            pair,
            pair,
            in_vmem((n_steps, 2, 1, points), jnp.float32),
        ],
        [HBM] * 4 + [VMEM],
        [
            pltpu.SMEM(flags.shape, jnp.int32),
            pltpu.SMEM(counts.shape, jnp.int32),
            pltpu.SemaphoreType.DMA((6,)),
        ],
        BEHIND,
    )(*in_hbm(flags, counts), *bases, chip_amp)
    theirs_chip, theirs_far, theirs_own = swapped(sent)
    bases = (mine_chip, mine_far, theirs_chip, theirs_far)
    part, weights = run(
        chip_kernel,
        [in_vmem((2, two_cols, points), jnp.float32), in_vmem((2, 1, points), jnp.float32)],
        mine_chip,
        theirs_chip,
        chip_amp,
        weight,
    )
    halves = run(first_kernel, [sums] * 2, mine_far, theirs_far, gate, weights, part, message)
    parts = summed(halves, n_steps - 1, (0, 0))
    low, high = [(other_core(block), exchanged(n_steps - 1, block, crossed=1)) for block in parts]
    (states,) = run(
        low_kernel,
        [in_vmem((4, two_cols, rows), jnp.float32)],
        *bases,
        *low,
        chip_amp,
        energies,
        message,
    )
    *halves, my_half, half_send = run(
        second_kernel,
        [sums, sums, segment, segment],
        *bases,
        states,
        *high,
        gate,
        weights,
    )
    other_half = other_core(half_send)
    fields = summed(halves, n_steps, (0, 1))
    low, high = swapped(fields)
    my_part, other_new = run(
        late_kernel,
        [segment, in_vmem((rows, two_cols), jnp.float32)],
        theirs_own,
        sent[0],
        *fields,
        energy,
        amp,
        my_half,
        other_half,
    )
    return run(
        last_kernel,
        [
            jax.ShapeDtypeStruct(tgt_amp.shape, jnp.float32),
            jax.ShapeDtypeStruct(proj_amp.shape, jnp.float32),
        ],
        mine_chip,
        theirs_chip,
        low,
        high,
        my_part,
        other_new,
    )


def solution(mesh):
    in_specs = (
        P(None, "tgt", "rep"),
        P(None, None, "prj", "rep"),
        P(("bpar", "rep")),
        P(("tgt", "prj", "rep")),
        P(("tgt", "rep"), "prj"),
        P("bpar", None),
        P("bpar", None),
        P(("bpar", "tgt", "prj", "rep"), None),
        P(("bpar", "tgt", "rep"), "prj", None),
    )
    out_specs = (P(("bpar", "tgt", "prj", "rep"), None), P(("bpar", "tgt", "rep"), "prj", None))

    def step(*args):
        return tuple(shards(*args))

    return jax.shard_map(step, mesh=mesh, in_specs=in_specs, out_specs=out_specs, check_vma=False)
```

```python
import functools

import jax
import jax.numpy as jnp
from jax import lax
from jax.experimental import pallas as pl
from jax.experimental.pallas import tpu as pltpu
from jax.sharding import PartitionSpec as P

time_step = 0.4
half_step = 0.5 * time_step
VMEM_LIMIT = 8 * 1024 * 1024
DEVICES = ("tgt", "prj", "rep")
HBM = pl.BlockSpec(memory_space=pl.ANY)
VMEM = pl.BlockSpec(memory_space=pltpu.VMEM)


def parity(place):
    odd = 0
    while place:
        odd, place = odd ^ (place & 1), place >> 1
    return odd


def my_kind():
    n_tgt, n_prj = lax.axis_size("tgt"), lax.axis_size("prj")
    place = lax.axis_index("tgt") * n_prj + lax.axis_index("prj")
    kind = lax.axis_index("rep")
    for bit in range((n_tgt * n_prj).bit_length() - 1):
        kind = jnp.bitwise_xor(kind, jnp.bitwise_and(lax.shift_right_logical(place, bit), 1))
    return kind


def by_core(body):
    for core in range(2):

        @pl.when(lax.axis_index("rep") == core)
        def _():
            body(core)


def ordered(core, first, second):
    return jnp.where(core == 0, first, second), jnp.where(core == 0, second, first)


def turned(block):
    half = block.shape[0] // 2
    return jnp.concatenate([block[half:], -block[:half]], axis=0)


def bf16(block):
    return block.astype(jnp.bfloat16)


def f32(block):
    return block.astype(jnp.float32)


def rows_of(bases, segment, amount):
    start = segment % 2 * amount
    return [bases[segment // 2][part, start : start + amount, :] for part in range(2)]


def project(basis, amp):
    return jnp.dot(bf16(amp), basis[0], preferred_element_type=jnp.float32) + jnp.dot(
        bf16(turned(amp)), basis[1], preferred_element_type=jnp.float32
    )


def expand(basis, field):
    contract = (((1,), (1,)), ((), ()))
    return lax.dot_general(
        turned(field), basis[0], contract, preferred_element_type=jnp.float32
    ) + lax.dot_general(field, basis[1], contract, preferred_element_type=jnp.float32)


PIECES = 16

BEHIND = pl.CostEstimate(flops=1 << 35, bytes_accessed=1 << 16, transcendentals=0)
EVEN = pl.CostEstimate(flops=1 << 30, bytes_accessed=1 << 16, transcendentals=0)


def split(row):
    index = lax.broadcasted_iota(jnp.int32, (PIECES, row.shape[1]), 0)
    block = jnp.zeros(index.shape, jnp.float32)
    for piece in range(3):
        rounded = f32(bf16(row))
        block = jnp.where(index == piece, rounded, block)
        row = row - rounded
    return bf16(block)


def joined(block):
    pieces = f32(block)
    return pieces[0:1] + pieces[1:2] + pieces[2:3]


def basis_copies(bases, sem, my, neighbours, sources):
    rows = sources[my].shape[2]
    place = lax.axis_index(("prj", "tgt")[my])
    copies = []
    for chip, there in enumerate((place, jnp.bitwise_xor(place, neighbours[my]))):
        for core in range(2):
            copies.append(
                pltpu.make_async_copy(
                    sources[my].at[:, 2 * there + core],
                    bases[chip].at[:, core * rows : (core + 1) * rows],
                    sem.at[2 * chip + core],
                )
            )
    return copies


def load_kernel(
    tgt_energy_hbm,
    proj_energy_hbm,
    tgt_own_hbm,
    proj_own_hbm,
    energy,
    amp_ref,
    flat_energy,
    tgt_own,
    proj_own,
    sems,
):
    pairs = [
        (tgt_own_hbm, tgt_own),
        (proj_own_hbm, proj_own),
        (tgt_energy_hbm, flat_energy),
        (proj_energy_hbm, energy.at[1]),
    ]
    copies = [pltpu.make_async_copy(src, dst, sems.at[k]) for k, (src, dst) in enumerate(pairs)]
    for copy in copies:
        copy.start()
    for copy in copies:
        copy.wait()
    energy[0] = flat_energy[...][None, :]
    amp_ref[0] = tgt_own[...].T
    amp_ref[1] = proj_own[0].T


def pack_kernel(
    amp_ref,
    energy,
    tgt_other,
    proj_other,
    tgt_energy_other,
    proj_energy_other,
    chip_amp,
    energies,
    message,
):
    core = lax.axis_index("rep")
    my = my_kind()
    cols = chip_amp.shape[1]
    other_amp, _ = ordered(my, tgt_other[...].T, proj_other[0].T)
    other_energy, _ = ordered(my, tgt_energy_other[...][None, :], proj_energy_other[...])
    amps = ordered(core, amp_ref[my], other_amp)
    rows = ordered(core, energy[my], other_energy)
    for segment in range(2):
        chip_amp[segment] = amps[segment]
        energies[segment] = rows[segment]
        message[segment, :cols] = bf16(amps[segment])
        message[segment, cols:] = split(rows[segment])


def sent_kernel(
    neighbours, weight_hbm, tgt_hbm, proj_hbm, chip_amp, sent_chip, sent_far, sent_own, weight, flat_weight, sems
):
    my = my_kind()
    sources = (tgt_hbm, proj_hbm)
    rows = chip_amp.shape[2]

    def copies_of(kind):
        own = pltpu.make_async_copy(
            sources[kind].at[:, 2 * lax.axis_index(("prj", "tgt")[kind]) + 1 - lax.axis_index("rep")],
            sent_own,
            sems.at[4],
        )
        return basis_copies((sent_chip, sent_far), sems, 1 - kind, neighbours, sources) + [own]

    weight_copy = pltpu.make_async_copy(weight_hbm, flat_weight, sems.at[5])
    weight_copy.start()
    for kind in range(2):

        @pl.when(my == kind)
        def _():
            for copy in copies_of(kind):
                copy.start()

    weight_copy.wait()
    weight[0] = flat_weight[...][None, :]
    for part in range(2):
        sent_chip[part, 2 * rows :] = split(weight[0])
    for copy in copies_of(0):
        copy.wait()


def side_kernel(
    gate_levels,
    neighbours,
    flags_hbm,
    counts_hbm,
    tgt_hbm,
    proj_hbm,
    chip_amp,
    mine_chip,
    mine_far,
    gate,
    flags,
    counts,
    sems,
):
    my = my_kind()
    tgt_index = lax.axis_index("tgt")
    prj_index = lax.axis_index("prj")
    sources = (tgt_hbm, proj_hbm)
    pairs = [(flags_hbm, flags), (counts_hbm, counts)]
    copies = [pltpu.make_async_copy(src, dst, sems.at[4 + k]) for k, (src, dst) in enumerate(pairs)]
    for copy in copies:
        copy.start()
    for kind in range(2):

        @pl.when(my == kind)
        def _():
            for copy in basis_copies((mine_chip, mine_far), sems, kind, neighbours, sources):
                copy.start()

    for copy in copies:
        copy.wait()
    tiles = 4
    width = gate.shape[-1] // tiles
    gate_level = jnp.where(my == 0, *gate_levels)
    for tile in range(tiles):
        live = jnp.logical_and(flags[prj_index, tgt_index] > 0, tile < counts[prj_index, tgt_index])
        value = jnp.where(live, 1.0, 0.0).astype(jnp.float32)
        for level in range(gate.shape[0]):
            here = jnp.where(level == gate_level, value, jnp.float32(1.0))
            gate[level, :, tile * width : (tile + 1) * width] = jnp.full((1, width), here, jnp.float32)
    for copy in basis_copies((mine_chip, mine_far), sems, 0, neighbours, sources):
        copy.wait()


def chip_kernel(mine_chip, theirs_chip, chip_amp, weight, part_ref, weights):
    mine, theirs = (mine_chip,), (theirs_chip,)
    rows = chip_amp.shape[2]

    def body(core):
        for half, basis in enumerate((mine, theirs) if core == 0 else (theirs, mine)):
            part_ref[half] = sum(
                project(rows_of(basis, segment, rows), chip_amp[segment]) for segment in range(2)
            )
        weights[core] = weight[0]
        weights[1 - core] = joined(theirs_chip[0, 2 * rows :, :])

    by_core(body)


def store(sums, gate, weights, long_ref, short_ref):
    points = weights.shape[-1]
    first, second = [
        bf16(gate[0, :, half * points : (half + 1) * points] * (weights[half] * total))
        for half, total in enumerate(sums)
    ]
    extra = long_ref.shape[1] - points
    long_ref[:, :points] = first
    long_ref[:, points:] = second[:, :extra]
    short_ref[...] = second[:, extra:]


def halves_of(long, short):
    points = (long.shape[1] + short.shape[1]) // 2
    return long[:, :points], jnp.concatenate([long[:, points:], short], axis=1)


def first_kernel(mine_far, theirs_far, gate, weights, part_ref, message, long_ref, short_ref):
    mine, theirs = (None, mine_far), (None, theirs_far)
    rows = message.shape[2]
    cols = part_ref.shape[1]

    def body(core):
        sums = [
            part_ref[half]
            + sum(
                project(rows_of(basis, 2 + segment, rows), f32(message[segment, :cols]))
                for segment in range(2)
            )
            for half, basis in enumerate((mine, theirs) if core == 0 else (theirs, mine))
        ]
        store(sums, gate, weights, long_ref, short_ref)

    by_core(body)


def add_kernel(level, first_point, gate, own, other, out_ref):
    points = slice(first_point, first_point + out_ref.shape[1])
    out_ref[...] = bf16(gate[level, :, points] * (f32(own[...]) + f32(other[...])))


def early_kernel(
    mine_chip,
    mine_far,
    theirs_chip,
    theirs_far,
    field,
    field_there,
    chip_amp,
    energies,
    message,
    states_ref,
):
    mine, theirs = (mine_chip, mine_far), (theirs_chip, theirs_far)
    _, cols, rows = chip_amp.shape
    points = mine_chip.shape[2]
    low = bf16(f32(field[:, :points]) + f32(field_there[:, :points]))

    def body(core):
        for segment in range(4):
            if segment < 2:
                amp, energy = chip_amp[segment], energies[segment]
            else:
                amp, energy = f32(message[segment - 2, :cols]), joined(message[segment - 2, cols:])
            change = expand(rows_of((mine, theirs)[core], segment, rows), low)
            states_ref[segment] = amp + half_step * (energy * turned(amp) + change)

    by_core(body)


def second_kernel(
    mine_chip,
    mine_far,
    theirs_chip,
    theirs_far,
    states_ref,
    field,
    field_there,
    short,
    short_there,
    gate,
    weights,
    long_ref,
    short_ref,
    half_ref,
    send_ref,
):
    mine, theirs = (mine_chip, mine_far), (theirs_chip, theirs_far)
    rows = states_ref.shape[2]
    points = mine_chip.shape[2]
    high = bf16(
        jnp.concatenate(
            [f32(field[:, points:]) + f32(field_there[:, points:]), f32(short[...]) + f32(short_there[...])],
            axis=1,
        )
    )

    def body(core):
        bases = (mine, theirs) if core == 0 else (theirs, mine)
        halves = [
            states_ref[segment] + half_step * expand(rows_of(bases[1], segment, rows), high)
            for segment in range(4)
        ]
        half_ref[...] = halves[core]
        send_ref[...] = halves[1 - core]
        sums = [
            sum(project(rows_of(basis, segment, rows), halves[segment]) for segment in range(4))
            for basis in bases
        ]
        store(sums, gate, weights, long_ref, short_ref)

    by_core(body)


def late_kernel(theirs_own, sent_chip, long, short, energy, amp_ref, my_half, other_half, my_part, other_new):
    rows = amp_ref.shape[2]

    def body(core):
        my = my_kind()
        low, high = halves_of(long[...], short[...])
        near, far = (low, high) if core == 0 else (high, low)
        change = expand(rows_of((sent_chip,), core, rows), near) + expand(
            rows_of((theirs_own,), 0, rows), far
        )
        rate = energy[1 - my] * turned(other_half[...]) + change
        other_new[...] = (amp_ref[1 - my] + time_step * rate).T
        my_part[...] = amp_ref[my] + time_step * (energy[my] * turned(my_half[...]))

    by_core(body)


def last_kernel(mine_chip, theirs_chip, long, short, my_part, other_new, new_tgt, new_proj):
    rows = my_part.shape[1]

    def body(core):
        low, high = halves_of(long[...], short[...])
        near, far = (low, high) if core == 0 else (high, low)
        change = expand(rows_of((mine_chip,), core, rows), near) + expand(
            rows_of((theirs_chip,), core, rows), far
        )
        my_new = (my_part[...] + time_step * change).T
        new_tgt[...], new_proj[0] = ordered(my_kind(), my_new, other_new[...])

    by_core(body)


def shards(
    tgt_basis,
    proj_basis,
    quad_weight,
    tgt_energy,
    proj_energy,
    pair_flags,
    tile_counts,
    tgt_amp,
    proj_amp,
):
    points = quad_weight.shape[0]
    rows, two_cols = tgt_amp.shape
    sizes = [lax.axis_size(axis) for axis in DEVICES]

    def call(kernel, out_shape, in_specs, scratch_shapes=(), cost=None):
        return pl.pallas_call(
            kernel,
            out_shape=out_shape,
            in_specs=in_specs,
            out_specs=[VMEM] * len(out_shape),
            scratch_shapes=scratch_shapes,
            cost_estimate=cost,
            compiler_params=pltpu.CompilerParams(vmem_limit_bytes=VMEM_LIMIT),
        )

    def run(kernel, out_shape, *blocks):
        return call(kernel, out_shape, [VMEM] * len(blocks))(*blocks)

    def other_core(block):
        return lax.ppermute(block, "rep", [(0, 1), (1, 0)])

    n_tgt, n_prj, n_core = sizes
    tgt_flips = [n_prj << bit for bit in range(n_tgt.bit_length() - 1)]
    prj_flips = [1 << bit for bit in range(n_prj.bit_length() - 1)]
    far_first = tgt_flips[::-1]
    flips = (prj_flips + far_first, far_first + prj_flips)
    neighbours = (prj_flips[0], far_first[0] // n_prj)
    gate_levels = (len(prj_flips) - 1, len(tgt_flips) - 1)
    n_steps = len(tgt_flips) + len(prj_flips)

    def exchanged(step, block, crossed=0):
        pairs = []
        for place in range(n_tgt * n_prj):
            for kind in range(2):
                there = place ^ flips[kind][step]
                to_core = kind ^ crossed ^ parity(there)
                pairs.append((place * n_core + (kind ^ parity(place)), there * n_core + to_core))
        return lax.ppermute(block, DEVICES, pairs)

    in_vmem = pltpu.VMEM
    blocks = [in_vmem((two_cols, size), jnp.bfloat16) for size in (3 * points // 2, points // 2)]
    segment = in_vmem((two_cols, rows), jnp.float32)

    def summed(blocks, until):
        totals = []
        first_point = 0
        for block in blocks:
            for step in range(1, until):
                other = exchanged(step, block)
                kernel = functools.partial(add_kernel, step, first_point)
                shape = in_vmem(block.shape, block.dtype)
                cost = EVEN if first_point else None
                (block,) = call(kernel, [shape], [VMEM] * 3, cost=cost)(gate, block, other)
            totals.append(block)
            first_point += block.shape[1]
        return totals

    def swapped(fields):
        return [other_core(block) for block in fields]

    def in_hbm(*blocks):
        return [pltpu.with_memory_space_constraint(block, pltpu.HBM) for block in blocks]

    others = swapped([tgt_amp, proj_amp, tgt_energy, proj_energy])
    energy, amp = call(
        load_kernel,
        [in_vmem((2, 1, rows), jnp.float32), in_vmem((2, two_cols, rows), jnp.float32)],
        [HBM] * 4,
        [
            pltpu.VMEM((rows,), jnp.float32),
            pltpu.VMEM(tgt_amp.shape, jnp.float32),
            pltpu.VMEM(proj_amp.shape, jnp.float32),
            pltpu.SemaphoreType.DMA((4,)),
        ],
        pl.CostEstimate(
            flops=2 * 4 * rows * two_cols * points, bytes_accessed=4 * 1024 * 1024, transcendentals=0
        ),
    )(*in_hbm(tgt_energy, proj_energy, tgt_amp, proj_amp))
    chip_amp, energies, message = run(
        pack_kernel,
        [
            in_vmem((2, two_cols, rows), jnp.float32),
            in_vmem((2, 1, rows), jnp.float32),
            in_vmem((2, two_cols + PIECES, rows), jnp.bfloat16),
        ],
        amp,
        energy,
        *others,
    )
    message = exchanged(0, message)
    flags, counts = pair_flags.T, tile_counts.T
    bases = in_hbm(tgt_basis.reshape(2, -1, rows, points), proj_basis)
    pair = in_vmem((2, 2 * rows, points), jnp.bfloat16)
    *sent, weight = call(
        functools.partial(sent_kernel, neighbours),
        [
            in_vmem((2, 2 * rows + PIECES, points), jnp.bfloat16),
            pair,
            in_vmem((2, rows, points), jnp.bfloat16),
            in_vmem((1, 1, points), jnp.float32),
        ],
        [HBM] * 3 + [VMEM],
        [pltpu.VMEM((points,), jnp.float32), pltpu.SemaphoreType.DMA((6,))],
    )(*in_hbm(quad_weight), *bases, chip_amp)
    mine_chip, mine_far, gate = call(
        functools.partial(side_kernel, gate_levels, neighbours),
        [
            pair,
            pair,
            in_vmem((n_steps, 1, 2 * points), jnp.float32),
        ],
        [HBM] * 4 + [VMEM],
        [
            pltpu.SMEM(flags.shape, jnp.int32),
            pltpu.SMEM(counts.shape, jnp.int32),
            pltpu.SemaphoreType.DMA((6,)),
        ],
        BEHIND,
    )(*in_hbm(flags, counts), *bases, chip_amp)
    theirs_chip, theirs_far, theirs_own = swapped(sent)
    bases = (mine_chip, mine_far, theirs_chip, theirs_far)
    part, weights = run(
        chip_kernel,
        [in_vmem((2, two_cols, points), jnp.float32), in_vmem((2, 1, points), jnp.float32)],
        mine_chip,
        theirs_chip,
        chip_amp,
        weight,
    )
    sums = run(first_kernel, blocks, mine_far, theirs_far, gate, weights, part, message)
    parts = summed(sums, n_steps - 1)
    long, short = [(other_core(block), exchanged(n_steps - 1, block, crossed=1)) for block in parts]
    (states,) = run(
        early_kernel,
        [in_vmem((4, two_cols, rows), jnp.float32)],
        *bases,
        *long,
        chip_amp,
        energies,
        message,
    )
    *sums, my_half, half_send = run(
        second_kernel,
        blocks + [segment, segment],
        *bases,
        states,
        *long,
        *short,
        gate,
        weights,
    )
    other_half = other_core(half_send)
    fields = summed(sums, n_steps)
    my_part, other_new = run(
        late_kernel,
        [segment, in_vmem((rows, two_cols), jnp.float32)],
        theirs_own,
        sent[0],
        *fields,
        energy,
        amp,
        my_half,
        other_half,
    )
    return run(
        last_kernel,
        [
            jax.ShapeDtypeStruct(tgt_amp.shape, jnp.float32),
            jax.ShapeDtypeStruct(proj_amp.shape, jnp.float32),
        ],
        mine_chip,
        theirs_chip,
        *swapped(fields),
        my_part,
        other_new,
    )


def solution(mesh):
    in_specs = (
        P(None, "tgt", "rep"),
        P(None, None, "prj", "rep"),
        P(("bpar", "rep")),
        P(("tgt", "prj", "rep")),
        P(("tgt", "rep"), "prj"),
        P("bpar", None),
        P("bpar", None),
        P(("bpar", "tgt", "prj", "rep"), None),
        P(("bpar", "tgt", "rep"), "prj", None),
    )
    out_specs = (P(("bpar", "tgt", "prj", "rep"), None), P(("bpar", "tgt", "rep"), "prj", None))

    def step(*args):
        return tuple(shards(*args))

    return jax.shard_map(step, mesh=mesh, in_specs=in_specs, out_specs=out_specs, check_vma=False)
```

```python
import functools

import jax
import jax.numpy as jnp
from jax import lax
from jax.experimental import pallas as pl
from jax.experimental.pallas import tpu as pltpu
from jax.sharding import PartitionSpec as P

time_step = 0.4
half_step = 0.5 * time_step
VMEM_LIMIT = 8 * 1024 * 1024
DEVICES = ("tgt", "prj", "rep")
HBM = pl.BlockSpec(memory_space=pl.ANY)
VMEM = pl.BlockSpec(memory_space=pltpu.VMEM)


def parity(place):
    odd = 0
    while place:
        odd, place = odd ^ (place & 1), place >> 1
    return odd


def my_kind():
    n_tgt, n_prj = lax.axis_size("tgt"), lax.axis_size("prj")
    place = lax.axis_index("tgt") * n_prj + lax.axis_index("prj")
    kind = lax.axis_index("rep")
    for bit in range((n_tgt * n_prj).bit_length() - 1):
        kind = jnp.bitwise_xor(kind, jnp.bitwise_and(lax.shift_right_logical(place, bit), 1))
    return kind


def by_core(body):
    for core in range(2):

        @pl.when(lax.axis_index("rep") == core)
        def _():
            body(core)


def ordered(core, first, second):
    return jnp.where(core == 0, first, second), jnp.where(core == 0, second, first)


def turned(block):
    half = block.shape[0] // 2
    return jnp.concatenate([block[half:], -block[:half]], axis=0)


def bf16(block):
    return block.astype(jnp.bfloat16)


def f32(block):
    return block.astype(jnp.float32)


def rows_of(bases, segment, amount):
    start = segment % 2 * amount
    return [bases[segment // 2][part, start : start + amount, :] for part in range(2)]


def project(basis, amp):
    return jnp.dot(bf16(amp), basis[0], preferred_element_type=jnp.float32) + jnp.dot(
        bf16(turned(amp)), basis[1], preferred_element_type=jnp.float32
    )


def expand(basis, field):
    contract = (((1,), (1,)), ((), ()))
    return lax.dot_general(
        turned(field), basis[0], contract, preferred_element_type=jnp.float32
    ) + lax.dot_general(field, basis[1], contract, preferred_element_type=jnp.float32)


PIECES = 16

BEHIND = pl.CostEstimate(flops=1 << 35, bytes_accessed=1 << 16, transcendentals=0)


def split(row):
    index = lax.broadcasted_iota(jnp.int32, (PIECES, row.shape[1]), 0)
    block = jnp.zeros(index.shape, jnp.float32)
    for piece in range(3):
        rounded = f32(bf16(row))
        block = jnp.where(index == piece, rounded, block)
        row = row - rounded
    return bf16(block)


def joined(block):
    pieces = f32(block)
    return pieces[0:1] + pieces[1:2] + pieces[2:3]


def basis_copies(bases, sem, my, neighbours, sources):
    rows = sources[my].shape[2]
    place = lax.axis_index(("prj", "tgt")[my])
    copies = []
    for chip, there in enumerate((place, jnp.bitwise_xor(place, neighbours[my]))):
        for core in range(2):
            copies.append(
                pltpu.make_async_copy(
                    sources[my].at[:, 2 * there + core],
                    bases[chip].at[:, core * rows : (core + 1) * rows],
                    sem.at[2 * chip + core],
                )
            )
    return copies


def load_kernel(
    tgt_energy_hbm,
    proj_energy_hbm,
    tgt_own_hbm,
    proj_own_hbm,
    energy,
    amp_ref,
    flat_energy,
    tgt_own,
    proj_own,
    sems,
):
    pairs = [
        (tgt_own_hbm, tgt_own),
        (proj_own_hbm, proj_own),
        (tgt_energy_hbm, flat_energy),
        (proj_energy_hbm, energy.at[1]),
    ]
    copies = [pltpu.make_async_copy(src, dst, sems.at[k]) for k, (src, dst) in enumerate(pairs)]
    for copy in copies:
        copy.start()
    for copy in copies:
        copy.wait()
    energy[0] = flat_energy[...][None, :]
    amp_ref[0] = tgt_own[...].T
    amp_ref[1] = proj_own[0].T


def pack_kernel(amp_ref, tgt_other, proj_other, chip_amp, message):
    my = my_kind()
    other_amp, _ = ordered(my, tgt_other[...].T, proj_other[0].T)
    amps = ordered(lax.axis_index("rep"), amp_ref[my], other_amp)
    for segment in range(2):
        chip_amp[segment] = amps[segment]
        message[segment] = bf16(amps[segment])


def sent_kernel(
    neighbours,
    weight_hbm,
    tgt_hbm,
    proj_hbm,
    chip_amp,
    energy,
    sent_chip,
    sent_far,
    sent_own,
    weight,
    flat_weight,
    sems,
):
    my = my_kind()
    sources = (tgt_hbm, proj_hbm)
    rows = chip_amp.shape[2]

    def copies_of(kind):
        own = pltpu.make_async_copy(
            sources[kind].at[:, 2 * lax.axis_index(("prj", "tgt")[kind]) + 1 - lax.axis_index("rep")],
            sent_own,
            sems.at[4],
        )
        return basis_copies((sent_chip, sent_far), sems, 1 - kind, neighbours, sources) + [own]

    weight_copy = pltpu.make_async_copy(weight_hbm, flat_weight, sems.at[5])
    weight_copy.start()
    for kind in range(2):

        @pl.when(my == kind)
        def _():
            for copy in copies_of(kind):
                copy.start()

    weight_copy.wait()
    weight[0] = flat_weight[...][None, :]
    for part in range(2):
        sent_chip[part, 2 * rows : 2 * rows + PIECES] = split(weight[0])
        sent_chip[part, 2 * rows + PIECES :, :rows] = split(energy[1 - my])
    for copy in copies_of(0):
        copy.wait()


def side_kernel(
    gate_levels,
    neighbours,
    flags_hbm,
    counts_hbm,
    tgt_hbm,
    proj_hbm,
    chip_amp,
    mine_chip,
    mine_far,
    gate,
    flags,
    counts,
    sems,
):
    my = my_kind()
    tgt_index = lax.axis_index("tgt")
    prj_index = lax.axis_index("prj")
    sources = (tgt_hbm, proj_hbm)
    pairs = [(flags_hbm, flags), (counts_hbm, counts)]
    copies = [pltpu.make_async_copy(src, dst, sems.at[4 + k]) for k, (src, dst) in enumerate(pairs)]
    for copy in copies:
        copy.start()
    for kind in range(2):

        @pl.when(my == kind)
        def _():
            for copy in basis_copies((mine_chip, mine_far), sems, kind, neighbours, sources):
                copy.start()

    for copy in copies:
        copy.wait()
    tiles = 2
    width = gate.shape[-1] // tiles
    gate_level = jnp.where(my == 0, *gate_levels)
    for half in range(2):
        for tile in range(tiles):
            live = jnp.logical_and(
                flags[prj_index, tgt_index] > 0, tiles * half + tile < counts[prj_index, tgt_index]
            )
            value = jnp.where(live, 1.0, 0.0).astype(jnp.float32)
            for level in range(gate.shape[0]):
                here = jnp.where(level == gate_level, value, jnp.float32(1.0))
                gate[level, half, :, tile * width : (tile + 1) * width] = jnp.full(
                    (1, width), here, jnp.float32
                )
    for copy in basis_copies((mine_chip, mine_far), sems, 0, neighbours, sources):
        copy.wait()


def chip_kernel(mine_chip, theirs_chip, chip_amp, weight, energy, part_ref, weights, energies):
    mine, theirs = (mine_chip,), (theirs_chip,)
    rows = chip_amp.shape[2]

    def body(core):
        for half, basis in enumerate((mine, theirs) if core == 0 else (theirs, mine)):
            part_ref[half] = sum(
                project(rows_of(basis, segment, rows), chip_amp[segment]) for segment in range(2)
            )
        weights[core] = weight[0]
        weights[1 - core] = joined(theirs_chip[0, 2 * rows : 2 * rows + PIECES, :])
        energies[core] = energy[my_kind()]
        energies[1 - core] = joined(theirs_chip[0, 2 * rows + PIECES :, :rows])

    by_core(body)


def first_kernel(mine_far, theirs_far, gate, weights, part_ref, message, *outs):
    mine, theirs = (None, mine_far), (None, theirs_far)
    rows = message.shape[2]

    def body(core):
        for half, basis in enumerate((mine, theirs) if core == 0 else (theirs, mine)):
            total = part_ref[half] + sum(
                project(rows_of(basis, 2 + segment, rows), f32(message[segment]))
                for segment in range(2)
            )
            outs[half][...] = bf16(gate[0, half] * (weights[half] * total))

    by_core(body)


def add_kernel(level, half, gate, own, other, out_ref):
    out_ref[...] = bf16(gate[level, half] * (f32(own[...]) + f32(other[...])))


def low_kernel(
    mine_chip,
    mine_far,
    theirs_chip,
    theirs_far,
    low,
    low_there,
    chip_amp,
    energies,
    message,
    neighbour_energies,
    states_ref,
):
    mine, theirs = (mine_chip, mine_far), (theirs_chip, theirs_far)
    rows = chip_amp.shape[2]
    field = bf16(f32(low[...]) + f32(low_there[...]))

    def body(core):
        for segment in range(4):
            if segment < 2:
                amp, energy = chip_amp[segment], energies[segment]
            else:
                amp, energy = f32(message[segment - 2]), neighbour_energies[segment - 2]
            change = expand(rows_of((mine, theirs)[core], segment, rows), field)
            states_ref[segment] = amp + half_step * (energy * turned(amp) + change)

    by_core(body)


def second_kernel(
    mine_chip,
    mine_far,
    theirs_chip,
    theirs_far,
    states_ref,
    high,
    high_there,
    gate,
    weights,
    low_ref,
    high_ref,
    half_ref,
    send_ref,
):
    mine, theirs = (mine_chip, mine_far), (theirs_chip, theirs_far)
    rows = states_ref.shape[2]
    field = bf16(f32(high[...]) + f32(high_there[...]))

    def body(core):
        bases = (mine, theirs) if core == 0 else (theirs, mine)
        halves = [
            states_ref[segment] + half_step * expand(rows_of(bases[1], segment, rows), field)
            for segment in range(4)
        ]
        half_ref[...] = halves[core]
        send_ref[...] = halves[1 - core]
        for half, out_ref in enumerate((low_ref, high_ref)):
            total = sum(
                project(rows_of(bases[half], segment, rows), halves[segment]) for segment in range(4)
            )
            out_ref[...] = bf16(gate[0, half] * (weights[half] * total))

    by_core(body)


def late_kernel(theirs_own, sent_chip, low, high, energy, amp_ref, my_half, other_half, my_part, other_new):
    rows = amp_ref.shape[2]

    def body(core):
        my = my_kind()
        near, far = (low, high) if core == 0 else (high, low)
        change = expand(rows_of((sent_chip,), core, rows), near[...]) + expand(
            rows_of((theirs_own,), 0, rows), far[...]
        )
        rate = energy[1 - my] * turned(other_half[...]) + change
        other_new[...] = (amp_ref[1 - my] + time_step * rate).T
        my_part[...] = amp_ref[my] + time_step * (energy[my] * turned(my_half[...]))

    by_core(body)


def last_kernel(mine_chip, theirs_chip, low, high, my_part, other_new, new_tgt, new_proj):
    rows = my_part.shape[1]

    def body(core):
        near, far = (low, high) if core == 0 else (high, low)
        change = expand(rows_of((mine_chip,), core, rows), near[...]) + expand(
            rows_of((theirs_chip,), core, rows), far[...]
        )
        my_new = (my_part[...] + time_step * change).T
        new_tgt[...], new_proj[0] = ordered(my_kind(), my_new, other_new[...])

    by_core(body)


def shards(
    tgt_basis,
    proj_basis,
    quad_weight,
    tgt_energy,
    proj_energy,
    pair_flags,
    tile_counts,
    tgt_amp,
    proj_amp,
):
    points = quad_weight.shape[0]
    rows, two_cols = tgt_amp.shape
    sizes = [lax.axis_size(axis) for axis in DEVICES]

    def call(kernel, out_shape, in_specs, scratch_shapes=(), cost=None):
        return pl.pallas_call(
            kernel,
            out_shape=out_shape,
            in_specs=in_specs,
            out_specs=[VMEM] * len(out_shape),
            scratch_shapes=scratch_shapes,
            cost_estimate=cost,
            compiler_params=pltpu.CompilerParams(vmem_limit_bytes=VMEM_LIMIT),
        )

    def run(kernel, out_shape, *blocks):
        return call(kernel, out_shape, [VMEM] * len(blocks))(*blocks)

    def other_core(block):
        return lax.ppermute(block, "rep", [(0, 1), (1, 0)])

    n_tgt, n_prj, n_core = sizes
    tgt_flips = [n_prj << bit for bit in range(n_tgt.bit_length() - 1)]
    prj_flips = [1 << bit for bit in range(n_prj.bit_length() - 1)]
    far_first = tgt_flips[::-1]
    flips = (prj_flips + far_first, far_first + prj_flips)
    neighbours = (prj_flips[0], far_first[0] // n_prj)
    gate_levels = (len(prj_flips) - 1, len(tgt_flips) - 1)
    n_steps = len(tgt_flips) + len(prj_flips)

    def exchanged(step, block, crossed=0):
        pairs = []
        for place in range(n_tgt * n_prj):
            for kind in range(2):
                there = place ^ flips[kind][step]
                to_core = kind ^ crossed ^ parity(there)
                pairs.append((place * n_core + (kind ^ parity(place)), there * n_core + to_core))
        return lax.ppermute(block, DEVICES, pairs)

    in_vmem = pltpu.VMEM
    sums = in_vmem((two_cols, points), jnp.bfloat16)
    segment = in_vmem((two_cols, rows), jnp.float32)

    def summed(halves, until):
        totals = []
        for half, block in enumerate(halves):
            for step in range(1, until):
                other = exchanged(step, block)
                (block,) = run(functools.partial(add_kernel, step, half), [sums], gate, block, other)
            totals.append(block)
        return totals

    def swapped(fields):
        return [other_core(block) for block in fields]

    def in_hbm(*blocks):
        return [pltpu.with_memory_space_constraint(block, pltpu.HBM) for block in blocks]

    others = swapped([tgt_amp, proj_amp])
    energy, amp = call(
        load_kernel,
        [in_vmem((2, 1, rows), jnp.float32), in_vmem((2, two_cols, rows), jnp.float32)],
        [HBM] * 4,
        [
            pltpu.VMEM((rows,), jnp.float32),
            pltpu.VMEM(tgt_amp.shape, jnp.float32),
            pltpu.VMEM(proj_amp.shape, jnp.float32),
            pltpu.SemaphoreType.DMA((4,)),
        ],
        pl.CostEstimate(
            flops=2 * 4 * rows * two_cols * points, bytes_accessed=4 * 1024 * 1024, transcendentals=0
        ),
    )(*in_hbm(tgt_energy, proj_energy, tgt_amp, proj_amp))
    chip_amp, message = run(
        pack_kernel,
        [in_vmem((2, two_cols, rows), jnp.float32), in_vmem((2, two_cols, rows), jnp.bfloat16)],
        amp,
        *others,
    )
    message = exchanged(0, message)
    flags, counts = pair_flags.T, tile_counts.T
    bases = in_hbm(tgt_basis.reshape(2, -1, rows, points), proj_basis)
    pair = in_vmem((2, 2 * rows, points), jnp.bfloat16)
    *sent, weight = call(
        functools.partial(sent_kernel, neighbours),
        [
            in_vmem((2, 2 * rows + 2 * PIECES, points), jnp.bfloat16),
            pair,
            in_vmem((2, rows, points), jnp.bfloat16),
            in_vmem((1, 1, points), jnp.float32),
        ],
        [HBM] * 3 + [VMEM] * 2,
        [pltpu.VMEM((points,), jnp.float32), pltpu.SemaphoreType.DMA((6,))],
    )(*in_hbm(quad_weight), *bases, chip_amp, energy)
    mine_chip, mine_far, gate = call(
        functools.partial(side_kernel, gate_levels, neighbours),
        [
            pair,
            pair,
            in_vmem((n_steps, 2, 1, points), jnp.float32),
        ],
        [HBM] * 4 + [VMEM],
        [
            pltpu.SMEM(flags.shape, jnp.int32),
            pltpu.SMEM(counts.shape, jnp.int32),
            pltpu.SemaphoreType.DMA((6,)),
        ],
        BEHIND,
    )(*in_hbm(flags, counts), *bases, chip_amp)
    theirs_chip, theirs_far, theirs_own = swapped(sent)
    bases = (mine_chip, mine_far, theirs_chip, theirs_far)
    part, weights, energies = run(
        chip_kernel,
        [
            in_vmem((2, two_cols, points), jnp.float32),
            in_vmem((2, 1, points), jnp.float32),
            in_vmem((2, 1, rows), jnp.float32),
        ],
        mine_chip,
        theirs_chip,
        chip_amp,
        weight,
        energy,
    )
    halves = run(first_kernel, [sums] * 2, mine_far, theirs_far, gate, weights, part, message)
    (low, high), energies = lax.optimization_barrier((halves, energies))
    neighbour_energies = exchanged(0, energies)
    halves = low, high
    parts = summed(halves, n_steps - 1)
    low, high = [(other_core(block), exchanged(n_steps - 1, block, crossed=1)) for block in parts]
    (states,) = run(
        low_kernel,
        [in_vmem((4, two_cols, rows), jnp.float32)],
        *bases,
        *low,
        chip_amp,
        energies,
        message,
        neighbour_energies,
    )
    *halves, my_half, half_send = run(
        second_kernel,
        [sums, sums, segment, segment],
        *bases,
        states,
        *high,
        gate,
        weights,
    )
    other_half = other_core(half_send)
    fields = summed(halves, n_steps)
    low, high = swapped(fields)
    my_part, other_new = run(
        late_kernel,
        [segment, in_vmem((rows, two_cols), jnp.float32)],
        theirs_own,
        sent[0],
        *fields,
        energy,
        amp,
        my_half,
        other_half,
    )
    return run(
        last_kernel,
        [
            jax.ShapeDtypeStruct(tgt_amp.shape, jnp.float32),
            jax.ShapeDtypeStruct(proj_amp.shape, jnp.float32),
        ],
        mine_chip,
        theirs_chip,
        low,
        high,
        my_part,
        other_new,
    )


def solution(mesh):
    in_specs = (
        P(None, "tgt", "rep"),
        P(None, None, "prj", "rep"),
        P(("bpar", "rep")),
        P(("tgt", "prj", "rep")),
        P(("tgt", "rep"), "prj"),
        P("bpar", None),
        P("bpar", None),
        P(("bpar", "tgt", "prj", "rep"), None),
        P(("bpar", "tgt", "rep"), "prj", None),
    )
    out_specs = (P(("bpar", "tgt", "prj", "rep"), None), P(("bpar", "tgt", "rep"), "prj", None))

    def step(*args):
        return tuple(shards(*args))

    return jax.shard_map(step, mesh=mesh, in_specs=in_specs, out_specs=out_specs, check_vma=False)
```

```python
import functools

import jax
import jax.numpy as jnp
from jax import lax
from jax.experimental import pallas as pl
from jax.experimental.pallas import tpu as pltpu
from jax.sharding import PartitionSpec as P

time_step = 0.4
half_step = 0.5 * time_step
VMEM_LIMIT = 8 * 1024 * 1024
DEVICES = ("tgt", "prj", "rep")
HBM = pl.BlockSpec(memory_space=pl.ANY)
VMEM = pl.BlockSpec(memory_space=pltpu.VMEM)


def parity(place):
    odd = 0
    while place:
        odd, place = odd ^ (place & 1), place >> 1
    return odd


def my_kind():
    n_tgt, n_prj = lax.axis_size("tgt"), lax.axis_size("prj")
    place = lax.axis_index("tgt") * n_prj + lax.axis_index("prj")
    kind = lax.axis_index("rep")
    for bit in range((n_tgt * n_prj).bit_length() - 1):
        kind = jnp.bitwise_xor(kind, jnp.bitwise_and(lax.shift_right_logical(place, bit), 1))
    return kind


def by_core(body):
    for core in range(2):

        @pl.when(lax.axis_index("rep") == core)
        def _():
            body(core)


def ordered(core, first, second):
    return jnp.where(core == 0, first, second), jnp.where(core == 0, second, first)


def turned(block):
    half = block.shape[0] // 2
    return jnp.concatenate([block[half:], -block[:half]], axis=0)


def bf16(block):
    return block.astype(jnp.bfloat16)


def f32(block):
    return block.astype(jnp.float32)


def rows_of(bases, segment, amount):
    start = segment % 2 * amount
    return [bases[segment // 2][part, start : start + amount, :] for part in range(2)]


def project(basis, amp):
    return jnp.dot(bf16(amp), basis[0], preferred_element_type=jnp.float32) + jnp.dot(
        bf16(turned(amp)), basis[1], preferred_element_type=jnp.float32
    )


def expand(basis, field):
    contract = (((1,), (1,)), ((), ()))
    return lax.dot_general(
        turned(field), basis[0], contract, preferred_element_type=jnp.float32
    ) + lax.dot_general(field, basis[1], contract, preferred_element_type=jnp.float32)


PIECES = 16

BEHIND = pl.CostEstimate(flops=1 << 35, bytes_accessed=1 << 16, transcendentals=0)


def split(row):
    index = lax.broadcasted_iota(jnp.int32, (PIECES, row.shape[1]), 0)
    block = jnp.zeros(index.shape, jnp.float32)
    for piece in range(3):
        rounded = f32(bf16(row))
        block = jnp.where(index == piece, rounded, block)
        row = row - rounded
    return bf16(block)


def joined(block):
    pieces = f32(block)
    return pieces[0:1] + pieces[1:2] + pieces[2:3]


def basis_copies(bases, sem, my, neighbours, sources):
    rows = sources[my].shape[2]
    place = lax.axis_index(("prj", "tgt")[my])
    copies = []
    for chip, there in enumerate((place, jnp.bitwise_xor(place, neighbours[my]))):
        for core in range(2):
            copies.append(
                pltpu.make_async_copy(
                    sources[my].at[:, 2 * there + core],
                    bases[chip].at[:, core * rows : (core + 1) * rows],
                    sem.at[2 * chip + core],
                )
            )
    return copies


def load_kernel(
    tgt_energy_hbm,
    proj_energy_hbm,
    tgt_own_hbm,
    proj_own_hbm,
    energy,
    amp_ref,
    flat_energy,
    tgt_own,
    proj_own,
    sems,
):
    pairs = [
        (tgt_own_hbm, tgt_own),
        (proj_own_hbm, proj_own),
        (tgt_energy_hbm, flat_energy),
        (proj_energy_hbm, energy.at[1]),
    ]
    copies = [pltpu.make_async_copy(src, dst, sems.at[k]) for k, (src, dst) in enumerate(pairs)]
    for copy in copies:
        copy.start()
    for copy in copies:
        copy.wait()
    energy[0] = flat_energy[...][None, :]
    amp_ref[0] = tgt_own[...].T
    amp_ref[1] = proj_own[0].T


def pack_kernel(amp_ref, tgt_other, proj_other, chip_amp, message):
    my = my_kind()
    other_amp, _ = ordered(my, tgt_other[...].T, proj_other[0].T)
    amps = ordered(lax.axis_index("rep"), amp_ref[my], other_amp)
    for segment in range(2):
        chip_amp[segment] = amps[segment]
        message[segment] = bf16(amps[segment])


def sent_kernel(
    neighbours,
    weight_hbm,
    tgt_hbm,
    proj_hbm,
    chip_amp,
    energy,
    sent_chip,
    sent_far,
    sent_own,
    weight,
    flat_weight,
    sems,
):
    my = my_kind()
    sources = (tgt_hbm, proj_hbm)
    rows = chip_amp.shape[2]

    def copies_of(kind):
        own = pltpu.make_async_copy(
            sources[kind].at[:, 2 * lax.axis_index(("prj", "tgt")[kind]) + 1 - lax.axis_index("rep")],
            sent_own,
            sems.at[4],
        )
        return basis_copies((sent_chip, sent_far), sems, 1 - kind, neighbours, sources) + [own]

    weight_copy = pltpu.make_async_copy(weight_hbm, flat_weight, sems.at[5])
    weight_copy.start()
    for kind in range(2):

        @pl.when(my == kind)
        def _():
            for copy in copies_of(kind):
                copy.start()

    weight_copy.wait()
    weight[0] = flat_weight[...][None, :]
    for part in range(2):
        sent_chip[part, 2 * rows : 2 * rows + PIECES] = split(weight[0])
        sent_chip[part, 2 * rows + PIECES :, :rows] = split(energy[1 - my])
    for copy in copies_of(0):
        copy.wait()


def side_kernel(
    gate_levels,
    neighbours,
    flags_hbm,
    counts_hbm,
    tgt_hbm,
    proj_hbm,
    chip_amp,
    mine_chip,
    mine_far,
    gate,
    flags,
    counts,
    sems,
):
    my = my_kind()
    tgt_index = lax.axis_index("tgt")
    prj_index = lax.axis_index("prj")
    sources = (tgt_hbm, proj_hbm)
    pairs = [(flags_hbm, flags), (counts_hbm, counts)]
    copies = [pltpu.make_async_copy(src, dst, sems.at[4 + k]) for k, (src, dst) in enumerate(pairs)]
    for copy in copies:
        copy.start()
    for kind in range(2):

        @pl.when(my == kind)
        def _():
            for copy in basis_copies((mine_chip, mine_far), sems, kind, neighbours, sources):
                copy.start()

    for copy in copies:
        copy.wait()
    tiles = 2
    width = gate.shape[-1] // tiles
    gate_level = jnp.where(my == 0, *gate_levels)
    for half in range(2):
        for tile in range(tiles):
            live = jnp.logical_and(
                flags[prj_index, tgt_index] > 0, tiles * half + tile < counts[prj_index, tgt_index]
            )
            value = jnp.where(live, 1.0, 0.0).astype(jnp.float32)
            for level in range(gate.shape[0]):
                here = jnp.where(level == gate_level, value, jnp.float32(1.0))
                gate[level, half, :, tile * width : (tile + 1) * width] = jnp.full(
                    (1, width), here, jnp.float32
                )
    for copy in basis_copies((mine_chip, mine_far), sems, 0, neighbours, sources):
        copy.wait()


def chip_kernel(mine_chip, theirs_chip, chip_amp, weight, energy, part_ref, weights, energies):
    mine, theirs = (mine_chip,), (theirs_chip,)
    rows = chip_amp.shape[2]

    def body(core):
        for half, basis in enumerate((mine, theirs) if core == 0 else (theirs, mine)):
            part_ref[half] = sum(
                project(rows_of(basis, segment, rows), chip_amp[segment]) for segment in range(2)
            )
        weights[core] = weight[0]
        weights[1 - core] = joined(theirs_chip[0, 2 * rows : 2 * rows + PIECES, :])
        energies[core] = energy[my_kind()]
        energies[1 - core] = joined(theirs_chip[0, 2 * rows + PIECES :, :rows])

    by_core(body)


def first_kernel(mine_far, theirs_far, gate, weights, part_ref, message, *outs):
    mine, theirs = (None, mine_far), (None, theirs_far)
    rows = message.shape[2]

    def body(core):
        for half, basis in enumerate((mine, theirs) if core == 0 else (theirs, mine)):
            total = part_ref[half] + sum(
                project(rows_of(basis, 2 + segment, rows), f32(message[segment]))
                for segment in range(2)
            )
            outs[half][...] = bf16(gate[0, half] * (weights[half] * total))

    by_core(body)


def add_kernel(level, half, gate, own, other, out_ref):
    out_ref[...] = bf16(gate[level, half] * (f32(own[...]) + f32(other[...])))


def low_kernel(
    mine_chip,
    mine_far,
    theirs_chip,
    theirs_far,
    low,
    low_there,
    chip_amp,
    energies,
    message,
    neighbour_energies,
    states_ref,
):
    mine, theirs = (mine_chip, mine_far), (theirs_chip, theirs_far)
    rows = chip_amp.shape[2]
    field = bf16(f32(low[...]) + f32(low_there[...]))

    def body(core):
        for segment in range(4):
            if segment < 2:
                amp, energy = chip_amp[segment], energies[segment]
            else:
                amp, energy = f32(message[segment - 2]), neighbour_energies[segment - 2]
            change = expand(rows_of((mine, theirs)[core], segment, rows), field)
            states_ref[segment] = amp + half_step * (energy * turned(amp) + change)

    by_core(body)


def second_kernel(
    mine_chip,
    mine_far,
    theirs_chip,
    theirs_far,
    states_ref,
    high,
    high_there,
    gate,
    weights,
    low_ref,
    high_ref,
    half_ref,
    send_ref,
):
    mine, theirs = (mine_chip, mine_far), (theirs_chip, theirs_far)
    rows = states_ref.shape[2]
    field = bf16(f32(high[...]) + f32(high_there[...]))

    def body(core):
        bases = (mine, theirs) if core == 0 else (theirs, mine)
        halves = [
            states_ref[segment] + half_step * expand(rows_of(bases[1], segment, rows), field)
            for segment in range(4)
        ]
        half_ref[...] = halves[core]
        send_ref[...] = halves[1 - core]
        for half, out_ref in enumerate((low_ref, high_ref)):
            total = sum(
                project(rows_of(bases[half], segment, rows), halves[segment]) for segment in range(4)
            )
            out_ref[...] = bf16(gate[0, half] * (weights[half] * total))

    by_core(body)


def late_kernel(
    mine_chip,
    theirs_chip,
    theirs_own,
    sent_chip,
    low,
    high,
    my_low,
    energy,
    amp_ref,
    my_half,
    other_half,
    my_part,
    other_new,
):
    rows = amp_ref.shape[2]

    def body(core):
        my = my_kind()
        near, far = (low, high) if core == 0 else (high, low)
        change = expand(rows_of((sent_chip,), core, rows), near[...]) + expand(
            rows_of((theirs_own,), 0, rows), far[...]
        )
        rate = energy[1 - my] * turned(other_half[...]) + change
        other_new[...] = (amp_ref[1 - my] + time_step * rate).T
        change = expand(rows_of(((mine_chip, theirs_chip)[core],), core, rows), my_low[...])
        my_part[...] = amp_ref[my] + time_step * (energy[my] * turned(my_half[...]) + change)

    by_core(body)


def last_kernel(
    mine_chip, theirs_chip, high, my_part, other_new, new_tgt, new_proj, my_new, sems
):
    cols, rows = my_part.shape
    my = my_kind()
    parts = 2
    size = rows // parts
    outs = (new_tgt, new_proj.at[0])

    def copies(kind):
        return [pltpu.make_async_copy(other_new, outs[1 - kind], sems.at[parts])] + [
            pltpu.make_async_copy(
                my_new.at[pl.ds(part * size, size)], outs[kind].at[pl.ds(part * size, size)], sems.at[part]
            )
            for part in range(parts)
        ]

    def start(number):
        for kind in range(2):

            @pl.when(my == kind)
            def _():
                copies(kind)[number].start()

    def body(core):
        basis = rows_of(((theirs_chip, mine_chip)[core],), core, rows)
        for part in range(parts):
            states = slice(part * size, (part + 1) * size)
            change = expand([block[states] for block in basis], high[...])
            my_new[states, :] = (my_part[:, states] + time_step * change).T
            start(1 + part)

    start(0)
    by_core(body)
    for copy in copies(0):
        copy.wait()


def shards(
    tgt_basis,
    proj_basis,
    quad_weight,
    tgt_energy,
    proj_energy,
    pair_flags,
    tile_counts,
    tgt_amp,
    proj_amp,
):
    points = quad_weight.shape[0]
    rows, two_cols = tgt_amp.shape
    sizes = [lax.axis_size(axis) for axis in DEVICES]

    def call(kernel, out_shape, in_specs, scratch_shapes=(), cost=None, out_spec=VMEM):
        return pl.pallas_call(
            kernel,
            out_shape=out_shape,
            in_specs=in_specs,
            out_specs=[out_spec] * len(out_shape),
            scratch_shapes=scratch_shapes,
            cost_estimate=cost,
            compiler_params=pltpu.CompilerParams(vmem_limit_bytes=VMEM_LIMIT),
        )

    def run(kernel, out_shape, *blocks):
        return call(kernel, out_shape, [VMEM] * len(blocks))(*blocks)

    def other_core(block):
        return lax.ppermute(block, "rep", [(0, 1), (1, 0)])

    n_tgt, n_prj, n_core = sizes
    tgt_flips = [n_prj << bit for bit in range(n_tgt.bit_length() - 1)]
    prj_flips = [1 << bit for bit in range(n_prj.bit_length() - 1)]
    far_first = tgt_flips[::-1]
    flips = (prj_flips + far_first, far_first + prj_flips)
    neighbours = (prj_flips[0], far_first[0] // n_prj)
    gate_levels = (len(prj_flips) - 1, len(tgt_flips) - 1)
    n_steps = len(tgt_flips) + len(prj_flips)

    def exchanged(step, block, crossed=0):
        pairs = []
        for place in range(n_tgt * n_prj):
            for kind in range(2):
                there = place ^ flips[kind][step]
                to_core = kind ^ crossed ^ parity(there)
                pairs.append((place * n_core + (kind ^ parity(place)), there * n_core + to_core))
        return lax.ppermute(block, DEVICES, pairs)

    in_vmem = pltpu.VMEM
    sums = in_vmem((two_cols, points), jnp.bfloat16)
    segment = in_vmem((two_cols, rows), jnp.float32)

    def summed(halves, until):
        totals = []
        for half, block in enumerate(halves):
            for step in range(1, until):
                other = exchanged(step, block)
                (block,) = run(functools.partial(add_kernel, step, half), [sums], gate, block, other)
            totals.append(block)
        return totals

    def swapped(fields):
        return [other_core(block) for block in fields]

    def in_hbm(*blocks):
        return [pltpu.with_memory_space_constraint(block, pltpu.HBM) for block in blocks]

    others = swapped([tgt_amp, proj_amp])
    energy, amp = call(
        load_kernel,
        [in_vmem((2, 1, rows), jnp.float32), in_vmem((2, two_cols, rows), jnp.float32)],
        [HBM] * 4,
        [
            pltpu.VMEM((rows,), jnp.float32),
            pltpu.VMEM(tgt_amp.shape, jnp.float32),
            pltpu.VMEM(proj_amp.shape, jnp.float32),
            pltpu.SemaphoreType.DMA((4,)),
        ],
        pl.CostEstimate(
            flops=2 * 4 * rows * two_cols * points, bytes_accessed=4 * 1024 * 1024, transcendentals=0
        ),
    )(*in_hbm(tgt_energy, proj_energy, tgt_amp, proj_amp))
    chip_amp, message = run(
        pack_kernel,
        [in_vmem((2, two_cols, rows), jnp.float32), in_vmem((2, two_cols, rows), jnp.bfloat16)],
        amp,
        *others,
    )
    message = exchanged(0, message)
    flags, counts = pair_flags.T, tile_counts.T
    bases = in_hbm(tgt_basis.reshape(2, -1, rows, points), proj_basis)
    pair = in_vmem((2, 2 * rows, points), jnp.bfloat16)
    *sent, weight = call(
        functools.partial(sent_kernel, neighbours),
        [
            in_vmem((2, 2 * rows + 2 * PIECES, points), jnp.bfloat16),
            pair,
            in_vmem((2, rows, points), jnp.bfloat16),
            in_vmem((1, 1, points), jnp.float32),
        ],
        [HBM] * 3 + [VMEM] * 2,
        [pltpu.VMEM((points,), jnp.float32), pltpu.SemaphoreType.DMA((6,))],
    )(*in_hbm(quad_weight), *bases, chip_amp, energy)
    mine_chip, mine_far, gate = call(
        functools.partial(side_kernel, gate_levels, neighbours),
        [
            pair,
            pair,
            in_vmem((n_steps, 2, 1, points), jnp.float32),
        ],
        [HBM] * 4 + [VMEM],
        [
            pltpu.SMEM(flags.shape, jnp.int32),
            pltpu.SMEM(counts.shape, jnp.int32),
            pltpu.SemaphoreType.DMA((6,)),
        ],
        BEHIND,
    )(*in_hbm(flags, counts), *bases, chip_amp)
    theirs_chip, theirs_far, theirs_own = swapped(sent)
    bases = (mine_chip, mine_far, theirs_chip, theirs_far)
    part, weights, energies = run(
        chip_kernel,
        [
            in_vmem((2, two_cols, points), jnp.float32),
            in_vmem((2, 1, points), jnp.float32),
            in_vmem((2, 1, rows), jnp.float32),
        ],
        mine_chip,
        theirs_chip,
        chip_amp,
        weight,
        energy,
    )
    halves = run(first_kernel, [sums] * 2, mine_far, theirs_far, gate, weights, part, message)
    (low, high), energies = lax.optimization_barrier((halves, energies))
    neighbour_energies = exchanged(0, energies)
    halves = low, high
    parts = summed(halves, n_steps - 1)
    low, high = [(other_core(block), exchanged(n_steps - 1, block, crossed=1)) for block in parts]
    (states,) = run(
        low_kernel,
        [in_vmem((4, two_cols, rows), jnp.float32)],
        *bases,
        *low,
        chip_amp,
        energies,
        message,
        neighbour_energies,
    )
    *halves, my_half, half_send = run(
        second_kernel,
        [sums, sums, segment, segment],
        *bases,
        states,
        *high,
        gate,
        weights,
    )
    other_half = other_core(half_send)
    fields = summed(halves, n_steps)
    low, high = swapped(fields)
    low, high = swapped(fields)
    my_part, other_new = run(
        late_kernel,
        [segment, in_vmem((rows, two_cols), jnp.float32)],
        mine_chip,
        theirs_chip,
        theirs_own,
        sent[0],
        *fields,
        low,
        energy,
        amp,
        my_half,
        other_half,
    )
    return call(
        last_kernel,
        [
            jax.ShapeDtypeStruct(tgt_amp.shape, jnp.float32),
            jax.ShapeDtypeStruct(proj_amp.shape, jnp.float32),
        ],
        [VMEM] * 5,
        [pltpu.VMEM((rows, two_cols), jnp.float32), pltpu.SemaphoreType.DMA((3,))],
        out_spec=HBM,
    )(mine_chip, theirs_chip, high, my_part, other_new)


def solution(mesh):
    in_specs = (
        P(None, "tgt", "rep"),
        P(None, None, "prj", "rep"),
        P(("bpar", "rep")),
        P(("tgt", "prj", "rep")),
        P(("tgt", "rep"), "prj"),
        P("bpar", None),
        P("bpar", None),
        P(("bpar", "tgt", "prj", "rep"), None),
        P(("bpar", "tgt", "rep"), "prj", None),
    )
    out_specs = (P(("bpar", "tgt", "prj", "rep"), None), P(("bpar", "tgt", "rep"), "prj", None))

    def step(*args):
        return tuple(shards(*args))

    return jax.shard_map(step, mesh=mesh, in_specs=in_specs, out_specs=out_specs, check_vma=False)
```

```python
import functools

import jax
import jax.numpy as jnp
from jax import lax
from jax.experimental import pallas as pl
from jax.experimental.pallas import tpu as pltpu
from jax.sharding import PartitionSpec as P

time_step = 0.4
half_step = 0.5 * time_step
VMEM_LIMIT = 8 * 1024 * 1024
DEVICES = ("tgt", "prj", "rep")
HBM = pl.BlockSpec(memory_space=pl.ANY)
VMEM = pl.BlockSpec(memory_space=pltpu.VMEM)


def parity(place):
    odd = 0
    while place:
        odd, place = odd ^ (place & 1), place >> 1
    return odd


def my_kind():
    n_tgt, n_prj = lax.axis_size("tgt"), lax.axis_size("prj")
    place = lax.axis_index("tgt") * n_prj + lax.axis_index("prj")
    kind = lax.axis_index("rep")
    for bit in range((n_tgt * n_prj).bit_length() - 1):
        kind = jnp.bitwise_xor(kind, jnp.bitwise_and(lax.shift_right_logical(place, bit), 1))
    return kind


def by_core(body):
    for core in range(2):

        @pl.when(lax.axis_index("rep") == core)
        def _():
            body(core)


def ordered(core, first, second):
    return jnp.where(core == 0, first, second), jnp.where(core == 0, second, first)


def turned(block):
    half = block.shape[0] // 2
    return jnp.concatenate([block[half:], -block[:half]], axis=0)


def bf16(block):
    return block.astype(jnp.bfloat16)


def f32(block):
    return block.astype(jnp.float32)


def rows_of(bases, segment, amount):
    start = segment % 2 * amount
    return [bases[segment // 2][part, start : start + amount, :] for part in range(2)]


def project(basis, amp):
    return jnp.dot(bf16(amp), basis[0], preferred_element_type=jnp.float32) + jnp.dot(
        bf16(turned(amp)), basis[1], preferred_element_type=jnp.float32
    )


def expand(basis, field):
    contract = (((1,), (1,)), ((), ()))
    return lax.dot_general(
        turned(field), basis[0], contract, preferred_element_type=jnp.float32
    ) + lax.dot_general(field, basis[1], contract, preferred_element_type=jnp.float32)


PIECES = 16

BEHIND = pl.CostEstimate(flops=1 << 35, bytes_accessed=1 << 16, transcendentals=0)


def split(row):
    index = lax.broadcasted_iota(jnp.int32, (PIECES, row.shape[1]), 0)
    block = jnp.zeros(index.shape, jnp.float32)
    for piece in range(3):
        rounded = f32(bf16(row))
        block = jnp.where(index == piece, rounded, block)
        row = row - rounded
    return bf16(block)


def joined(block):
    pieces = f32(block)
    return pieces[0:1] + pieces[1:2] + pieces[2:3]


def basis_copies(bases, sem, my, neighbours, sources):
    rows = sources[my].shape[2]
    place = lax.axis_index(("prj", "tgt")[my])
    copies = []
    for chip, there in enumerate((place, jnp.bitwise_xor(place, neighbours[my]))):
        for core in range(2):
            copies.append(
                pltpu.make_async_copy(
                    sources[my].at[:, 2 * there + core],
                    bases[chip].at[:, core * rows : (core + 1) * rows],
                    sem.at[2 * chip + core],
                )
            )
    return copies


def load_kernel(
    tgt_energy_hbm,
    proj_energy_hbm,
    tgt_own_hbm,
    proj_own_hbm,
    energy,
    amp_ref,
    flat_energy,
    tgt_own,
    proj_own,
    sems,
):
    pairs = [
        (tgt_own_hbm, tgt_own),
        (proj_own_hbm, proj_own),
        (tgt_energy_hbm, flat_energy),
        (proj_energy_hbm, energy.at[1]),
    ]
    copies = [pltpu.make_async_copy(src, dst, sems.at[k]) for k, (src, dst) in enumerate(pairs)]
    for copy in copies:
        copy.start()
    for copy in copies:
        copy.wait()
    energy[0] = flat_energy[...][None, :]
    amp_ref[0] = tgt_own[...].T
    amp_ref[1] = proj_own[0].T


def pack_kernel(amp_ref, tgt_other, proj_other, chip_amp, message):
    my = my_kind()
    other_amp, _ = ordered(my, tgt_other[...].T, proj_other[0].T)
    amps = ordered(lax.axis_index("rep"), amp_ref[my], other_amp)
    for segment in range(2):
        chip_amp[segment] = amps[segment]
        message[segment] = bf16(amps[segment])


def sent_kernel(
    neighbours,
    weight_hbm,
    tgt_hbm,
    proj_hbm,
    chip_amp,
    energy,
    sent_chip,
    sent_far,
    sent_own,
    weight,
    flat_weight,
    sems,
):
    my = my_kind()
    sources = (tgt_hbm, proj_hbm)
    rows = chip_amp.shape[2]

    def copies_of(kind):
        own = pltpu.make_async_copy(
            sources[kind].at[:, 2 * lax.axis_index(("prj", "tgt")[kind]) + 1 - lax.axis_index("rep")],
            sent_own,
            sems.at[4],
        )
        return basis_copies((sent_chip, sent_far), sems, 1 - kind, neighbours, sources) + [own]

    weight_copy = pltpu.make_async_copy(weight_hbm, flat_weight, sems.at[5])
    weight_copy.start()
    for kind in range(2):

        @pl.when(my == kind)
        def _():
            for copy in copies_of(kind):
                copy.start()

    weight_copy.wait()
    weight[0] = flat_weight[...][None, :]
    for part in range(2):
        sent_chip[part, 2 * rows : 2 * rows + PIECES] = split(weight[0])
        sent_chip[part, 2 * rows + PIECES :, :rows] = split(energy[1 - my])
    for copy in copies_of(0):
        copy.wait()


def side_kernel(
    gate_levels,
    neighbours,
    flags_hbm,
    counts_hbm,
    tgt_hbm,
    proj_hbm,
    chip_amp,
    mine_chip,
    mine_far,
    gate,
    flags,
    counts,
    sems,
):
    my = my_kind()
    tgt_index = lax.axis_index("tgt")
    prj_index = lax.axis_index("prj")
    sources = (tgt_hbm, proj_hbm)
    pairs = [(flags_hbm, flags), (counts_hbm, counts)]
    copies = [pltpu.make_async_copy(src, dst, sems.at[4 + k]) for k, (src, dst) in enumerate(pairs)]
    for copy in copies:
        copy.start()
    for kind in range(2):

        @pl.when(my == kind)
        def _():
            for copy in basis_copies((mine_chip, mine_far), sems, kind, neighbours, sources):
                copy.start()

    for copy in copies:
        copy.wait()
    tiles = 2
    width = gate.shape[-1] // tiles
    gate_level = jnp.where(my == 0, *gate_levels)
    for half in range(2):
        for tile in range(tiles):
            live = jnp.logical_and(
                flags[prj_index, tgt_index] > 0, tiles * half + tile < counts[prj_index, tgt_index]
            )
            value = jnp.where(live, 1.0, 0.0).astype(jnp.float32)
            for level in range(gate.shape[0]):
                here = jnp.where(level == gate_level, value, jnp.float32(1.0))
                gate[level, half, :, tile * width : (tile + 1) * width] = jnp.full(
                    (1, width), here, jnp.float32
                )
    for copy in basis_copies((mine_chip, mine_far), sems, 0, neighbours, sources):
        copy.wait()


def chip_kernel(mine_chip, theirs_chip, chip_amp, weight, energy, part_ref, weights, energies):
    mine, theirs = (mine_chip,), (theirs_chip,)
    rows = chip_amp.shape[2]

    def body(core):
        for half, basis in enumerate((mine, theirs) if core == 0 else (theirs, mine)):
            part_ref[half] = sum(
                project(rows_of(basis, segment, rows), chip_amp[segment]) for segment in range(2)
            )
        weights[core] = weight[0]
        weights[1 - core] = joined(theirs_chip[0, 2 * rows : 2 * rows + PIECES, :])
        energies[core] = energy[my_kind()]
        energies[1 - core] = joined(theirs_chip[0, 2 * rows + PIECES :, :rows])

    by_core(body)


def first_kernel(mine_far, theirs_far, gate, weights, part_ref, message, *outs):
    mine, theirs = (None, mine_far), (None, theirs_far)
    rows = message.shape[2]

    def body(core):
        for half, basis in enumerate((mine, theirs) if core == 0 else (theirs, mine)):
            total = part_ref[half] + sum(
                project(rows_of(basis, 2 + segment, rows), f32(message[segment]))
                for segment in range(2)
            )
            outs[half][...] = bf16(gate[0, half] * (weights[half] * total))

    by_core(body)


def add_kernel(level, half, gate, own, other, out_ref):
    out_ref[...] = bf16(gate[level, half] * (f32(own[...]) + f32(other[...])))


def low_kernel(
    mine_chip,
    mine_far,
    theirs_chip,
    theirs_far,
    low,
    low_there,
    chip_amp,
    energies,
    message,
    neighbour_energies,
    states_ref,
):
    mine, theirs = (mine_chip, mine_far), (theirs_chip, theirs_far)
    rows = chip_amp.shape[2]
    field = bf16(f32(low[...]) + f32(low_there[...]))

    def body(core):
        for segment in range(4):
            if segment < 2:
                amp, energy = chip_amp[segment], energies[segment]
            else:
                amp, energy = f32(message[segment - 2]), neighbour_energies[segment - 2]
            change = expand(rows_of((mine, theirs)[core], segment, rows), field)
            states_ref[segment] = amp + half_step * (energy * turned(amp) + change)

    by_core(body)


def second_kernel(
    mine_chip,
    mine_far,
    theirs_chip,
    theirs_far,
    states_ref,
    high,
    high_there,
    gate,
    weights,
    low_ref,
    high_ref,
    half_ref,
    send_ref,
):
    mine, theirs = (mine_chip, mine_far), (theirs_chip, theirs_far)
    rows = states_ref.shape[2]
    field = bf16(f32(high[...]) + f32(high_there[...]))

    def body(core):
        bases = (mine, theirs) if core == 0 else (theirs, mine)
        halves = [
            states_ref[segment] + half_step * expand(rows_of(bases[1], segment, rows), field)
            for segment in range(4)
        ]
        half_ref[...] = halves[core]
        send_ref[...] = halves[1 - core]
        for half, out_ref in enumerate((low_ref, high_ref)):
            total = sum(
                project(rows_of(bases[half], segment, rows), halves[segment]) for segment in range(4)
            )
            out_ref[...] = bf16(gate[0, half] * (weights[half] * total))

    by_core(body)


def late_kernel(
    mine_chip,
    theirs_chip,
    theirs_own,
    sent_chip,
    low,
    high,
    my_low,
    energy,
    amp_ref,
    my_half,
    other_half,
    my_part,
    other_new,
):
    rows = amp_ref.shape[2]

    def body(core):
        my = my_kind()
        near, far = (low, high) if core == 0 else (high, low)
        change = expand(rows_of((sent_chip,), core, rows), near[...]) + expand(
            rows_of((theirs_own,), 0, rows), far[...]
        )
        rate = energy[1 - my] * turned(other_half[...]) + change
        other_new[...] = (amp_ref[1 - my] + time_step * rate).T
        change = expand(rows_of(((mine_chip, theirs_chip)[core],), core, rows), my_low[...])
        my_part[...] = amp_ref[my] + time_step * (energy[my] * turned(my_half[...]) + change)

    by_core(body)


def last_kernel(
    mine_chip, theirs_chip, high, my_part, other_new, new_tgt, new_proj, my_new, sems
):
    cols, rows = my_part.shape
    my = my_kind()
    parts = 2
    size = rows // parts
    outs = (new_tgt, new_proj.at[0])

    def copies(kind):
        return [pltpu.make_async_copy(other_new, outs[1 - kind], sems.at[parts])] + [
            pltpu.make_async_copy(
                my_new.at[pl.ds(part * size, size)], outs[kind].at[pl.ds(part * size, size)], sems.at[part]
            )
            for part in range(parts)
        ]

    def start(number):
        for kind in range(2):

            @pl.when(my == kind)
            def _():
                copies(kind)[number].start()

    def body(core):
        basis = rows_of(((theirs_chip, mine_chip)[core],), core, rows)
        for part in range(parts):
            states = slice(part * size, (part + 1) * size)
            change = expand([block[states] for block in basis], high[...])
            my_new[states, :] = (my_part[:, states] + time_step * change).T
            start(1 + part)

    start(0)
    by_core(body)
    for copy in copies(0):
        copy.wait()


def shards(
    tgt_basis,
    proj_basis,
    quad_weight,
    tgt_energy,
    proj_energy,
    pair_flags,
    tile_counts,
    tgt_amp,
    proj_amp,
):
    points = quad_weight.shape[0]
    rows, two_cols = tgt_amp.shape
    sizes = [lax.axis_size(axis) for axis in DEVICES]

    def call(kernel, out_shape, in_specs, scratch_shapes=(), cost=None, out_spec=VMEM):
        return pl.pallas_call(
            kernel,
            out_shape=out_shape,
            in_specs=in_specs,
            out_specs=[out_spec] * len(out_shape),
            scratch_shapes=scratch_shapes,
            cost_estimate=cost,
            compiler_params=pltpu.CompilerParams(vmem_limit_bytes=VMEM_LIMIT),
        )

    def run(kernel, out_shape, *blocks):
        return call(kernel, out_shape, [VMEM] * len(blocks))(*blocks)

    def other_core(block):
        return lax.ppermute(block, "rep", [(0, 1), (1, 0)])

    n_tgt, n_prj, n_core = sizes
    tgt_flips = [n_prj << bit for bit in range(n_tgt.bit_length() - 1)]
    prj_flips = [1 << bit for bit in range(n_prj.bit_length() - 1)]
    far_first = tgt_flips[::-1]
    flips = (prj_flips + far_first, far_first + prj_flips)
    neighbours = (prj_flips[0], far_first[0] // n_prj)
    gate_levels = (len(prj_flips) - 1, len(tgt_flips) - 1)
    n_steps = len(tgt_flips) + len(prj_flips)

    def exchanged(step, block, crossed=0):
        pairs = []
        for place in range(n_tgt * n_prj):
            for kind in range(2):
                there = place ^ flips[kind][step]
                to_core = kind ^ crossed ^ parity(there)
                pairs.append((place * n_core + (kind ^ parity(place)), there * n_core + to_core))
        return lax.ppermute(block, DEVICES, pairs)

    in_vmem = pltpu.VMEM
    sums = in_vmem((two_cols, points), jnp.bfloat16)
    segment = in_vmem((two_cols, rows), jnp.float32)

    def summed(halves, until):
        totals = []
        for half, block in enumerate(halves):
            for step in range(1, until):
                other = exchanged(step, block)
                (block,) = run(functools.partial(add_kernel, step, half), [sums], gate, block, other)
            totals.append(block)
        return totals

    def swapped(fields):
        return [other_core(block) for block in fields]

    def in_hbm(*blocks):
        return [pltpu.with_memory_space_constraint(block, pltpu.HBM) for block in blocks]

    def handed(kind, block):
        pairs = []
        for place in range(n_tgt * n_prj):
            to_core = kind ^ parity(place)
            pairs.append((place * n_core + 1 - to_core, place * n_core + to_core))
        return lax.ppermute(block, DEVICES, pairs)

    others = handed(0, tgt_amp), handed(1, proj_amp)
    energy, amp = call(
        load_kernel,
        [in_vmem((2, 1, rows), jnp.float32), in_vmem((2, two_cols, rows), jnp.float32)],
        [HBM] * 4,
        [
            pltpu.VMEM((rows,), jnp.float32),
            pltpu.VMEM(tgt_amp.shape, jnp.float32),
            pltpu.VMEM(proj_amp.shape, jnp.float32),
            pltpu.SemaphoreType.DMA((4,)),
        ],
        pl.CostEstimate(
            flops=2 * 4 * rows * two_cols * points, bytes_accessed=4 * 1024 * 1024, transcendentals=0
        ),
    )(*in_hbm(tgt_energy, proj_energy, tgt_amp, proj_amp))
    chip_amp, message = run(
        pack_kernel,
        [in_vmem((2, two_cols, rows), jnp.float32), in_vmem((2, two_cols, rows), jnp.bfloat16)],
        amp,
        *others,
    )
    message = exchanged(0, message)
    flags, counts = pair_flags.T, tile_counts.T
    bases = in_hbm(tgt_basis.reshape(2, -1, rows, points), proj_basis)
    pair = in_vmem((2, 2 * rows, points), jnp.bfloat16)
    *sent, weight = call(
        functools.partial(sent_kernel, neighbours),
        [
            in_vmem((2, 2 * rows + 2 * PIECES, points), jnp.bfloat16),
            pair,
            in_vmem((2, rows, points), jnp.bfloat16),
            in_vmem((1, 1, points), jnp.float32),
        ],
        [HBM] * 3 + [VMEM] * 2,
        [pltpu.VMEM((points,), jnp.float32), pltpu.SemaphoreType.DMA((6,))],
    )(*in_hbm(quad_weight), *bases, chip_amp, energy)
    mine_chip, mine_far, gate = call(
        functools.partial(side_kernel, gate_levels, neighbours),
        [
            pair,
            pair,
            in_vmem((n_steps, 2, 1, points), jnp.float32),
        ],
        [HBM] * 4 + [VMEM],
        [
            pltpu.SMEM(flags.shape, jnp.int32),
            pltpu.SMEM(counts.shape, jnp.int32),
            pltpu.SemaphoreType.DMA((6,)),
        ],
        BEHIND,
    )(*in_hbm(flags, counts), *bases, chip_amp)
    theirs_chip, theirs_far, theirs_own = swapped(sent)
    bases = (mine_chip, mine_far, theirs_chip, theirs_far)
    part, weights, energies = run(
        chip_kernel,
        [
            in_vmem((2, two_cols, points), jnp.float32),
            in_vmem((2, 1, points), jnp.float32),
            in_vmem((2, 1, rows), jnp.float32),
        ],
        mine_chip,
        theirs_chip,
        chip_amp,
        weight,
        energy,
    )
    halves = run(first_kernel, [sums] * 2, mine_far, theirs_far, gate, weights, part, message)
    (low, high), energies = lax.optimization_barrier((halves, energies))
    neighbour_energies = exchanged(0, energies)
    halves = low, high
    parts = summed(halves, n_steps - 1)
    low, high = [(other_core(block), exchanged(n_steps - 1, block, crossed=1)) for block in parts]
    (states,) = run(
        low_kernel,
        [in_vmem((4, two_cols, rows), jnp.float32)],
        *bases,
        *low,
        chip_amp,
        energies,
        message,
        neighbour_energies,
    )
    *halves, my_half, half_send = run(
        second_kernel,
        [sums, sums, segment, segment],
        *bases,
        states,
        *high,
        gate,
        weights,
    )
    other_half = other_core(half_send)
    fields = summed(halves, n_steps)
    low, high = swapped(fields)
    low, high = swapped(fields)
    my_part, other_new = run(
        late_kernel,
        [segment, in_vmem((rows, two_cols), jnp.float32)],
        mine_chip,
        theirs_chip,
        theirs_own,
        sent[0],
        *fields,
        low,
        energy,
        amp,
        my_half,
        other_half,
    )
    return call(
        last_kernel,
        [
            jax.ShapeDtypeStruct(tgt_amp.shape, jnp.float32),
            jax.ShapeDtypeStruct(proj_amp.shape, jnp.float32),
        ],
        [VMEM] * 5,
        [pltpu.VMEM((rows, two_cols), jnp.float32), pltpu.SemaphoreType.DMA((3,))],
        out_spec=HBM,
    )(mine_chip, theirs_chip, high, my_part, other_new)


def solution(mesh):
    in_specs = (
        P(None, "tgt", "rep"),
        P(None, None, "prj", "rep"),
        P(("bpar", "rep")),
        P(("tgt", "prj", "rep")),
        P(("tgt", "rep"), "prj"),
        P("bpar", None),
        P("bpar", None),
        P(("bpar", "tgt", "prj", "rep"), None),
        P(("bpar", "tgt", "rep"), "prj", None),
    )
    out_specs = (P(("bpar", "tgt", "prj", "rep"), None), P(("bpar", "tgt", "rep"), "prj", None))

    def step(*args):
        return tuple(shards(*args))

    return jax.shard_map(step, mesh=mesh, in_specs=in_specs, out_specs=out_specs, check_vma=False)
```

```python
import functools

import jax
import jax.numpy as jnp
from jax import lax
from jax.experimental import pallas as pl
from jax.experimental.pallas import tpu as pltpu
from jax.sharding import PartitionSpec as P

time_step = 0.4
half_step = 0.5 * time_step
VMEM_LIMIT = 8 * 1024 * 1024
DEVICES = ("tgt", "prj", "rep")
HBM = pl.BlockSpec(memory_space=pl.ANY)
VMEM = pl.BlockSpec(memory_space=pltpu.VMEM)


def parity(place):
    even = 1
    while place:
        even, place = even ^ (place & 1), place >> 1
    return even


def my_kind():
    n_tgt, n_prj = lax.axis_size("tgt"), lax.axis_size("prj")
    place = lax.axis_index("tgt") * n_prj + lax.axis_index("prj")
    kind = 1 - lax.axis_index("rep")
    for bit in range((n_tgt * n_prj).bit_length() - 1):
        kind = jnp.bitwise_xor(kind, jnp.bitwise_and(lax.shift_right_logical(place, bit), 1))
    return kind


def by_core(body):
    for core in range(2):

        @pl.when(lax.axis_index("rep") == core)
        def _():
            body(core)


def ordered(core, first, second):
    return jnp.where(core == 0, first, second), jnp.where(core == 0, second, first)


def turned(block):
    half = block.shape[0] // 2
    return jnp.concatenate([block[half:], -block[:half]], axis=0)


def bf16(block):
    return block.astype(jnp.bfloat16)


def f32(block):
    return block.astype(jnp.float32)


def rows_of(bases, segment, amount):
    start = segment % 2 * amount
    return [bases[segment // 2][part, start : start + amount, :] for part in range(2)]


def project(basis, amp):
    return jnp.dot(bf16(amp), basis[0], preferred_element_type=jnp.float32) + jnp.dot(
        bf16(turned(amp)), basis[1], preferred_element_type=jnp.float32
    )


def expand(basis, field):
    contract = (((1,), (1,)), ((), ()))
    return lax.dot_general(
        turned(field), basis[0], contract, preferred_element_type=jnp.float32
    ) + lax.dot_general(field, basis[1], contract, preferred_element_type=jnp.float32)


PIECES = 16

BEHIND = pl.CostEstimate(flops=1 << 35, bytes_accessed=1 << 16, transcendentals=0)


def split(row):
    index = lax.broadcasted_iota(jnp.int32, (PIECES, row.shape[1]), 0)
    block = jnp.zeros(index.shape, jnp.float32)
    for piece in range(3):
        rounded = f32(bf16(row))
        block = jnp.where(index == piece, rounded, block)
        row = row - rounded
    return bf16(block)


def joined(block):
    pieces = f32(block)
    return pieces[0:1] + pieces[1:2] + pieces[2:3]


def basis_copies(bases, sem, my, neighbours, sources):
    rows = sources[my].shape[2]
    place = lax.axis_index(("prj", "tgt")[my])
    copies = []
    for chip, there in enumerate((place, jnp.bitwise_xor(place, neighbours[my]))):
        for core in range(2):
            copies.append(
                pltpu.make_async_copy(
                    sources[my].at[:, 2 * there + core],
                    bases[chip].at[:, core * rows : (core + 1) * rows],
                    sem.at[2 * chip + core],
                )
            )
    return copies


def load_kernel(
    tgt_energy_hbm,
    proj_energy_hbm,
    tgt_own_hbm,
    proj_own_hbm,
    energy,
    amp_ref,
    flat_energy,
    tgt_own,
    proj_own,
    sems,
):
    pairs = [
        (tgt_own_hbm, tgt_own),
        (proj_own_hbm, proj_own),
        (tgt_energy_hbm, flat_energy),
        (proj_energy_hbm, energy.at[1]),
    ]
    copies = [pltpu.make_async_copy(src, dst, sems.at[k]) for k, (src, dst) in enumerate(pairs)]
    for copy in copies:
        copy.start()
    for copy in copies:
        copy.wait()
    energy[0] = flat_energy[...][None, :]
    amp_ref[0] = tgt_own[...].T
    amp_ref[1] = proj_own[0].T


def pack_kernel(amp_ref, tgt_other, proj_other, chip_amp, message):
    my = my_kind()
    other_amp, _ = ordered(my, tgt_other[...].T, proj_other[0].T)
    amps = ordered(lax.axis_index("rep"), amp_ref[my], other_amp)
    for segment in range(2):
        chip_amp[segment] = amps[segment]
        message[segment] = bf16(amps[segment])


def sent_kernel(
    neighbours,
    weight_hbm,
    tgt_hbm,
    proj_hbm,
    chip_amp,
    energy,
    sent_chip,
    sent_far,
    sent_own,
    weight,
    flat_weight,
    sems,
):
    my = my_kind()
    sources = (tgt_hbm, proj_hbm)
    rows = chip_amp.shape[2]

    def copies_of(kind):
        own = pltpu.make_async_copy(
            sources[kind].at[:, 2 * lax.axis_index(("prj", "tgt")[kind]) + 1 - lax.axis_index("rep")],
            sent_own,
            sems.at[4],
        )
        return basis_copies((sent_chip, sent_far), sems, 1 - kind, neighbours, sources) + [own]

    weight_copy = pltpu.make_async_copy(weight_hbm, flat_weight, sems.at[5])
    weight_copy.start()
    for kind in range(2):

        @pl.when(my == kind)
        def _():
            for copy in copies_of(kind):
                copy.start()

    weight_copy.wait()
    weight[0] = flat_weight[...][None, :]
    for part in range(2):
        sent_chip[part, 2 * rows : 2 * rows + PIECES] = split(weight[0])
        sent_chip[part, 2 * rows + PIECES :, :rows] = split(energy[1 - my])
    for copy in copies_of(0):
        copy.wait()


def side_kernel(
    gate_levels,
    neighbours,
    flags_hbm,
    counts_hbm,
    tgt_hbm,
    proj_hbm,
    chip_amp,
    mine_chip,
    mine_far,
    gate,
    flags,
    counts,
    sems,
):
    my = my_kind()
    tgt_index = lax.axis_index("tgt")
    prj_index = lax.axis_index("prj")
    sources = (tgt_hbm, proj_hbm)
    pairs = [(flags_hbm, flags), (counts_hbm, counts)]
    copies = [pltpu.make_async_copy(src, dst, sems.at[4 + k]) for k, (src, dst) in enumerate(pairs)]
    for copy in copies:
        copy.start()
    for kind in range(2):

        @pl.when(my == kind)
        def _():
            for copy in basis_copies((mine_chip, mine_far), sems, kind, neighbours, sources):
                copy.start()

    for copy in copies:
        copy.wait()
    tiles = 2
    width = gate.shape[-1] // tiles
    gate_level = jnp.where(my == 0, *gate_levels)
    for half in range(2):
        for tile in range(tiles):
            live = jnp.logical_and(
                flags[prj_index, tgt_index] > 0, tiles * half + tile < counts[prj_index, tgt_index]
            )
            value = jnp.where(live, 1.0, 0.0).astype(jnp.float32)
            for level in range(gate.shape[0]):
                here = jnp.where(level == gate_level, value, jnp.float32(1.0))
                gate[level, half, :, tile * width : (tile + 1) * width] = jnp.full(
                    (1, width), here, jnp.float32
                )
    for copy in basis_copies((mine_chip, mine_far), sems, 0, neighbours, sources):
        copy.wait()


def chip_kernel(mine_chip, theirs_chip, chip_amp, weight, energy, part_ref, weights, energies):
    mine, theirs = (mine_chip,), (theirs_chip,)
    rows = chip_amp.shape[2]

    def body(core):
        for half, basis in enumerate((mine, theirs) if core == 0 else (theirs, mine)):
            part_ref[half] = sum(
                project(rows_of(basis, segment, rows), chip_amp[segment]) for segment in range(2)
            )
        weights[core] = weight[0]
        weights[1 - core] = joined(theirs_chip[0, 2 * rows : 2 * rows + PIECES, :])
        energies[core] = energy[my_kind()]
        energies[1 - core] = joined(theirs_chip[0, 2 * rows + PIECES :, :rows])

    by_core(body)


def first_kernel(mine_far, theirs_far, gate, weights, part_ref, message, *outs):
    mine, theirs = (None, mine_far), (None, theirs_far)
    rows = message.shape[2]

    def body(core):
        for half, basis in enumerate((mine, theirs) if core == 0 else (theirs, mine)):
            total = part_ref[half] + sum(
                project(rows_of(basis, 2 + segment, rows), f32(message[segment]))
                for segment in range(2)
            )
            outs[half][...] = bf16(gate[0, half] * (weights[half] * total))

    by_core(body)


def add_kernel(level, half, gate, own, other, out_ref):
    out_ref[...] = bf16(gate[level, half] * (f32(own[...]) + f32(other[...])))


def low_kernel(
    mine_chip,
    mine_far,
    theirs_chip,
    theirs_far,
    low,
    low_there,
    chip_amp,
    energies,
    message,
    neighbour_energies,
    states_ref,
):
    mine, theirs = (mine_chip, mine_far), (theirs_chip, theirs_far)
    rows = chip_amp.shape[2]
    field = bf16(f32(low[...]) + f32(low_there[...]))

    def body(core):
        for segment in range(4):
            if segment < 2:
                amp, energy = chip_amp[segment], energies[segment]
            else:
                amp, energy = f32(message[segment - 2]), neighbour_energies[segment - 2]
            change = expand(rows_of((mine, theirs)[core], segment, rows), field)
            states_ref[segment] = amp + half_step * (energy * turned(amp) + change)

    by_core(body)


def second_kernel(
    mine_chip,
    mine_far,
    theirs_chip,
    theirs_far,
    states_ref,
    high,
    high_there,
    gate,
    weights,
    low_ref,
    high_ref,
    half_ref,
    send_ref,
):
    mine, theirs = (mine_chip, mine_far), (theirs_chip, theirs_far)
    rows = states_ref.shape[2]
    field = bf16(f32(high[...]) + f32(high_there[...]))

    def body(core):
        bases = (mine, theirs) if core == 0 else (theirs, mine)
        halves = [
            states_ref[segment] + half_step * expand(rows_of(bases[1], segment, rows), field)
            for segment in range(4)
        ]
        half_ref[...] = halves[core]
        send_ref[...] = halves[1 - core]
        for half, out_ref in enumerate((low_ref, high_ref)):
            total = sum(
                project(rows_of(bases[half], segment, rows), halves[segment]) for segment in range(4)
            )
            out_ref[...] = bf16(gate[0, half] * (weights[half] * total))

    by_core(body)


def late_kernel(
    mine_chip,
    theirs_chip,
    theirs_own,
    sent_chip,
    low,
    high,
    my_low,
    energy,
    amp_ref,
    my_half,
    other_half,
    my_part,
    other_new,
):
    rows = amp_ref.shape[2]

    def body(core):
        my = my_kind()
        near, far = (low, high) if core == 0 else (high, low)
        change = expand(rows_of((sent_chip,), core, rows), near[...]) + expand(
            rows_of((theirs_own,), 0, rows), far[...]
        )
        rate = energy[1 - my] * turned(other_half[...]) + change
        other_new[...] = (amp_ref[1 - my] + time_step * rate).T
        change = expand(rows_of(((mine_chip, theirs_chip)[core],), core, rows), my_low[...])
        my_part[...] = amp_ref[my] + time_step * (energy[my] * turned(my_half[...]) + change)

    by_core(body)


def last_kernel(
    mine_chip, theirs_chip, high, my_part, other_new, new_tgt, new_proj, my_new, sems
):
    cols, rows = my_part.shape
    my = my_kind()
    parts = 2
    size = rows // parts
    outs = (new_tgt, new_proj.at[0])

    def copies(kind):
        return [pltpu.make_async_copy(other_new, outs[1 - kind], sems.at[parts])] + [
            pltpu.make_async_copy(
                my_new.at[pl.ds(part * size, size)], outs[kind].at[pl.ds(part * size, size)], sems.at[part]
            )
            for part in range(parts)
        ]

    def start(number):
        for kind in range(2):

            @pl.when(my == kind)
            def _():
                copies(kind)[number].start()

    def body(core):
        basis = rows_of(((theirs_chip, mine_chip)[core],), core, rows)
        for part in range(parts):
            states = slice(part * size, (part + 1) * size)
            change = expand([block[states] for block in basis], high[...])
            my_new[states, :] = (my_part[:, states] + time_step * change).T
            start(1 + part)

    start(0)
    by_core(body)
    for copy in copies(0):
        copy.wait()


def shards(
    tgt_basis,
    proj_basis,
    quad_weight,
    tgt_energy,
    proj_energy,
    pair_flags,
    tile_counts,
    tgt_amp,
    proj_amp,
):
    points = quad_weight.shape[0]
    rows, two_cols = tgt_amp.shape
    sizes = [lax.axis_size(axis) for axis in DEVICES]

    def call(kernel, out_shape, in_specs, scratch_shapes=(), cost=None, out_spec=VMEM):
        return pl.pallas_call(
            kernel,
            out_shape=out_shape,
            in_specs=in_specs,
            out_specs=[out_spec] * len(out_shape),
            scratch_shapes=scratch_shapes,
            cost_estimate=cost,
            compiler_params=pltpu.CompilerParams(vmem_limit_bytes=VMEM_LIMIT),
        )

    def run(kernel, out_shape, *blocks):
        return call(kernel, out_shape, [VMEM] * len(blocks))(*blocks)

    def other_core(block):
        return lax.ppermute(block, "rep", [(0, 1), (1, 0)])

    n_tgt, n_prj, n_core = sizes
    tgt_flips = [n_prj << bit for bit in range(n_tgt.bit_length() - 1)]
    prj_flips = [1 << bit for bit in range(n_prj.bit_length() - 1)]
    far_first = tgt_flips[::-1]
    flips = (prj_flips + far_first, far_first + prj_flips)
    neighbours = (prj_flips[0], far_first[0] // n_prj)
    gate_levels = (len(prj_flips) - 1, len(tgt_flips) - 1)
    n_steps = len(tgt_flips) + len(prj_flips)

    def exchanged(step, block, crossed=0):
        pairs = []
        for place in range(n_tgt * n_prj):
            for kind in range(2):
                there = place ^ flips[kind][step]
                to_core = kind ^ crossed ^ parity(there)
                pairs.append((place * n_core + (kind ^ parity(place)), there * n_core + to_core))
        return lax.ppermute(block, DEVICES, pairs)

    in_vmem = pltpu.VMEM
    sums = in_vmem((two_cols, points), jnp.bfloat16)
    segment = in_vmem((two_cols, rows), jnp.float32)

    def summed(halves, until):
        totals = []
        for half, block in enumerate(halves):
            for step in range(1, until):
                other = exchanged(step, block)
                (block,) = run(functools.partial(add_kernel, step, half), [sums], gate, block, other)
            totals.append(block)
        return totals

    def swapped(fields):
        return [other_core(block) for block in fields]

    def in_hbm(*blocks):
        return [pltpu.with_memory_space_constraint(block, pltpu.HBM) for block in blocks]

    others = swapped([tgt_amp, proj_amp])
    energy, amp = call(
        load_kernel,
        [in_vmem((2, 1, rows), jnp.float32), in_vmem((2, two_cols, rows), jnp.float32)],
        [HBM] * 4,
        [
            pltpu.VMEM((rows,), jnp.float32),
            pltpu.VMEM(tgt_amp.shape, jnp.float32),
            pltpu.VMEM(proj_amp.shape, jnp.float32),
            pltpu.SemaphoreType.DMA((4,)),
        ],
        pl.CostEstimate(
            flops=2 * 4 * rows * two_cols * points, bytes_accessed=4 * 1024 * 1024, transcendentals=0
        ),
    )(*in_hbm(tgt_energy, proj_energy, tgt_amp, proj_amp))
    chip_amp, message = run(
        pack_kernel,
        [in_vmem((2, two_cols, rows), jnp.float32), in_vmem((2, two_cols, rows), jnp.bfloat16)],
        amp,
        *others,
    )
    message = exchanged(0, message)
    flags, counts = pair_flags.T, tile_counts.T
    bases = in_hbm(tgt_basis.reshape(2, -1, rows, points), proj_basis)
    pair = in_vmem((2, 2 * rows, points), jnp.bfloat16)
    *sent, weight = call(
        functools.partial(sent_kernel, neighbours),
        [
            in_vmem((2, 2 * rows + 2 * PIECES, points), jnp.bfloat16),
            pair,
            in_vmem((2, rows, points), jnp.bfloat16),
            in_vmem((1, 1, points), jnp.float32),
        ],
        [HBM] * 3 + [VMEM] * 2,
        [pltpu.VMEM((points,), jnp.float32), pltpu.SemaphoreType.DMA((6,))],
    )(*in_hbm(quad_weight), *bases, chip_amp, energy)
    mine_chip, mine_far, gate = call(
        functools.partial(side_kernel, gate_levels, neighbours),
        [
            pair,
            pair,
            in_vmem((n_steps, 2, 1, points), jnp.float32),
        ],
        [HBM] * 4 + [VMEM],
        [
            pltpu.SMEM(flags.shape, jnp.int32),
            pltpu.SMEM(counts.shape, jnp.int32),
            pltpu.SemaphoreType.DMA((6,)),
        ],
        BEHIND,
    )(*in_hbm(flags, counts), *bases, chip_amp)
    theirs_chip, theirs_far, theirs_own = swapped(sent)
    bases = (mine_chip, mine_far, theirs_chip, theirs_far)
    part, weights, energies = run(
        chip_kernel,
        [
            in_vmem((2, two_cols, points), jnp.float32),
            in_vmem((2, 1, points), jnp.float32),
            in_vmem((2, 1, rows), jnp.float32),
        ],
        mine_chip,
        theirs_chip,
        chip_amp,
        weight,
        energy,
    )
    halves = run(first_kernel, [sums] * 2, mine_far, theirs_far, gate, weights, part, message)
    (low, high), energies = lax.optimization_barrier((halves, energies))
    neighbour_energies = exchanged(0, energies)
    halves = low, high
    parts = summed(halves, n_steps - 1)
    low, high = [(other_core(block), exchanged(n_steps - 1, block, crossed=1)) for block in parts]
    (states,) = run(
        low_kernel,
        [in_vmem((4, two_cols, rows), jnp.float32)],
        *bases,
        *low,
        chip_amp,
        energies,
        message,
        neighbour_energies,
    )
    *halves, my_half, half_send = run(
        second_kernel,
        [sums, sums, segment, segment],
        *bases,
        states,
        *high,
        gate,
        weights,
    )
    other_half = other_core(half_send)
    fields = summed(halves, n_steps)
    low, high = swapped(fields)
    low, high = swapped(fields)
    my_part, other_new = run(
        late_kernel,
        [segment, in_vmem((rows, two_cols), jnp.float32)],
        mine_chip,
        theirs_chip,
        theirs_own,
        sent[0],
        *fields,
        low,
        energy,
        amp,
        my_half,
        other_half,
    )
    return call(
        last_kernel,
        [
            jax.ShapeDtypeStruct(tgt_amp.shape, jnp.float32),
            jax.ShapeDtypeStruct(proj_amp.shape, jnp.float32),
        ],
        [VMEM] * 5,
        [pltpu.VMEM((rows, two_cols), jnp.float32), pltpu.SemaphoreType.DMA((3,))],
        out_spec=HBM,
    )(mine_chip, theirs_chip, high, my_part, other_new)


def solution(mesh):
    in_specs = (
        P(None, "tgt", "rep"),
        P(None, None, "prj", "rep"),
        P(("bpar", "rep")),
        P(("tgt", "prj", "rep")),
        P(("tgt", "rep"), "prj"),
        P("bpar", None),
        P("bpar", None),
        P(("bpar", "tgt", "prj", "rep"), None),
        P(("bpar", "tgt", "rep"), "prj", None),
    )
    out_specs = (P(("bpar", "tgt", "prj", "rep"), None), P(("bpar", "tgt", "rep"), "prj", None))

    def step(*args):
        return tuple(shards(*args))

    return jax.shard_map(step, mesh=mesh, in_specs=in_specs, out_specs=out_specs, check_vma=False)
```

```python
import functools

import jax
import jax.numpy as jnp
from jax import lax
from jax.experimental import pallas as pl
from jax.experimental.pallas import tpu as pltpu
from jax.sharding import PartitionSpec as P

time_step = 0.4
half_step = 0.5 * time_step
VMEM_LIMIT = 8 * 1024 * 1024
DEVICES = ("tgt", "prj", "rep")
HBM = pl.BlockSpec(memory_space=pl.ANY)
VMEM = pl.BlockSpec(memory_space=pltpu.VMEM)


def parity(place):
    odd = 0
    while place:
        odd, place = odd ^ (place & 1), place >> 1
    return odd


def my_kind():
    n_tgt, n_prj = lax.axis_size("tgt"), lax.axis_size("prj")
    place = lax.axis_index("tgt") * n_prj + lax.axis_index("prj")
    kind = lax.axis_index("rep")
    for bit in range((n_tgt * n_prj).bit_length() - 1):
        kind = jnp.bitwise_xor(kind, jnp.bitwise_and(lax.shift_right_logical(place, bit), 1))
    return kind


def by_core(body):
    for core in range(2):

        @pl.when(lax.axis_index("rep") == core)
        def _():
            body(core)


def ordered(core, first, second):
    return jnp.where(core == 0, first, second), jnp.where(core == 0, second, first)


def turned(block):
    half = block.shape[0] // 2
    return jnp.concatenate([block[half:], -block[:half]], axis=0)


def bf16(block):
    return block.astype(jnp.bfloat16)


def f32(block):
    return block.astype(jnp.float32)


def rows_of(bases, segment, amount):
    start = segment % 2 * amount
    return [bases[segment // 2][part, start : start + amount, :] for part in range(2)]


def project(basis, amp):
    return jnp.dot(bf16(amp), basis[0], preferred_element_type=jnp.float32) + jnp.dot(
        bf16(turned(amp)), basis[1], preferred_element_type=jnp.float32
    )


def expand(basis, field):
    contract = (((1,), (1,)), ((), ()))
    return lax.dot_general(
        turned(field), basis[0], contract, preferred_element_type=jnp.float32
    ) + lax.dot_general(field, basis[1], contract, preferred_element_type=jnp.float32)


PIECES = 16

BEHIND = pl.CostEstimate(flops=1 << 35, bytes_accessed=1 << 16, transcendentals=0)


def split(row):
    index = lax.broadcasted_iota(jnp.int32, (PIECES, row.shape[1]), 0)
    block = jnp.zeros(index.shape, jnp.float32)
    for piece in range(3):
        rounded = f32(bf16(row))
        block = jnp.where(index == piece, rounded, block)
        row = row - rounded
    return bf16(block)


def joined(block):
    pieces = f32(block)
    return pieces[0:1] + pieces[1:2] + pieces[2:3]


def both(basis, rows):
    return basis.at[:, : 2 * rows], basis.at[:, 2 * rows : 4 * rows]


def basis_copies(bases, sem, my, neighbours, sources):
    rows = sources[my].shape[2]
    place = lax.axis_index(("prj", "tgt")[my])
    copies = []
    for chip, there in enumerate((place, jnp.bitwise_xor(place, neighbours[my]))):
        for core in range(2):
            copies.append(
                pltpu.make_async_copy(
                    sources[my].at[:, 2 * there + core],
                    bases[chip].at[:, core * rows : (core + 1) * rows],
                    sem.at[2 * chip + core],
                )
            )
    return copies


def load_kernel(
    tgt_energy_hbm,
    proj_energy_hbm,
    tgt_own_hbm,
    proj_own_hbm,
    energy,
    amp_ref,
    flat_energy,
    tgt_own,
    proj_own,
    sems,
):
    pairs = [
        (tgt_own_hbm, tgt_own),
        (proj_own_hbm, proj_own),
        (tgt_energy_hbm, flat_energy),
        (proj_energy_hbm, energy.at[1]),
    ]
    copies = [pltpu.make_async_copy(src, dst, sems.at[k]) for k, (src, dst) in enumerate(pairs)]
    for copy in copies:
        copy.start()
    for copy in copies:
        copy.wait()
    energy[0] = flat_energy[...][None, :]
    amp_ref[0] = tgt_own[...].T
    amp_ref[1] = proj_own[0].T


def pack_kernel(amp_ref, tgt_other, proj_other, chip_amp, message):
    my = my_kind()
    other_amp, _ = ordered(my, tgt_other[...].T, proj_other[0].T)
    amps = ordered(lax.axis_index("rep"), amp_ref[my], other_amp)
    for segment in range(2):
        chip_amp[segment] = amps[segment]
        message[segment] = bf16(amps[segment])


def sent_kernel(neighbours, weight_hbm, tgt_hbm, proj_hbm, chip_amp, energy, sent, weight, flat_weight, sems):
    my = my_kind()
    sources = (tgt_hbm, proj_hbm)
    rows = chip_amp.shape[2]

    def copies_of(kind):
        return basis_copies(both(sent, rows), sems, 1 - kind, neighbours, sources)

    weight_copy = pltpu.make_async_copy(weight_hbm, flat_weight, sems.at[4])
    weight_copy.start()
    for kind in range(2):

        @pl.when(my == kind)
        def _():
            for copy in copies_of(kind):
                copy.start()

    weight_copy.wait()
    weight[0] = flat_weight[...][None, :]
    for part in range(2):
        sent[part, 4 * rows : 4 * rows + PIECES] = split(weight[0])
        sent[part, 4 * rows + PIECES :, :rows] = split(energy[1 - my])
    for copy in copies_of(0):
        copy.wait()


def side_kernel(
    gate_levels,
    neighbours,
    flags_hbm,
    counts_hbm,
    tgt_hbm,
    proj_hbm,
    chip_amp,
    mine_chip,
    mine_far,
    send_own,
    gate,
    flags,
    counts,
    sems,
):
    my = my_kind()
    tgt_index = lax.axis_index("tgt")
    prj_index = lax.axis_index("prj")
    sources = (tgt_hbm, proj_hbm)
    pairs = [(flags_hbm, flags), (counts_hbm, counts)]
    copies = [pltpu.make_async_copy(src, dst, sems.at[4 + k]) for k, (src, dst) in enumerate(pairs)]
    for copy in copies:
        copy.start()
    for kind in range(2):

        @pl.when(my == kind)
        def _():
            for copy in basis_copies((mine_chip, mine_far), sems, kind, neighbours, sources):
                copy.start()

    for copy in copies:
        copy.wait()
    tiles = 2
    width = gate.shape[-1] // tiles
    gate_level = jnp.where(my == 0, *gate_levels)
    for half in range(2):
        for tile in range(tiles):
            live = jnp.logical_and(
                flags[prj_index, tgt_index] > 0, tiles * half + tile < counts[prj_index, tgt_index]
            )
            value = jnp.where(live, 1.0, 0.0).astype(jnp.float32)
            for level in range(gate.shape[0]):
                here = jnp.where(level == gate_level, value, jnp.float32(1.0))
                gate[level, half, :, tile * width : (tile + 1) * width] = jnp.full(
                    (1, width), here, jnp.float32
                )
    for copy in basis_copies((mine_chip, mine_far), sems, 0, neighbours, sources):
        copy.wait()
    core = lax.axis_index("rep")
    rows = send_own.shape[1]
    for part in range(2):
        send_own[part] = mine_chip[part, pl.ds(pl.multiple_of((1 - core) * rows, rows), rows), :]


def chip_kernel(mine_chip, theirs, chip_amp, weight, energy, part_ref, weights, energies):
    rows = chip_amp.shape[2]
    near, far = (mine_chip,), both(theirs, rows)

    def body(core):
        for half, basis in enumerate((near, far) if core == 0 else (far, near)):
            part_ref[half] = sum(
                project(rows_of(basis, segment, rows), chip_amp[segment]) for segment in range(2)
            )
        weights[core] = weight[0]
        weights[1 - core] = joined(theirs[0, 4 * rows : 4 * rows + PIECES, :])
        energies[core] = energy[my_kind()]
        energies[1 - core] = joined(theirs[0, 4 * rows + PIECES :, :rows])

    by_core(body)


def first_kernel(mine_far, theirs, gate, weights, part_ref, message, *outs):
    rows = message.shape[2]
    near, far = (None, mine_far), both(theirs, rows)

    def body(core):
        for half, basis in enumerate((near, far) if core == 0 else (far, near)):
            total = part_ref[half] + sum(
                project(rows_of(basis, 2 + segment, rows), f32(message[segment]))
                for segment in range(2)
            )
            outs[half][...] = bf16(gate[0, half] * (weights[half] * total))

    by_core(body)


def add_kernel(level, half, gate, own, other, out_ref):
    out_ref[...] = bf16(gate[level, half] * (f32(own[...]) + f32(other[...])))


def low_kernel(
    mine_chip,
    mine_far,
    theirs,
    low,
    low_there,
    chip_amp,
    energies,
    message,
    neighbour_energies,
    states_ref,
):
    rows = chip_amp.shape[2]
    mine, theirs = (mine_chip, mine_far), both(theirs, rows)
    field = bf16(f32(low[...]) + f32(low_there[...]))

    def body(core):
        for segment in range(4):
            if segment < 2:
                amp, energy = chip_amp[segment], energies[segment]
            else:
                amp, energy = f32(message[segment - 2]), neighbour_energies[segment - 2]
            change = expand(rows_of((mine, theirs)[core], segment, rows), field)
            states_ref[segment] = amp + half_step * (energy * turned(amp) + change)

    by_core(body)


def second_kernel(
    mine_chip,
    mine_far,
    theirs,
    states_ref,
    high,
    high_there,
    gate,
    weights,
    low_ref,
    high_ref,
    half_ref,
    send_ref,
):
    rows = states_ref.shape[2]
    mine, theirs = (mine_chip, mine_far), both(theirs, rows)
    field = bf16(f32(high[...]) + f32(high_there[...]))

    def body(core):
        bases = (mine, theirs) if core == 0 else (theirs, mine)
        halves = [
            states_ref[segment] + half_step * expand(rows_of(bases[1], segment, rows), field)
            for segment in range(4)
        ]
        half_ref[...] = halves[core]
        send_ref[...] = halves[1 - core]
        for half, out_ref in enumerate((low_ref, high_ref)):
            total = sum(
                project(rows_of(bases[half], segment, rows), halves[segment]) for segment in range(4)
            )
            out_ref[...] = bf16(gate[0, half] * (weights[half] * total))

    by_core(body)


def late_kernel(
    mine_chip,
    theirs,
    theirs_own,
    sent,
    low,
    high,
    my_low,
    energy,
    amp_ref,
    my_half,
    other_half,
    my_part,
    other_new,
):
    rows = amp_ref.shape[2]

    def body(core):
        my = my_kind()
        near, far = (low, high) if core == 0 else (high, low)
        change = expand(rows_of(both(sent, rows), core, rows), near[...]) + expand(
            rows_of((theirs_own,), 0, rows), far[...]
        )
        rate = energy[1 - my] * turned(other_half[...]) + change
        other_new[...] = (amp_ref[1 - my] + time_step * rate).T
        change = expand(rows_of(((mine_chip,), both(theirs, rows))[core], core, rows), my_low[...])
        my_part[...] = amp_ref[my] + time_step * (energy[my] * turned(my_half[...]) + change)

    by_core(body)


def last_kernel(
    mine_chip, theirs, high, my_part, other_new, new_tgt, new_proj, my_new, sems
):
    cols, rows = my_part.shape
    my = my_kind()
    parts = 2
    size = rows // parts
    outs = (new_tgt, new_proj.at[0])

    def copies(kind):
        return [pltpu.make_async_copy(other_new, outs[1 - kind], sems.at[parts])] + [
            pltpu.make_async_copy(
                my_new.at[pl.ds(part * size, size)], outs[kind].at[pl.ds(part * size, size)], sems.at[part]
            )
            for part in range(parts)
        ]

    def start(number):
        for kind in range(2):

            @pl.when(my == kind)
            def _():
                copies(kind)[number].start()

    def body(core):
        basis = rows_of((both(theirs, rows), (mine_chip,))[core], core, rows)
        for part in range(parts):
            states = slice(part * size, (part + 1) * size)
            change = expand([block[states] for block in basis], high[...])
            my_new[states, :] = (my_part[:, states] + time_step * change).T
            start(1 + part)

    start(0)
    by_core(body)
    for copy in copies(0):
        copy.wait()


def shards(
    tgt_basis,
    proj_basis,
    quad_weight,
    tgt_energy,
    proj_energy,
    pair_flags,
    tile_counts,
    tgt_amp,
    proj_amp,
):
    points = quad_weight.shape[0]
    rows, two_cols = tgt_amp.shape
    sizes = [lax.axis_size(axis) for axis in DEVICES]

    def call(kernel, out_shape, in_specs, scratch_shapes=(), cost=None, out_spec=VMEM):
        return pl.pallas_call(
            kernel,
            out_shape=out_shape,
            in_specs=in_specs,
            out_specs=[out_spec] * len(out_shape),
            scratch_shapes=scratch_shapes,
            cost_estimate=cost,
            compiler_params=pltpu.CompilerParams(vmem_limit_bytes=VMEM_LIMIT),
        )

    def run(kernel, out_shape, *blocks):
        return call(kernel, out_shape, [VMEM] * len(blocks))(*blocks)

    def other_core(block):
        return lax.ppermute(block, "rep", [(0, 1), (1, 0)])

    n_tgt, n_prj, n_core = sizes
    tgt_flips = [n_prj << bit for bit in range(n_tgt.bit_length() - 1)]
    prj_flips = [1 << bit for bit in range(n_prj.bit_length() - 1)]
    far_first = tgt_flips[::-1]
    flips = (prj_flips + far_first, far_first + prj_flips)
    neighbours = (prj_flips[0], far_first[0] // n_prj)
    gate_levels = (len(prj_flips) - 1, len(tgt_flips) - 1)
    n_steps = len(tgt_flips) + len(prj_flips)

    def exchanged(step, block, crossed=0):
        pairs = []
        for place in range(n_tgt * n_prj):
            for kind in range(2):
                there = place ^ flips[kind][step]
                to_core = kind ^ crossed ^ parity(there)
                pairs.append((place * n_core + (kind ^ parity(place)), there * n_core + to_core))
        return lax.ppermute(block, DEVICES, pairs)

    in_vmem = pltpu.VMEM
    sums = in_vmem((two_cols, points), jnp.bfloat16)
    segment = in_vmem((two_cols, rows), jnp.float32)

    def summed(halves, until):
        totals = []
        for half, block in enumerate(halves):
            for step in range(1, until):
                other = exchanged(step, block)
                (block,) = run(functools.partial(add_kernel, step, half), [sums], gate, block, other)
            totals.append(block)
        return totals

    def swapped(fields):
        return [other_core(block) for block in fields]

    def in_hbm(*blocks):
        return [pltpu.with_memory_space_constraint(block, pltpu.HBM) for block in blocks]

    others = swapped([tgt_amp, proj_amp])
    energy, amp = call(
        load_kernel,
        [in_vmem((2, 1, rows), jnp.float32), in_vmem((2, two_cols, rows), jnp.float32)],
        [HBM] * 4,
        [
            pltpu.VMEM((rows,), jnp.float32),
            pltpu.VMEM(tgt_amp.shape, jnp.float32),
            pltpu.VMEM(proj_amp.shape, jnp.float32),
            pltpu.SemaphoreType.DMA((4,)),
        ],
        pl.CostEstimate(
            flops=2 * 4 * rows * two_cols * points, bytes_accessed=4 * 1024 * 1024, transcendentals=0
        ),
    )(*in_hbm(tgt_energy, proj_energy, tgt_amp, proj_amp))
    chip_amp, message = run(
        pack_kernel,
        [in_vmem((2, two_cols, rows), jnp.float32), in_vmem((2, two_cols, rows), jnp.bfloat16)],
        amp,
        *others,
    )
    message = exchanged(0, message)
    flags, counts = pair_flags.T, tile_counts.T
    bases = in_hbm(tgt_basis.reshape(2, -1, rows, points), proj_basis)
    pair = in_vmem((2, 2 * rows, points), jnp.bfloat16)
    sent, weight = call(
        functools.partial(sent_kernel, neighbours),
        [
            in_vmem((2, 4 * rows + 2 * PIECES, points), jnp.bfloat16),
            in_vmem((1, 1, points), jnp.float32),
        ],
        [HBM] * 3 + [VMEM] * 2,
        [pltpu.VMEM((points,), jnp.float32), pltpu.SemaphoreType.DMA((5,))],
    )(*in_hbm(quad_weight), *bases, chip_amp, energy)
    mine_chip, mine_far, send_own, gate = call(
        functools.partial(side_kernel, gate_levels, neighbours),
        [
            pair,
            pair,
            in_vmem((2, rows, points), jnp.bfloat16),
            in_vmem((n_steps, 2, 1, points), jnp.float32),
        ],
        [HBM] * 4 + [VMEM],
        [
            pltpu.SMEM(flags.shape, jnp.int32),
            pltpu.SMEM(counts.shape, jnp.int32),
            pltpu.SemaphoreType.DMA((6,)),
        ],
        BEHIND,
    )(*in_hbm(flags, counts), *bases, chip_amp)
    theirs, theirs_own = swapped([sent, send_own])
    bases = (mine_chip, mine_far, theirs)
    part, weights, energies = run(
        chip_kernel,
        [
            in_vmem((2, two_cols, points), jnp.float32),
            in_vmem((2, 1, points), jnp.float32),
            in_vmem((2, 1, rows), jnp.float32),
        ],
        mine_chip,
        theirs,
        chip_amp,
        weight,
        energy,
    )
    halves = run(first_kernel, [sums] * 2, mine_far, theirs, gate, weights, part, message)
    (low, high), energies = lax.optimization_barrier((halves, energies))
    neighbour_energies = exchanged(0, energies)
    halves = low, high
    parts = summed(halves, n_steps - 1)
    low, high = [(other_core(block), exchanged(n_steps - 1, block, crossed=1)) for block in parts]
    (states,) = run(
        low_kernel,
        [in_vmem((4, two_cols, rows), jnp.float32)],
        *bases,
        *low,
        chip_amp,
        energies,
        message,
        neighbour_energies,
    )
    *halves, my_half, half_send = run(
        second_kernel,
        [sums, sums, segment, segment],
        *bases,
        states,
        *high,
        gate,
        weights,
    )
    other_half = other_core(half_send)
    fields = summed(halves, n_steps)
    low, high = swapped(fields)
    low, high = swapped(fields)
    my_part, other_new = run(
        late_kernel,
        [segment, in_vmem((rows, two_cols), jnp.float32)],
        mine_chip,
        theirs,
        theirs_own,
        sent,
        *fields,
        low,
        energy,
        amp,
        my_half,
        other_half,
    )
    return call(
        last_kernel,
        [
            jax.ShapeDtypeStruct(tgt_amp.shape, jnp.float32),
            jax.ShapeDtypeStruct(proj_amp.shape, jnp.float32),
        ],
        [VMEM] * 5,
        [pltpu.VMEM((rows, two_cols), jnp.float32), pltpu.SemaphoreType.DMA((3,))],
        out_spec=HBM,
    )(mine_chip, theirs, high, my_part, other_new)


def solution(mesh):
    in_specs = (
        P(None, "tgt", "rep"),
        P(None, None, "prj", "rep"),
        P(("bpar", "rep")),
        P(("tgt", "prj", "rep")),
        P(("tgt", "rep"), "prj"),
        P("bpar", None),
        P("bpar", None),
        P(("bpar", "tgt", "prj", "rep"), None),
        P(("bpar", "tgt", "rep"), "prj", None),
    )
    out_specs = (P(("bpar", "tgt", "prj", "rep"), None), P(("bpar", "tgt", "rep"), "prj", None))

    def step(*args):
        return tuple(shards(*args))

    return jax.shard_map(step, mesh=mesh, in_specs=in_specs, out_specs=out_specs, check_vma=False)
```

```python
import functools

import jax
import jax.numpy as jnp
from jax import lax
from jax.experimental import pallas as pl
from jax.experimental.pallas import tpu as pltpu
from jax.sharding import PartitionSpec as P

time_step = 0.4
half_step = 0.5 * time_step
VMEM_LIMIT = 8 * 1024 * 1024
DEVICES = ("tgt", "prj", "rep")
HBM = pl.BlockSpec(memory_space=pl.ANY)
VMEM = pl.BlockSpec(memory_space=pltpu.VMEM)


def parity(place):
    odd = 0
    while place:
        odd, place = odd ^ (place & 1), place >> 1
    return odd


def my_kind():
    n_tgt, n_prj = lax.axis_size("tgt"), lax.axis_size("prj")
    place = lax.axis_index("tgt") * n_prj + lax.axis_index("prj")
    kind = lax.axis_index("rep")
    for bit in range((n_tgt * n_prj).bit_length() - 1):
        kind = jnp.bitwise_xor(kind, jnp.bitwise_and(lax.shift_right_logical(place, bit), 1))
    return kind


def by_core(body):
    for core in range(2):

        @pl.when(lax.axis_index("rep") == core)
        def _():
            body(core)


def ordered(core, first, second):
    return jnp.where(core == 0, first, second), jnp.where(core == 0, second, first)


def turned(block):
    half = block.shape[0] // 2
    return jnp.concatenate([block[half:], -block[:half]], axis=0)


def bf16(block):
    return block.astype(jnp.bfloat16)


def f32(block):
    return block.astype(jnp.float32)


def rows_of(bases, segment, amount):
    start = segment % 2 * amount
    return [bases[segment // 2][part, start : start + amount, :] for part in range(2)]


def project(basis, amp):
    return jnp.dot(bf16(amp), basis[0], preferred_element_type=jnp.float32) + jnp.dot(
        bf16(turned(amp)), basis[1], preferred_element_type=jnp.float32
    )


def expand(basis, field):
    contract = (((1,), (1,)), ((), ()))
    return lax.dot_general(
        turned(field), basis[0], contract, preferred_element_type=jnp.float32
    ) + lax.dot_general(field, basis[1], contract, preferred_element_type=jnp.float32)


PIECES = 16

BEHIND = pl.CostEstimate(flops=1 << 35, bytes_accessed=1 << 16, transcendentals=0)


def split(row):
    index = lax.broadcasted_iota(jnp.int32, (PIECES, row.shape[1]), 0)
    block = jnp.zeros(index.shape, jnp.float32)
    for piece in range(3):
        rounded = f32(bf16(row))
        block = jnp.where(index == piece, rounded, block)
        row = row - rounded
    return bf16(block)


def joined(block):
    pieces = f32(block)
    return pieces[0:1] + pieces[1:2] + pieces[2:3]


def both(basis, rows):
    return basis.at[:, : 2 * rows], basis.at[:, 2 * rows : 4 * rows]


def basis_copies(bases, sem, my, neighbours, sources):
    rows = sources[my].shape[2]
    place = lax.axis_index(("prj", "tgt")[my])
    copies = []
    for chip, there in enumerate((place, jnp.bitwise_xor(place, neighbours[my]))):
        for core in range(2):
            copies.append(
                pltpu.make_async_copy(
                    sources[my].at[:, 2 * there + core],
                    bases[chip].at[:, core * rows : (core + 1) * rows],
                    sem.at[2 * chip + core],
                )
            )
    return copies


def load_kernel(
    tgt_energy_hbm,
    proj_energy_hbm,
    tgt_own_hbm,
    proj_own_hbm,
    energy,
    amp_ref,
    flat_energy,
    tgt_own,
    proj_own,
    sems,
):
    pairs = [
        (tgt_own_hbm, tgt_own),
        (proj_own_hbm, proj_own),
        (tgt_energy_hbm, flat_energy),
        (proj_energy_hbm, energy.at[1]),
    ]
    copies = [pltpu.make_async_copy(src, dst, sems.at[k]) for k, (src, dst) in enumerate(pairs)]
    for copy in copies:
        copy.start()
    for copy in copies:
        copy.wait()
    energy[0] = flat_energy[...][None, :]
    amp_ref[0] = tgt_own[...].T
    amp_ref[1] = proj_own[0].T


def pack_kernel(amp_ref, tgt_other, proj_other, chip_amp, message):
    my = my_kind()
    other_amp, _ = ordered(my, tgt_other[...].T, proj_other[0].T)
    amps = ordered(lax.axis_index("rep"), amp_ref[my], other_amp)
    for segment in range(2):
        chip_amp[segment] = amps[segment]
        message[segment] = bf16(amps[segment])


def sent_kernel(neighbours, weight_hbm, tgt_hbm, proj_hbm, chip_amp, energy, sent, weight, flat_weight, sems):
    my = my_kind()
    sources = (tgt_hbm, proj_hbm)
    rows = chip_amp.shape[2]

    def copies_of(kind):
        return basis_copies(both(sent, rows), sems, 1 - kind, neighbours, sources)

    weight_copy = pltpu.make_async_copy(weight_hbm, flat_weight, sems.at[4])
    weight_copy.start()
    for kind in range(2):

        @pl.when(my == kind)
        def _():
            for copy in copies_of(kind):
                copy.start()

    weight_copy.wait()
    weight[0] = flat_weight[...][None, :]
    for part in range(2):
        sent[part, 4 * rows : 4 * rows + PIECES] = split(weight[0])
        sent[part, 4 * rows + PIECES :, :rows] = split(energy[1 - my])
    for copy in copies_of(0):
        copy.wait()


def side_kernel(
    gate_levels,
    neighbours,
    flags_hbm,
    counts_hbm,
    tgt_hbm,
    proj_hbm,
    chip_amp,
    mine_chip,
    mine_far,
    send_own,
    gate,
    flags,
    counts,
    sems,
):
    my = my_kind()
    tgt_index = lax.axis_index("tgt")
    prj_index = lax.axis_index("prj")
    sources = (tgt_hbm, proj_hbm)
    pairs = [(flags_hbm, flags), (counts_hbm, counts)]
    copies = [pltpu.make_async_copy(src, dst, sems.at[4 + k]) for k, (src, dst) in enumerate(pairs)]
    for copy in copies:
        copy.start()
    for kind in range(2):

        @pl.when(my == kind)
        def _():
            for copy in basis_copies((mine_chip, mine_far), sems, kind, neighbours, sources):
                copy.start()

    for copy in copies:
        copy.wait()
    tiles = 2
    width = gate.shape[-1] // tiles
    gate_level = jnp.where(my == 0, *gate_levels)
    for half in range(2):
        for tile in range(tiles):
            live = jnp.logical_and(
                flags[prj_index, tgt_index] > 0, tiles * half + tile < counts[prj_index, tgt_index]
            )
            value = jnp.where(live, 1.0, 0.0).astype(jnp.float32)
            for level in range(gate.shape[0]):
                here = jnp.where(level == gate_level, value, jnp.float32(1.0))
                gate[level, half, :, tile * width : (tile + 1) * width] = jnp.full(
                    (1, width), here, jnp.float32
                )
    for copy in basis_copies((mine_chip, mine_far), sems, 0, neighbours, sources):
        copy.wait()
    core = lax.axis_index("rep")
    rows = send_own.shape[1]
    for part in range(2):
        send_own[part] = mine_chip[part, pl.ds(pl.multiple_of((1 - core) * rows, rows), rows), :]


def chip_kernel(mine_chip, theirs, chip_amp, weight, energy, part_ref, weights, energies):
    rows = chip_amp.shape[2]
    near, far = (mine_chip,), both(theirs, rows)

    def body(core):
        for half, basis in enumerate((near, far) if core == 0 else (far, near)):
            part_ref[half] = sum(
                project(rows_of(basis, segment, rows), chip_amp[segment]) for segment in range(2)
            )
        weights[core] = weight[0]
        weights[1 - core] = joined(theirs[0, 4 * rows : 4 * rows + PIECES, :])
        energies[core] = energy[my_kind()]
        energies[1 - core] = joined(theirs[0, 4 * rows + PIECES :, :rows])

    by_core(body)


def first_kernel(half, mine_far, theirs, gate, weights, part_ref, message, out_ref):
    rows = message.shape[2]
    near, far = (None, mine_far), (None, both(theirs, rows)[1])

    def body(core):
        basis = near if core == half else far
        total = part_ref[half] + sum(
            project(rows_of(basis, 2 + segment, rows), f32(message[segment])) for segment in range(2)
        )
        out_ref[...] = bf16(gate[0, half] * (weights[half] * total))

    by_core(body)


def add_kernel(level, half, gate, own, other, out_ref):
    out_ref[...] = bf16(gate[level, half] * (f32(own[...]) + f32(other[...])))


def low_kernel(
    mine_chip,
    mine_far,
    theirs,
    low,
    low_there,
    chip_amp,
    energies,
    message,
    neighbour_energies,
    states_ref,
):
    rows = chip_amp.shape[2]
    mine, theirs = (mine_chip, mine_far), both(theirs, rows)
    field = bf16(f32(low[...]) + f32(low_there[...]))

    def body(core):
        for segment in range(4):
            if segment < 2:
                amp, energy = chip_amp[segment], energies[segment]
            else:
                amp, energy = f32(message[segment - 2]), neighbour_energies[segment - 2]
            change = expand(rows_of((mine, theirs)[core], segment, rows), field)
            states_ref[segment] = amp + half_step * (energy * turned(amp) + change)

    by_core(body)


def second_kernel(
    mine_chip,
    mine_far,
    theirs,
    states_ref,
    high,
    high_there,
    gate,
    weights,
    low_ref,
    halves_ref,
    half_ref,
    send_ref,
):
    rows = states_ref.shape[2]
    mine, theirs = (mine_chip, mine_far), both(theirs, rows)
    field = bf16(f32(high[...]) + f32(high_there[...]))

    def body(core):
        bases = (mine, theirs) if core == 0 else (theirs, mine)
        halves = [
            states_ref[segment] + half_step * expand(rows_of(bases[1], segment, rows), field)
            for segment in range(4)
        ]
        total = sum(
            project(rows_of(bases[0], segment, rows), halves[segment]) for segment in range(4)
        )
        low_ref[...] = bf16(gate[0, 0] * (weights[0] * total))
        for segment in range(4):
            halves_ref[segment] = halves[segment]
        half_ref[...] = halves[core]
        send_ref[...] = halves[1 - core]

    by_core(body)


def high_kernel(mine_chip, mine_far, theirs, gate, weights, halves_ref, high_ref):
    rows = halves_ref.shape[2]
    mine, theirs = (mine_chip, mine_far), both(theirs, rows)

    def body(core):
        basis = (theirs, mine)[core]
        total = sum(
            project(rows_of(basis, segment, rows), halves_ref[segment]) for segment in range(4)
        )
        high_ref[...] = bf16(gate[0, 1] * (weights[1] * total))

    by_core(body)


def late_kernel(
    mine_chip,
    theirs,
    theirs_own,
    sent,
    low,
    high,
    my_low,
    energy,
    amp_ref,
    my_half,
    other_half,
    my_part,
    other_new,
):
    rows = amp_ref.shape[2]

    def body(core):
        my = my_kind()
        near, far = (low, high) if core == 0 else (high, low)
        change = expand(rows_of(both(sent, rows), core, rows), near[...]) + expand(
            rows_of((theirs_own,), 0, rows), far[...]
        )
        rate = energy[1 - my] * turned(other_half[...]) + change
        other_new[...] = (amp_ref[1 - my] + time_step * rate).T
        change = expand(rows_of(((mine_chip,), both(theirs, rows))[core], core, rows), my_low[...])
        my_part[...] = amp_ref[my] + time_step * (energy[my] * turned(my_half[...]) + change)

    by_core(body)


def last_kernel(
    mine_chip, theirs, high, my_part, other_new, new_tgt, new_proj, my_new, sems
):
    cols, rows = my_part.shape
    my = my_kind()
    parts = 2
    size = rows // parts
    outs = (new_tgt, new_proj.at[0])

    def copies(kind):
        return [pltpu.make_async_copy(other_new, outs[1 - kind], sems.at[parts])] + [
            pltpu.make_async_copy(
                my_new.at[pl.ds(part * size, size)], outs[kind].at[pl.ds(part * size, size)], sems.at[part]
            )
            for part in range(parts)
        ]

    def start(number):
        for kind in range(2):

            @pl.when(my == kind)
            def _():
                copies(kind)[number].start()

    def body(core):
        basis = rows_of((both(theirs, rows), (mine_chip,))[core], core, rows)
        for part in range(parts):
            states = slice(part * size, (part + 1) * size)
            change = expand([block[states] for block in basis], high[...])
            my_new[states, :] = (my_part[:, states] + time_step * change).T
            start(1 + part)

    start(0)
    by_core(body)
    for copy in copies(0):
        copy.wait()


def shards(
    tgt_basis,
    proj_basis,
    quad_weight,
    tgt_energy,
    proj_energy,
    pair_flags,
    tile_counts,
    tgt_amp,
    proj_amp,
):
    points = quad_weight.shape[0]
    rows, two_cols = tgt_amp.shape
    sizes = [lax.axis_size(axis) for axis in DEVICES]

    def call(kernel, out_shape, in_specs, scratch_shapes=(), cost=None, out_spec=VMEM):
        return pl.pallas_call(
            kernel,
            out_shape=out_shape,
            in_specs=in_specs,
            out_specs=[out_spec] * len(out_shape),
            scratch_shapes=scratch_shapes,
            cost_estimate=cost,
            compiler_params=pltpu.CompilerParams(vmem_limit_bytes=VMEM_LIMIT),
        )

    def run(kernel, out_shape, *blocks):
        return call(kernel, out_shape, [VMEM] * len(blocks))(*blocks)

    def other_core(block):
        return lax.ppermute(block, "rep", [(0, 1), (1, 0)])

    n_tgt, n_prj, n_core = sizes
    tgt_flips = [n_prj << bit for bit in range(n_tgt.bit_length() - 1)]
    prj_flips = [1 << bit for bit in range(n_prj.bit_length() - 1)]
    far_first = tgt_flips[::-1]
    flips = (prj_flips + far_first, far_first + prj_flips)
    neighbours = (prj_flips[0], far_first[0] // n_prj)
    gate_levels = (len(prj_flips) - 1, len(tgt_flips) - 1)
    n_steps = len(tgt_flips) + len(prj_flips)

    def exchanged(step, block, crossed=0):
        pairs = []
        for place in range(n_tgt * n_prj):
            for kind in range(2):
                there = place ^ flips[kind][step]
                to_core = kind ^ crossed ^ parity(there)
                pairs.append((place * n_core + (kind ^ parity(place)), there * n_core + to_core))
        return lax.ppermute(block, DEVICES, pairs)

    in_vmem = pltpu.VMEM
    sums = in_vmem((two_cols, points), jnp.bfloat16)
    segment = in_vmem((two_cols, rows), jnp.float32)

    def summed(halves, until):
        totals = []
        for half, block in enumerate(halves):
            for step in range(1, until):
                other = exchanged(step, block)
                (block,) = run(functools.partial(add_kernel, step, half), [sums], gate, block, other)
            totals.append(block)
        return totals

    def swapped(fields):
        return [other_core(block) for block in fields]

    def in_hbm(*blocks):
        return [pltpu.with_memory_space_constraint(block, pltpu.HBM) for block in blocks]

    others = swapped([tgt_amp, proj_amp])
    energy, amp = call(
        load_kernel,
        [in_vmem((2, 1, rows), jnp.float32), in_vmem((2, two_cols, rows), jnp.float32)],
        [HBM] * 4,
        [
            pltpu.VMEM((rows,), jnp.float32),
            pltpu.VMEM(tgt_amp.shape, jnp.float32),
            pltpu.VMEM(proj_amp.shape, jnp.float32),
            pltpu.SemaphoreType.DMA((4,)),
        ],
        pl.CostEstimate(
            flops=2 * 4 * rows * two_cols * points, bytes_accessed=4 * 1024 * 1024, transcendentals=0
        ),
    )(*in_hbm(tgt_energy, proj_energy, tgt_amp, proj_amp))
    chip_amp, message = run(
        pack_kernel,
        [in_vmem((2, two_cols, rows), jnp.float32), in_vmem((2, two_cols, rows), jnp.bfloat16)],
        amp,
        *others,
    )
    message = exchanged(0, message)
    flags, counts = pair_flags.T, tile_counts.T
    bases = in_hbm(tgt_basis.reshape(2, -1, rows, points), proj_basis)
    pair = in_vmem((2, 2 * rows, points), jnp.bfloat16)
    sent, weight = call(
        functools.partial(sent_kernel, neighbours),
        [
            in_vmem((2, 4 * rows + 2 * PIECES, points), jnp.bfloat16),
            in_vmem((1, 1, points), jnp.float32),
        ],
        [HBM] * 3 + [VMEM] * 2,
        [pltpu.VMEM((points,), jnp.float32), pltpu.SemaphoreType.DMA((5,))],
    )(*in_hbm(quad_weight), *bases, chip_amp, energy)
    mine_chip, mine_far, send_own, gate = call(
        functools.partial(side_kernel, gate_levels, neighbours),
        [
            pair,
            pair,
            in_vmem((2, rows, points), jnp.bfloat16),
            in_vmem((n_steps, 2, 1, points), jnp.float32),
        ],
        [HBM] * 4 + [VMEM],
        [
            pltpu.SMEM(flags.shape, jnp.int32),
            pltpu.SMEM(counts.shape, jnp.int32),
            pltpu.SemaphoreType.DMA((6,)),
        ],
        BEHIND,
    )(*in_hbm(flags, counts), *bases, chip_amp)
    theirs, theirs_own = swapped([sent, send_own])
    bases = (mine_chip, mine_far, theirs)
    part, weights, energies = run(
        chip_kernel,
        [
            in_vmem((2, two_cols, points), jnp.float32),
            in_vmem((2, 1, points), jnp.float32),
            in_vmem((2, 1, rows), jnp.float32),
        ],
        mine_chip,
        theirs,
        chip_amp,
        weight,
        energy,
    )
    halves = [
        run(functools.partial(first_kernel, half), [sums], mine_far, theirs, gate, weights, part, message)[0]
        for half in range(2)
    ]
    neighbour_energies = exchanged(0, energies)
    parts = summed(halves, n_steps - 1)
    low, high = [(other_core(block), exchanged(n_steps - 1, block, crossed=1)) for block in parts]
    (states,) = run(
        low_kernel,
        [in_vmem((4, two_cols, rows), jnp.float32)],
        *bases,
        *low,
        chip_amp,
        energies,
        message,
        neighbour_energies,
    )
    low, states, my_half, half_send = run(
        second_kernel,
        [sums, in_vmem((4, two_cols, rows), jnp.float32), segment, segment],
        *bases,
        states,
        *high,
        gate,
        weights,
    )
    (high,) = run(high_kernel, [sums], *bases, gate, weights, states)
    other_half = other_core(half_send)
    fields = summed((low, high), n_steps)
    low, high = swapped(fields)
    low, high = swapped(fields)
    my_part, other_new = run(
        late_kernel,
        [segment, in_vmem((rows, two_cols), jnp.float32)],
        mine_chip,
        theirs,
        theirs_own,
        sent,
        *fields,
        low,
        energy,
        amp,
        my_half,
        other_half,
    )
    return call(
        last_kernel,
        [
            jax.ShapeDtypeStruct(tgt_amp.shape, jnp.float32),
            jax.ShapeDtypeStruct(proj_amp.shape, jnp.float32),
        ],
        [VMEM] * 5,
        [pltpu.VMEM((rows, two_cols), jnp.float32), pltpu.SemaphoreType.DMA((3,))],
        out_spec=HBM,
    )(mine_chip, theirs, high, my_part, other_new)


def solution(mesh):
    in_specs = (
        P(None, "tgt", "rep"),
        P(None, None, "prj", "rep"),
        P(("bpar", "rep")),
        P(("tgt", "prj", "rep")),
        P(("tgt", "rep"), "prj"),
        P("bpar", None),
        P("bpar", None),
        P(("bpar", "tgt", "prj", "rep"), None),
        P(("bpar", "tgt", "rep"), "prj", None),
    )
    out_specs = (P(("bpar", "tgt", "prj", "rep"), None), P(("bpar", "tgt", "rep"), "prj", None))

    def step(*args):
        return tuple(shards(*args))

    return jax.shard_map(step, mesh=mesh, in_specs=in_specs, out_specs=out_specs, check_vma=False)
```

```python
import functools

import jax
import jax.numpy as jnp
from jax import lax
from jax.experimental import pallas as pl
from jax.experimental.pallas import tpu as pltpu
from jax.sharding import PartitionSpec as P

time_step = 0.4
half_step = 0.5 * time_step
VMEM_LIMIT = 8 * 1024 * 1024
DEVICES = ("tgt", "prj", "rep")
HBM = pl.BlockSpec(memory_space=pl.ANY)
VMEM = pl.BlockSpec(memory_space=pltpu.VMEM)


def parity(place):
    odd = 0
    while place:
        odd, place = odd ^ (place & 1), place >> 1
    return odd


def my_kind():
    n_tgt, n_prj = lax.axis_size("tgt"), lax.axis_size("prj")
    place = lax.axis_index("tgt") * n_prj + lax.axis_index("prj")
    kind = lax.axis_index("rep")
    for bit in range((n_tgt * n_prj).bit_length() - 1):
        kind = jnp.bitwise_xor(kind, jnp.bitwise_and(lax.shift_right_logical(place, bit), 1))
    return kind


def by_core(body):
    for core in range(2):

        @pl.when(lax.axis_index("rep") == core)
        def _():
            body(core)


def ordered(core, first, second):
    return jnp.where(core == 0, first, second), jnp.where(core == 0, second, first)


def turned(block):
    half = block.shape[0] // 2
    return jnp.concatenate([block[half:], -block[:half]], axis=0)


def bf16(block):
    return block.astype(jnp.bfloat16)


def f32(block):
    return block.astype(jnp.float32)


def rows_of(bases, segment, amount):
    start = segment % 2 * amount
    return [bases[segment // 2][part, start : start + amount, :] for part in range(2)]


def project(basis, amp):
    return jnp.dot(bf16(amp), basis[0], preferred_element_type=jnp.float32) + jnp.dot(
        bf16(turned(amp)), basis[1], preferred_element_type=jnp.float32
    )


def expand(basis, field):
    contract = (((1,), (1,)), ((), ()))
    return lax.dot_general(
        turned(field), basis[0], contract, preferred_element_type=jnp.float32
    ) + lax.dot_general(field, basis[1], contract, preferred_element_type=jnp.float32)


PIECES = 16

BEHIND = pl.CostEstimate(flops=1 << 35, bytes_accessed=1 << 16, transcendentals=0)


def split(row):
    index = lax.broadcasted_iota(jnp.int32, (PIECES, row.shape[1]), 0)
    block = jnp.zeros(index.shape, jnp.float32)
    for piece in range(3):
        rounded = f32(bf16(row))
        block = jnp.where(index == piece, rounded, block)
        row = row - rounded
    return bf16(block)


def joined(block):
    pieces = f32(block)
    return pieces[0:1] + pieces[1:2] + pieces[2:3]


def both(basis, rows):
    return basis.at[:, : 2 * rows], basis.at[:, 2 * rows : 4 * rows]


def basis_copies(bases, sem, my, neighbours, sources):
    rows = sources[my].shape[2]
    place = lax.axis_index(("prj", "tgt")[my])
    copies = []
    for chip, there in enumerate((place, jnp.bitwise_xor(place, neighbours[my]))):
        for core in range(2):
            copies.append(
                pltpu.make_async_copy(
                    sources[my].at[:, 2 * there + core],
                    bases[chip].at[:, core * rows : (core + 1) * rows],
                    sem.at[2 * chip + core],
                )
            )
    return copies


def load_kernel(
    tgt_energy_hbm,
    proj_energy_hbm,
    tgt_own_hbm,
    proj_own_hbm,
    energy,
    amp_ref,
    flat_energy,
    tgt_own,
    proj_own,
    sems,
):
    pairs = [
        (tgt_own_hbm, tgt_own),
        (proj_own_hbm, proj_own),
        (tgt_energy_hbm, flat_energy),
        (proj_energy_hbm, energy.at[1]),
    ]
    copies = [pltpu.make_async_copy(src, dst, sems.at[k]) for k, (src, dst) in enumerate(pairs)]
    for copy in copies:
        copy.start()
    for copy in copies:
        copy.wait()
    energy[0] = flat_energy[...][None, :]
    amp_ref[0] = tgt_own[...].T
    amp_ref[1] = proj_own[0].T


def pack_kernel(amp_ref, tgt_other, proj_other, chip_amp, message):
    my = my_kind()
    other_amp, _ = ordered(my, tgt_other[...].T, proj_other[0].T)
    amps = ordered(lax.axis_index("rep"), amp_ref[my], other_amp)
    for segment in range(2):
        chip_amp[segment] = amps[segment]
        message[segment] = bf16(amps[segment])


def sent_kernel(neighbours, weight_hbm, tgt_hbm, proj_hbm, chip_amp, energy, sent, weight, flat_weight, sems):
    my = my_kind()
    sources = (tgt_hbm, proj_hbm)
    rows = chip_amp.shape[2]

    def copies_of(kind):
        return basis_copies(both(sent, rows), sems, 1 - kind, neighbours, sources)

    weight_copy = pltpu.make_async_copy(weight_hbm, flat_weight, sems.at[4])
    weight_copy.start()
    for kind in range(2):

        @pl.when(my == kind)
        def _():
            for copy in copies_of(kind):
                copy.start()

    weight_copy.wait()
    weight[0] = flat_weight[...][None, :]
    for part in range(2):
        sent[part, 4 * rows : 4 * rows + PIECES] = split(weight[0])
        sent[part, 4 * rows + PIECES :, :rows] = split(energy[1 - my])
    for copy in copies_of(0):
        copy.wait()


def side_kernel(
    gate_levels,
    neighbours,
    flags_hbm,
    counts_hbm,
    tgt_hbm,
    proj_hbm,
    chip_amp,
    mine_chip,
    mine_far,
    send_own,
    gate,
    flags,
    counts,
    sems,
):
    my = my_kind()
    tgt_index = lax.axis_index("tgt")
    prj_index = lax.axis_index("prj")
    sources = (tgt_hbm, proj_hbm)
    pairs = [(flags_hbm, flags), (counts_hbm, counts)]
    copies = [pltpu.make_async_copy(src, dst, sems.at[4 + k]) for k, (src, dst) in enumerate(pairs)]
    for copy in copies:
        copy.start()
    for kind in range(2):

        @pl.when(my == kind)
        def _():
            for copy in basis_copies((mine_chip, mine_far), sems, kind, neighbours, sources):
                copy.start()

    for copy in copies:
        copy.wait()
    tiles = 2
    width = gate.shape[-1] // tiles
    gate_level = jnp.where(my == 0, *gate_levels)
    for half in range(2):
        for tile in range(tiles):
            live = jnp.logical_and(
                flags[prj_index, tgt_index] > 0, tiles * half + tile < counts[prj_index, tgt_index]
            )
            value = jnp.where(live, 1.0, 0.0).astype(jnp.float32)
            for level in range(gate.shape[0]):
                here = jnp.where(level == gate_level, value, jnp.float32(1.0))
                gate[level, half, :, tile * width : (tile + 1) * width] = jnp.full(
                    (1, width), here, jnp.float32
                )
    for copy in basis_copies((mine_chip, mine_far), sems, 0, neighbours, sources):
        copy.wait()
    core = lax.axis_index("rep")
    rows = send_own.shape[1]
    for part in range(2):
        send_own[part] = mine_chip[part, pl.ds(pl.multiple_of((1 - core) * rows, rows), rows), :]


def chip_kernel(mine_chip, theirs, chip_amp, weight, energy, part_ref, weights, energies):
    rows = chip_amp.shape[2]
    near, far = (mine_chip,), both(theirs, rows)

    def body(core):
        for half, basis in enumerate((near, far) if core == 0 else (far, near)):
            part_ref[half] = sum(
                project(rows_of(basis, segment, rows), chip_amp[segment]) for segment in range(2)
            )
        weights[core] = weight[0]
        weights[1 - core] = joined(theirs[0, 4 * rows : 4 * rows + PIECES, :])
        energies[core] = energy[my_kind()]
        energies[1 - core] = joined(theirs[0, 4 * rows + PIECES :, :rows])

    by_core(body)


def first_kernel(mine_far, theirs, gate, weights, part_ref, message, *outs):
    rows = message.shape[2]
    near, far = (None, mine_far), both(theirs, rows)

    def body(core):
        for half, basis in enumerate((near, far) if core == 0 else (far, near)):
            total = part_ref[half] + sum(
                project(rows_of(basis, 2 + segment, rows), f32(message[segment]))
                for segment in range(2)
            )
            outs[half][...] = bf16(gate[0, half] * (weights[half] * total))

    by_core(body)


def add_kernel(level, half, gate, own, other, out_ref):
    out_ref[...] = bf16(gate[level, half] * (f32(own[...]) + f32(other[...])))


def low_kernel(
    mine_chip,
    mine_far,
    theirs,
    low,
    low_there,
    chip_amp,
    energies,
    message,
    neighbour_energies,
    states_ref,
):
    rows = chip_amp.shape[2]
    mine, theirs = (mine_chip, mine_far), both(theirs, rows)
    field = bf16(f32(low[...]) + f32(low_there[...]))

    def body(core):
        for segment in range(4):
            if segment < 2:
                amp, energy = chip_amp[segment], energies[segment]
            else:
                amp, energy = f32(message[segment - 2]), neighbour_energies[segment - 2]
            change = expand(rows_of((mine, theirs)[core], segment, rows), field)
            states_ref[segment] = amp + half_step * (energy * turned(amp) + change)

    by_core(body)


def second_kernel(
    mine_chip,
    mine_far,
    theirs,
    states_ref,
    high,
    high_there,
    gate,
    weights,
    low_ref,
    high_ref,
    half_ref,
    send_ref,
):
    rows = states_ref.shape[2]
    mine, theirs = (mine_chip, mine_far), both(theirs, rows)
    field = bf16(f32(high[...]) + f32(high_there[...]))

    def body(core):
        bases = (mine, theirs) if core == 0 else (theirs, mine)
        halves = [
            states_ref[segment] + half_step * expand(rows_of(bases[1], segment, rows), field)
            for segment in range(4)
        ]
        half_ref[...] = halves[core]
        send_ref[...] = halves[1 - core]
        for half, out_ref in enumerate((low_ref, high_ref)):
            total = sum(
                project(rows_of(bases[half], segment, rows), halves[segment]) for segment in range(4)
            )
            out_ref[...] = bf16(gate[0, half] * (weights[half] * total))

    by_core(body)


def late_kernel(
    mine_chip,
    theirs,
    theirs_own,
    sent,
    low,
    high,
    my_low,
    energy,
    amp_ref,
    my_half,
    other_half,
    my_part,
    other_new,
):
    rows = amp_ref.shape[2]

    def body(core):
        my = my_kind()
        near, far = (low, high) if core == 0 else (high, low)
        change = expand(rows_of(both(sent, rows), core, rows), near[...]) + expand(
            rows_of((theirs_own,), 0, rows), far[...]
        )
        rate = energy[1 - my] * turned(other_half[...]) + change
        other_new[...] = (amp_ref[1 - my] + time_step * rate).T
        change = expand(rows_of(((mine_chip,), both(theirs, rows))[core], core, rows), my_low[...])
        my_part[...] = amp_ref[my] + time_step * (energy[my] * turned(my_half[...]) + change)

    by_core(body)


def last_kernel(
    mine_chip, theirs, high, my_part, other_new, new_tgt, new_proj, my_new, sems
):
    cols, rows = my_part.shape
    my = my_kind()
    parts = 2
    size = rows // parts
    outs = (new_tgt, new_proj.at[0])

    def copies(kind):
        return [pltpu.make_async_copy(other_new, outs[1 - kind], sems.at[parts])] + [
            pltpu.make_async_copy(
                my_new.at[pl.ds(part * size, size)], outs[kind].at[pl.ds(part * size, size)], sems.at[part]
            )
            for part in range(parts)
        ]

    def start(number):
        for kind in range(2):

            @pl.when(my == kind)
            def _():
                copies(kind)[number].start()

    def body(core):
        basis = rows_of((both(theirs, rows), (mine_chip,))[core], core, rows)
        for part in range(parts):
            states = slice(part * size, (part + 1) * size)
            change = expand([block[states] for block in basis], high[...])
            my_new[states, :] = (my_part[:, states] + time_step * change).T
            start(1 + part)

    start(0)
    by_core(body)
    for copy in copies(0):
        copy.wait()


def shards(
    tgt_basis,
    proj_basis,
    quad_weight,
    tgt_energy,
    proj_energy,
    pair_flags,
    tile_counts,
    tgt_amp,
    proj_amp,
):
    points = quad_weight.shape[0]
    rows, two_cols = tgt_amp.shape
    sizes = [lax.axis_size(axis) for axis in DEVICES]

    def call(kernel, out_shape, in_specs, scratch_shapes=(), cost=None, out_spec=VMEM):
        return pl.pallas_call(
            kernel,
            out_shape=out_shape,
            in_specs=in_specs,
            out_specs=[out_spec] * len(out_shape),
            scratch_shapes=scratch_shapes,
            cost_estimate=cost,
            compiler_params=pltpu.CompilerParams(vmem_limit_bytes=VMEM_LIMIT),
        )

    def run(kernel, out_shape, *blocks):
        return call(kernel, out_shape, [VMEM] * len(blocks))(*blocks)

    def other_core(block):
        return lax.ppermute(block, "rep", [(0, 1), (1, 0)])

    n_tgt, n_prj, n_core = sizes
    tgt_flips = [n_prj << bit for bit in range(n_tgt.bit_length() - 1)]
    prj_flips = [1 << bit for bit in range(n_prj.bit_length() - 1)]
    far_first = tgt_flips[::-1]
    flips = [(prj_flips + order, far_first + prj_flips) for order in (far_first, tgt_flips)]
    neighbours = (prj_flips[0], far_first[0] // n_prj)
    gate_levels = (len(prj_flips) - 1, len(tgt_flips) - 1)
    n_steps = len(tgt_flips) + len(prj_flips)

    def exchanged(step, block, rate=0, crossed=0):
        pairs = []
        for place in range(n_tgt * n_prj):
            for kind in range(2):
                there = place ^ flips[rate][kind][step]
                to_core = kind ^ crossed ^ parity(there)
                pairs.append((place * n_core + (kind ^ parity(place)), there * n_core + to_core))
        return lax.ppermute(block, DEVICES, pairs)

    in_vmem = pltpu.VMEM
    sums = in_vmem((two_cols, points), jnp.bfloat16)
    segment = in_vmem((two_cols, rows), jnp.float32)

    def summed(halves, until, rate):
        totals = []
        for half, block in enumerate(halves):
            for step in range(1, until):
                other = exchanged(step, block, rate)
                (block,) = run(functools.partial(add_kernel, step, half), [sums], gate, block, other)
            totals.append(block)
        return totals

    def swapped(fields):
        return [other_core(block) for block in fields]

    def in_hbm(*blocks):
        return [pltpu.with_memory_space_constraint(block, pltpu.HBM) for block in blocks]

    others = swapped([tgt_amp, proj_amp])
    energy, amp = call(
        load_kernel,
        [in_vmem((2, 1, rows), jnp.float32), in_vmem((2, two_cols, rows), jnp.float32)],
        [HBM] * 4,
        [
            pltpu.VMEM((rows,), jnp.float32),
            pltpu.VMEM(tgt_amp.shape, jnp.float32),
            pltpu.VMEM(proj_amp.shape, jnp.float32),
            pltpu.SemaphoreType.DMA((4,)),
        ],
        pl.CostEstimate(
            flops=2 * 4 * rows * two_cols * points, bytes_accessed=4 * 1024 * 1024, transcendentals=0
        ),
    )(*in_hbm(tgt_energy, proj_energy, tgt_amp, proj_amp))
    chip_amp, message = run(
        pack_kernel,
        [in_vmem((2, two_cols, rows), jnp.float32), in_vmem((2, two_cols, rows), jnp.bfloat16)],
        amp,
        *others,
    )
    message = exchanged(0, message)
    flags, counts = pair_flags.T, tile_counts.T
    bases = in_hbm(tgt_basis.reshape(2, -1, rows, points), proj_basis)
    pair = in_vmem((2, 2 * rows, points), jnp.bfloat16)
    sent, weight = call(
        functools.partial(sent_kernel, neighbours),
        [
            in_vmem((2, 4 * rows + 2 * PIECES, points), jnp.bfloat16),
            in_vmem((1, 1, points), jnp.float32),
        ],
        [HBM] * 3 + [VMEM] * 2,
        [pltpu.VMEM((points,), jnp.float32), pltpu.SemaphoreType.DMA((5,))],
    )(*in_hbm(quad_weight), *bases, chip_amp, energy)
    mine_chip, mine_far, send_own, gate = call(
        functools.partial(side_kernel, gate_levels, neighbours),
        [
            pair,
            pair,
            in_vmem((2, rows, points), jnp.bfloat16),
            in_vmem((n_steps, 2, 1, points), jnp.float32),
        ],
        [HBM] * 4 + [VMEM],
        [
            pltpu.SMEM(flags.shape, jnp.int32),
            pltpu.SMEM(counts.shape, jnp.int32),
            pltpu.SemaphoreType.DMA((6,)),
        ],
        BEHIND,
    )(*in_hbm(flags, counts), *bases, chip_amp)
    theirs, theirs_own = swapped([sent, send_own])
    bases = (mine_chip, mine_far, theirs)
    part, weights, energies = run(
        chip_kernel,
        [
            in_vmem((2, two_cols, points), jnp.float32),
            in_vmem((2, 1, points), jnp.float32),
            in_vmem((2, 1, rows), jnp.float32),
        ],
        mine_chip,
        theirs,
        chip_amp,
        weight,
        energy,
    )
    halves = run(first_kernel, [sums] * 2, mine_far, theirs, gate, weights, part, message)
    (low, high), energies = lax.optimization_barrier((halves, energies))
    neighbour_energies = exchanged(0, energies)
    halves = low, high
    parts = summed(halves, n_steps - 1, 0)
    low, high = [(other_core(block), exchanged(n_steps - 1, block, crossed=1)) for block in parts]
    (states,) = run(
        low_kernel,
        [in_vmem((4, two_cols, rows), jnp.float32)],
        *bases,
        *low,
        chip_amp,
        energies,
        message,
        neighbour_energies,
    )
    *halves, my_half, half_send = run(
        second_kernel,
        [sums, sums, segment, segment],
        *bases,
        states,
        *high,
        gate,
        weights,
    )
    other_half = other_core(half_send)
    fields = summed(halves, n_steps, 1)
    low, high = swapped(fields)
    low, high = swapped(fields)
    my_part, other_new = run(
        late_kernel,
        [segment, in_vmem((rows, two_cols), jnp.float32)],
        mine_chip,
        theirs,
        theirs_own,
        sent,
        *fields,
        low,
        energy,
        amp,
        my_half,
        other_half,
    )
    return call(
        last_kernel,
        [
            jax.ShapeDtypeStruct(tgt_amp.shape, jnp.float32),
            jax.ShapeDtypeStruct(proj_amp.shape, jnp.float32),
        ],
        [VMEM] * 5,
        [pltpu.VMEM((rows, two_cols), jnp.float32), pltpu.SemaphoreType.DMA((3,))],
        out_spec=HBM,
    )(mine_chip, theirs, high, my_part, other_new)


def solution(mesh):
    in_specs = (
        P(None, "tgt", "rep"),
        P(None, None, "prj", "rep"),
        P(("bpar", "rep")),
        P(("tgt", "prj", "rep")),
        P(("tgt", "rep"), "prj"),
        P("bpar", None),
        P("bpar", None),
        P(("bpar", "tgt", "prj", "rep"), None),
        P(("bpar", "tgt", "rep"), "prj", None),
    )
    out_specs = (P(("bpar", "tgt", "prj", "rep"), None), P(("bpar", "tgt", "rep"), "prj", None))

    def step(*args):
        return tuple(shards(*args))

    return jax.shard_map(step, mesh=mesh, in_specs=in_specs, out_specs=out_specs, check_vma=False)
```

```python
import functools

import jax
import jax.numpy as jnp
from jax import lax
from jax.experimental import pallas as pl
from jax.experimental.pallas import tpu as pltpu
from jax.sharding import PartitionSpec as P

time_step = 0.4
half_step = 0.5 * time_step
VMEM_LIMIT = 8 * 1024 * 1024
DEVICES = ("tgt", "prj", "rep")
HBM = pl.BlockSpec(memory_space=pl.ANY)
VMEM = pl.BlockSpec(memory_space=pltpu.VMEM)


def parity(place):
    odd = 0
    while place:
        odd, place = odd ^ (place & 1), place >> 1
    return odd


def my_kind():
    n_tgt, n_prj = lax.axis_size("tgt"), lax.axis_size("prj")
    place = lax.axis_index("tgt") * n_prj + lax.axis_index("prj")
    kind = lax.axis_index("rep")
    for bit in range((n_tgt * n_prj).bit_length() - 1):
        kind = jnp.bitwise_xor(kind, jnp.bitwise_and(lax.shift_right_logical(place, bit), 1))
    return kind


def by_core(body):
    for core in range(2):

        @pl.when(lax.axis_index("rep") == core)
        def _():
            body(core)


def ordered(core, first, second):
    return jnp.where(core == 0, first, second), jnp.where(core == 0, second, first)


def turned(block):
    half = block.shape[0] // 2
    return jnp.concatenate([block[half:], -block[:half]], axis=0)


def bf16(block):
    return block.astype(jnp.bfloat16)


def f32(block):
    return block.astype(jnp.float32)


def rows_of(bases, segment, amount):
    start = segment % 2 * amount
    return [bases[segment // 2][part, start : start + amount, :] for part in range(2)]


def project(basis, amp):
    return jnp.dot(bf16(amp), basis[0], preferred_element_type=jnp.float32) + jnp.dot(
        bf16(turned(amp)), basis[1], preferred_element_type=jnp.float32
    )


def expand(basis, field):
    contract = (((1,), (1,)), ((), ()))
    return lax.dot_general(
        turned(field), basis[0], contract, preferred_element_type=jnp.float32
    ) + lax.dot_general(field, basis[1], contract, preferred_element_type=jnp.float32)


PIECES = 16

EVEN = pl.CostEstimate(flops=1 << 32, bytes_accessed=1 << 16, transcendentals=0)
BEHIND = pl.CostEstimate(flops=1 << 35, bytes_accessed=1 << 16, transcendentals=0)


def split(row):
    index = lax.broadcasted_iota(jnp.int32, (PIECES, row.shape[1]), 0)
    block = jnp.zeros(index.shape, jnp.float32)
    for piece in range(3):
        rounded = f32(bf16(row))
        block = jnp.where(index == piece, rounded, block)
        row = row - rounded
    return bf16(block)


def joined(block):
    pieces = f32(block)
    return pieces[0:1] + pieces[1:2] + pieces[2:3]


def both(basis, rows):
    return basis.at[:, : 2 * rows], basis.at[:, 2 * rows : 4 * rows]


def basis_copies(bases, sem, my, neighbours, sources):
    rows = sources[my].shape[2]
    place = lax.axis_index(("prj", "tgt")[my])
    copies = []
    for chip, there in enumerate((place, jnp.bitwise_xor(place, neighbours[my]))):
        for core in range(2):
            copies.append(
                pltpu.make_async_copy(
                    sources[my].at[:, 2 * there + core],
                    bases[chip].at[:, core * rows : (core + 1) * rows],
                    sem.at[2 * chip + core],
                )
            )
    return copies


def load_kernel(
    tgt_energy_hbm,
    proj_energy_hbm,
    tgt_own_hbm,
    proj_own_hbm,
    energy,
    amp_ref,
    flat_energy,
    tgt_own,
    proj_own,
    sems,
):
    pairs = [
        (tgt_own_hbm, tgt_own),
        (proj_own_hbm, proj_own),
        (tgt_energy_hbm, flat_energy),
        (proj_energy_hbm, energy.at[1]),
    ]
    copies = [pltpu.make_async_copy(src, dst, sems.at[k]) for k, (src, dst) in enumerate(pairs)]
    for copy in copies:
        copy.start()
    for copy in copies:
        copy.wait()
    energy[0] = flat_energy[...][None, :]
    amp_ref[0] = tgt_own[...].T
    amp_ref[1] = proj_own[0].T


def pack_kernel(amp_ref, tgt_other, proj_other, chip_amp, message):
    my = my_kind()
    other_amp, _ = ordered(my, tgt_other[...].T, proj_other[0].T)
    amps = ordered(lax.axis_index("rep"), amp_ref[my], other_amp)
    for segment in range(2):
        chip_amp[segment] = amps[segment]
        message[segment] = bf16(amps[segment])


def sent_kernel(neighbours, weight_hbm, tgt_hbm, proj_hbm, chip_amp, energy, sent, weight, flat_weight, sems):
    my = my_kind()
    sources = (tgt_hbm, proj_hbm)
    rows = chip_amp.shape[2]

    def copies_of(kind):
        return basis_copies(both(sent, rows), sems, 1 - kind, neighbours, sources)

    weight_copy = pltpu.make_async_copy(weight_hbm, flat_weight, sems.at[4])
    weight_copy.start()
    for kind in range(2):

        @pl.when(my == kind)
        def _():
            for copy in copies_of(kind):
                copy.start()

    weight_copy.wait()
    weight[0] = flat_weight[...][None, :]
    for part in range(2):
        sent[part, 4 * rows : 4 * rows + PIECES] = split(weight[0])
        sent[part, 4 * rows + PIECES :, :rows] = split(energy[1 - my])
    for copy in copies_of(0):
        copy.wait()


def side_kernel(
    gate_levels,
    neighbours,
    flags_hbm,
    counts_hbm,
    tgt_hbm,
    proj_hbm,
    chip_amp,
    mine_chip,
    mine_far,
    send_own,
    gate,
    flags,
    counts,
    sems,
):
    my = my_kind()
    tgt_index = lax.axis_index("tgt")
    prj_index = lax.axis_index("prj")
    sources = (tgt_hbm, proj_hbm)
    pairs = [(flags_hbm, flags), (counts_hbm, counts)]
    copies = [pltpu.make_async_copy(src, dst, sems.at[4 + k]) for k, (src, dst) in enumerate(pairs)]
    for copy in copies:
        copy.start()
    for kind in range(2):

        @pl.when(my == kind)
        def _():
            for copy in basis_copies((mine_chip, mine_far), sems, kind, neighbours, sources):
                copy.start()

    for copy in copies:
        copy.wait()
    tiles = 2
    width = gate.shape[-1] // tiles
    gate_level = jnp.where(my == 0, *gate_levels)
    for half in range(2):
        for tile in range(tiles):
            live = jnp.logical_and(
                flags[prj_index, tgt_index] > 0, tiles * half + tile < counts[prj_index, tgt_index]
            )
            value = jnp.where(live, 1.0, 0.0).astype(jnp.float32)
            for level in range(gate.shape[0]):
                here = jnp.where(level == gate_level, value, jnp.float32(1.0))
                gate[level, half, :, tile * width : (tile + 1) * width] = jnp.full(
                    (1, width), here, jnp.float32
                )
    for copy in basis_copies((mine_chip, mine_far), sems, 0, neighbours, sources):
        copy.wait()
    core = lax.axis_index("rep")
    rows = send_own.shape[1]
    for part in range(2):
        send_own[part] = mine_chip[part, pl.ds(pl.multiple_of((1 - core) * rows, rows), rows), :]


def chip_kernel(mine_chip, theirs, chip_amp, weight, energy, part_ref, weights, energies):
    rows = chip_amp.shape[2]
    near, far = (mine_chip,), both(theirs, rows)

    def body(core):
        for half, basis in enumerate((near, far) if core == 0 else (far, near)):
            part_ref[half] = sum(
                project(rows_of(basis, segment, rows), chip_amp[segment]) for segment in range(2)
            )
        weights[core] = weight[0]
        weights[1 - core] = joined(theirs[0, 4 * rows : 4 * rows + PIECES, :])
        energies[core] = energy[my_kind()]
        energies[1 - core] = joined(theirs[0, 4 * rows + PIECES :, :rows])

    by_core(body)


def first_kernel(mine_far, theirs, gate, weights, part_ref, message, *outs):
    rows = message.shape[2]
    near, far = (None, mine_far), both(theirs, rows)

    def body(core):
        for half, basis in enumerate((near, far) if core == 0 else (far, near)):
            total = part_ref[half] + sum(
                project(rows_of(basis, 2 + segment, rows), f32(message[segment]))
                for segment in range(2)
            )
            outs[half][...] = bf16(gate[0, half] * (weights[half] * total))

    by_core(body)


def add_kernel(level, half, gate, own, other, *rest):
    out_ref = rest[-1]
    out_ref[...] = bf16(gate[level, half] * (f32(own[...]) + f32(other[...])))


def low_kernel(
    mine_chip,
    mine_far,
    theirs,
    low,
    low_there,
    chip_amp,
    energies,
    message,
    neighbour_energies,
    states_ref,
):
    rows = chip_amp.shape[2]
    mine, theirs = (mine_chip, mine_far), both(theirs, rows)
    field = bf16(f32(low[...]) + f32(low_there[...]))

    def body(core):
        for segment in range(4):
            if segment < 2:
                amp, energy = chip_amp[segment], energies[segment]
            else:
                amp, energy = f32(message[segment - 2]), neighbour_energies[segment - 2]
            change = expand(rows_of((mine, theirs)[core], segment, rows), field)
            states_ref[segment] = amp + half_step * (energy * turned(amp) + change)

    by_core(body)


def second_kernel(
    mine_chip,
    mine_far,
    theirs,
    states_ref,
    high,
    high_there,
    gate,
    weights,
    low_ref,
    high_ref,
    half_ref,
    send_ref,
):
    rows = states_ref.shape[2]
    mine, theirs = (mine_chip, mine_far), both(theirs, rows)
    field = bf16(f32(high[...]) + f32(high_there[...]))

    def body(core):
        bases = (mine, theirs) if core == 0 else (theirs, mine)
        halves = [
            states_ref[segment] + half_step * expand(rows_of(bases[1], segment, rows), field)
            for segment in range(4)
        ]
        half_ref[...] = halves[core]
        send_ref[...] = halves[1 - core]
        for half, out_ref in enumerate((low_ref, high_ref)):
            total = sum(
                project(rows_of(bases[half], segment, rows), halves[segment]) for segment in range(4)
            )
            out_ref[...] = bf16(gate[0, half] * (weights[half] * total))

    by_core(body)


def late_kernel(
    mine_chip,
    theirs,
    theirs_own,
    sent,
    low,
    high,
    my_low,
    energy,
    amp_ref,
    my_half,
    other_half,
    my_part,
    other_new,
):
    rows = amp_ref.shape[2]

    def body(core):
        my = my_kind()
        near, far = (low, high) if core == 0 else (high, low)
        change = expand(rows_of(both(sent, rows), core, rows), near[...]) + expand(
            rows_of((theirs_own,), 0, rows), far[...]
        )
        rate = energy[1 - my] * turned(other_half[...]) + change
        other_new[...] = (amp_ref[1 - my] + time_step * rate).T
        change = expand(rows_of(((mine_chip,), both(theirs, rows))[core], core, rows), my_low[...])
        my_part[...] = amp_ref[my] + time_step * (energy[my] * turned(my_half[...]) + change)

    by_core(body)


def last_kernel(
    mine_chip, theirs, high, my_part, other_new, new_tgt, new_proj, my_new, sems
):
    cols, rows = my_part.shape
    my = my_kind()
    parts = 2
    size = rows // parts
    outs = (new_tgt, new_proj.at[0])

    def copies(kind):
        return [pltpu.make_async_copy(other_new, outs[1 - kind], sems.at[parts])] + [
            pltpu.make_async_copy(
                my_new.at[pl.ds(part * size, size)], outs[kind].at[pl.ds(part * size, size)], sems.at[part]
            )
            for part in range(parts)
        ]

    def start(number):
        for kind in range(2):

            @pl.when(my == kind)
            def _():
                copies(kind)[number].start()

    def body(core):
        basis = rows_of((both(theirs, rows), (mine_chip,))[core], core, rows)
        for part in range(parts):
            states = slice(part * size, (part + 1) * size)
            change = expand([block[states] for block in basis], high[...])
            my_new[states, :] = (my_part[:, states] + time_step * change).T
            start(1 + part)

    start(0)
    by_core(body)
    for copy in copies(0):
        copy.wait()


def shards(
    tgt_basis,
    proj_basis,
    quad_weight,
    tgt_energy,
    proj_energy,
    pair_flags,
    tile_counts,
    tgt_amp,
    proj_amp,
):
    points = quad_weight.shape[0]
    rows, two_cols = tgt_amp.shape
    sizes = [lax.axis_size(axis) for axis in DEVICES]

    def call(kernel, out_shape, in_specs, scratch_shapes=(), cost=None, out_spec=VMEM):
        return pl.pallas_call(
            kernel,
            out_shape=out_shape,
            in_specs=in_specs,
            out_specs=[out_spec] * len(out_shape),
            scratch_shapes=scratch_shapes,
            cost_estimate=cost,
            compiler_params=pltpu.CompilerParams(vmem_limit_bytes=VMEM_LIMIT),
        )

    def run(kernel, out_shape, *blocks):
        return call(kernel, out_shape, [VMEM] * len(blocks))(*blocks)

    def other_core(block):
        return lax.ppermute(block, "rep", [(0, 1), (1, 0)])

    n_tgt, n_prj, n_core = sizes
    tgt_flips = [n_prj << bit for bit in range(n_tgt.bit_length() - 1)]
    prj_flips = [1 << bit for bit in range(n_prj.bit_length() - 1)]
    far_first = tgt_flips[::-1]
    flips = (prj_flips + far_first, far_first + prj_flips)
    neighbours = (prj_flips[0], far_first[0] // n_prj)
    gate_levels = (len(prj_flips) - 1, len(tgt_flips) - 1)
    n_steps = len(tgt_flips) + len(prj_flips)

    def exchanged(step, block, crossed=0):
        pairs = []
        for place in range(n_tgt * n_prj):
            for kind in range(2):
                there = place ^ flips[kind][step]
                to_core = kind ^ crossed ^ parity(there)
                pairs.append((place * n_core + (kind ^ parity(place)), there * n_core + to_core))
        return lax.ppermute(block, DEVICES, pairs)

    in_vmem = pltpu.VMEM
    sums = in_vmem((two_cols, points), jnp.bfloat16)
    segment = in_vmem((two_cols, rows), jnp.float32)

    def summed(halves, until, *ahead):
        totals = []
        for half, block in enumerate(halves):
            for step in range(1, until):
                other = exchanged(step, block)
                kernel = functools.partial(add_kernel, step, half)
                blocks = [gate, block, other] + (list(ahead) if half and step == 1 else [])
                cost = EVEN if half else None
                (block,) = call(kernel, [sums], [VMEM] * len(blocks), cost=cost)(*blocks)
            totals.append(block)
        return totals

    def swapped(fields):
        return [other_core(block) for block in fields]

    def in_hbm(*blocks):
        return [pltpu.with_memory_space_constraint(block, pltpu.HBM) for block in blocks]

    others = swapped([tgt_amp, proj_amp])
    energy, amp = call(
        load_kernel,
        [in_vmem((2, 1, rows), jnp.float32), in_vmem((2, two_cols, rows), jnp.float32)],
        [HBM] * 4,
        [
            pltpu.VMEM((rows,), jnp.float32),
            pltpu.VMEM(tgt_amp.shape, jnp.float32),
            pltpu.VMEM(proj_amp.shape, jnp.float32),
            pltpu.SemaphoreType.DMA((4,)),
        ],
        pl.CostEstimate(
            flops=2 * 4 * rows * two_cols * points, bytes_accessed=4 * 1024 * 1024, transcendentals=0
        ),
    )(*in_hbm(tgt_energy, proj_energy, tgt_amp, proj_amp))
    chip_amp, message = run(
        pack_kernel,
        [in_vmem((2, two_cols, rows), jnp.float32), in_vmem((2, two_cols, rows), jnp.bfloat16)],
        amp,
        *others,
    )
    message = exchanged(0, message)
    flags, counts = pair_flags.T, tile_counts.T
    bases = in_hbm(tgt_basis.reshape(2, -1, rows, points), proj_basis)
    pair = in_vmem((2, 2 * rows, points), jnp.bfloat16)
    sent, weight = call(
        functools.partial(sent_kernel, neighbours),
        [
            in_vmem((2, 4 * rows + 2 * PIECES, points), jnp.bfloat16),
            in_vmem((1, 1, points), jnp.float32),
        ],
        [HBM] * 3 + [VMEM] * 2,
        [pltpu.VMEM((points,), jnp.float32), pltpu.SemaphoreType.DMA((5,))],
    )(*in_hbm(quad_weight), *bases, chip_amp, energy)
    mine_chip, mine_far, send_own, gate = call(
        functools.partial(side_kernel, gate_levels, neighbours),
        [
            pair,
            pair,
            in_vmem((2, rows, points), jnp.bfloat16),
            in_vmem((n_steps, 2, 1, points), jnp.float32),
        ],
        [HBM] * 4 + [VMEM],
        [
            pltpu.SMEM(flags.shape, jnp.int32),
            pltpu.SMEM(counts.shape, jnp.int32),
            pltpu.SemaphoreType.DMA((6,)),
        ],
        BEHIND,
    )(*in_hbm(flags, counts), *bases, chip_amp)
    theirs, theirs_own = swapped([sent, send_own])
    bases = (mine_chip, mine_far, theirs)
    part, weights, energies = run(
        chip_kernel,
        [
            in_vmem((2, two_cols, points), jnp.float32),
            in_vmem((2, 1, points), jnp.float32),
            in_vmem((2, 1, rows), jnp.float32),
        ],
        mine_chip,
        theirs,
        chip_amp,
        weight,
        energy,
    )
    halves = run(first_kernel, [sums] * 2, mine_far, theirs, gate, weights, part, message)
    (low, high), energies = lax.optimization_barrier((halves, energies))
    neighbour_energies = exchanged(0, energies)
    halves = low, high
    parts = summed(halves, n_steps - 1, neighbour_energies)
    low, high = [(other_core(block), exchanged(n_steps - 1, block, crossed=1)) for block in parts]
    (states,) = run(
        low_kernel,
        [in_vmem((4, two_cols, rows), jnp.float32)],
        *bases,
        *low,
        chip_amp,
        energies,
        message,
        neighbour_energies,
    )
    *halves, my_half, half_send = run(
        second_kernel,
        [sums, sums, segment, segment],
        *bases,
        states,
        *high,
        gate,
        weights,
    )
    fields = summed(halves, n_steps)
    fields[0], half_send = lax.optimization_barrier((fields[0], half_send))
    other_half = other_core(half_send)
    low, high = swapped(fields)
    low, high = swapped(fields)
    my_part, other_new = run(
        late_kernel,
        [segment, in_vmem((rows, two_cols), jnp.float32)],
        mine_chip,
        theirs,
        theirs_own,
        sent,
        *fields,
        low,
        energy,
        amp,
        my_half,
        other_half,
    )
    return call(
        last_kernel,
        [
            jax.ShapeDtypeStruct(tgt_amp.shape, jnp.float32),
            jax.ShapeDtypeStruct(proj_amp.shape, jnp.float32),
        ],
        [VMEM] * 5,
        [pltpu.VMEM((rows, two_cols), jnp.float32), pltpu.SemaphoreType.DMA((3,))],
        out_spec=HBM,
    )(mine_chip, theirs, high, my_part, other_new)


def solution(mesh):
    in_specs = (
        P(None, "tgt", "rep"),
        P(None, None, "prj", "rep"),
        P(("bpar", "rep")),
        P(("tgt", "prj", "rep")),
        P(("tgt", "rep"), "prj"),
        P("bpar", None),
        P("bpar", None),
        P(("bpar", "tgt", "prj", "rep"), None),
        P(("bpar", "tgt", "rep"), "prj", None),
    )
    out_specs = (P(("bpar", "tgt", "prj", "rep"), None), P(("bpar", "tgt", "rep"), "prj", None))

    def step(*args):
        return tuple(shards(*args))

    return jax.shard_map(step, mesh=mesh, in_specs=in_specs, out_specs=out_specs, check_vma=False)
```

```python
import functools

import jax
import jax.numpy as jnp
from jax import lax
from jax.experimental import pallas as pl
from jax.experimental.pallas import tpu as pltpu
from jax.sharding import PartitionSpec as P

time_step = 0.4
half_step = 0.5 * time_step
VMEM_LIMIT = 8 * 1024 * 1024
DEVICES = ("tgt", "prj", "rep")
HBM = pl.BlockSpec(memory_space=pl.ANY)
VMEM = pl.BlockSpec(memory_space=pltpu.VMEM)


def parity(place):
    odd = 0
    while place:
        odd, place = odd ^ (place & 1), place >> 1
    return odd


def my_kind():
    n_tgt, n_prj = lax.axis_size("tgt"), lax.axis_size("prj")
    place = lax.axis_index("tgt") * n_prj + lax.axis_index("prj")
    kind = lax.axis_index("rep")
    for bit in range((n_tgt * n_prj).bit_length() - 1):
        kind = jnp.bitwise_xor(kind, jnp.bitwise_and(lax.shift_right_logical(place, bit), 1))
    return kind


def by_core(body):
    for core in range(2):

        @pl.when(lax.axis_index("rep") == core)
        def _():
            body(core)


def ordered(core, first, second):
    return jnp.where(core == 0, first, second), jnp.where(core == 0, second, first)


def turned(block):
    half = block.shape[0] // 2
    return jnp.concatenate([block[half:], -block[:half]], axis=0)


def bf16(block):
    return block.astype(jnp.bfloat16)


def f32(block):
    return block.astype(jnp.float32)


def rows_of(bases, segment, amount):
    start = segment % 2 * amount
    return [bases[segment // 2][part, start : start + amount, :] for part in range(2)]


def project(basis, amp):
    return jnp.dot(bf16(amp), basis[0], preferred_element_type=jnp.float32) + jnp.dot(
        bf16(turned(amp)), basis[1], preferred_element_type=jnp.float32
    )


def expand(basis, field):
    contract = (((1,), (1,)), ((), ()))
    return lax.dot_general(
        turned(field), basis[0], contract, preferred_element_type=jnp.float32
    ) + lax.dot_general(field, basis[1], contract, preferred_element_type=jnp.float32)


PIECES = 16

EVEN = pl.CostEstimate(flops=1 << 32, bytes_accessed=1 << 16, transcendentals=0)
BEHIND = pl.CostEstimate(flops=1 << 35, bytes_accessed=1 << 16, transcendentals=0)


def split(row):
    index = lax.broadcasted_iota(jnp.int32, (PIECES, row.shape[1]), 0)
    block = jnp.zeros(index.shape, jnp.float32)
    for piece in range(3):
        rounded = f32(bf16(row))
        block = jnp.where(index == piece, rounded, block)
        row = row - rounded
    return bf16(block)


def joined(block):
    pieces = f32(block)
    return pieces[0:1] + pieces[1:2] + pieces[2:3]


def both(basis, rows):
    return basis.at[:, : 2 * rows], basis.at[:, 2 * rows : 4 * rows]


def basis_copies(bases, sem, my, neighbours, sources):
    rows = sources[my].shape[2]
    place = lax.axis_index(("prj", "tgt")[my])
    copies = []
    for chip, there in enumerate((place, jnp.bitwise_xor(place, neighbours[my]))):
        for core in range(2):
            copies.append(
                pltpu.make_async_copy(
                    sources[my].at[:, 2 * there + core],
                    bases[chip].at[:, core * rows : (core + 1) * rows],
                    sem.at[2 * chip + core],
                )
            )
    return copies


def load_kernel(
    tgt_energy_hbm,
    proj_energy_hbm,
    tgt_own_hbm,
    proj_own_hbm,
    energy,
    amp_ref,
    flat_energy,
    tgt_own,
    proj_own,
    sems,
):
    pairs = [
        (tgt_own_hbm, tgt_own),
        (proj_own_hbm, proj_own),
        (tgt_energy_hbm, flat_energy),
        (proj_energy_hbm, energy.at[1]),
    ]
    copies = [pltpu.make_async_copy(src, dst, sems.at[k]) for k, (src, dst) in enumerate(pairs)]
    for copy in copies:
        copy.start()
    for copy in copies:
        copy.wait()
    energy[0] = flat_energy[...][None, :]
    amp_ref[0] = tgt_own[...].T
    amp_ref[1] = proj_own[0].T


def pack_kernel(amp_ref, tgt_other, proj_other, chip_amp, message):
    my = my_kind()
    other_amp, _ = ordered(my, tgt_other[...].T, proj_other[0].T)
    amps = ordered(lax.axis_index("rep"), amp_ref[my], other_amp)
    for segment in range(2):
        chip_amp[segment] = amps[segment]
        message[segment] = bf16(amps[segment])


def sent_kernel(neighbours, weight_hbm, tgt_hbm, proj_hbm, chip_amp, energy, sent, weight, flat_weight, sems):
    my = my_kind()
    sources = (tgt_hbm, proj_hbm)
    rows = chip_amp.shape[2]

    def copies_of(kind):
        return basis_copies(both(sent, rows), sems, 1 - kind, neighbours, sources)

    weight_copy = pltpu.make_async_copy(weight_hbm, flat_weight, sems.at[4])
    weight_copy.start()
    for kind in range(2):

        @pl.when(my == kind)
        def _():
            for copy in copies_of(kind):
                copy.start()

    weight_copy.wait()
    weight[0] = flat_weight[...][None, :]
    for part in range(2):
        sent[part, 4 * rows : 4 * rows + PIECES] = split(weight[0])
        sent[part, 4 * rows + PIECES :, :rows] = split(energy[1 - my])
    for copy in copies_of(0):
        copy.wait()


def side_kernel(
    gate_levels,
    neighbours,
    flags_hbm,
    counts_hbm,
    tgt_hbm,
    proj_hbm,
    chip_amp,
    mine_chip,
    mine_far,
    send_own,
    gate,
    flags,
    counts,
    sems,
):
    my = my_kind()
    tgt_index = lax.axis_index("tgt")
    prj_index = lax.axis_index("prj")
    sources = (tgt_hbm, proj_hbm)
    pairs = [(flags_hbm, flags), (counts_hbm, counts)]
    copies = [pltpu.make_async_copy(src, dst, sems.at[4 + k]) for k, (src, dst) in enumerate(pairs)]
    for copy in copies:
        copy.start()
    for kind in range(2):

        @pl.when(my == kind)
        def _():
            for copy in basis_copies((mine_chip, mine_far), sems, kind, neighbours, sources):
                copy.start()

    for copy in copies:
        copy.wait()
    tiles = 2
    width = gate.shape[-1] // tiles
    gate_level = jnp.where(my == 0, *gate_levels)
    for half in range(2):
        for tile in range(tiles):
            live = jnp.logical_and(
                flags[prj_index, tgt_index] > 0, tiles * half + tile < counts[prj_index, tgt_index]
            )
            value = jnp.where(live, 1.0, 0.0).astype(jnp.float32)
            for level in range(gate.shape[0]):
                here = jnp.where(level == gate_level, value, jnp.float32(1.0))
                gate[level, half, :, tile * width : (tile + 1) * width] = jnp.full(
                    (1, width), here, jnp.float32
                )
    for copy in basis_copies((mine_chip, mine_far), sems, 0, neighbours, sources):
        copy.wait()
    core = lax.axis_index("rep")
    rows = send_own.shape[1]
    for part in range(2):
        send_own[part] = mine_chip[part, pl.ds(pl.multiple_of((1 - core) * rows, rows), rows), :]


def chip_kernel(mine_chip, theirs, chip_amp, weight, energy, part_ref, weights, energies):
    rows = chip_amp.shape[2]
    near, far = (mine_chip,), both(theirs, rows)

    def body(core):
        for half, basis in enumerate((near, far) if core == 0 else (far, near)):
            part_ref[half] = sum(
                project(rows_of(basis, segment, rows), chip_amp[segment]) for segment in range(2)
            )
        weights[core] = weight[0]
        weights[1 - core] = joined(theirs[0, 4 * rows : 4 * rows + PIECES, :])
        energies[core] = energy[my_kind()]
        energies[1 - core] = joined(theirs[0, 4 * rows + PIECES :, :rows])

    by_core(body)


def first_kernel(mine_far, theirs, gate, weights, part_ref, message, *outs):
    rows = message.shape[2]
    near, far = (None, mine_far), both(theirs, rows)

    def body(core):
        for half, basis in enumerate((near, far) if core == 0 else (far, near)):
            total = part_ref[half] + sum(
                project(rows_of(basis, 2 + segment, rows), f32(message[segment]))
                for segment in range(2)
            )
            outs[half][...] = bf16(gate[0, half] * (weights[half] * total))

    by_core(body)


def add_kernel(level, half, gate, own, other, *rest):
    out_ref = rest[-1]
    out_ref[...] = bf16(gate[level, half] * (f32(own[...]) + f32(other[...])))


def low_kernel(
    mine_chip,
    mine_far,
    theirs,
    low,
    low_there,
    chip_amp,
    energies,
    message,
    neighbour_energies,
    states_ref,
):
    rows = chip_amp.shape[2]
    mine, theirs = (mine_chip, mine_far), both(theirs, rows)
    field = bf16(f32(low[...]) + f32(low_there[...]))

    def body(core):
        for segment in range(4):
            if segment < 2:
                amp, energy = chip_amp[segment], energies[segment]
            else:
                amp, energy = f32(message[segment - 2]), neighbour_energies[segment - 2]
            change = expand(rows_of((mine, theirs)[core], segment, rows), field)
            states_ref[segment] = amp + half_step * (energy * turned(amp) + change)

    by_core(body)


def second_kernel(
    mine_chip,
    mine_far,
    theirs,
    states_ref,
    high,
    high_there,
    gate,
    weights,
    low_ref,
    high_ref,
    half_ref,
    send_ref,
):
    rows = states_ref.shape[2]
    mine, theirs = (mine_chip, mine_far), both(theirs, rows)
    field = bf16(f32(high[...]) + f32(high_there[...]))

    def body(core):
        bases = (mine, theirs) if core == 0 else (theirs, mine)
        halves = [
            states_ref[segment] + half_step * expand(rows_of(bases[1], segment, rows), field)
            for segment in range(4)
        ]
        half_ref[...] = halves[core]
        send_ref[...] = halves[1 - core]
        for half, out_ref in enumerate((low_ref, high_ref)):
            total = sum(
                project(rows_of(bases[half], segment, rows), halves[segment]) for segment in range(4)
            )
            out_ref[...] = bf16(gate[0, half] * (weights[half] * total))

    by_core(body)


def late_kernel(
    mine_chip,
    theirs,
    theirs_own,
    sent,
    low,
    high,
    my_low,
    energy,
    amp_ref,
    my_half,
    other_half,
    my_part,
    other_new,
):
    rows = amp_ref.shape[2]

    def body(core):
        my = my_kind()
        near, far = (low, high) if core == 0 else (high, low)
        change = expand(rows_of(both(sent, rows), core, rows), near[...]) + expand(
            rows_of((theirs_own,), 0, rows), far[...]
        )
        rate = energy[1 - my] * turned(other_half[...]) + change
        other_new[...] = (amp_ref[1 - my] + time_step * rate).T
        change = expand(rows_of(((mine_chip,), both(theirs, rows))[core], core, rows), my_low[...])
        my_part[...] = amp_ref[my] + time_step * (energy[my] * turned(my_half[...]) + change)

    by_core(body)


def last_kernel(
    mine_chip, theirs, high, my_part, other_new, new_tgt, new_proj, my_new, sems
):
    cols, rows = my_part.shape
    my = my_kind()
    parts = 2
    size = rows // parts
    outs = (new_tgt, new_proj.at[0])

    def copies(kind):
        return [pltpu.make_async_copy(other_new, outs[1 - kind], sems.at[parts])] + [
            pltpu.make_async_copy(
                my_new.at[pl.ds(part * size, size)], outs[kind].at[pl.ds(part * size, size)], sems.at[part]
            )
            for part in range(parts)
        ]

    def start(number):
        for kind in range(2):

            @pl.when(my == kind)
            def _():
                copies(kind)[number].start()

    def body(core):
        basis = rows_of((both(theirs, rows), (mine_chip,))[core], core, rows)
        for part in range(parts):
            states = slice(part * size, (part + 1) * size)
            change = expand([block[states] for block in basis], high[...])
            my_new[states, :] = (my_part[:, states] + time_step * change).T
            start(1 + part)

    start(0)
    by_core(body)
    for copy in copies(0):
        copy.wait()


def shards(
    tgt_basis,
    proj_basis,
    quad_weight,
    tgt_energy,
    proj_energy,
    pair_flags,
    tile_counts,
    tgt_amp,
    proj_amp,
):
    points = quad_weight.shape[0]
    rows, two_cols = tgt_amp.shape
    sizes = [lax.axis_size(axis) for axis in DEVICES]

    def call(kernel, out_shape, in_specs, scratch_shapes=(), cost=None, out_spec=VMEM):
        return pl.pallas_call(
            kernel,
            out_shape=out_shape,
            in_specs=in_specs,
            out_specs=[out_spec] * len(out_shape),
            scratch_shapes=scratch_shapes,
            cost_estimate=cost,
            compiler_params=pltpu.CompilerParams(vmem_limit_bytes=VMEM_LIMIT),
        )

    def run(kernel, out_shape, *blocks):
        return call(kernel, out_shape, [VMEM] * len(blocks))(*blocks)

    def other_core(block):
        return lax.ppermute(block, "rep", [(0, 1), (1, 0)])

    n_tgt, n_prj, n_core = sizes
    tgt_flips = [n_prj << bit for bit in range(n_tgt.bit_length() - 1)]
    prj_flips = [1 << bit for bit in range(n_prj.bit_length() - 1)]
    far_first = tgt_flips[::-1]
    flips = (prj_flips + far_first, far_first + prj_flips)
    neighbours = (prj_flips[0], far_first[0] // n_prj)
    gate_levels = (len(prj_flips) - 1, len(tgt_flips) - 1)
    n_steps = len(tgt_flips) + len(prj_flips)

    def exchanged(step, block, crossed=0):
        pairs = []
        for place in range(n_tgt * n_prj):
            for kind in range(2):
                there = place ^ flips[kind][step]
                to_core = kind ^ crossed ^ parity(there)
                pairs.append((place * n_core + (kind ^ parity(place)), there * n_core + to_core))
        return lax.ppermute(block, DEVICES, pairs)

    in_vmem = pltpu.VMEM
    sums = in_vmem((two_cols, points), jnp.bfloat16)
    segment = in_vmem((two_cols, rows), jnp.float32)

    def summed(halves, until, *ahead):
        totals = []
        for half, block in enumerate(halves):
            for step in range(1, until):
                other = exchanged(step, block)
                kernel = functools.partial(add_kernel, step, half)
                blocks = [gate, block, other] + (list(ahead) if half and step == 1 else [])
                cost = EVEN if half else None
                (block,) = call(kernel, [sums], [VMEM] * len(blocks), cost=cost)(*blocks)
            totals.append(block)
        return totals

    def swapped(fields):
        return [other_core(block) for block in fields]

    def in_hbm(*blocks):
        return [pltpu.with_memory_space_constraint(block, pltpu.HBM) for block in blocks]

    others = swapped([tgt_amp, proj_amp])
    energy, amp = call(
        load_kernel,
        [in_vmem((2, 1, rows), jnp.float32), in_vmem((2, two_cols, rows), jnp.float32)],
        [HBM] * 4,
        [
            pltpu.VMEM((rows,), jnp.float32),
            pltpu.VMEM(tgt_amp.shape, jnp.float32),
            pltpu.VMEM(proj_amp.shape, jnp.float32),
            pltpu.SemaphoreType.DMA((4,)),
        ],
        pl.CostEstimate(
            flops=2 * 4 * rows * two_cols * points, bytes_accessed=4 * 1024 * 1024, transcendentals=0
        ),
    )(*in_hbm(tgt_energy, proj_energy, tgt_amp, proj_amp))
    chip_amp, message = run(
        pack_kernel,
        [in_vmem((2, two_cols, rows), jnp.float32), in_vmem((2, two_cols, rows), jnp.bfloat16)],
        amp,
        *others,
    )
    message = exchanged(0, message)
    flags, counts = pair_flags.T, tile_counts.T
    bases = in_hbm(tgt_basis.reshape(2, -1, rows, points), proj_basis)
    pair = in_vmem((2, 2 * rows, points), jnp.bfloat16)
    sent, weight = call(
        functools.partial(sent_kernel, neighbours),
        [
            in_vmem((2, 4 * rows + 2 * PIECES, points), jnp.bfloat16),
            in_vmem((1, 1, points), jnp.float32),
        ],
        [HBM] * 3 + [VMEM] * 2,
        [pltpu.VMEM((points,), jnp.float32), pltpu.SemaphoreType.DMA((5,))],
    )(*in_hbm(quad_weight), *bases, chip_amp, energy)
    mine_chip, mine_far, send_own, gate = call(
        functools.partial(side_kernel, gate_levels, neighbours),
        [
            pair,
            pair,
            in_vmem((2, rows, points), jnp.bfloat16),
            in_vmem((n_steps, 2, 1, points), jnp.float32),
        ],
        [HBM] * 4 + [VMEM],
        [
            pltpu.SMEM(flags.shape, jnp.int32),
            pltpu.SMEM(counts.shape, jnp.int32),
            pltpu.SemaphoreType.DMA((6,)),
        ],
        BEHIND,
    )(*in_hbm(flags, counts), *bases, chip_amp)
    theirs = other_core(sent)
    bases = (mine_chip, mine_far, theirs)
    part, weights, energies = run(
        chip_kernel,
        [
            in_vmem((2, two_cols, points), jnp.float32),
            in_vmem((2, 1, points), jnp.float32),
            in_vmem((2, 1, rows), jnp.float32),
        ],
        mine_chip,
        theirs,
        chip_amp,
        weight,
        energy,
    )
    halves = run(first_kernel, [sums] * 2, mine_far, theirs, gate, weights, part, message)
    (low, high), energies = lax.optimization_barrier((halves, energies))
    neighbour_energies = exchanged(0, energies)
    halves = low, high
    parts = summed(halves, n_steps - 1, neighbour_energies)
    low, high = [(other_core(block), exchanged(n_steps - 1, block, crossed=1)) for block in parts]
    (states,) = run(
        low_kernel,
        [in_vmem((4, two_cols, rows), jnp.float32)],
        *bases,
        *low,
        chip_amp,
        energies,
        message,
        neighbour_energies,
    )
    *halves, my_half, half_send = run(
        second_kernel,
        [sums, sums, segment, segment],
        *bases,
        states,
        *high,
        gate,
        weights,
    )
    fields = summed(halves, n_steps)
    fields[0], send_own, half_send = lax.optimization_barrier((fields[0], send_own, half_send))
    theirs_own, other_half = swapped([send_own, half_send])
    low, high = swapped(fields)
    low, high = swapped(fields)
    my_part, other_new = run(
        late_kernel,
        [segment, in_vmem((rows, two_cols), jnp.float32)],
        mine_chip,
        theirs,
        theirs_own,
        sent,
        *fields,
        low,
        energy,
        amp,
        my_half,
        other_half,
    )
    return call(
        last_kernel,
        [
            jax.ShapeDtypeStruct(tgt_amp.shape, jnp.float32),
            jax.ShapeDtypeStruct(proj_amp.shape, jnp.float32),
        ],
        [VMEM] * 5,
        [pltpu.VMEM((rows, two_cols), jnp.float32), pltpu.SemaphoreType.DMA((3,))],
        out_spec=HBM,
    )(mine_chip, theirs, high, my_part, other_new)


def solution(mesh):
    in_specs = (
        P(None, "tgt", "rep"),
        P(None, None, "prj", "rep"),
        P(("bpar", "rep")),
        P(("tgt", "prj", "rep")),
        P(("tgt", "rep"), "prj"),
        P("bpar", None),
        P("bpar", None),
        P(("bpar", "tgt", "prj", "rep"), None),
        P(("bpar", "tgt", "rep"), "prj", None),
    )
    out_specs = (P(("bpar", "tgt", "prj", "rep"), None), P(("bpar", "tgt", "rep"), "prj", None))

    def step(*args):
        return tuple(shards(*args))

    return jax.shard_map(step, mesh=mesh, in_specs=in_specs, out_specs=out_specs, check_vma=False)
```

```python
import functools

import jax
import jax.numpy as jnp
from jax import lax
from jax.experimental import pallas as pl
from jax.experimental.pallas import tpu as pltpu
from jax.sharding import PartitionSpec as P

time_step = 0.4
half_step = 0.5 * time_step
VMEM_LIMIT = 8 * 1024 * 1024
DEVICES = ("tgt", "prj", "rep")
HBM = pl.BlockSpec(memory_space=pl.ANY)
VMEM = pl.BlockSpec(memory_space=pltpu.VMEM)


def parity(place):
    odd = 0
    while place:
        odd, place = odd ^ (place & 1), place >> 1
    return odd


def my_kind():
    n_tgt, n_prj = lax.axis_size("tgt"), lax.axis_size("prj")
    place = lax.axis_index("tgt") * n_prj + lax.axis_index("prj")
    kind = lax.axis_index("rep")
    for bit in range((n_tgt * n_prj).bit_length() - 1):
        kind = jnp.bitwise_xor(kind, jnp.bitwise_and(lax.shift_right_logical(place, bit), 1))
    return kind


def by_core(body):
    for core in range(2):

        @pl.when(lax.axis_index("rep") == core)
        def _():
            body(core)


def ordered(core, first, second):
    return jnp.where(core == 0, first, second), jnp.where(core == 0, second, first)


def turned(block):
    half = block.shape[0] // 2
    return jnp.concatenate([block[half:], -block[:half]], axis=0)


def bf16(block):
    return block.astype(jnp.bfloat16)


def f32(block):
    return block.astype(jnp.float32)


def rows_of(bases, segment, amount):
    start = segment % 2 * amount
    return [bases[segment // 2][part, start : start + amount, :] for part in range(2)]


def project(basis, amp):
    return jnp.dot(bf16(amp), basis[0], preferred_element_type=jnp.float32) + jnp.dot(
        bf16(turned(amp)), basis[1], preferred_element_type=jnp.float32
    )


def expand(basis, field):
    contract = (((1,), (1,)), ((), ()))
    return lax.dot_general(
        turned(field), basis[0], contract, preferred_element_type=jnp.float32
    ) + lax.dot_general(field, basis[1], contract, preferred_element_type=jnp.float32)


PIECES = 16

EVEN = pl.CostEstimate(flops=1 << 32, bytes_accessed=1 << 16, transcendentals=0)
BEHIND = pl.CostEstimate(flops=1 << 35, bytes_accessed=1 << 16, transcendentals=0)


def split(row):
    index = lax.broadcasted_iota(jnp.int32, (PIECES, row.shape[1]), 0)
    block = jnp.zeros(index.shape, jnp.float32)
    for piece in range(3):
        rounded = f32(bf16(row))
        block = jnp.where(index == piece, rounded, block)
        row = row - rounded
    return bf16(block)


def joined(block):
    pieces = f32(block)
    return pieces[0:1] + pieces[1:2] + pieces[2:3]


def both(basis, rows):
    return basis.at[:, : 2 * rows], basis.at[:, 2 * rows : 4 * rows]


def basis_copies(bases, sem, my, neighbours, sources):
    rows = sources[my].shape[2]
    place = lax.axis_index(("prj", "tgt")[my])
    copies = []
    for chip, there in enumerate((place, jnp.bitwise_xor(place, neighbours[my]))):
        for core in range(2):
            copies.append(
                pltpu.make_async_copy(
                    sources[my].at[:, 2 * there + core],
                    bases[chip].at[:, core * rows : (core + 1) * rows],
                    sem.at[2 * chip + core],
                )
            )
    return copies


def load_kernel(
    tgt_energy_hbm,
    proj_energy_hbm,
    tgt_own_hbm,
    proj_own_hbm,
    energy,
    amp_ref,
    flat_energy,
    tgt_own,
    proj_own,
    sems,
):
    pairs = [
        (tgt_own_hbm, tgt_own),
        (proj_own_hbm, proj_own),
        (tgt_energy_hbm, flat_energy),
        (proj_energy_hbm, energy.at[1]),
    ]
    copies = [pltpu.make_async_copy(src, dst, sems.at[k]) for k, (src, dst) in enumerate(pairs)]
    for copy in copies:
        copy.start()
    for copy in copies:
        copy.wait()
    energy[0] = flat_energy[...][None, :]
    amp_ref[0] = tgt_own[...].T
    amp_ref[1] = proj_own[0].T


def pack_kernel(amp_ref, tgt_other, proj_other, chip_amp, message):
    my = my_kind()
    other_amp, _ = ordered(my, tgt_other[...].T, proj_other[0].T)
    amps = ordered(lax.axis_index("rep"), amp_ref[my], other_amp)
    for segment in range(2):
        chip_amp[segment] = amps[segment]
        message[segment] = bf16(amps[segment])


def sent_kernel(neighbours, weight_hbm, tgt_hbm, proj_hbm, chip_amp, energy, sent, weight, flat_weight, sems):
    my = my_kind()
    sources = (tgt_hbm, proj_hbm)
    rows = chip_amp.shape[2]

    def copies_of(kind):
        return basis_copies(both(sent, rows), sems, 1 - kind, neighbours, sources)

    weight_copy = pltpu.make_async_copy(weight_hbm, flat_weight, sems.at[4])
    weight_copy.start()
    for kind in range(2):

        @pl.when(my == kind)
        def _():
            for copy in copies_of(kind):
                copy.start()

    weight_copy.wait()
    weight[0] = flat_weight[...][None, :]
    for part in range(2):
        sent[part, 4 * rows : 4 * rows + PIECES] = split(weight[0])
        sent[part, 4 * rows + PIECES :, :rows] = split(energy[1 - my])
    for copy in copies_of(0):
        copy.wait()


def side_kernel(
    gate_levels,
    neighbours,
    flags_hbm,
    counts_hbm,
    tgt_hbm,
    proj_hbm,
    chip_amp,
    mine_chip,
    mine_far,
    send_own,
    gate,
    flags,
    counts,
    sems,
):
    my = my_kind()
    tgt_index = lax.axis_index("tgt")
    prj_index = lax.axis_index("prj")
    sources = (tgt_hbm, proj_hbm)
    pairs = [(flags_hbm, flags), (counts_hbm, counts)]
    copies = [pltpu.make_async_copy(src, dst, sems.at[4 + k]) for k, (src, dst) in enumerate(pairs)]
    for copy in copies:
        copy.start()
    for kind in range(2):

        @pl.when(my == kind)
        def _():
            for copy in basis_copies((mine_chip, mine_far), sems, kind, neighbours, sources):
                copy.start()

    for copy in copies:
        copy.wait()
    tiles = 2
    width = gate.shape[-1] // tiles
    gate_level = jnp.where(my == 0, *gate_levels)
    for half in range(2):
        for tile in range(tiles):
            live = jnp.logical_and(
                flags[prj_index, tgt_index] > 0, tiles * half + tile < counts[prj_index, tgt_index]
            )
            value = jnp.where(live, 1.0, 0.0).astype(jnp.float32)
            for level in range(gate.shape[0]):
                here = jnp.where(level == gate_level, value, jnp.float32(1.0))
                gate[level, half, :, tile * width : (tile + 1) * width] = jnp.full(
                    (1, width), here, jnp.float32
                )
    for copy in basis_copies((mine_chip, mine_far), sems, 0, neighbours, sources):
        copy.wait()
    core = lax.axis_index("rep")
    rows = send_own.shape[1]
    for part in range(2):
        send_own[part] = mine_chip[part, pl.ds(pl.multiple_of((1 - core) * rows, rows), rows), :]


def chip_kernel(mine_chip, theirs, chip_amp, weight, energy, part_ref, weights, energies):
    rows = chip_amp.shape[2]
    near, far = (mine_chip,), both(theirs, rows)

    def body(core):
        for half, basis in enumerate((near, far) if core == 0 else (far, near)):
            part_ref[half] = sum(
                project(rows_of(basis, segment, rows), chip_amp[segment]) for segment in range(2)
            )
        weights[core] = weight[0]
        weights[1 - core] = joined(theirs[0, 4 * rows : 4 * rows + PIECES, :])
        energies[core] = energy[my_kind()]
        energies[1 - core] = joined(theirs[0, 4 * rows + PIECES :, :rows])

    by_core(body)


def first_kernel(mine_far, theirs, gate, weights, part_ref, message, *outs):
    rows = message.shape[2]
    near, far = (None, mine_far), both(theirs, rows)

    def body(core):
        for half, basis in enumerate((near, far) if core == 0 else (far, near)):
            total = part_ref[half] + sum(
                project(rows_of(basis, 2 + segment, rows), f32(message[segment]))
                for segment in range(2)
            )
            outs[half][...] = bf16(gate[0, half] * (weights[half] * total))

    by_core(body)


def add_kernel(level, half, gate, own, other, *rest):
    out_ref = rest[-1]
    out_ref[...] = bf16(gate[level, half] * (f32(own[...]) + f32(other[...])))


def low_kernel(
    mine_chip,
    mine_far,
    theirs,
    low,
    low_there,
    chip_amp,
    energies,
    message,
    neighbour_energies,
    states_ref,
):
    rows = chip_amp.shape[2]
    mine, theirs = (mine_chip, mine_far), both(theirs, rows)
    field = bf16(f32(low[...]) + f32(low_there[...]))

    def body(core):
        for segment in range(4):
            if segment < 2:
                amp, energy = chip_amp[segment], energies[segment]
            else:
                amp, energy = f32(message[segment - 2]), neighbour_energies[segment - 2]
            change = expand(rows_of((mine, theirs)[core], segment, rows), field)
            states_ref[segment] = amp + half_step * (energy * turned(amp) + change)

    by_core(body)


def second_kernel(
    mine_chip,
    mine_far,
    theirs,
    states_ref,
    high,
    high_there,
    gate,
    weights,
    low_ref,
    high_ref,
    half_ref,
    send_ref,
):
    rows = states_ref.shape[2]
    mine, theirs = (mine_chip, mine_far), both(theirs, rows)
    field = bf16(f32(high[...]) + f32(high_there[...]))

    def body(core):
        bases = (mine, theirs) if core == 0 else (theirs, mine)
        halves = [
            states_ref[segment] + half_step * expand(rows_of(bases[1], segment, rows), field)
            for segment in range(4)
        ]
        half_ref[...] = halves[core]
        send_ref[...] = halves[1 - core]
        for half, out_ref in enumerate((low_ref, high_ref)):
            total = sum(
                project(rows_of(bases[half], segment, rows), halves[segment]) for segment in range(4)
            )
            out_ref[...] = bf16(gate[0, half] * (weights[half] * total))

    by_core(body)


def late_kernel(
    mine_chip,
    theirs,
    theirs_own,
    sent,
    low,
    high,
    my_low,
    energy,
    amp_ref,
    my_half,
    other_half,
    my_part,
    other_new,
):
    rows = amp_ref.shape[2]

    def body(core):
        my = my_kind()
        near, far = (low, high) if core == 0 else (high, low)
        change = expand(rows_of(both(sent, rows), core, rows), near[...]) + expand(
            rows_of((theirs_own,), 0, rows), far[...]
        )
        rate = energy[1 - my] * turned(other_half[...]) + change
        other_new[...] = (amp_ref[1 - my] + time_step * rate).T
        change = expand(rows_of(((mine_chip,), both(theirs, rows))[core], core, rows), my_low[...])
        my_part[...] = amp_ref[my] + time_step * (energy[my] * turned(my_half[...]) + change)

    by_core(body)


def last_kernel(
    mine_chip, theirs, high, my_part, other_new, new_tgt, new_proj, my_new, sems
):
    cols, rows = my_part.shape
    my = my_kind()
    parts = 2
    size = rows // parts
    outs = (new_tgt, new_proj.at[0])

    def copies(kind):
        return [pltpu.make_async_copy(other_new, outs[1 - kind], sems.at[parts])] + [
            pltpu.make_async_copy(
                my_new.at[pl.ds(part * size, size)], outs[kind].at[pl.ds(part * size, size)], sems.at[part]
            )
            for part in range(parts)
        ]

    def start(number):
        for kind in range(2):

            @pl.when(my == kind)
            def _():
                copies(kind)[number].start()

    def body(core):
        basis = rows_of((both(theirs, rows), (mine_chip,))[core], core, rows)
        for part in range(parts):
            states = slice(part * size, (part + 1) * size)
            change = expand([block[states] for block in basis], high[...])
            my_new[states, :] = (my_part[:, states] + time_step * change).T
            start(1 + part)

    start(0)
    by_core(body)
    for copy in copies(0):
        copy.wait()


def shards(
    tgt_basis,
    proj_basis,
    quad_weight,
    tgt_energy,
    proj_energy,
    pair_flags,
    tile_counts,
    tgt_amp,
    proj_amp,
):
    points = quad_weight.shape[0]
    rows, two_cols = tgt_amp.shape
    sizes = [lax.axis_size(axis) for axis in DEVICES]

    def call(kernel, out_shape, in_specs, scratch_shapes=(), cost=None, out_spec=VMEM):
        return pl.pallas_call(
            kernel,
            out_shape=out_shape,
            in_specs=in_specs,
            out_specs=[out_spec] * len(out_shape),
            scratch_shapes=scratch_shapes,
            cost_estimate=cost,
            compiler_params=pltpu.CompilerParams(vmem_limit_bytes=VMEM_LIMIT),
        )

    def run(kernel, out_shape, *blocks):
        return call(kernel, out_shape, [VMEM] * len(blocks))(*blocks)

    def other_core(block):
        return lax.ppermute(block, "rep", [(0, 1), (1, 0)])

    n_tgt, n_prj, n_core = sizes
    tgt_flips = [n_prj << bit for bit in range(n_tgt.bit_length() - 1)]
    prj_flips = [1 << bit for bit in range(n_prj.bit_length() - 1)]
    far_first = tgt_flips[::-1]
    flips = [(prj_flips + order, far_first + prj_flips) for order in (far_first, tgt_flips)]
    neighbours = (prj_flips[0], far_first[0] // n_prj)
    gate_levels = (len(prj_flips) - 1, len(tgt_flips) - 1)
    n_steps = len(tgt_flips) + len(prj_flips)

    def exchanged(step, block, order=0, crossed=0):
        pairs = []
        for place in range(n_tgt * n_prj):
            for kind in range(2):
                there = place ^ flips[order][kind][step]
                to_core = kind ^ crossed ^ parity(there)
                pairs.append((place * n_core + (kind ^ parity(place)), there * n_core + to_core))
        return lax.ppermute(block, DEVICES, pairs)

    in_vmem = pltpu.VMEM
    sums = in_vmem((two_cols, points), jnp.bfloat16)
    segment = in_vmem((two_cols, rows), jnp.float32)

    def summed(halves, until, orders, *ahead):
        totals = []
        for half, block in enumerate(halves):
            for step in range(1, until):
                other = exchanged(step, block, orders[half])
                kernel = functools.partial(add_kernel, step, half)
                blocks = [gate, block, other] + (list(ahead) if half and step == 1 else [])
                cost = EVEN if half else None
                (block,) = call(kernel, [sums], [VMEM] * len(blocks), cost=cost)(*blocks)
            totals.append(block)
        return totals

    def swapped(fields):
        return [other_core(block) for block in fields]

    def in_hbm(*blocks):
        return [pltpu.with_memory_space_constraint(block, pltpu.HBM) for block in blocks]

    others = swapped([tgt_amp, proj_amp])
    energy, amp = call(
        load_kernel,
        [in_vmem((2, 1, rows), jnp.float32), in_vmem((2, two_cols, rows), jnp.float32)],
        [HBM] * 4,
        [
            pltpu.VMEM((rows,), jnp.float32),
            pltpu.VMEM(tgt_amp.shape, jnp.float32),
            pltpu.VMEM(proj_amp.shape, jnp.float32),
            pltpu.SemaphoreType.DMA((4,)),
        ],
        pl.CostEstimate(
            flops=2 * 4 * rows * two_cols * points, bytes_accessed=4 * 1024 * 1024, transcendentals=0
        ),
    )(*in_hbm(tgt_energy, proj_energy, tgt_amp, proj_amp))
    chip_amp, message = run(
        pack_kernel,
        [in_vmem((2, two_cols, rows), jnp.float32), in_vmem((2, two_cols, rows), jnp.bfloat16)],
        amp,
        *others,
    )
    message = exchanged(0, message)
    flags, counts = pair_flags.T, tile_counts.T
    bases = in_hbm(tgt_basis.reshape(2, -1, rows, points), proj_basis)
    pair = in_vmem((2, 2 * rows, points), jnp.bfloat16)
    sent, weight = call(
        functools.partial(sent_kernel, neighbours),
        [
            in_vmem((2, 4 * rows + 2 * PIECES, points), jnp.bfloat16),
            in_vmem((1, 1, points), jnp.float32),
        ],
        [HBM] * 3 + [VMEM] * 2,
        [pltpu.VMEM((points,), jnp.float32), pltpu.SemaphoreType.DMA((5,))],
    )(*in_hbm(quad_weight), *bases, chip_amp, energy)
    mine_chip, mine_far, send_own, gate = call(
        functools.partial(side_kernel, gate_levels, neighbours),
        [
            pair,
            pair,
            in_vmem((2, rows, points), jnp.bfloat16),
            in_vmem((n_steps, 2, 1, points), jnp.float32),
        ],
        [HBM] * 4 + [VMEM],
        [
            pltpu.SMEM(flags.shape, jnp.int32),
            pltpu.SMEM(counts.shape, jnp.int32),
            pltpu.SemaphoreType.DMA((6,)),
        ],
        BEHIND,
    )(*in_hbm(flags, counts), *bases, chip_amp)
    theirs, theirs_own = swapped([sent, send_own])
    bases = (mine_chip, mine_far, theirs)
    part, weights, energies = run(
        chip_kernel,
        [
            in_vmem((2, two_cols, points), jnp.float32),
            in_vmem((2, 1, points), jnp.float32),
            in_vmem((2, 1, rows), jnp.float32),
        ],
        mine_chip,
        theirs,
        chip_amp,
        weight,
        energy,
    )
    halves = run(first_kernel, [sums] * 2, mine_far, theirs, gate, weights, part, message)
    (low, high), energies = lax.optimization_barrier((halves, energies))
    neighbour_energies = exchanged(0, energies)
    halves = low, high
    parts = summed(halves, n_steps - 1, (0, 0), neighbour_energies)
    low, high = [(other_core(block), exchanged(n_steps - 1, block, crossed=1)) for block in parts]
    (states,) = run(
        low_kernel,
        [in_vmem((4, two_cols, rows), jnp.float32)],
        *bases,
        *low,
        chip_amp,
        energies,
        message,
        neighbour_energies,
    )
    *halves, my_half, half_send = run(
        second_kernel,
        [sums, sums, segment, segment],
        *bases,
        states,
        *high,
        gate,
        weights,
    )
    fields = summed(halves, n_steps, (0, 1))
    fields[0], half_send = lax.optimization_barrier((fields[0], half_send))
    other_half = other_core(half_send)
    low, high = swapped(fields)
    low, high = swapped(fields)
    my_part, other_new = run(
        late_kernel,
        [segment, in_vmem((rows, two_cols), jnp.float32)],
        mine_chip,
        theirs,
        theirs_own,
        sent,
        *fields,
        low,
        energy,
        amp,
        my_half,
        other_half,
    )
    return call(
        last_kernel,
        [
            jax.ShapeDtypeStruct(tgt_amp.shape, jnp.float32),
            jax.ShapeDtypeStruct(proj_amp.shape, jnp.float32),
        ],
        [VMEM] * 5,
        [pltpu.VMEM((rows, two_cols), jnp.float32), pltpu.SemaphoreType.DMA((3,))],
        out_spec=HBM,
    )(mine_chip, theirs, high, my_part, other_new)


def solution(mesh):
    in_specs = (
        P(None, "tgt", "rep"),
        P(None, None, "prj", "rep"),
        P(("bpar", "rep")),
        P(("tgt", "prj", "rep")),
        P(("tgt", "rep"), "prj"),
        P("bpar", None),
        P("bpar", None),
        P(("bpar", "tgt", "prj", "rep"), None),
        P(("bpar", "tgt", "rep"), "prj", None),
    )
    out_specs = (P(("bpar", "tgt", "prj", "rep"), None), P(("bpar", "tgt", "rep"), "prj", None))

    def step(*args):
        return tuple(shards(*args))

    return jax.shard_map(step, mesh=mesh, in_specs=in_specs, out_specs=out_specs, check_vma=False)
```

```python
import functools

import jax
import jax.numpy as jnp
from jax import lax
from jax.experimental import pallas as pl
from jax.experimental.pallas import tpu as pltpu
from jax.sharding import PartitionSpec as P

time_step = 0.4
half_step = 0.5 * time_step
VMEM_LIMIT = 8 * 1024 * 1024
DEVICES = ("tgt", "prj", "rep")
HBM = pl.BlockSpec(memory_space=pl.ANY)
VMEM = pl.BlockSpec(memory_space=pltpu.VMEM)


def parity(place):
    even = 1
    while place:
        even, place = even ^ (place & 1), place >> 1
    return even


def my_kind():
    n_tgt, n_prj = lax.axis_size("tgt"), lax.axis_size("prj")
    place = lax.axis_index("tgt") * n_prj + lax.axis_index("prj")
    kind = 1 - lax.axis_index("rep")
    for bit in range((n_tgt * n_prj).bit_length() - 1):
        kind = jnp.bitwise_xor(kind, jnp.bitwise_and(lax.shift_right_logical(place, bit), 1))
    return kind


def by_core(body):
    for core in range(2):

        @pl.when(lax.axis_index("rep") == core)
        def _():
            body(core)


def ordered(core, first, second):
    return jnp.where(core == 0, first, second), jnp.where(core == 0, second, first)


def turned(block):
    half = block.shape[0] // 2
    return jnp.concatenate([block[half:], -block[:half]], axis=0)


def bf16(block):
    return block.astype(jnp.bfloat16)


def f32(block):
    return block.astype(jnp.float32)


def rows_of(bases, segment, amount):
    start = segment % 2 * amount
    return [bases[segment // 2][part, start : start + amount, :] for part in range(2)]


def project(basis, amp):
    return jnp.dot(bf16(amp), basis[0], preferred_element_type=jnp.float32) + jnp.dot(
        bf16(turned(amp)), basis[1], preferred_element_type=jnp.float32
    )


def expand(basis, field):
    contract = (((1,), (1,)), ((), ()))
    return lax.dot_general(
        turned(field), basis[0], contract, preferred_element_type=jnp.float32
    ) + lax.dot_general(field, basis[1], contract, preferred_element_type=jnp.float32)


PIECES = 16

BEHIND = pl.CostEstimate(flops=1 << 35, bytes_accessed=1 << 16, transcendentals=0)


def split(row):
    index = lax.broadcasted_iota(jnp.int32, (PIECES, row.shape[1]), 0)
    block = jnp.zeros(index.shape, jnp.float32)
    for piece in range(3):
        rounded = f32(bf16(row))
        block = jnp.where(index == piece, rounded, block)
        row = row - rounded
    return bf16(block)


def joined(block):
    pieces = f32(block)
    return pieces[0:1] + pieces[1:2] + pieces[2:3]


def both(basis, rows):
    return basis.at[:, : 2 * rows], basis.at[:, 2 * rows : 4 * rows]


def basis_copies(bases, sem, my, neighbours, sources):
    rows = sources[my].shape[2]
    place = lax.axis_index(("prj", "tgt")[my])
    copies = []
    for chip, there in enumerate((place, jnp.bitwise_xor(place, neighbours[my]))):
        for core in range(2):
            copies.append(
                pltpu.make_async_copy(
                    sources[my].at[:, 2 * there + core],
                    bases[chip].at[:, core * rows : (core + 1) * rows],
                    sem.at[2 * chip + core],
                )
            )
    return copies


def load_kernel(
    tgt_energy_hbm,
    proj_energy_hbm,
    tgt_own_hbm,
    proj_own_hbm,
    energy,
    amp_ref,
    flat_energy,
    tgt_own,
    proj_own,
    sems,
):
    pairs = [
        (tgt_own_hbm, tgt_own),
        (proj_own_hbm, proj_own),
        (tgt_energy_hbm, flat_energy),
        (proj_energy_hbm, energy.at[1]),
    ]
    copies = [pltpu.make_async_copy(src, dst, sems.at[k]) for k, (src, dst) in enumerate(pairs)]
    for copy in copies:
        copy.start()
    for copy in copies:
        copy.wait()
    energy[0] = flat_energy[...][None, :]
    amp_ref[0] = tgt_own[...].T
    amp_ref[1] = proj_own[0].T


def pack_kernel(amp_ref, tgt_other, proj_other, chip_amp, message):
    my = my_kind()
    other_amp, _ = ordered(my, tgt_other[...].T, proj_other[0].T)
    amps = ordered(lax.axis_index("rep"), amp_ref[my], other_amp)
    for segment in range(2):
        chip_amp[segment] = amps[segment]
        message[segment] = bf16(amps[segment])


def sent_kernel(neighbours, weight_hbm, tgt_hbm, proj_hbm, chip_amp, energy, sent, weight, flat_weight, sems):
    my = my_kind()
    sources = (tgt_hbm, proj_hbm)
    rows = chip_amp.shape[2]

    def copies_of(kind):
        return basis_copies(both(sent, rows), sems, 1 - kind, neighbours, sources)

    weight_copy = pltpu.make_async_copy(weight_hbm, flat_weight, sems.at[4])
    weight_copy.start()
    for kind in range(2):

        @pl.when(my == kind)
        def _():
            for copy in copies_of(kind):
                copy.start()

    weight_copy.wait()
    weight[0] = flat_weight[...][None, :]
    for part in range(2):
        sent[part, 4 * rows : 4 * rows + PIECES] = split(weight[0])
        sent[part, 4 * rows + PIECES :, :rows] = split(energy[1 - my])
    for copy in copies_of(0):
        copy.wait()


def side_kernel(
    gate_levels,
    neighbours,
    flags_hbm,
    counts_hbm,
    tgt_hbm,
    proj_hbm,
    chip_amp,
    mine_chip,
    mine_far,
    send_own,
    gate,
    flags,
    counts,
    sems,
):
    my = my_kind()
    tgt_index = lax.axis_index("tgt")
    prj_index = lax.axis_index("prj")
    sources = (tgt_hbm, proj_hbm)
    pairs = [(flags_hbm, flags), (counts_hbm, counts)]
    copies = [pltpu.make_async_copy(src, dst, sems.at[4 + k]) for k, (src, dst) in enumerate(pairs)]
    for copy in copies:
        copy.start()
    for kind in range(2):

        @pl.when(my == kind)
        def _():
            for copy in basis_copies((mine_chip, mine_far), sems, kind, neighbours, sources):
                copy.start()

    for copy in copies:
        copy.wait()
    tiles = 2
    width = gate.shape[-1] // tiles
    gate_level = jnp.where(my == 0, *gate_levels)
    for half in range(2):
        for tile in range(tiles):
            live = jnp.logical_and(
                flags[prj_index, tgt_index] > 0, tiles * half + tile < counts[prj_index, tgt_index]
            )
            value = jnp.where(live, 1.0, 0.0).astype(jnp.float32)
            for level in range(gate.shape[0]):
                here = jnp.where(level == gate_level, value, jnp.float32(1.0))
                gate[level, half, :, tile * width : (tile + 1) * width] = jnp.full(
                    (1, width), here, jnp.float32
                )
    for copy in basis_copies((mine_chip, mine_far), sems, 0, neighbours, sources):
        copy.wait()
    core = lax.axis_index("rep")
    rows = send_own.shape[1]
    for part in range(2):
        send_own[part] = mine_chip[part, pl.ds(pl.multiple_of((1 - core) * rows, rows), rows), :]


def chip_kernel(mine_chip, theirs, chip_amp, weight, energy, part_ref, weights, energies):
    rows = chip_amp.shape[2]
    near, far = (mine_chip,), both(theirs, rows)

    def body(core):
        for half, basis in enumerate((near, far) if core == 0 else (far, near)):
            part_ref[half] = sum(
                project(rows_of(basis, segment, rows), chip_amp[segment]) for segment in range(2)
            )
        weights[core] = weight[0]
        weights[1 - core] = joined(theirs[0, 4 * rows : 4 * rows + PIECES, :])
        energies[core] = energy[my_kind()]
        energies[1 - core] = joined(theirs[0, 4 * rows + PIECES :, :rows])

    by_core(body)


def first_kernel(mine_far, theirs, gate, weights, part_ref, message, *outs):
    rows = message.shape[2]
    near, far = (None, mine_far), both(theirs, rows)

    def body(core):
        for half, basis in enumerate((near, far) if core == 0 else (far, near)):
            total = part_ref[half] + sum(
                project(rows_of(basis, 2 + segment, rows), f32(message[segment]))
                for segment in range(2)
            )
            outs[half][...] = bf16(gate[0, half] * (weights[half] * total))

    by_core(body)


def add_kernel(level, half, gate, own, other, out_ref):
    out_ref[...] = bf16(gate[level, half] * (f32(own[...]) + f32(other[...])))


def low_kernel(
    mine_chip,
    mine_far,
    theirs,
    low,
    low_there,
    chip_amp,
    energies,
    message,
    neighbour_energies,
    states_ref,
):
    rows = chip_amp.shape[2]
    mine, theirs = (mine_chip, mine_far), both(theirs, rows)
    field = bf16(f32(low[...]) + f32(low_there[...]))

    def body(core):
        for segment in range(4):
            if segment < 2:
                amp, energy = chip_amp[segment], energies[segment]
            else:
                amp, energy = f32(message[segment - 2]), neighbour_energies[segment - 2]
            change = expand(rows_of((mine, theirs)[core], segment, rows), field)
            states_ref[segment] = amp + half_step * (energy * turned(amp) + change)

    by_core(body)


def second_kernel(
    mine_chip,
    mine_far,
    theirs,
    states_ref,
    high,
    high_there,
    gate,
    weights,
    low_ref,
    high_ref,
    half_ref,
    send_ref,
):
    rows = states_ref.shape[2]
    mine, theirs = (mine_chip, mine_far), both(theirs, rows)
    field = bf16(f32(high[...]) + f32(high_there[...]))

    def body(core):
        bases = (mine, theirs) if core == 0 else (theirs, mine)
        halves = [
            states_ref[segment] + half_step * expand(rows_of(bases[1], segment, rows), field)
            for segment in range(4)
        ]
        half_ref[...] = halves[core]
        send_ref[...] = halves[1 - core]
        for half, out_ref in enumerate((low_ref, high_ref)):
            total = sum(
                project(rows_of(bases[half], segment, rows), halves[segment]) for segment in range(4)
            )
            out_ref[...] = bf16(gate[0, half] * (weights[half] * total))

    by_core(body)


def late_kernel(
    mine_chip,
    theirs,
    theirs_own,
    sent,
    low,
    high,
    my_low,
    energy,
    amp_ref,
    my_half,
    other_half,
    my_part,
    other_new,
):
    rows = amp_ref.shape[2]

    def body(core):
        my = my_kind()
        near, far = (low, high) if core == 0 else (high, low)
        change = expand(rows_of(both(sent, rows), core, rows), near[...]) + expand(
            rows_of((theirs_own,), 0, rows), far[...]
        )
        rate = energy[1 - my] * turned(other_half[...]) + change
        other_new[...] = (amp_ref[1 - my] + time_step * rate).T
        change = expand(rows_of(((mine_chip,), both(theirs, rows))[core], core, rows), my_low[...])
        my_part[...] = amp_ref[my] + time_step * (energy[my] * turned(my_half[...]) + change)

    by_core(body)


def last_kernel(
    mine_chip, theirs, high, my_part, other_new, new_tgt, new_proj, my_new, sems
):
    cols, rows = my_part.shape
    my = my_kind()
    parts = 2
    size = rows // parts
    outs = (new_tgt, new_proj.at[0])

    def copies(kind):
        return [pltpu.make_async_copy(other_new, outs[1 - kind], sems.at[parts])] + [
            pltpu.make_async_copy(
                my_new.at[pl.ds(part * size, size)], outs[kind].at[pl.ds(part * size, size)], sems.at[part]
            )
            for part in range(parts)
        ]

    def start(number):
        for kind in range(2):

            @pl.when(my == kind)
            def _():
                copies(kind)[number].start()

    def body(core):
        basis = rows_of((both(theirs, rows), (mine_chip,))[core], core, rows)
        for part in range(parts):
            states = slice(part * size, (part + 1) * size)
            change = expand([block[states] for block in basis], high[...])
            my_new[states, :] = (my_part[:, states] + time_step * change).T
            start(1 + part)

    start(0)
    by_core(body)
    for copy in copies(0):
        copy.wait()


def shards(
    tgt_basis,
    proj_basis,
    quad_weight,
    tgt_energy,
    proj_energy,
    pair_flags,
    tile_counts,
    tgt_amp,
    proj_amp,
):
    points = quad_weight.shape[0]
    rows, two_cols = tgt_amp.shape
    sizes = [lax.axis_size(axis) for axis in DEVICES]

    def call(kernel, out_shape, in_specs, scratch_shapes=(), cost=None, out_spec=VMEM):
        return pl.pallas_call(
            kernel,
            out_shape=out_shape,
            in_specs=in_specs,
            out_specs=[out_spec] * len(out_shape),
            scratch_shapes=scratch_shapes,
            cost_estimate=cost,
            compiler_params=pltpu.CompilerParams(vmem_limit_bytes=VMEM_LIMIT),
        )

    def run(kernel, out_shape, *blocks):
        return call(kernel, out_shape, [VMEM] * len(blocks))(*blocks)

    def other_core(block):
        return lax.ppermute(block, "rep", [(0, 1), (1, 0)])

    n_tgt, n_prj, n_core = sizes
    tgt_flips = [n_prj << bit for bit in range(n_tgt.bit_length() - 1)]
    prj_flips = [1 << bit for bit in range(n_prj.bit_length() - 1)]
    far_first = tgt_flips[::-1]
    flips = (prj_flips + far_first, far_first + prj_flips)
    neighbours = (prj_flips[0], far_first[0] // n_prj)
    gate_levels = (len(prj_flips) - 1, len(tgt_flips) - 1)
    n_steps = len(tgt_flips) + len(prj_flips)

    def exchanged(step, block, crossed=0):
        pairs = []
        for place in range(n_tgt * n_prj):
            for kind in range(2):
                there = place ^ flips[kind][step]
                to_core = kind ^ crossed ^ parity(there)
                pairs.append((place * n_core + (kind ^ parity(place)), there * n_core + to_core))
        return lax.ppermute(block, DEVICES, pairs)

    in_vmem = pltpu.VMEM
    sums = in_vmem((two_cols, points), jnp.bfloat16)
    segment = in_vmem((two_cols, rows), jnp.float32)

    def summed(halves, until):
        totals = []
        for half, block in enumerate(halves):
            for step in range(1, until):
                other = exchanged(step, block)
                (block,) = run(functools.partial(add_kernel, step, half), [sums], gate, block, other)
            totals.append(block)
        return totals

    def swapped(fields):
        return [other_core(block) for block in fields]

    def in_hbm(*blocks):
        return [pltpu.with_memory_space_constraint(block, pltpu.HBM) for block in blocks]

    others = swapped([tgt_amp, proj_amp])
    energy, amp = call(
        load_kernel,
        [in_vmem((2, 1, rows), jnp.float32), in_vmem((2, two_cols, rows), jnp.float32)],
        [HBM] * 4,
        [
            pltpu.VMEM((rows,), jnp.float32),
            pltpu.VMEM(tgt_amp.shape, jnp.float32),
            pltpu.VMEM(proj_amp.shape, jnp.float32),
            pltpu.SemaphoreType.DMA((4,)),
        ],
        pl.CostEstimate(
            flops=2 * 4 * rows * two_cols * points, bytes_accessed=4 * 1024 * 1024, transcendentals=0
        ),
    )(*in_hbm(tgt_energy, proj_energy, tgt_amp, proj_amp))
    chip_amp, message = run(
        pack_kernel,
        [in_vmem((2, two_cols, rows), jnp.float32), in_vmem((2, two_cols, rows), jnp.bfloat16)],
        amp,
        *others,
    )
    message = exchanged(0, message)
    flags, counts = pair_flags.T, tile_counts.T
    bases = in_hbm(tgt_basis.reshape(2, -1, rows, points), proj_basis)
    pair = in_vmem((2, 2 * rows, points), jnp.bfloat16)
    sent, weight = call(
        functools.partial(sent_kernel, neighbours),
        [
            in_vmem((2, 4 * rows + 2 * PIECES, points), jnp.bfloat16),
            in_vmem((1, 1, points), jnp.float32),
        ],
        [HBM] * 3 + [VMEM] * 2,
        [pltpu.VMEM((points,), jnp.float32), pltpu.SemaphoreType.DMA((5,))],
    )(*in_hbm(quad_weight), *bases, chip_amp, energy)
    mine_chip, mine_far, send_own, gate = call(
        functools.partial(side_kernel, gate_levels, neighbours),
        [
            pair,
            pair,
            in_vmem((2, rows, points), jnp.bfloat16),
            in_vmem((n_steps, 2, 1, points), jnp.float32),
        ],
        [HBM] * 4 + [VMEM],
        [
            pltpu.SMEM(flags.shape, jnp.int32),
            pltpu.SMEM(counts.shape, jnp.int32),
            pltpu.SemaphoreType.DMA((6,)),
        ],
        BEHIND,
    )(*in_hbm(flags, counts), *bases, chip_amp)
    theirs, theirs_own = swapped([sent, send_own])
    bases = (mine_chip, mine_far, theirs)
    part, weights, energies = run(
        chip_kernel,
        [
            in_vmem((2, two_cols, points), jnp.float32),
            in_vmem((2, 1, points), jnp.float32),
            in_vmem((2, 1, rows), jnp.float32),
        ],
        mine_chip,
        theirs,
        chip_amp,
        weight,
        energy,
    )
    halves = run(first_kernel, [sums] * 2, mine_far, theirs, gate, weights, part, message)
    (low, high), energies = lax.optimization_barrier((halves, energies))
    neighbour_energies = exchanged(0, energies)
    halves = low, high
    parts = summed(halves, n_steps - 1)
    low, high = [(other_core(block), exchanged(n_steps - 1, block, crossed=1)) for block in parts]
    (states,) = run(
        low_kernel,
        [in_vmem((4, two_cols, rows), jnp.float32)],
        *bases,
        *low,
        chip_amp,
        energies,
        message,
        neighbour_energies,
    )
    *halves, my_half, half_send = run(
        second_kernel,
        [sums, sums, segment, segment],
        *bases,
        states,
        *high,
        gate,
        weights,
    )
    other_half = other_core(half_send)
    fields = summed(halves, n_steps)
    low, high = swapped(fields)
    low, high = swapped(fields)
    my_part, other_new = run(
        late_kernel,
        [segment, in_vmem((rows, two_cols), jnp.float32)],
        mine_chip,
        theirs,
        theirs_own,
        sent,
        *fields,
        low,
        energy,
        amp,
        my_half,
        other_half,
    )
    return call(
        last_kernel,
        [
            jax.ShapeDtypeStruct(tgt_amp.shape, jnp.float32),
            jax.ShapeDtypeStruct(proj_amp.shape, jnp.float32),
        ],
        [VMEM] * 5,
        [pltpu.VMEM((rows, two_cols), jnp.float32), pltpu.SemaphoreType.DMA((3,))],
        out_spec=HBM,
    )(mine_chip, theirs, high, my_part, other_new)


def solution(mesh):
    in_specs = (
        P(None, "tgt", "rep"),
        P(None, None, "prj", "rep"),
        P(("bpar", "rep")),
        P(("tgt", "prj", "rep")),
        P(("tgt", "rep"), "prj"),
        P("bpar", None),
        P("bpar", None),
        P(("bpar", "tgt", "prj", "rep"), None),
        P(("bpar", "tgt", "rep"), "prj", None),
    )
    out_specs = (P(("bpar", "tgt", "prj", "rep"), None), P(("bpar", "tgt", "rep"), "prj", None))

    def step(*args):
        return tuple(shards(*args))

    return jax.shard_map(step, mesh=mesh, in_specs=in_specs, out_specs=out_specs, check_vma=False)
```

```python
import functools

import jax
import jax.numpy as jnp
from jax import lax
from jax.experimental import pallas as pl
from jax.experimental.pallas import tpu as pltpu
from jax.sharding import PartitionSpec as P

time_step = 0.4
half_step = 0.5 * time_step
VMEM_LIMIT = 8 * 1024 * 1024
DEVICES = ("tgt", "prj", "rep")
HBM = pl.BlockSpec(memory_space=pl.ANY)
VMEM = pl.BlockSpec(memory_space=pltpu.VMEM)


def parity(place):
    odd = 0
    while place:
        odd, place = odd ^ (place & 1), place >> 1
    return odd


def my_kind():
    n_tgt, n_prj = lax.axis_size("tgt"), lax.axis_size("prj")
    place = lax.axis_index("tgt") * n_prj + lax.axis_index("prj")
    kind = lax.axis_index("rep")
    for bit in range((n_tgt * n_prj).bit_length() - 1):
        kind = jnp.bitwise_xor(kind, jnp.bitwise_and(lax.shift_right_logical(place, bit), 1))
    return kind


def by_core(body):
    for core in range(2):

        @pl.when(lax.axis_index("rep") == core)
        def _():
            body(core)


def ordered(core, first, second):
    return jnp.where(core == 0, first, second), jnp.where(core == 0, second, first)


def turned(block):
    half = block.shape[0] // 2
    return jnp.concatenate([block[half:], -block[:half]], axis=0)


def bf16(block):
    return block.astype(jnp.bfloat16)


def f32(block):
    return block.astype(jnp.float32)


def rows_of(bases, segment, amount):
    start = segment % 2 * amount
    return [bases[segment // 2][part, start : start + amount, :] for part in range(2)]


def project(basis, amp):
    return jnp.dot(bf16(amp), basis[0], preferred_element_type=jnp.float32) + jnp.dot(
        bf16(turned(amp)), basis[1], preferred_element_type=jnp.float32
    )


def expand(basis, field):
    contract = (((1,), (1,)), ((), ()))
    return lax.dot_general(
        turned(field), basis[0], contract, preferred_element_type=jnp.float32
    ) + lax.dot_general(field, basis[1], contract, preferred_element_type=jnp.float32)


PIECES = 16

BEHIND = pl.CostEstimate(flops=1 << 35, bytes_accessed=1 << 16, transcendentals=0)


def split(row):
    index = lax.broadcasted_iota(jnp.int32, (PIECES, row.shape[1]), 0)
    block = jnp.zeros(index.shape, jnp.float32)
    for piece in range(3):
        rounded = f32(bf16(row))
        block = jnp.where(index == piece, rounded, block)
        row = row - rounded
    return bf16(block)


def joined(block):
    pieces = f32(block)
    return pieces[0:1] + pieces[1:2] + pieces[2:3]


def both(basis, rows):
    return basis.at[:, : 2 * rows], basis.at[:, 2 * rows : 4 * rows]


def basis_copies(bases, sem, my, neighbours, sources):
    rows = sources[my].shape[2]
    place = lax.axis_index(("prj", "tgt")[my])
    copies = []
    for chip, there in enumerate((place, jnp.bitwise_xor(place, neighbours[my]))):
        for core in range(2):
            copies.append(
                pltpu.make_async_copy(
                    sources[my].at[:, 2 * there + core],
                    bases[chip].at[:, core * rows : (core + 1) * rows],
                    sem.at[2 * chip + core],
                )
            )
    return copies


def load_kernel(tgt_own_hbm, proj_own_hbm, amp_ref, tgt_own, proj_own, sems):
    pairs = [(tgt_own_hbm, tgt_own), (proj_own_hbm, proj_own)]
    copies = [pltpu.make_async_copy(src, dst, sems.at[k]) for k, (src, dst) in enumerate(pairs)]
    for copy in copies:
        copy.start()
    for copy in copies:
        copy.wait()
    amp_ref[0] = tgt_own[...].T
    amp_ref[1] = proj_own[0].T


def pack_kernel(amp_ref, tgt_other, proj_other, chip_amp, message):
    my = my_kind()
    other_amp = jnp.where(my == 0, tgt_other[...], proj_other[0]).T
    amps = ordered(lax.axis_index("rep"), amp_ref[my], other_amp)
    for segment in range(2):
        chip_amp[segment] = amps[segment]
        message[segment] = bf16(amps[segment])


def sent_kernel(
    neighbours,
    weight_hbm,
    tgt_energy_hbm,
    proj_energy_hbm,
    tgt_hbm,
    proj_hbm,
    chip_amp,
    sent,
    weight,
    energy,
    flat_weight,
    flat_energy,
    sems,
):
    my = my_kind()
    sources = (tgt_hbm, proj_hbm)
    rows = chip_amp.shape[2]

    def copies_of(kind):
        return basis_copies(both(sent, rows), sems, 1 - kind, neighbours, sources)

    pairs = [(weight_hbm, flat_weight), (tgt_energy_hbm, flat_energy), (proj_energy_hbm, energy.at[1])]
    rows_copies = [pltpu.make_async_copy(src, dst, sems.at[4 + k]) for k, (src, dst) in enumerate(pairs)]
    for copy in rows_copies:
        copy.start()
    for kind in range(2):

        @pl.when(my == kind)
        def _():
            for copy in copies_of(kind):
                copy.start()

    for copy in rows_copies:
        copy.wait()
    weight[0] = flat_weight[...][None, :]
    energy[0] = flat_energy[...][None, :]
    for part in range(2):
        sent[part, 4 * rows : 4 * rows + PIECES] = split(weight[0])
        sent[part, 4 * rows + PIECES :, :rows] = split(energy[1 - my])
    for copy in copies_of(0):
        copy.wait()


def side_kernel(
    gate_levels,
    neighbours,
    flags_hbm,
    counts_hbm,
    tgt_hbm,
    proj_hbm,
    chip_amp,
    mine_chip,
    mine_far,
    send_own,
    gate,
    flags,
    counts,
    sems,
):
    my = my_kind()
    tgt_index = lax.axis_index("tgt")
    prj_index = lax.axis_index("prj")
    sources = (tgt_hbm, proj_hbm)
    pairs = [(flags_hbm, flags), (counts_hbm, counts)]
    copies = [pltpu.make_async_copy(src, dst, sems.at[4 + k]) for k, (src, dst) in enumerate(pairs)]
    for copy in copies:
        copy.start()
    for kind in range(2):

        @pl.when(my == kind)
        def _():
            for copy in basis_copies((mine_chip, mine_far), sems, kind, neighbours, sources):
                copy.start()

    for copy in copies:
        copy.wait()
    tiles = 2
    width = gate.shape[-1] // tiles
    gate_level = jnp.where(my == 0, *gate_levels)
    for half in range(2):
        for tile in range(tiles):
            live = jnp.logical_and(
                flags[prj_index, tgt_index] > 0, tiles * half + tile < counts[prj_index, tgt_index]
            )
            value = jnp.where(live, 1.0, 0.0).astype(jnp.float32)
            for level in range(gate.shape[0]):
                here = jnp.where(level == gate_level, value, jnp.float32(1.0))
                gate[level, half, :, tile * width : (tile + 1) * width] = jnp.full(
                    (1, width), here, jnp.float32
                )
    for copy in basis_copies((mine_chip, mine_far), sems, 0, neighbours, sources):
        copy.wait()
    core = lax.axis_index("rep")
    rows = send_own.shape[1]
    for part in range(2):
        send_own[part] = mine_chip[part, pl.ds(pl.multiple_of((1 - core) * rows, rows), rows), :]


def chip_kernel(mine_chip, theirs, chip_amp, weight, energy, part_ref, weights, energies):
    rows = chip_amp.shape[2]
    near, far = (mine_chip,), both(theirs, rows)

    def body(core):
        for half, basis in enumerate((near, far) if core == 0 else (far, near)):
            part_ref[half] = sum(
                project(rows_of(basis, segment, rows), chip_amp[segment]) for segment in range(2)
            )
        weights[core] = weight[0]
        weights[1 - core] = joined(theirs[0, 4 * rows : 4 * rows + PIECES, :])
        energies[core] = energy[my_kind()]
        energies[1 - core] = joined(theirs[0, 4 * rows + PIECES :, :rows])

    by_core(body)


def first_kernel(mine_far, theirs, gate, weights, part_ref, message, *outs):
    rows = message.shape[2]
    near, far = (None, mine_far), both(theirs, rows)

    def body(core):
        for half, basis in enumerate((near, far) if core == 0 else (far, near)):
            total = part_ref[half] + sum(
                project(rows_of(basis, 2 + segment, rows), f32(message[segment]))
                for segment in range(2)
            )
            outs[half][...] = bf16(gate[0, half] * (weights[half] * total))

    by_core(body)


def add_kernel(level, half, gate, own, other, out_ref):
    out_ref[...] = bf16(gate[level, half] * (f32(own[...]) + f32(other[...])))


def low_kernel(
    mine_chip,
    mine_far,
    theirs,
    low,
    low_there,
    chip_amp,
    energies,
    message,
    neighbour_energies,
    states_ref,
):
    rows = chip_amp.shape[2]
    mine, theirs = (mine_chip, mine_far), both(theirs, rows)
    field = bf16(f32(low[...]) + f32(low_there[...]))

    def body(core):
        for segment in range(4):
            if segment < 2:
                amp, energy = chip_amp[segment], energies[segment]
            else:
                amp, energy = f32(message[segment - 2]), neighbour_energies[segment - 2]
            change = expand(rows_of((mine, theirs)[core], segment, rows), field)
            states_ref[segment] = amp + half_step * (energy * turned(amp) + change)

    by_core(body)


def second_kernel(
    mine_chip,
    mine_far,
    theirs,
    states_ref,
    high,
    high_there,
    gate,
    weights,
    low_ref,
    high_ref,
    half_ref,
    send_ref,
):
    rows = states_ref.shape[2]
    mine, theirs = (mine_chip, mine_far), both(theirs, rows)
    field = bf16(f32(high[...]) + f32(high_there[...]))

    def body(core):
        bases = (mine, theirs) if core == 0 else (theirs, mine)
        halves = [
            states_ref[segment] + half_step * expand(rows_of(bases[1], segment, rows), field)
            for segment in range(4)
        ]
        half_ref[...] = halves[core]
        send_ref[...] = halves[1 - core]
        for half, out_ref in enumerate((low_ref, high_ref)):
            total = sum(
                project(rows_of(bases[half], segment, rows), halves[segment]) for segment in range(4)
            )
            out_ref[...] = bf16(gate[0, half] * (weights[half] * total))

    by_core(body)


def late_kernel(
    mine_chip,
    theirs,
    theirs_own,
    sent,
    low,
    high,
    my_low,
    energy,
    amp_ref,
    my_half,
    other_half,
    my_part,
    other_new,
):
    rows = amp_ref.shape[2]

    def body(core):
        my = my_kind()
        near, far = (low, high) if core == 0 else (high, low)
        change = expand(rows_of(both(sent, rows), core, rows), near[...]) + expand(
            rows_of((theirs_own,), 0, rows), far[...]
        )
        rate = energy[1 - my] * turned(other_half[...]) + change
        other_new[...] = (amp_ref[1 - my] + time_step * rate).T
        change = expand(rows_of(((mine_chip,), both(theirs, rows))[core], core, rows), my_low[...])
        my_part[...] = amp_ref[my] + time_step * (energy[my] * turned(my_half[...]) + change)

    by_core(body)


def last_kernel(
    mine_chip, theirs, high, my_part, other_new, new_tgt, new_proj, my_new, sems
):
    cols, rows = my_part.shape
    my = my_kind()
    parts = 2
    size = rows // parts
    outs = (new_tgt, new_proj.at[0])

    def copies(kind):
        return [pltpu.make_async_copy(other_new, outs[1 - kind], sems.at[parts])] + [
            pltpu.make_async_copy(
                my_new.at[pl.ds(part * size, size)], outs[kind].at[pl.ds(part * size, size)], sems.at[part]
            )
            for part in range(parts)
        ]

    def start(number):
        for kind in range(2):

            @pl.when(my == kind)
            def _():
                copies(kind)[number].start()

    def body(core):
        basis = rows_of((both(theirs, rows), (mine_chip,))[core], core, rows)
        for part in range(parts):
            states = slice(part * size, (part + 1) * size)
            change = expand([block[states] for block in basis], high[...])
            my_new[states, :] = (my_part[:, states] + time_step * change).T
            start(1 + part)

    start(0)
    by_core(body)
    for copy in copies(0):
        copy.wait()


def shards(
    tgt_basis,
    proj_basis,
    quad_weight,
    tgt_energy,
    proj_energy,
    pair_flags,
    tile_counts,
    tgt_amp,
    proj_amp,
):
    points = quad_weight.shape[0]
    rows, two_cols = tgt_amp.shape
    sizes = [lax.axis_size(axis) for axis in DEVICES]

    def call(kernel, out_shape, in_specs, scratch_shapes=(), cost=None, out_spec=VMEM):
        return pl.pallas_call(
            kernel,
            out_shape=out_shape,
            in_specs=in_specs,
            out_specs=[out_spec] * len(out_shape),
            scratch_shapes=scratch_shapes,
            cost_estimate=cost,
            compiler_params=pltpu.CompilerParams(vmem_limit_bytes=VMEM_LIMIT),
        )

    def run(kernel, out_shape, *blocks):
        return call(kernel, out_shape, [VMEM] * len(blocks))(*blocks)

    def other_core(block):
        return lax.ppermute(block, "rep", [(0, 1), (1, 0)])

    n_tgt, n_prj, n_core = sizes
    tgt_flips = [n_prj << bit for bit in range(n_tgt.bit_length() - 1)]
    prj_flips = [1 << bit for bit in range(n_prj.bit_length() - 1)]
    far_first = tgt_flips[::-1]
    flips = (prj_flips + far_first, far_first + prj_flips)
    neighbours = (prj_flips[0], far_first[0] // n_prj)
    gate_levels = (len(prj_flips) - 1, len(tgt_flips) - 1)
    n_steps = len(tgt_flips) + len(prj_flips)

    def exchanged(step, block, crossed=0):
        pairs = []
        for place in range(n_tgt * n_prj):
            for kind in range(2):
                there = place ^ flips[kind][step]
                to_core = kind ^ crossed ^ parity(there)
                pairs.append((place * n_core + (kind ^ parity(place)), there * n_core + to_core))
        return lax.ppermute(block, DEVICES, pairs)

    in_vmem = pltpu.VMEM
    sums = in_vmem((two_cols, points), jnp.bfloat16)
    segment = in_vmem((two_cols, rows), jnp.float32)

    def summed(halves, until):
        totals = []
        for half, block in enumerate(halves):
            for step in range(1, until):
                other = exchanged(step, block)
                (block,) = run(functools.partial(add_kernel, step, half), [sums], gate, block, other)
            totals.append(block)
        return totals

    def swapped(fields):
        return [other_core(block) for block in fields]

    def in_hbm(*blocks):
        return [pltpu.with_memory_space_constraint(block, pltpu.HBM) for block in blocks]

    others = swapped([tgt_amp, proj_amp])
    (amp,) = call(
        load_kernel,
        [in_vmem((2, two_cols, rows), jnp.float32)],
        [HBM] * 2,
        [
            pltpu.VMEM(tgt_amp.shape, jnp.float32),
            pltpu.VMEM(proj_amp.shape, jnp.float32),
            pltpu.SemaphoreType.DMA((2,)),
        ],
        pl.CostEstimate(
            flops=2 * 4 * rows * two_cols * points, bytes_accessed=4 * 1024 * 1024, transcendentals=0
        ),
    )(*in_hbm(tgt_amp, proj_amp))
    chip_amp, message = run(
        pack_kernel,
        [in_vmem((2, two_cols, rows), jnp.float32), in_vmem((2, two_cols, rows), jnp.bfloat16)],
        amp,
        *others,
    )
    message = exchanged(0, message)
    flags, counts = pair_flags.T, tile_counts.T
    bases = in_hbm(tgt_basis.reshape(2, -1, rows, points), proj_basis)
    pair = in_vmem((2, 2 * rows, points), jnp.bfloat16)
    sent, weight, energy = call(
        functools.partial(sent_kernel, neighbours),
        [
            in_vmem((2, 4 * rows + 2 * PIECES, points), jnp.bfloat16),
            in_vmem((1, 1, points), jnp.float32),
            in_vmem((2, 1, rows), jnp.float32),
        ],
        [HBM] * 5 + [VMEM],
        [
            pltpu.VMEM((points,), jnp.float32),
            pltpu.VMEM((rows,), jnp.float32),
            pltpu.SemaphoreType.DMA((7,)),
        ],
    )(*in_hbm(quad_weight, tgt_energy, proj_energy), *bases, chip_amp)
    mine_chip, mine_far, send_own, gate = call(
        functools.partial(side_kernel, gate_levels, neighbours),
        [
            pair,
            pair,
            in_vmem((2, rows, points), jnp.bfloat16),
            in_vmem((n_steps, 2, 1, points), jnp.float32),
        ],
        [HBM] * 4 + [VMEM],
        [
            pltpu.SMEM(flags.shape, jnp.int32),
            pltpu.SMEM(counts.shape, jnp.int32),
            pltpu.SemaphoreType.DMA((6,)),
        ],
        BEHIND,
    )(*in_hbm(flags, counts), *bases, chip_amp)
    theirs, theirs_own = swapped([sent, send_own])
    bases = (mine_chip, mine_far, theirs)
    part, weights, energies = run(
        chip_kernel,
        [
            in_vmem((2, two_cols, points), jnp.float32),
            in_vmem((2, 1, points), jnp.float32),
            in_vmem((2, 1, rows), jnp.float32),
        ],
        mine_chip,
        theirs,
        chip_amp,
        weight,
        energy,
    )
    halves = run(first_kernel, [sums] * 2, mine_far, theirs, gate, weights, part, message)
    (low, high), energies = lax.optimization_barrier((halves, energies))
    neighbour_energies = exchanged(0, energies)
    halves = low, high
    parts = summed(halves, n_steps - 1)
    low, high = [(other_core(block), exchanged(n_steps - 1, block, crossed=1)) for block in parts]
    (states,) = run(
        low_kernel,
        [in_vmem((4, two_cols, rows), jnp.float32)],
        *bases,
        *low,
        chip_amp,
        energies,
        message,
        neighbour_energies,
    )
    *halves, my_half, half_send = run(
        second_kernel,
        [sums, sums, segment, segment],
        *bases,
        states,
        *high,
        gate,
        weights,
    )
    other_half = other_core(half_send)
    fields = summed(halves, n_steps)
    low, high = swapped(fields)
    low, high = swapped(fields)
    my_part, other_new = run(
        late_kernel,
        [segment, in_vmem((rows, two_cols), jnp.float32)],
        mine_chip,
        theirs,
        theirs_own,
        sent,
        *fields,
        low,
        energy,
        amp,
        my_half,
        other_half,
    )
    return call(
        last_kernel,
        [
            jax.ShapeDtypeStruct(tgt_amp.shape, jnp.float32),
            jax.ShapeDtypeStruct(proj_amp.shape, jnp.float32),
        ],
        [VMEM] * 5,
        [pltpu.VMEM((rows, two_cols), jnp.float32), pltpu.SemaphoreType.DMA((3,))],
        out_spec=HBM,
    )(mine_chip, theirs, high, my_part, other_new)


def solution(mesh):
    in_specs = (
        P(None, "tgt", "rep"),
        P(None, None, "prj", "rep"),
        P(("bpar", "rep")),
        P(("tgt", "prj", "rep")),
        P(("tgt", "rep"), "prj"),
        P("bpar", None),
        P("bpar", None),
        P(("bpar", "tgt", "prj", "rep"), None),
        P(("bpar", "tgt", "rep"), "prj", None),
    )
    out_specs = (P(("bpar", "tgt", "prj", "rep"), None), P(("bpar", "tgt", "rep"), "prj", None))

    def step(*args):
        return tuple(shards(*args))

    return jax.shard_map(step, mesh=mesh, in_specs=in_specs, out_specs=out_specs, check_vma=False)
```

```python
import functools

import jax
import jax.numpy as jnp
from jax import lax
from jax.experimental import pallas as pl
from jax.experimental.pallas import tpu as pltpu
from jax.sharding import PartitionSpec as P

time_step = 0.4
half_step = 0.5 * time_step
VMEM_LIMIT = 8 * 1024 * 1024
DEVICES = ("tgt", "prj", "rep")
HBM = pl.BlockSpec(memory_space=pl.ANY)
VMEM = pl.BlockSpec(memory_space=pltpu.VMEM)


def parity(place):
    odd = 0
    while place:
        odd, place = odd ^ (place & 1), place >> 1
    return odd


def my_kind():
    n_tgt, n_prj = lax.axis_size("tgt"), lax.axis_size("prj")
    place = lax.axis_index("tgt") * n_prj + lax.axis_index("prj")
    kind = lax.axis_index("rep")
    for bit in range((n_tgt * n_prj).bit_length() - 1):
        kind = jnp.bitwise_xor(kind, jnp.bitwise_and(lax.shift_right_logical(place, bit), 1))
    return kind


def by_core(body):
    for core in range(2):

        @pl.when(lax.axis_index("rep") == core)
        def _():
            body(core)


def ordered(core, first, second):
    return jnp.where(core == 0, first, second), jnp.where(core == 0, second, first)


def turned(block):
    half = block.shape[0] // 2
    return jnp.concatenate([block[half:], -block[:half]], axis=0)


def bf16(block):
    return block.astype(jnp.bfloat16)


def f32(block):
    return block.astype(jnp.float32)


def rows_of(bases, segment, amount):
    start = segment % 2 * amount
    return [bases[segment // 2][part, start : start + amount, :] for part in range(2)]


def project(basis, amp):
    return jnp.dot(bf16(amp), basis[0], preferred_element_type=jnp.float32) + jnp.dot(
        bf16(turned(amp)), basis[1], preferred_element_type=jnp.float32
    )


def expand(basis, field):
    contract = (((1,), (1,)), ((), ()))
    return lax.dot_general(
        turned(field), basis[0], contract, preferred_element_type=jnp.float32
    ) + lax.dot_general(field, basis[1], contract, preferred_element_type=jnp.float32)


PIECES = 16

EVEN = pl.CostEstimate(flops=1 << 32, bytes_accessed=1 << 16, transcendentals=0)
BEHIND = pl.CostEstimate(flops=1 << 35, bytes_accessed=1 << 16, transcendentals=0)


def split(row):
    index = lax.broadcasted_iota(jnp.int32, (PIECES, row.shape[1]), 0)
    block = jnp.zeros(index.shape, jnp.float32)
    for piece in range(3):
        rounded = f32(bf16(row))
        block = jnp.where(index == piece, rounded, block)
        row = row - rounded
    return bf16(block)


def joined(block):
    pieces = f32(block)
    return pieces[0:1] + pieces[1:2] + pieces[2:3]


def both(basis, rows):
    return basis.at[:, : 2 * rows], basis.at[:, 2 * rows : 4 * rows]


def basis_copies(bases, sem, my, neighbours, sources):
    rows = sources[my].shape[2]
    place = lax.axis_index(("prj", "tgt")[my])
    copies = []
    for chip, there in enumerate((place, jnp.bitwise_xor(place, neighbours[my]))):
        for core in range(2):
            copies.append(
                pltpu.make_async_copy(
                    sources[my].at[:, 2 * there + core],
                    bases[chip].at[:, core * rows : (core + 1) * rows],
                    sem.at[2 * chip + core],
                )
            )
    return copies


def load_kernel(tgt_own_hbm, proj_own_hbm, amp_ref, tgt_own, proj_own, sems):
    pairs = [(tgt_own_hbm, tgt_own), (proj_own_hbm, proj_own)]
    copies = [pltpu.make_async_copy(src, dst, sems.at[k]) for k, (src, dst) in enumerate(pairs)]
    for copy in copies:
        copy.start()
    for copy in copies:
        copy.wait()
    amp_ref[0] = tgt_own[...].T
    amp_ref[1] = proj_own[0].T


def pack_kernel(amp_ref, tgt_other, proj_other, chip_amp, message):
    my = my_kind()
    other_amp = jnp.where(my == 0, tgt_other[...], proj_other[0]).T
    amps = ordered(lax.axis_index("rep"), amp_ref[my], other_amp)
    for segment in range(2):
        chip_amp[segment] = amps[segment]
        message[segment] = bf16(amps[segment])


def sent_kernel(
    neighbours,
    weight_hbm,
    tgt_energy_hbm,
    proj_energy_hbm,
    tgt_hbm,
    proj_hbm,
    chip_amp,
    sent,
    weight,
    energy,
    flat_weight,
    flat_energy,
    sems,
):
    my = my_kind()
    sources = (tgt_hbm, proj_hbm)
    rows = chip_amp.shape[2]

    def copies_of(kind):
        return basis_copies(both(sent, rows), sems, 1 - kind, neighbours, sources)

    pairs = [(weight_hbm, flat_weight), (tgt_energy_hbm, flat_energy), (proj_energy_hbm, energy.at[1])]
    rows_copies = [pltpu.make_async_copy(src, dst, sems.at[4 + k]) for k, (src, dst) in enumerate(pairs)]
    for copy in rows_copies:
        copy.start()
    for kind in range(2):

        @pl.when(my == kind)
        def _():
            for copy in copies_of(kind):
                copy.start()

    for copy in rows_copies:
        copy.wait()
    weight[0] = flat_weight[...][None, :]
    energy[0] = flat_energy[...][None, :]
    for part in range(2):
        sent[part, 4 * rows : 4 * rows + PIECES] = split(weight[0])
        sent[part, 4 * rows + PIECES :, :rows] = split(energy[1 - my])
    for copy in copies_of(0):
        copy.wait()


def side_kernel(
    gate_levels,
    neighbours,
    flags_hbm,
    counts_hbm,
    tgt_hbm,
    proj_hbm,
    chip_amp,
    mine_chip,
    mine_far,
    send_own,
    gate,
    flags,
    counts,
    sems,
):
    my = my_kind()
    tgt_index = lax.axis_index("tgt")
    prj_index = lax.axis_index("prj")
    sources = (tgt_hbm, proj_hbm)
    pairs = [(flags_hbm, flags), (counts_hbm, counts)]
    copies = [pltpu.make_async_copy(src, dst, sems.at[4 + k]) for k, (src, dst) in enumerate(pairs)]
    for copy in copies:
        copy.start()
    for kind in range(2):

        @pl.when(my == kind)
        def _():
            for copy in basis_copies((mine_chip, mine_far), sems, kind, neighbours, sources):
                copy.start()

    for copy in copies:
        copy.wait()
    tiles = 2
    width = gate.shape[-1] // tiles
    gate_level = jnp.where(my == 0, *gate_levels)
    for half in range(2):
        for tile in range(tiles):
            live = jnp.logical_and(
                flags[prj_index, tgt_index] > 0, tiles * half + tile < counts[prj_index, tgt_index]
            )
            value = jnp.where(live, 1.0, 0.0).astype(jnp.float32)
            for level in range(gate.shape[0]):
                here = jnp.where(level == gate_level, value, jnp.float32(1.0))
                gate[level, half, :, tile * width : (tile + 1) * width] = jnp.full(
                    (1, width), here, jnp.float32
                )
    for copy in basis_copies((mine_chip, mine_far), sems, 0, neighbours, sources):
        copy.wait()
    core = lax.axis_index("rep")
    rows = send_own.shape[1]
    for part in range(2):
        send_own[part] = mine_chip[part, pl.ds(pl.multiple_of((1 - core) * rows, rows), rows), :]


def chip_kernel(mine_chip, theirs, chip_amp, weight, energy, part_ref, weights, energies):
    rows = chip_amp.shape[2]
    near, far = (mine_chip,), both(theirs, rows)

    def body(core):
        for half, basis in enumerate((near, far) if core == 0 else (far, near)):
            part_ref[half] = sum(
                project(rows_of(basis, segment, rows), chip_amp[segment]) for segment in range(2)
            )
        weights[core] = weight[0]
        weights[1 - core] = joined(theirs[0, 4 * rows : 4 * rows + PIECES, :])
        energies[core] = energy[my_kind()]
        energies[1 - core] = joined(theirs[0, 4 * rows + PIECES :, :rows])

    by_core(body)


def first_kernel(mine_far, theirs, gate, weights, part_ref, message, *outs):
    rows = message.shape[2]
    near, far = (None, mine_far), both(theirs, rows)

    def body(core):
        for half, basis in enumerate((near, far) if core == 0 else (far, near)):
            total = part_ref[half] + sum(
                project(rows_of(basis, 2 + segment, rows), f32(message[segment]))
                for segment in range(2)
            )
            outs[half][...] = bf16(gate[0, half] * (weights[half] * total))

    by_core(body)


def add_kernel(level, half, gate, own, other, *rest):
    out_ref = rest[-1]
    out_ref[...] = bf16(gate[level, half] * (f32(own[...]) + f32(other[...])))


def low_kernel(
    mine_chip,
    mine_far,
    theirs,
    low,
    low_there,
    chip_amp,
    energies,
    message,
    neighbour_energies,
    states_ref,
):
    rows = chip_amp.shape[2]
    mine, theirs = (mine_chip, mine_far), both(theirs, rows)
    field = bf16(f32(low[...]) + f32(low_there[...]))

    def body(core):
        for segment in range(4):
            if segment < 2:
                amp, energy = chip_amp[segment], energies[segment]
            else:
                amp, energy = f32(message[segment - 2]), neighbour_energies[segment - 2]
            change = expand(rows_of((mine, theirs)[core], segment, rows), field)
            states_ref[segment] = amp + half_step * (energy * turned(amp) + change)

    by_core(body)


def second_kernel(
    mine_chip,
    mine_far,
    theirs,
    states_ref,
    high,
    high_there,
    gate,
    weights,
    low_ref,
    high_ref,
    half_ref,
    send_ref,
):
    rows = states_ref.shape[2]
    mine, theirs = (mine_chip, mine_far), both(theirs, rows)
    field = bf16(f32(high[...]) + f32(high_there[...]))

    def body(core):
        bases = (mine, theirs) if core == 0 else (theirs, mine)
        halves = [
            states_ref[segment] + half_step * expand(rows_of(bases[1], segment, rows), field)
            for segment in range(4)
        ]
        half_ref[...] = halves[core]
        send_ref[...] = halves[1 - core]
        for half, out_ref in enumerate((low_ref, high_ref)):
            total = sum(
                project(rows_of(bases[half], segment, rows), halves[segment]) for segment in range(4)
            )
            out_ref[...] = bf16(gate[0, half] * (weights[half] * total))

    by_core(body)


def late_kernel(
    mine_chip,
    theirs,
    theirs_own,
    sent,
    low,
    high,
    my_low,
    energy,
    amp_ref,
    my_half,
    other_half,
    my_part,
    other_new,
):
    rows = amp_ref.shape[2]

    def body(core):
        my = my_kind()
        near, far = (low, high) if core == 0 else (high, low)
        change = expand(rows_of(both(sent, rows), core, rows), near[...]) + expand(
            rows_of((theirs_own,), 0, rows), far[...]
        )
        rate = energy[1 - my] * turned(other_half[...]) + change
        other_new[...] = (amp_ref[1 - my] + time_step * rate).T
        change = expand(rows_of(((mine_chip,), both(theirs, rows))[core], core, rows), my_low[...])
        my_part[...] = amp_ref[my] + time_step * (energy[my] * turned(my_half[...]) + change)

    by_core(body)


def last_kernel(
    mine_chip, theirs, high, my_part, other_new, new_tgt, new_proj, my_new, sems
):
    cols, rows = my_part.shape
    my = my_kind()
    parts = 2
    size = rows // parts
    outs = (new_tgt, new_proj.at[0])

    def copies(kind):
        return [pltpu.make_async_copy(other_new, outs[1 - kind], sems.at[parts])] + [
            pltpu.make_async_copy(
                my_new.at[pl.ds(part * size, size)], outs[kind].at[pl.ds(part * size, size)], sems.at[part]
            )
            for part in range(parts)
        ]

    def start(number):
        for kind in range(2):

            @pl.when(my == kind)
            def _():
                copies(kind)[number].start()

    def body(core):
        basis = rows_of((both(theirs, rows), (mine_chip,))[core], core, rows)
        for part in range(parts):
            states = slice(part * size, (part + 1) * size)
            change = expand([block[states] for block in basis], high[...])
            my_new[states, :] = (my_part[:, states] + time_step * change).T
            start(1 + part)

    start(0)
    by_core(body)
    for copy in copies(0):
        copy.wait()


def shards(
    tgt_basis,
    proj_basis,
    quad_weight,
    tgt_energy,
    proj_energy,
    pair_flags,
    tile_counts,
    tgt_amp,
    proj_amp,
):
    points = quad_weight.shape[0]
    rows, two_cols = tgt_amp.shape
    sizes = [lax.axis_size(axis) for axis in DEVICES]

    def call(kernel, out_shape, in_specs, scratch_shapes=(), cost=None, out_spec=VMEM):
        return pl.pallas_call(
            kernel,
            out_shape=out_shape,
            in_specs=in_specs,
            out_specs=[out_spec] * len(out_shape),
            scratch_shapes=scratch_shapes,
            cost_estimate=cost,
            compiler_params=pltpu.CompilerParams(vmem_limit_bytes=VMEM_LIMIT),
        )

    def run(kernel, out_shape, *blocks):
        return call(kernel, out_shape, [VMEM] * len(blocks))(*blocks)

    def other_core(block):
        return lax.ppermute(block, "rep", [(0, 1), (1, 0)])

    n_tgt, n_prj, n_core = sizes
    tgt_flips = [n_prj << bit for bit in range(n_tgt.bit_length() - 1)]
    prj_flips = [1 << bit for bit in range(n_prj.bit_length() - 1)]
    far_first = tgt_flips[::-1]
    flips = (prj_flips + far_first, far_first + prj_flips)
    neighbours = (prj_flips[0], far_first[0] // n_prj)
    gate_levels = (len(prj_flips) - 1, len(tgt_flips) - 1)
    n_steps = len(tgt_flips) + len(prj_flips)

    def exchanged(step, block, crossed=0):
        pairs = []
        for place in range(n_tgt * n_prj):
            for kind in range(2):
                there = place ^ flips[kind][step]
                to_core = kind ^ crossed ^ parity(there)
                pairs.append((place * n_core + (kind ^ parity(place)), there * n_core + to_core))
        return lax.ppermute(block, DEVICES, pairs)

    in_vmem = pltpu.VMEM
    sums = in_vmem((two_cols, points), jnp.bfloat16)
    segment = in_vmem((two_cols, rows), jnp.float32)

    def summed(halves, until, *ahead):
        totals = []
        for half, block in enumerate(halves):
            for step in range(1, until):
                other = exchanged(step, block)
                kernel = functools.partial(add_kernel, step, half)
                blocks = [gate, block, other] + (list(ahead) if half and step == 1 else [])
                cost = EVEN if half else None
                (block,) = call(kernel, [sums], [VMEM] * len(blocks), cost=cost)(*blocks)
            totals.append(block)
        return totals

    def swapped(fields):
        return [other_core(block) for block in fields]

    def in_hbm(*blocks):
        return [pltpu.with_memory_space_constraint(block, pltpu.HBM) for block in blocks]

    others = swapped([tgt_amp, proj_amp])
    (amp,) = call(
        load_kernel,
        [in_vmem((2, two_cols, rows), jnp.float32)],
        [HBM] * 2,
        [
            pltpu.VMEM(tgt_amp.shape, jnp.float32),
            pltpu.VMEM(proj_amp.shape, jnp.float32),
            pltpu.SemaphoreType.DMA((2,)),
        ],
        pl.CostEstimate(
            flops=2 * 4 * rows * two_cols * points, bytes_accessed=4 * 1024 * 1024, transcendentals=0
        ),
    )(*in_hbm(tgt_amp, proj_amp))
    chip_amp, message = run(
        pack_kernel,
        [in_vmem((2, two_cols, rows), jnp.float32), in_vmem((2, two_cols, rows), jnp.bfloat16)],
        amp,
        *others,
    )
    message = exchanged(0, message)
    flags, counts = pair_flags.T, tile_counts.T
    bases = in_hbm(tgt_basis.reshape(2, -1, rows, points), proj_basis)
    pair = in_vmem((2, 2 * rows, points), jnp.bfloat16)
    sent, weight, energy = call(
        functools.partial(sent_kernel, neighbours),
        [
            in_vmem((2, 4 * rows + 2 * PIECES, points), jnp.bfloat16),
            in_vmem((1, 1, points), jnp.float32),
            in_vmem((2, 1, rows), jnp.float32),
        ],
        [HBM] * 5 + [VMEM],
        [
            pltpu.VMEM((points,), jnp.float32),
            pltpu.VMEM((rows,), jnp.float32),
            pltpu.SemaphoreType.DMA((7,)),
        ],
    )(*in_hbm(quad_weight, tgt_energy, proj_energy), *bases, chip_amp)
    mine_chip, mine_far, send_own, gate = call(
        functools.partial(side_kernel, gate_levels, neighbours),
        [
            pair,
            pair,
            in_vmem((2, rows, points), jnp.bfloat16),
            in_vmem((n_steps, 2, 1, points), jnp.float32),
        ],
        [HBM] * 4 + [VMEM],
        [
            pltpu.SMEM(flags.shape, jnp.int32),
            pltpu.SMEM(counts.shape, jnp.int32),
            pltpu.SemaphoreType.DMA((6,)),
        ],
        BEHIND,
    )(*in_hbm(flags, counts), *bases, chip_amp)
    theirs, theirs_own = swapped([sent, send_own])
    bases = (mine_chip, mine_far, theirs)
    part, weights, energies = run(
        chip_kernel,
        [
            in_vmem((2, two_cols, points), jnp.float32),
            in_vmem((2, 1, points), jnp.float32),
            in_vmem((2, 1, rows), jnp.float32),
        ],
        mine_chip,
        theirs,
        chip_amp,
        weight,
        energy,
    )
    halves = run(first_kernel, [sums] * 2, mine_far, theirs, gate, weights, part, message)
    (low, high), energies = lax.optimization_barrier((halves, energies))
    neighbour_energies = exchanged(0, energies)
    halves = low, high
    parts = summed(halves, n_steps - 1, neighbour_energies)
    low, high = [(other_core(block), exchanged(n_steps - 1, block, crossed=1)) for block in parts]
    (states,) = run(
        low_kernel,
        [in_vmem((4, two_cols, rows), jnp.float32)],
        *bases,
        *low,
        chip_amp,
        energies,
        message,
        neighbour_energies,
    )
    *halves, my_half, half_send = run(
        second_kernel,
        [sums, sums, segment, segment],
        *bases,
        states,
        *high,
        gate,
        weights,
    )
    fields = summed(halves, n_steps)
    fields[0], half_send = lax.optimization_barrier((fields[0], half_send))
    other_half = other_core(half_send)
    low, high = swapped(fields)
    low, high = swapped(fields)
    my_part, other_new = run(
        late_kernel,
        [segment, in_vmem((rows, two_cols), jnp.float32)],
        mine_chip,
        theirs,
        theirs_own,
        sent,
        *fields,
        low,
        energy,
        amp,
        my_half,
        other_half,
    )
    return call(
        last_kernel,
        [
            jax.ShapeDtypeStruct(tgt_amp.shape, jnp.float32),
            jax.ShapeDtypeStruct(proj_amp.shape, jnp.float32),
        ],
        [VMEM] * 5,
        [pltpu.VMEM((rows, two_cols), jnp.float32), pltpu.SemaphoreType.DMA((3,))],
        out_spec=HBM,
    )(mine_chip, theirs, high, my_part, other_new)


def solution(mesh):
    in_specs = (
        P(None, "tgt", "rep"),
        P(None, None, "prj", "rep"),
        P(("bpar", "rep")),
        P(("tgt", "prj", "rep")),
        P(("tgt", "rep"), "prj"),
        P("bpar", None),
        P("bpar", None),
        P(("bpar", "tgt", "prj", "rep"), None),
        P(("bpar", "tgt", "rep"), "prj", None),
    )
    out_specs = (P(("bpar", "tgt", "prj", "rep"), None), P(("bpar", "tgt", "rep"), "prj", None))

    def step(*args):
        return tuple(shards(*args))

    return jax.shard_map(step, mesh=mesh, in_specs=in_specs, out_specs=out_specs, check_vma=False)
```
